32 devices in a mesh: dp: 4 (over y, core), mp: 8 (over z, x).
Axes of the slice: x: 2, y: 2, z: 4, core: 2. Of those that a mesh axis runs over, the one named last changes fastest.
Arguments:
- hidden_in: bfloat16 [8, 512, 768], P('dp', 'mp'), may hold values from -6 to 6
- cotangent: bfloat16 [8, 512, 768], P('dp', 'mp'), may hold values from -6 to 6
- lengths: int32 [8], P('dp'), may hold values from 64 to 512, as said below
- teacher_attn_in: bfloat16 [768, 2304], P(('dp', 'mp')), may hold values from -0.21875 to 0.21875
- teacher_attn_out: bfloat16 [768, 768], P(None, ('dp', 'mp')), may hold values from -2.5 to 2.5
- teacher_ffn_in: bfloat16 [768, 3072], P('dp', 'mp'), may hold values from -0.21875 to 0.21875
- teacher_ffn_out: bfloat16 [3072, 768], P('mp', 'dp'), may hold values from -0.109375 to 0.109375
- teacher_shifts: bfloat16 [7680], P(('dp', 'mp')), may hold values from -3 to 3
- teacher_gains: bfloat16 [1536], P(('dp', 'mp')), may hold values from 0.25 to 1.75
- student_attn_in: bfloat16 [768, 1152], P(('dp', 'mp')), may hold values from -0.21875 to 0.21875
- student_attn_out: bfloat16 [384, 768], P(None, ('dp', 'mp')), may hold values from -3.5 to 3.5
- student_ffn_in: bfloat16 [768, 1536], P('dp', 'mp'), may hold values from -0.21875 to 0.21875
- student_ffn_out: bfloat16 [1536, 768], P('mp', 'dp'), may hold values from -0.15625 to 0.15625
- student_shifts: bfloat16 [5376], P(('dp', 'mp')), may hold values from -3 to 3
- student_gains: bfloat16 [1536], P(('dp', 'mp')), may hold values from 0.25 to 1.75
Outputs:
- out: bfloat16 [8, 512, 768], P('dp', 'mp')
- grad_hidden: float32 [8, 512, 768], P('dp', 'mp')
- grad_teacher_attn_in: float32 [768, 2304], P(('dp', 'mp'))
- grad_teacher_attn_out: float32 [768, 768], P(None, ('dp', 'mp'))
- grad_teacher_ffn_in: float32 [768, 3072], P('dp', 'mp')
- grad_teacher_ffn_out: float32 [3072, 768], P('mp', 'dp')
- grad_teacher_shifts: float32 [7680], P(('dp', 'mp'))
- grad_teacher_gains: float32 [1536], P(('dp', 'mp'))
- grad_student_attn_in: float32 [768, 1152], P(('dp', 'mp'))
- grad_student_attn_out: float32 [384, 768], P(None, ('dp', 'mp'))
- grad_student_ffn_in: float32 [768, 1536], P('dp', 'mp')
- grad_student_ffn_out: float32 [1536, 768], P('mp', 'dp')
- grad_student_shifts: float32 [5376], P(('dp', 'mp'))
- grad_student_gains: float32 [1536], P(('dp', 'mp'))
The draws below stay inside these ranges and needn't reach their ends.
Inputs may be any that keep to these rules, and one draw needn't show every extreme that they name: `lengths`: each length lies between 64 and 512; in every aligned block of 2 rows at least one row has length 512.
All inputs are finite; a program needn't handle non-finite values.
Results may differ from the reference program's by a relative error of at most 0.028.
Values may be sent and summed in bfloat16 or wider, within the bound.
A program may use at most 192 MiB of HBM per device.

```python
import jax
import jax.numpy as jnp
from jax import lax

D = 768
FF = 3072
HEADS = 12
HEAD = 64
S_HEADS = 6
FF_S = 1536
ROW_DEV = 2
ROWS = 8
SEQ = 512


def draw_lengths(key, part):
    key = jax.random.fold_in(key, 11)
    first_key, second_key = jax.random.split(key)
    base = jax.random.randint(first_key, (ROWS,), SEQ // 8, SEQ + 1)
    picked = jax.random.randint(second_key, (ROWS // ROW_DEV,), 0, ROW_DEV)
    chosen = jnp.repeat(picked, ROW_DEV, total_repeat_length=ROWS)
    full_row = jnp.arange(ROWS) % ROW_DEV == chosen
    return jnp.where(full_row, SEQ, base).astype(jnp.int32)


def levels(rng, shape, shards, low, top_value):
    level, own = 1.0, jax.random.fold_in(rng, 6)
    for axis_at, shards_of in shards:
        heights = jnp.exp(jax.random.uniform(jax.random.fold_in(own, axis_at), (shards_of,), jnp.float32, low / len(shards), top_value / len(shards)))
        level = level * jnp.repeat(heights, shape[axis_at] // shards_of).reshape([-1 if axis == axis_at else 1 for axis in range(len(shape))])
    return level


def gaussian(own_key, shape, deviation, reach, shards=(), kind=jnp.bfloat16):
    values = jax.random.normal(own_key, shape, jnp.float32) * deviation
    if len(shards) > 0:
        values = levels(own_key, shape, shards, -0.22, 0.18) * values
    return jnp.clip(values, min=-reach, max=reach).astype(kind)


def setup_inputs(seed: int = 0) -> dict:
    key_list = jax.random.split(jax.random.key(seed), 16)
    hidden_in = gaussian(key_list[0], (ROWS, SEQ, D), 1.0, 6.0, ((0, 4), (1, 8)))
    cotangent = gaussian(key_list[1], (ROWS, SEQ, D), 1.0, 6.0, ((0, 4), (1, 8)))
    lengths = draw_lengths(jax.random.fold_in(key_list[15], 71), 0)
    teacher_attn_in = gaussian(key_list[3], (D, 3 * HEADS * HEAD), D ** -0.5, 0.21875, ((0, 32),))
    teacher_attn_out = gaussian(key_list[4], (HEADS * HEAD, D), (max(1, 4 * HEADS * HEAD // SEQ)) ** -0.5, 2.5, ((1, 32),))
    teacher_ffn_in = gaussian(key_list[5], (D, FF), D ** -0.5, 0.21875, ((0, 4), (1, 8)))
    teacher_ffn_out = gaussian(key_list[6], (FF, D), FF ** -0.5, 0.109375, ((0, 8), (1, 4)))
    teacher_shifts = gaussian(key_list[7], (2 * HEADS * HEAD + 4 * D + FF,), 0.5, 3.0, ((0, 32),))
    teacher_gains = jnp.clip(1.0 + 0.15 * jax.random.normal(key_list[8], (2 * D,), jnp.float32), 0.25, 1.75).astype(jnp.bfloat16)
    student_attn_in = gaussian(key_list[9], (D, 3 * S_HEADS * HEAD), D ** -0.5, 0.21875, ((0, 32),))
    student_attn_out = gaussian(key_list[10], (S_HEADS * HEAD, D), (max(1, 4 * S_HEADS * HEAD // SEQ)) ** -0.5, 3.5, ((1, 32),))
    student_ffn_in = gaussian(key_list[11], (D, FF_S), D ** -0.5, 0.21875, ((0, 4), (1, 8)))
    student_ffn_out = gaussian(key_list[12], (FF_S, D), FF_S ** -0.5, 0.15625, ((0, 8), (1, 4)))
    student_shifts = gaussian(key_list[13], (2 * S_HEADS * HEAD + 4 * D + FF_S,), 0.5, 3.0, ((0, 32),))
    student_gains = jnp.clip(1.0 + 0.15 * jax.random.normal(key_list[14], (2 * D,), jnp.float32), 0.25, 1.75).astype(jnp.bfloat16)
    return dict(hidden_in=hidden_in, cotangent=cotangent, lengths=lengths, teacher_attn_in=teacher_attn_in, teacher_attn_out=teacher_attn_out, teacher_ffn_in=teacher_ffn_in, teacher_ffn_out=teacher_ffn_out, teacher_shifts=teacher_shifts, teacher_gains=teacher_gains, student_attn_in=student_attn_in, student_attn_out=student_attn_out, student_ffn_in=student_ffn_in, student_ffn_out=student_ffn_out, student_shifts=student_shifts, student_gains=student_gains)


EPSILON = 1e-06
NEGATIVE = -1e+30
HIGHEST = lax.Precision.HIGHEST

@jax.custom_vjp
def low(v):
    return lax.optimization_barrier(v.astype(jnp.bfloat16)).astype(jnp.float32)

@jax.custom_vjp
def low_back(v):
    return v

def low_keep(v):
    return (low(v), None)

def low_pass(kept, grad):
    return (grad,)

def back_keep(v):
    return (v, None)

def back_low(kept, grad):
    return (low(grad),)
low.defvjp(low_keep, low_pass)
low_back.defvjp(back_keep, back_low)

def layer_norm(values, gain, shift):
    centered = values - lax.optimization_barrier(jnp.mean(values, axis=-1, keepdims=True))
    variance = lax.optimization_barrier(jnp.mean(centered * centered, axis=-1, keepdims=True))
    return centered * lax.rsqrt(variance + EPSILON) * gain + shift

def split_shifts(shifts, head_width, model_width, hidden_width):
    spans_list = [head_width, head_width, model_width, model_width, hidden_width, model_width, model_width]
    pieces = []
    offset = 0
    for length in spans_list:
        pieces.append(shifts[offset:offset + length])
        offset = offset + length
    return pieces

def attend_row(queries, all_keys, values, valid_keys):
    seg_len, head_width = queries.shape
    head_count = head_width // HEAD
    query_heads = queries.reshape(seg_len, head_count, HEAD)
    key_heads = all_keys.reshape(all_keys.shape[0], head_count, HEAD)
    value_heads = values.reshape(values.shape[0], head_count, HEAD)
    raw = jnp.einsum('qhd,khd->hqk', query_heads, key_heads, precision=HIGHEST)
    scores = jnp.where(valid_keys[None, None, :], low_back(raw) * 0.125, NEGATIVE)
    row_max = lax.optimization_barrier(jnp.max(scores, axis=-1, keepdims=True))
    exponent = jnp.exp(scores - row_max)
    weights = exponent / lax.optimization_barrier(jnp.sum(exponent, axis=-1, keepdims=True))
    mixed = jnp.einsum('hqk,khd->qhd', low(weights), value_heads, precision=HIGHEST)
    return low(low_back(mixed.reshape(seg_len, head_width)))

def row_step(packed):
    queries, all_keys, values, valid_keys = packed
    return jax.checkpoint(attend_row)(queries, all_keys, values, valid_keys)

def layer(hidden, attn_in, attn_out, ffn_in, ffn_out, shifts, gains, valid_keys):
    model_width = hidden.shape[-1]
    head_width = attn_in.shape[1] // 3
    hidden_width = ffn_in.shape[1]
    pieces = split_shifts(shifts, head_width, model_width, hidden_width)
    bias_query, bias_value, bias_output, shift_one, bias_up, bias_down, shift_two = pieces
    projected = jnp.einsum('rsd,de->rse', low(hidden), attn_in, precision=HIGHEST)
    queries = low(low_back(projected[..., :head_width] + bias_query))
    all_keys = low(low_back(projected[..., head_width:2 * head_width]))
    values = low(low_back(projected[..., 2 * head_width:] + bias_value))
    context = lax.map(row_step, (queries, all_keys, values, valid_keys))
    branch = low_back(jnp.einsum('rsh,hd->rsd', context, attn_out, precision=HIGHEST) + bias_output)
    normed_one = layer_norm(hidden + branch, gains[:model_width], shift_one)
    pre_act = low_back(jnp.einsum('rsd,df->rsf', low(normed_one), ffn_in, precision=HIGHEST) + bias_up)
    activated = low(jax.nn.gelu(pre_act, approximate=False))
    ffn_down = low_back(jnp.einsum('rsf,fd->rsd', activated, ffn_out, precision=HIGHEST) + bias_down)
    return layer_norm(normed_one + ffn_down, gains[model_width:], shift_two)

def reference(hidden_in, cotangent, lengths, teacher_attn_in, teacher_attn_out, teacher_ffn_in, teacher_ffn_out, teacher_shifts, teacher_gains, student_attn_in, student_attn_out, student_ffn_in, student_ffn_out, student_shifts, student_gains):
    positions = jnp.arange(SEQ).astype(jnp.int32)
    valid_keys = positions[None, :] < lengths[:, None]
    params = tuple((weight.astype(jnp.float32) for weight in (teacher_attn_in, teacher_attn_out, teacher_ffn_in, teacher_ffn_out, teacher_shifts, teacher_gains, student_attn_in, student_attn_out, student_ffn_in, student_ffn_out, student_shifts, student_gains)))

    def forward(hidden, *layer_params):
        middle = layer(hidden, *layer_params[:6], valid_keys)
        return layer(middle, *layer_params[6:], valid_keys)
    result, pullback = jax.vjp(forward, hidden_in.astype(jnp.float32), *params)
    grads = pullback(cotangent.astype(jnp.float32))
    return (result.astype(jnp.bfloat16), grads[0], grads[1], grads[2], grads[3], grads[4], grads[5], grads[6], grads[7], grads[8], grads[9], grads[10], grads[11], grads[12])
```

```python
import functools
import types

import jax
import jax.numpy as jnp
from jax import lax
from jax.experimental import pallas as pl
from jax.experimental.pallas import tpu as pltpu
from jax.sharding import PartitionSpec as P

HEAD = 64


EPSILON = 1e-06
NEGATIVE = -1e30


def layer_norm(values, gain, shift):
    centered = values - jnp.mean(values, axis=-1, keepdims=True)
    variance = jnp.mean(centered * centered, axis=-1, keepdims=True)
    return centered * lax.rsqrt(variance + EPSILON) * gain + shift


def smooth_gate(pre_act):
    return jax.nn.gelu(pre_act, approximate=False)


def split_shifts(shifts, head_width, model_width, hidden_width):
    spans_list = [
        head_width,
        head_width,
        model_width,
        model_width,
        hidden_width,
        model_width,
        model_width,
    ]
    pieces = []
    offset = 0
    for length in spans_list:
        pieces.append(shifts[offset : offset + length])
        offset = offset + length
    return pieces


def to_heads(values):
    return values.reshape(values.shape[0], values.shape[1], values.shape[2] // HEAD, HEAD)


def score_block(queries, all_keys, valid_keys):
    raw = jnp.einsum(
        "rqhd,rkhd->rhqk", to_heads(queries), to_heads(all_keys), preferred_element_type=jnp.float32
    )
    return jnp.where(valid_keys[:, None, None, :], raw * 0.125, NEGATIVE)


def fetch(attn_in, attn_out, ffn_in, ffn_out, shifts, gains):
    whole_in, whole_out, whole_shifts, whole_gains = (
        lax.all_gather(attn_in, ("dp", "mp"), axis=0, tiled=True),
        lax.all_gather(attn_out, ("dp", "mp"), axis=1, tiled=True),
        lax.all_gather(shifts, ("dp", "mp"), axis=0, tiled=True),
        lax.all_gather(gains, ("dp", "mp"), axis=0, tiled=True),
    )
    ffn_first, ffn_second = (
        lax.all_gather(ffn_in, "dp", axis=0, tiled=True),
        lax.all_gather(ffn_out, "dp", axis=1, tiled=True),
    )
    return (
        whole_in,
        whole_out,
        ffn_first,
        ffn_second,
        whole_shifts.astype(jnp.float32),
        whole_gains.astype(jnp.float32),
    )


def forward_layer(hidden, params, valid_keys):
    attn_in, attn_out, ffn_first, ffn_second, shifts, gains = params
    model_width = hidden.shape[-1]
    head_width = attn_in.shape[1] // 3
    hidden_width = shifts.shape[0] - 2 * head_width - 4 * model_width
    pieces = split_shifts(shifts, head_width, model_width, hidden_width)
    bias_query, bias_value, bias_output, shift_one, bias_up, bias_down, shift_two = pieces
    hidden_low = hidden.astype(jnp.bfloat16)
    projected = jnp.einsum("rsd,de->rse", hidden_low, attn_in, preferred_element_type=jnp.float32)
    queries = (projected[..., :head_width] + bias_query).astype(jnp.bfloat16)
    local_keys = projected[..., head_width : 2 * head_width].astype(jnp.bfloat16)
    local_values = (projected[..., 2 * head_width :] + bias_value).astype(jnp.bfloat16)
    all_keys, all_values = (
        lax.all_gather(local_keys, "mp", axis=1, tiled=True),
        lax.all_gather(local_values, "mp", axis=1, tiled=True),
    )
    scores = score_block(queries, all_keys, valid_keys)
    row_max = jnp.max(scores, axis=-1, keepdims=True)
    exponent = jnp.exp(scores - row_max)
    row_total = jnp.sum(exponent, axis=-1, keepdims=True)
    log_total = row_max + jnp.log(row_total)
    weights_low = (exponent / row_total).astype(jnp.bfloat16)
    mixed = jnp.einsum(
        "rhqk,rkhd->rqhd", weights_low, to_heads(all_values), preferred_element_type=jnp.float32
    )
    context = mixed.reshape(queries.shape).astype(jnp.bfloat16)
    branch = (
        jnp.einsum("rsh,hd->rsd", context, attn_out, preferred_element_type=jnp.float32)
        + bias_output
    )
    summed_one = hidden + branch
    normed_one = layer_norm(summed_one, gains[:model_width], shift_one)
    normed_low = normed_one.astype(jnp.bfloat16)
    ffn_tokens = lax.all_gather(normed_low, "mp", axis=1, tiled=True)
    local_hidden = ffn_first.shape[1]
    bias_part = lax.dynamic_slice_in_dim(bias_up, lax.axis_index("mp") * local_hidden, local_hidden)
    pre_act = (
        jnp.einsum("rsd,df->rsf", ffn_tokens, ffn_first, preferred_element_type=jnp.float32)
        + bias_part
    )
    act_low = smooth_gate(pre_act).astype(jnp.bfloat16)
    down_terms = jnp.einsum("rsf,fd->rsd", act_low, ffn_second, preferred_element_type=jnp.float32)
    ffn_down = lax.psum_scatter(
        down_terms.astype(jnp.bfloat16), "mp", scatter_dimension=1, tiled=True
    ).astype(jnp.float32)
    summed_two = normed_one + ffn_down + bias_down
    result = layer_norm(summed_two, gains[model_width:], shift_two)
    key_store = (all_keys, all_values)
    kept = (
        hidden_low,
        queries,
        key_store,
        log_total,
        context,
        summed_one,
        ffn_tokens,
        pre_act,
        act_low,
        summed_two,
    )
    return (result, kept)


def backward_layer(grad_out, kept, params, valid_keys):
    attn_in, attn_out, ffn_first, ffn_second, shifts, gains = params
    (
        hidden_low,
        queries,
        key_store,
        log_total,
        context,
        summed_one,
        ffn_tokens,
        pre_act,
        act_low,
        summed_two,
    ) = kept
    model_width = summed_one.shape[-1]
    head_width = attn_in.shape[1] // 3
    hidden_width = shifts.shape[0] - 2 * head_width - 4 * model_width
    pieces = split_shifts(shifts, head_width, model_width, hidden_width)
    bias_query, bias_value, bias_output, shift_one, bias_up, bias_down, shift_two = pieces
    sum_axes = (0, 1)
    unused_two, norm_two_back = jax.vjp(layer_norm, summed_two, gains[model_width:], shift_two)
    grad_two, grad_gain_two, grad_shift_two = norm_two_back(grad_out)
    grad_down = grad_two.astype(jnp.bfloat16)
    grad_bias_down = jnp.sum(grad_down.astype(jnp.float32), axis=sum_axes)
    grad_tokens = lax.all_gather(grad_down, "mp", axis=1, tiled=True)
    grad_act = jnp.einsum(
        "rsd,fd->rsf", grad_tokens, ffn_second, preferred_element_type=jnp.float32
    )
    grad_second = jnp.einsum(
        "rsf,rsd->fd", act_low, grad_tokens, preferred_element_type=jnp.float32
    )
    unused_gate, gate_back = jax.vjp(smooth_gate, pre_act)
    grad_pre = gate_back(grad_act)[0].astype(jnp.bfloat16)
    grad_bias_part = jnp.sum(grad_pre.astype(jnp.float32), axis=sum_axes)
    grad_first = jnp.einsum("rsd,rsf->df", ffn_tokens, grad_pre, preferred_element_type=jnp.float32)
    back_terms = jnp.einsum("rsf,df->rsd", grad_pre, ffn_first, preferred_element_type=jnp.float32)
    grad_normed = lax.psum_scatter(
        back_terms.astype(jnp.bfloat16), "mp", scatter_dimension=1, tiled=True
    ).astype(jnp.float32)
    blank_bias = jnp.zeros((hidden_width,), jnp.float32)
    grad_bias_up = lax.dynamic_update_slice_in_dim(
        blank_bias, grad_bias_part, lax.axis_index("mp") * ffn_first.shape[1], 0
    )
    grad_normed = grad_normed + grad_two
    unused_one, norm_one_back = jax.vjp(layer_norm, summed_one, gains[:model_width], shift_one)
    grad_one, grad_gain_one, grad_shift_one = norm_one_back(grad_normed)
    grad_branch = grad_one.astype(jnp.bfloat16)
    grad_bias_output = jnp.sum(grad_branch.astype(jnp.float32), axis=sum_axes)
    grad_attn_out = jnp.einsum(
        "rsh,rsd->hd", context, grad_branch, preferred_element_type=jnp.float32
    )
    grad_context = jnp.einsum(
        "rsd,hd->rsh", grad_branch, attn_out, preferred_element_type=jnp.float32
    ).astype(jnp.bfloat16)
    stored_keys, stored_values = key_store
    all_keys, all_values = (stored_keys, stored_values)
    weights = jnp.exp(score_block(queries, all_keys, valid_keys) - log_total)
    context_heads = to_heads(grad_context)
    grad_weights = jnp.einsum(
        "rqhd,rkhd->rhqk", context_heads, to_heads(all_values), preferred_element_type=jnp.float32
    )
    inner_sum = jnp.sum(weights * grad_weights, axis=-1, keepdims=True)
    grad_raw = (0.125 * weights * (grad_weights - inner_sum)).astype(jnp.bfloat16)
    grad_queries = jnp.einsum(
        "rhqk,rkhd->rqhd", grad_raw, to_heads(all_keys), preferred_element_type=jnp.float32
    )
    grad_queries = grad_queries.reshape(queries.shape).astype(jnp.bfloat16)
    weights_low = weights.astype(jnp.bfloat16)
    value_terms = jnp.einsum(
        "rhqk,rqhd->rkhd", weights_low, context_heads, preferred_element_type=jnp.float32
    )
    key_terms = jnp.einsum(
        "rhqk,rqhd->rkhd", grad_raw, to_heads(queries), preferred_element_type=jnp.float32
    )
    key_terms = key_terms.reshape(all_keys.shape)
    value_terms = value_terms.reshape(all_values.shape)
    grad_keys, grad_values = (
        lax.psum_scatter(
            key_terms.astype(jnp.bfloat16), "mp", scatter_dimension=1, tiled=True
        ).astype(jnp.float32),
        lax.psum_scatter(
            value_terms.astype(jnp.bfloat16), "mp", scatter_dimension=1, tiled=True
        ).astype(jnp.float32),
    )
    grad_values_low = grad_values.astype(jnp.bfloat16)
    grad_projected = jnp.concatenate(
        [grad_queries, grad_keys.astype(jnp.bfloat16), grad_values_low], axis=-1
    )
    grad_attn_in = jnp.einsum(
        "rsd,rse->de", hidden_low, grad_projected, preferred_element_type=jnp.float32
    )
    grad_hidden = grad_one + jnp.einsum(
        "rse,de->rsd", grad_projected, attn_in, preferred_element_type=jnp.float32
    )
    grad_bias_query = jnp.sum(grad_queries.astype(jnp.float32), axis=sum_axes)
    grad_bias_value = jnp.sum(grad_values_low.astype(jnp.float32), axis=sum_axes)
    grad_shifts = jnp.concatenate(
        [
            grad_bias_query,
            grad_bias_value,
            grad_bias_output,
            grad_shift_one,
            grad_bias_up,
            grad_bias_down,
            grad_shift_two,
        ]
    )
    grad_gains = jnp.concatenate([grad_gain_one, grad_gain_two])
    return (
        grad_hidden,
        (grad_attn_in, grad_attn_out, grad_first, grad_second, grad_shifts, grad_gains),
    )


def reduce_grads(grads):
    grad_attn_in, grad_attn_out, grad_first, grad_second, grad_shifts, grad_gains = grads
    total_in, total_out, total_shifts, total_gains = (
        lax.psum_scatter(grad_attn_in, ("dp", "mp"), scatter_dimension=0, tiled=True),
        lax.psum_scatter(grad_attn_out, ("dp", "mp"), scatter_dimension=1, tiled=True),
        lax.psum_scatter(grad_shifts, ("dp", "mp"), scatter_dimension=0, tiled=True),
        lax.psum_scatter(grad_gains, ("dp", "mp"), scatter_dimension=0, tiled=True),
    )
    total_first, total_second = (
        lax.psum_scatter(
            grad_first.astype(jnp.bfloat16), "dp", scatter_dimension=0, tiled=True
        ).astype(jnp.float32),
        lax.psum_scatter(
            grad_second.astype(jnp.bfloat16), "dp", scatter_dimension=1, tiled=True
        ).astype(jnp.float32),
    )
    return (total_in, total_out, total_first, total_second, total_shifts, total_gains)


BF = jnp.bfloat16
F32 = jnp.float32
MESH = pl.DeviceIdType.MESH
SIDE = 2
DEPTH = 4
PARTNERS = 9


def mm(left, right, left_dim, right_dim):
    return lax.dot_general(
        left, right, (((left_dim,), (right_dim,)), ((), ())), preferred_element_type=F32
    )


def rowsum(values):
    return jnp.sum(values, axis=0, keepdims=True)


def normalize(values):
    centered = values - jnp.mean(values, axis=-1, keepdims=True)
    variance = jnp.mean(centered * centered, axis=-1, keepdims=True)
    scale = lax.rsqrt(variance + EPSILON)
    return centered * scale, scale


def normalize_back(grad, normed, scale):
    along = jnp.mean(grad * normed, axis=-1, keepdims=True)
    return scale * (grad - jnp.mean(grad, axis=-1, keepdims=True) - normed * along)


def layer_sizes(model, heads_width, hidden):
    half = heads_width // 2
    start = 3 * half // 128 * 128
    return types.SimpleNamespace(
        hc=half,
        heads=half // HEAD,
        wide=4 * half,
        start=start,
        pad=3 * half - start,
        nr=hidden // 16,
        nc=hidden // 2,
        zb=model * 8 // hidden,
    )


def vec_rows(model, sizes):
    rows, at = {}, 0
    for name, length in (
        ("qv", 4 * sizes.hc),
        ("bo", model),
        ("beta1", model),
        ("b1", 2 * sizes.nc),
        ("b2", model),
        ("beta2", model),
        ("g1", model),
        ("g2", model),
    ):
        rows[name] = at
        at += length // model
    return rows, at


def fused_kernel(dims, names, *refs):
    r = types.SimpleNamespace(**dict(zip(names, refs)))
    model, tok, seq, layers = dims.model, dims.tok, dims.seq, dims.layers
    half_lanes = model // 2
    dp, mp = lax.axis_index("dp"), lax.axis_index("mp")
    y, c = dp // SIDE, lax.rem(dp, SIDE)
    z, x = mp // SIDE, lax.rem(mp, SIDE)

    def device(c, x, y, z):
        return {"dp": y * SIDE + c, "mp": z * SIDE + x}

    sib = device(1 - c, x, y, z)
    xn, yn = device(c, 1 - x, y, z), device(c, x, 1 - y, z)
    zdev = [device(c, x, y, lax.rem(z + d, DEPTH)) for d in range(1, DEPTH)]
    zpair = z + 1 - 2 * lax.rem(z, 2)
    zn = device(c, x, y, zpair)
    zfar = device(c, x, y, lax.rem(z + 2, DEPTH))

    bar = pltpu.get_barrier_semaphore()
    for step in range(1, DEPTH * SIDE):
        other = lax.rem(mp + step, DEPTH * SIDE)
        pl.semaphore_signal(bar, inc=1, device_id={"dp": dp, "mp": other}, device_id_type=MESH)
    pl.semaphore_signal(bar, inc=1, device_id=sib, device_id_type=MESH)
    pl.semaphore_signal(bar, inc=1, device_id=yn, device_id_type=MESH)
    pl.semaphore_wait(bar, PARTNERS)

    sent = []

    def remote(src, dst, send, recv, dev):
        return pltpu.make_async_remote_copy(
            src_ref=src, dst_ref=dst, send_sem=send, recv_sem=recv, device_id=dev, device_id_type=MESH
        )

    def push(src, dst, send, recv, dev):
        copy = remote(src, dst, send, recv, dev)
        copy.start()
        sent.append(copy)

    def arrived(dst, recv, send):
        remote(dst, dst, send, recv, sib).wait_recv()

    row_core = z // 2
    mine = c == row_core
    half = lax.rem(z, 2)

    def spread(src, land, sends, recvs):
        block = 2 * lax.rem(z, 2) + x
        target = 2 * c + z // 2
        for j in range(2):
            local = (x == j) & (z == target)
            copy = remote(src.at[j], land.at[block], sends.at[j], recvs.at[block], device(c, j, y, target))
            pl.when(local)(pltpu.make_async_copy(src.at[j], land.at[block], recvs.at[block]).start)
            pl.when(jnp.logical_not(local))(copy.start)

    def spread_done(src, land, sends, recvs, on_chip_send, on_chip_recv):
        target = 2 * c + z // 2
        for j in range(2):
            local = (x == j) & (z == target)
            copy = remote(src.at[j], land.at[0], sends.at[j], recvs.at[0], sib)
            pl.when(jnp.logical_not(local))(copy.wait_send)
        whole = remote(land, land, on_chip_send, on_chip_recv, sib)

        @pl.when(mine)
        def _():
            for block in range(4):
                arrived(land.at[block], recvs.at[block], sends.at[0])
            whole.start()
            whole.wait_send()

        @pl.when(jnp.logical_not(mine))
        def _():
            whole.wait_recv()

    def collect(src, land, sends, recvs):
        @pl.when(mine)
        def _():
            for block in range(4):
                z_to, x_to = 2 * half + block // 2, block % 2
                local = (x == x_to) & (z == z_to)
                slot = land.at[x]
                copy = remote(
                    src.at[block], slot, sends.at[block], recvs.at[x], device(c, x_to, y, z_to)
                )
                pl.when(local)(pltpu.make_async_copy(src.at[block], slot, recvs.at[x]).start)
                pl.when(jnp.logical_not(local))(copy.start)

    def collect_done(src, land, sends, recvs):
        for j in range(2):
            arrived(land.at[j], recvs.at[j], sends.at[0])

        @pl.when(mine)
        def _():
            for block in range(4):
                z_to, x_to = 2 * half + block // 2, block % 2
                local = (x == x_to) & (z == z_to)
                copy = remote(src.at[block], src.at[block], sends.at[block], recvs.at[0], sib)
                pl.when(jnp.logical_not(local))(copy.wait_send)

    chunks = dims.chunks

    def unit(i, grads, z_slice, x_at, y_at):
        kind, layer, which, part = chunks[i]
        if kind == "A":
            ref = r.ga0 if layer == 0 else r.ga1
            return ref.at[y_at, z_slice, x_at, :, pl.ds(part * model, model)]
        ref = (r.dw0, r.dw1)[layer] if grads else (r.w0, r.w1)[layer]
        lanes = pl.ds(pl.multiple_of(y_at * half_lanes, 128), half_lanes)
        return ref.at[which, z_slice, x_at, pl.ds(part * dims.rows, dims.rows), lanes]

    every, first, second = pl.ds(0, DEPTH), pl.ds(0, 2), pl.ds(2, 2)

    def gather_z(i):
        own = unit(i, False, pl.ds(z, 1), x, y)
        for d in range(1, DEPTH):
            push(own, own, r.gs.at[i, d - 1], r.gr.at[i, d - 1], zdev[d - 1])

    def gather_xy(i):
        for d in range(1, DEPTH):
            got = unit(i, False, pl.ds(lax.rem(z + DEPTH - d, DEPTH), 1), x, y)
            arrived(got, r.gr.at[i, d - 1], r.gs.at[i, d - 1])
        own = unit(i, False, every, x, y)
        push(own, own, r.gs.at[i, 3], r.gr.at[i, 3], xn)
        push(own, own, r.gs.at[i, 4], r.gr.at[i, 4], yn)

    def gather_on(i):
        arrived(unit(i, False, every, 1 - x, y), r.gr.at[i, 3], r.gs.at[i, 3])
        arrived(unit(i, False, every, x, 1 - y), r.gr.at[i, 4], r.gs.at[i, 4])
        over_x = unit(i, False, first, x, 1 - y)
        over_y = unit(i, False, second, 1 - x, y)
        push(over_x, over_x, r.gs.at[i, 5], r.gr.at[i, 5], xn)
        push(over_y, over_y, r.gs.at[i, 6], r.gr.at[i, 6], yn)

    def gather_end(i):
        arrived(unit(i, False, first, 1 - x, 1 - y), r.gr.at[i, 5], r.gs.at[i, 5])
        arrived(unit(i, False, second, 1 - x, 1 - y), r.gr.at[i, 6], r.gs.at[i, 6])

    def slots(i):
        kind, layer, which, part = chunks[i]
        at = dims.slot[i]
        if kind == "A":
            return r.raa.at[at], r.rba.at[at], r.rca.at[at]
        return r.raf.at[at], r.rbf.at[at], r.rcf.at[at]

    def add_into(ref, extra):
        total = ref[...].astype(F32)
        for more in extra:
            total = total + more[...].astype(F32)
        ref[...] = total.astype(BF)

    def reduce_a(i):
        ra, rb, rc = slots(i)
        push(unit(i, True, first, 1 - x, 1 - y), ra.at[0], r.ss.at[i, 5], r.sr.at[i, 5], xn)
        push(unit(i, True, second, 1 - x, 1 - y), ra.at[1], r.ss.at[i, 6], r.sr.at[i, 6], yn)

    def reduce_b(i):
        ra, rb, rc = slots(i)
        arrived(ra.at[0], r.sr.at[i, 5], r.ss.at[i, 5])
        add_into(unit(i, True, first, x, 1 - y), [ra.at[0]])
        arrived(ra.at[1], r.sr.at[i, 6], r.ss.at[i, 6])
        add_into(unit(i, True, second, 1 - x, y), [ra.at[1]])
        push(unit(i, True, every, 1 - x, y), rb.at[0], r.ss.at[i, 3], r.sr.at[i, 3], xn)
        push(unit(i, True, every, x, 1 - y), rb.at[1], r.ss.at[i, 4], r.sr.at[i, 4], yn)

    def reduce_c(i):
        ra, rb, rc = slots(i)
        arrived(rb.at[0], r.sr.at[i, 3], r.ss.at[i, 3])
        arrived(rb.at[1], r.sr.at[i, 4], r.ss.at[i, 4])
        add_into(unit(i, True, every, x, y), [rb.at[0], rb.at[1]])
        for d in range(1, DEPTH):
            src = unit(i, True, pl.ds(lax.rem(z + d, DEPTH), 1), x, y)
            push(src, rc.at[pl.ds(d - 1, 1)], r.ss.at[i, d - 1], r.sr.at[i, d - 1], zdev[d - 1])

    def reduce_end(i):
        kind, layer, which, part = chunks[i]
        at = dims.slot[i]
        ra, rb, rc = slots(i)
        total = unit(i, True, pl.ds(z, 1), x, y)[...].astype(F32)[0]
        for d in range(1, DEPTH):
            arrived(rc.at[pl.ds(d - 1, 1)], r.sr.at[i, d - 1], r.ss.at[i, d - 1])
            total = total + rc[d - 1].astype(F32)
        if kind == "A":
            out = (r.da0, r.da1)[layer]
            rows = total.shape[0] // 2
            out[c, :, part * model : (part + 1) * model] = jnp.where(c == 0, total[:rows], total[rows:])
            r.fsa[at] = jnp.where(c == 0, total[rows:], total[:rows])
            push(r.fsa.at[at], r.fra.at[at], r.fs.at[i], r.fr.at[i], sib)
        else:
            out = (r.df0, r.df1)[layer]
            rows = pl.ds(part * dims.rows, dims.rows)
            out[c, which, rows, :] = total
            push(out.at[c, which, rows, :], r.frf.at[at], r.fs.at[i], r.fr.at[i], sib)

    def reduce_out(i):
        kind, layer, which, part = chunks[i]
        at = dims.slot[i]
        if kind == "A":
            arrived(r.fra.at[at], r.fr.at[i], r.fs.at[i])
            (r.da0, r.da1)[layer][1 - c, :, part * model : (part + 1) * model] = r.fra[at]
        else:
            arrived(r.frf.at[at], r.fr.at[i], r.fs.at[i])
            rows = pl.ds(part * dims.rows, dims.rows)
            (r.df0, r.df1)[layer][1 - c, which, rows, :] = r.frf[at]

    def total_step(work, land, step, sends, recvs):
        dev = (sib, xn, yn, zn, zfar)[step]
        push(work.at[step], land.at[step], sends.at[step], recvs.at[step], dev)

    def total_add(work, land, step, sends, recvs):
        arrived(land.at[step], recvs.at[step], sends.at[step])
        work[step + 1] = work[step] + land[step]

    exchanges = []

    def exchange(part):
        slot = len(exchanges) % 2
        r.xs[slot] = part.astype(BF)
        copy = remote(r.xs.at[slot], r.xr.at[slot], r.es.at[slot], r.er.at[slot], sib)
        copy.start()
        exchanges.append(copy)

        def finish():
            copy.wait()
            return r.xs[slot].astype(F32) + r.xr[slot].astype(F32)

        return finish

    def vec_row(row):
        return r.vw[5, row : row + 1, :]

    def layer_vecs(at):
        sizes, rows, base = layers[at], dims.rows_of[at], dims.base[at]
        if sizes.hc * 2 == model:
            qv = r.vw[5, pl.ds(base + rows["qv"] + c, 1), :]
        else:
            both = vec_row(base + rows["qv"])
            qv = jnp.where(c == 0, both[:, : 2 * sizes.hc], both[:, 2 * sizes.hc :])
        span = sizes.nc // model
        b1 = [r.vw[5, pl.ds(base + rows["b1"] + c * span + s, 1), :] for s in range(span)]
        found = types.SimpleNamespace(bq=qv[:, : sizes.hc], bv=qv[:, sizes.hc :], b1=b1)
        for name in ("bo", "beta1", "b2", "beta2", "g1", "g2"):
            setattr(found, name, vec_row(base + rows[name]))
        return found

    kept = [
        types.SimpleNamespace(
            **{
                name: getattr(r, f"{name}{at}")
                for name in ("xb", "q", "kv", "a", "ctx", "n1", "s1", "hb", "g", "gp", "n2", "s2")
            }
        )
        for at in range(2)
    ]
    wa = (r.wa0, r.wa1)
    weights = (r.w0, r.w1)

    def order_rows(at, part):
        gathered, whole = (r.ga0, r.ga1)[at], wa[at]
        cols = slice(part * model, (part + 1) * model)
        rows = gathered.shape[3] // 2
        span = DEPTH * 2 * rows
        for y_at in range(SIDE):
            for z_at in range(DEPTH):
                left = gathered[y_at, z_at, 0, :, cols].astype(F32)
                right = gathered[y_at, z_at, 1, :, cols].astype(F32)
                for core in range(SIDE):
                    own = slice(core * rows, (core + 1) * rows)
                    both = jnp.concatenate([left[own], right[own]], axis=0).astype(BF)
                    begin = (y_at * SIDE + core) * span + z_at * 2 * rows
                    whole[begin : begin + 2 * rows, cols] = both

    def store_grad_rows(at, y_at, value, cols):
        blocks = (r.ga0, r.ga1)[at]
        rows = blocks.shape[3] // 2
        span = DEPTH * 2 * rows
        for z_at in range(DEPTH):
            for x_at in range(SIDE):
                begin = (z_at * 2 + x_at) * rows
                both = [value[begin : begin + rows], value[span + begin : span + begin + rows]]
                blocks[y_at, z_at, x_at, :, cols] = jnp.concatenate(both, axis=0).astype(BF)

    def send_kv(at):
        kv = kept[at].kv
        push(kv.at[half], kv.at[half], r.ks.at[at], r.kr.at[at], zn)

    def wait_kv(at):
        kv = kept[at].kv
        arrived(kv.at[1 - half], r.kr.at[at], r.ks.at[at])

    def head_kv(at, h):
        sizes, kv = layers[at], kept[at].kv
        k = kv[:, :, h * HEAD : (h + 1) * HEAD].reshape(seq, HEAD)
        v = kv[:, :, sizes.hc + h * HEAD : sizes.hc + (h + 1) * HEAD].reshape(seq, HEAD)
        return k, v

    def attention(at):
        sizes, keep = layers[at], kept[at]
        lane = lax.broadcasted_iota(jnp.int32, (1, model), 1)
        row = (y * SIDE + row_core) * 2 + x
        length = jnp.sum(jnp.where(lane == row, vec_row(dims.length_row), 0.0), axis=1, keepdims=True)
        valid = lax.broadcasted_iota(jnp.int32, (1, seq), 1).astype(F32) < length
        for h in range(sizes.heads):
            q = keep.q[:, h * HEAD : (h + 1) * HEAD]
            k, v = head_kv(at, h)
            scores = jnp.where(valid, mm(q, k, 1, 1) * 0.125, NEGATIVE)
            exponent = jnp.exp(scores - jnp.max(scores, axis=1, keepdims=True))
            low = (exponent / jnp.sum(exponent, axis=1, keepdims=True)).astype(BF)
            keep.a[h] = low
            begin = sizes.pad + h * HEAD
            keep.ctx[:, begin : begin + HEAD] = mm(low, v, 1, 0).astype(BF)

    def attention_back(at, grad_ctx):
        sizes, keep = layers[at], kept[at]
        dkv, gp = (r.dkv0, r.dkv1)[at], (r.dp0, r.dp1)[at]
        for h in range(sizes.heads):
            q = keep.q[:, h * HEAD : (h + 1) * HEAD]
            k, v = head_kv(at, h)
            begin = sizes.pad + h * HEAD
            dc = grad_ctx[:, begin : begin + HEAD]
            low = keep.a[h]
            a = low.astype(F32)
            da = mm(dc, v, 1, 1)
            inner = jnp.sum(a * da, axis=1, keepdims=True)
            ds = (0.125 * a * (da - inner)).astype(BF)
            gp[:, h * HEAD : (h + 1) * HEAD] = mm(ds, k, 1, 0).astype(BF)
            dk = mm(ds, q, 0, 0).astype(BF).reshape(2, tok, HEAD)
            dv = mm(low, dc, 0, 0).astype(BF).reshape(2, tok, HEAD)
            dkv[:, :, h * HEAD : (h + 1) * HEAD] = dk
            dkv[:, :, sizes.hc + h * HEAD : sizes.hc + (h + 1) * HEAD] = dv

    def block(at, which, b):
        sizes = layers[at]
        w = weights[at][which, b * sizes.zb : (b + 1) * sizes.zb]
        return w.reshape(model, model)

    def up(at, vecs):
        sizes, keep = layers[at], kept[at]
        for b in range(sizes.nc // model):
            cols = slice(b * model, (b + 1) * model)
            u = mm(keep.hb[...], block(at, 0, b), 1, 1) + vecs.b1[b]
            phi = 0.5 * (1.0 + lax.erf(u * 0.7071067811865476))
            keep.g[:, cols] = (u * phi).astype(BF)
            density = jnp.exp(u * u * -0.5) * 0.3989422804014327
            keep.gp[:, cols] = (phi + u * density).astype(BF)

    def down(at):
        sizes, keep = layers[at], kept[at]
        total = None
        for b in range(sizes.nc // model):
            term = mm(keep.g[:, b * model : (b + 1) * model], block(at, 1, b), 1, 0)
            total = term if total is None else total + term
        return total

    def weight_grad(at, which, left, right):
        sizes = layers[at]
        dw = (r.dw0, r.dw1)[at]
        span = model // 2
        zb = sizes.zb // 2
        for b in range(sizes.nc // span):
            value = mm(left[:, b * span : (b + 1) * span], right[...], 0, 0).astype(BF)
            dw[which, b * zb : (b + 1) * zb] = value.reshape(zb, 2, sizes.nr, model)

    spread(r.hid, r.xin, r.hs, r.hr)
    push(r.vec, r.vl.at[0], r.vs.at[0], r.vr.at[0], sib)
    push(r.pa0.at[1 - c], r.ar0, r.is_.at[0], r.ir.at[0], sib)
    push(r.pf0.at[1 - c], r.fr0, r.is_.at[1], r.ir.at[1], sib)
    push(r.pa1.at[1 - c], r.ar1, r.is_.at[2], r.ir.at[2], sib)
    push(r.pf1.at[1 - c], r.fr1, r.is_.at[3], r.ir.at[3], sib)

    def prepare_a(at):
        own_ref, land, blocks = (r.pa0, r.pa1)[at], (r.ar0, r.ar1)[at], (r.ga0, r.ga1)[at]
        arrived(land, r.ir.at[2 * at], r.is_.at[2 * at])
        own, other = own_ref[c], land[...]
        both = [jnp.where(c == 0, own, other), jnp.where(c == 0, other, own)]
        blocks[y, z, x] = jnp.concatenate(both, axis=0).astype(BF)

    def prepare_f(at):
        own_ref, land = (r.pf0, r.pf1)[at], (r.fr0, r.fr1)[at]
        arrived(land, r.ir.at[2 * at + 1], r.is_.at[2 * at + 1])
        lanes = pl.ds(pl.multiple_of(y * half_lanes, 128), half_lanes)
        weights[at][:, z, x, :, lanes] = own_ref[c] + land[...]

    prepare_a(0)
    gather_z(0)
    gather_z(1)
    prepare_f(0)
    gather_z(2)
    arrived(r.vl.at[0], r.vr.at[0], r.vs.at[0])
    r.vw[1] = r.vec[...] + r.vl[0]
    total_step(r.vw, r.vl, 1, r.vs, r.vr)
    spread_done(r.hid, r.xin, r.hs, r.hr, r.os.at[0], r.os.at[1])
    gather_xy(0)
    gather_z(3)
    total_add(r.vw, r.vl, 1, r.vs, r.vr)
    total_step(r.vw, r.vl, 2, r.vs, r.vr)
    prepare_a(1)
    prepare_f(1)
    gather_xy(1)
    gather_on(0)
    gather_z(4)
    total_add(r.vw, r.vl, 2, r.vs, r.vr)
    total_step(r.vw, r.vl, 3, r.vs, r.vr)
    gather_xy(2)
    gather_on(1)
    gather_z(5)
    total_add(r.vw, r.vl, 3, r.vs, r.vr)
    total_step(r.vw, r.vl, 4, r.vs, r.vr)
    gather_end(0)
    total_add(r.vw, r.vl, 4, r.vs, r.vr)
    vecs = [layer_vecs(0), layer_vecs(1)]

    def project(at, hidden_low, parts):
        sizes, keep = layers[at], kept[at]
        for part in parts:
            order_rows(at, part)
        if sizes.wide == model:
            p = mm(hidden_low, wa[at][...], 1, 0)
            keep.q[...] = (p[:, : sizes.hc] + vecs[at].bq).astype(BF)
            keep.kv[half, :, : sizes.hc] = p[:, sizes.hc : 2 * sizes.hc].astype(BF)
            keep.kv[half, :, sizes.hc :] = (p[:, 2 * sizes.hc : 3 * sizes.hc] + vecs[at].bv).astype(BF)
        elif parts == (0,):
            p = mm(hidden_low, wa[at][:, : 2 * sizes.hc], 1, 0)
            keep.q[...] = (p[:, : sizes.hc] + vecs[at].bq).astype(BF)
            keep.kv[half, :, : sizes.hc] = p[:, sizes.hc :].astype(BF)
        else:
            p = mm(hidden_low, wa[at][:, 2 * sizes.hc : 3 * sizes.hc], 1, 0)
            keep.kv[half, :, sizes.hc :] = (p + vecs[at].bv).astype(BF)

    def attend_out(at):
        return mm(kept[at].ctx[...], wa[at][:, layers[at].start :], 1, 1)

    def norm_one(at, base, branch):
        keep, v = kept[at], vecs[at]
        normed, scale = normalize(base + branch + v.bo)
        keep.n1[...] = normed
        keep.s1[...] = scale
        result = normed * v.g1 + v.beta1
        keep.hb[...] = result.astype(BF)
        return result

    def norm_two(at, base, branch):
        keep, v = kept[at], vecs[at]
        normed, scale = normalize(base + branch + v.b2)
        keep.n2[...] = normed
        keep.s2[...] = scale
        return normed * v.g2 + v.beta2

    if layers[1].pad:
        kept[1].ctx[...] = jnp.zeros_like(kept[1].ctx)
        r.dp1[...] = jnp.zeros_like(r.dp1)
    kept[0].xb[...] = r.xin[...].reshape(tok, model)
    project(0, kept[0].xb[...], (0,))
    gather_xy(3)
    gather_on(2)
    gather_z(6)
    gather_end(1)
    project(0, kept[0].xb[...], (1,))
    send_kv(0)
    spread(r.cot, r.cin, r.cs, r.cr)
    gather_xy(4)
    gather_on(3)
    gather_z(7)
    gather_end(2)
    wait_kv(0)
    attention(0)
    wait_branch = exchange(attend_out(0))
    gather_xy(5)
    gather_on(4)
    gather_z(8)
    gather_end(3)
    normed = norm_one(0, kept[0].xb[...].astype(F32), wait_branch())
    up(0, vecs[0])
    gather_xy(6)
    gather_on(5)
    gather_end(4)
    spread_done(r.cot, r.cin, r.cs, r.cr, r.os.at[2], r.os.at[3])
    gather_xy(7)
    gather_on(6)
    gather_end(5)
    wait_branch = exchange(down(0))
    gather_xy(8)
    gather_on(7)
    gather_end(6)
    middle = norm_two(0, normed, wait_branch())
    kept[1].xb[...] = middle.astype(BF)
    project(1, kept[1].xb[...], (0,))
    send_kv(1)
    wait_kv(1)
    attention(1)
    wait_branch = exchange(attend_out(1))
    gather_on(8)
    gather_end(7)
    normed = norm_one(1, middle, wait_branch())
    up(1, vecs[1])
    gather_end(8)
    wait_branch = exchange(down(1))
    final = norm_two(1, normed, wait_branch())
    r.oblk[...] = final.astype(BF).reshape(r.oblk.shape)
    collect(r.oblk, r.oland, r.ys, r.yr)
    for copy in sent:
        copy.wait_send()
    sent.clear()

    r.vw[0] = jnp.zeros_like(r.vw[0])
    once = jnp.where(c == 0, 1.0, 0.0)

    def put_vec(at, name, value):
        row = dims.base[at] + dims.rows_of[at][name]
        r.vw[0, row : row + 1, :] = value * once

    def back_two(at, grad):
        keep, v = kept[at], vecs[at]
        n2 = keep.n2[...]
        put_vec(at, "g2", rowsum(grad * n2))
        put_vec(at, "beta2", rowsum(grad))
        dz2 = normalize_back(grad * v.g2, n2, keep.s2[...])
        r.eo[...] = dz2.astype(BF)
        put_vec(at, "b2", rowsum(r.eo[...].astype(F32)))
        return dz2

    def back_up(at):
        sizes, keep = layers[at], kept[at]
        base = dims.base[at] + dims.rows_of[at]["b1"]
        span = sizes.nc // model
        for b in range(span):
            cols = slice(b * model, (b + 1) * model)
            dg = mm(r.eo[...], block(at, 1, b), 1, 1)
            du = (dg * keep.gp[:, cols].astype(F32)).astype(BF)
            keep.g[:, cols] = du
            r.vw[0, pl.ds(base + c * span + b, 1), :] = rowsum(du.astype(F32))

    def back_in(at):
        sizes, keep = layers[at], kept[at]
        total = None
        for b in range(sizes.nc // model):
            term = mm(keep.g[:, b * model : (b + 1) * model], block(at, 0, b), 1, 0)
            total = term if total is None else total + term
        return total

    def back_one(at, grad):
        keep, v = kept[at], vecs[at]
        n1 = keep.n1[...]
        put_vec(at, "g1", rowsum(grad * n1))
        put_vec(at, "beta1", rowsum(grad))
        dz1 = normalize_back(grad * v.g1, n1, keep.s1[...])
        r.eo[...] = dz1.astype(BF)
        put_vec(at, "bo", rowsum(r.eo[...].astype(F32)))
        grad_ctx = mm(r.eo[...], wa[at][:, layers[at].start :], 1, 0).astype(BF)
        return dz1, grad_ctx

    def send_dkv(at):
        dkv, land = (r.dkv0, r.dkv1)[at], (r.dkr0, r.dkr1)[at]
        push(dkv.at[1 - half], land, r.ks.at[2 + at], r.kr.at[2 + at], zn)

    def take_dkv(at):
        sizes = layers[at]
        dkv, land, gp = (r.dkv0, r.dkv1)[at], (r.dkr0, r.dkr1)[at], (r.dp0, r.dp1)[at]
        arrived(land, r.kr.at[2 + at], r.ks.at[2 + at])
        total = (dkv[half].astype(F32) + land[...].astype(F32)).astype(BF)
        gp[:, sizes.hc : 3 * sizes.hc] = total
        qsum = rowsum(gp[:, : sizes.hc].astype(F32))
        vsum = rowsum(total[:, sizes.hc :].astype(F32))
        both = jnp.concatenate([qsum, vsum], axis=1)
        row = dims.base[at] + dims.rows_of[at]["qv"]
        if 2 * sizes.hc == model:
            r.vw[0, pl.ds(row + c, 1), :] = both
        else:
            blank = jnp.zeros_like(both)
            left, right = jnp.where(c == 0, both, blank), jnp.where(c == 0, blank, both)
            r.vw[0, row : row + 1, :] = jnp.concatenate([left, right], axis=1)

    def projection_grad(at, part):
        sizes, keep, gp = layers[at], kept[at], (r.dp0, r.dp1)[at]
        begin, end = part * model, (part + 1) * model
        for y_at in range(SIDE):
            rows = slice(y_at * half_lanes, (y_at + 1) * half_lanes)
            pieces = []
            xb = keep.xb[:, rows]
            split = min(end, sizes.start)
            if begin < split:
                pieces.append(mm(xb, gp[:, begin:split], 0, 0))
            if end > sizes.start:
                value = mm(r.eo[:, rows], keep.ctx[...], 0, 0)
                if sizes.pad:
                    value = value + mm(xb, gp[:, sizes.start : end], 0, 0)
                pieces.append(value)
            value = pieces[0] if len(pieces) == 1 else jnp.concatenate(pieces, axis=1)
            store_grad_rows(at, y_at, value, slice(begin, end))

    def back_hidden(at):
        gp = (r.dp0, r.dp1)[at]
        width = gp.shape[1]
        return mm(gp[...], wa[at][:, :width], 1, 1)

    grad = r.cin[...].reshape(tok, model).astype(F32)
    dz2 = back_two(1, grad)
    weight_grad(1, 1, kept[1].g, r.eo)
    reduce_a(8)
    back_up(1)
    weight_grad(1, 0, kept[1].g, kept[1].hb)
    reduce_a(7)
    wait_branch = exchange(back_in(1))
    reduce_b(8)
    dz1, grad_ctx = back_one(1, dz2 + wait_branch())
    reduce_b(7)
    reduce_c(8)
    attention_back(1, grad_ctx)
    send_dkv(1)
    reduce_c(7)
    reduce_end(8)
    take_dkv(1)
    projection_grad(1, 0)
    reduce_a(6)
    wait_branch = exchange(back_hidden(1))
    reduce_end(7)
    reduce_b(6)
    grad = dz1 + wait_branch()
    dz2 = back_two(0, grad)
    weight_grad(0, 1, kept[0].g, r.eo)
    reduce_a(4)
    reduce_a(5)
    reduce_c(6)
    back_up(0)
    weight_grad(0, 0, kept[0].g, kept[0].hb)
    reduce_a(2)
    reduce_a(3)
    wait_branch = exchange(back_in(0))
    reduce_b(4)
    reduce_b(5)
    reduce_end(6)
    dz1, grad_ctx = back_one(0, dz2 + wait_branch())
    reduce_b(2)
    reduce_b(3)
    reduce_c(4)
    attention_back(0, grad_ctx)
    send_dkv(0)
    reduce_c(5)
    take_dkv(0)
    projection_grad(0, 0)
    reduce_a(0)
    projection_grad(0, 1)
    reduce_a(1)
    total_step(r.vw, r.vl, 0, r.ws, r.wr)
    wait_branch = exchange(back_hidden(0))
    reduce_c(2)
    reduce_end(4)
    grad = dz1 + wait_branch()
    r.gblk[...] = grad.astype(BF).reshape(r.gblk.shape)
    collect(r.gblk, r.gland, r.zs, r.zr)
    reduce_b(0)
    reduce_b(1)
    reduce_c(3)
    reduce_end(5)
    total_add(r.vw, r.vl, 0, r.ws, r.wr)
    total_step(r.vw, r.vl, 1, r.ws, r.wr)
    reduce_end(2)
    reduce_end(3)
    total_add(r.vw, r.vl, 1, r.ws, r.wr)
    total_step(r.vw, r.vl, 2, r.ws, r.wr)
    reduce_c(0)
    total_add(r.vw, r.vl, 2, r.ws, r.wr)
    total_step(r.vw, r.vl, 3, r.ws, r.wr)
    reduce_c(1)
    total_add(r.vw, r.vl, 3, r.ws, r.wr)
    total_step(r.vw, r.vl, 4, r.ws, r.wr)
    for i in (8, 7, 6, 4, 5, 2, 3):
        reduce_out(i)
    total_add(r.vw, r.vl, 4, r.ws, r.wr)
    r.dvec[...] = r.vw[5]
    collect_done(r.oblk, r.oland, r.ys, r.yr)
    r.out[...] = r.oland[...]
    reduce_end(0)
    reduce_end(1)
    collect_done(r.gblk, r.gland, r.zs, r.zr)
    r.gh[...] = r.gland[...].astype(F32)
    reduce_out(0)
    reduce_out(1)
    for copy in sent:
        copy.wait_send()


def fused_call(hid, cot, vec, shards, dims):
    model, tok, seq = dims.model, dims.tok, dims.seq
    block = (4, tok // 4, model)
    vmem = pltpu.VMEM
    dma = pltpu.SemaphoreType.DMA
    names = ["hid", "cot", "vec", "pa0", "pf0", "pa1", "pf1"]
    inputs = [hid, cot, vec] + list(shards)
    outs = {
        "out": jax.ShapeDtypeStruct(hid.shape, BF),
        "gh": jax.ShapeDtypeStruct(hid.shape, F32),
        "da0": jax.ShapeDtypeStruct(shards[0].shape, F32),
        "df0": jax.ShapeDtypeStruct(shards[1].shape, F32),
        "da1": jax.ShapeDtypeStruct(shards[2].shape, F32),
        "df1": jax.ShapeDtypeStruct(shards[3].shape, F32),
        "dvec": jax.ShapeDtypeStruct(vec.shape, F32),
    }
    rows_a = 2 * shards[0].shape[1]
    count_a = sum(chunk[0] == "A" for chunk in dims.chunks)
    count_f = len(dims.chunks) - count_a
    shape_a, shape_f = (rows_a, model), (dims.rows, model // 2)
    n = len(dims.chunks)
    scratch = {
        "xin": vmem(block, BF),
        "cin": vmem(block, BF),
        "oblk": vmem(block, BF),
        "gblk": vmem(block, BF),
        "oland": vmem(hid.shape, BF),
        "gland": vmem(hid.shape, BF),
        "vw": vmem((6,) + vec.shape, F32),
        "vl": vmem((5,) + vec.shape, F32),
        "xs": vmem((2, tok, model), BF),
        "xr": vmem((2, tok, model), BF),
        "eo": vmem((tok, model), BF),
        "raa": vmem((count_a, 2, 2) + shape_a, BF),
        "rba": vmem((count_a, 2, 4) + shape_a, BF),
        "rca": vmem((count_a, 3) + shape_a, BF),
        "raf": vmem((count_f, 2, 2) + shape_f, BF),
        "rbf": vmem((count_f, 2, 4) + shape_f, BF),
        "rcf": vmem((count_f, 3) + shape_f, BF),
        "fsa": vmem((count_a, rows_a // 2, model), F32),
        "fra": vmem((count_a, rows_a // 2, model), F32),
        "frf": vmem((count_f,) + shape_f, F32),
    }
    for at, sizes in enumerate(dims.layers):
        scratch |= {
            f"ar{at}": vmem((rows_a // 2, sizes.wide), F32),
            f"fr{at}": vmem((2, sizes.nr, model // 2), BF),
            f"ga{at}": vmem((SIDE, DEPTH, SIDE, rows_a, sizes.wide), BF),
            f"wa{at}": vmem((model, sizes.wide), BF),
            f"w{at}": vmem((2, DEPTH, SIDE, sizes.nr, model), BF),
            f"dw{at}": vmem((2, DEPTH, SIDE, sizes.nr, model), BF),
            f"xb{at}": vmem((tok, model), BF),
            f"q{at}": vmem((tok, sizes.hc), BF),
            f"kv{at}": vmem((2, tok, 2 * sizes.hc), BF),
            f"a{at}": vmem((sizes.heads, tok, seq), BF),
            f"ctx{at}": vmem((tok, sizes.wide - sizes.start), BF),
            f"n1{at}": vmem((tok, model), F32),
            f"s1{at}": vmem((tok, 1), F32),
            f"hb{at}": vmem((tok, model), BF),
            f"g{at}": vmem((tok, sizes.nc), BF),
            f"gp{at}": vmem((tok, sizes.nc), BF),
            f"n2{at}": vmem((tok, model), F32),
            f"s2{at}": vmem((tok, 1), F32),
            f"dkv{at}": vmem((2, tok, 2 * sizes.hc), BF),
            f"dkr{at}": vmem((tok, 2 * sizes.hc), BF),
            f"dp{at}": vmem((tok, sizes.wide if sizes.pad else sizes.start), BF),
        }
    scratch |= {name: dma((n, 7)) for name in ("gs", "gr", "ss", "sr")}
    scratch |= {name: dma((n,)) for name in ("fs", "fr")}
    scratch |= {name: dma((5,)) for name in ("vs", "vr", "ws", "wr")}
    scratch |= {name: dma((4,)) for name in ("hs", "hr", "cs", "cr", "ys", "yr", "zs", "zr")}
    scratch |= {name: dma((4,)) for name in ("is_", "ir", "os", "ks", "kr")}
    scratch |= {name: dma((2,)) for name in ("es", "er")}
    names = names + list(outs) + list(scratch)
    whole = pl.BlockSpec(memory_space=pltpu.VMEM)
    return pl.pallas_call(
        functools.partial(fused_kernel, dims, names),
        out_shape=list(outs.values()),
        in_specs=[whole] * len(inputs),
        out_specs=[whole] * len(outs),
        scratch_shapes=list(scratch.values()),
        compiler_params=pltpu.CompilerParams(
            collective_id=0, has_side_effects=True, vmem_limit_bytes=dims.vmem
        ),
        name="layers",
    )(*inputs)


def pack_layer(attn_in, attn_out, ffn_in, ffn_out, core):
    rows, heads_width = attn_in.shape[0], attn_in.shape[1] // 3
    first = attn_in.reshape(rows, 3, 2, heads_width // 2).transpose(2, 0, 1, 3)
    first = first.reshape(2, rows, 3 * heads_width // 2)
    second = attn_out.T.reshape(rows, 2, heads_width // 2).transpose(1, 0, 2)
    attn = jnp.concatenate([first, second], axis=2).astype(F32)
    both = jnp.stack([ffn_in.T, ffn_out])
    both = both.reshape(2, 2, both.shape[1] // 2, both.shape[2]).transpose(1, 0, 2, 3)
    blank = jnp.zeros_like(both)
    left, right = jnp.where(core == 0, both, blank), jnp.where(core == 0, blank, both)
    return attn, jnp.concatenate([left, right], axis=3)


def unpack_layer(attn, ffn, core):
    rows, half = attn.shape[1], attn.shape[2] // 4
    grad_in = attn[:, :, : 3 * half].reshape(2, rows, 3, half).transpose(1, 2, 0, 3)
    grad_out = attn[:, :, 3 * half :].transpose(0, 2, 1).reshape(2 * half, rows)
    lanes = ffn.shape[3] // 2
    own = jnp.where(core == 0, ffn[..., :lanes], ffn[..., lanes:])
    own = own.transpose(1, 0, 2, 3).reshape(2, 2 * ffn.shape[2], lanes)
    return grad_in.reshape(rows, 6 * half), grad_out, own[0].T, own[1]


def pack_vectors(shifts, gains, sizes, model, device):
    total = 4 * sizes.hc + 4 * model + 2 * sizes.nc
    flat = jnp.zeros((total,), F32)
    flat = lax.dynamic_update_slice_in_dim(flat, shifts.astype(F32), device * shifts.shape[0], 0)
    query, value, rest = flat[: 2 * sizes.hc], flat[2 * sizes.hc : 4 * sizes.hc], flat[4 * sizes.hc :]
    both = jnp.concatenate([query.reshape(2, sizes.hc), value.reshape(2, sizes.hc)], axis=1)
    up = rest[2 * model : 2 * model + 2 * sizes.nc].reshape(8, 2, sizes.nr).transpose(1, 0, 2)
    scale = jnp.zeros((2 * model,), F32)
    scale = lax.dynamic_update_slice_in_dim(scale, gains.astype(F32), device * gains.shape[0], 0)
    return [both.reshape(-1), rest[: 2 * model], up.reshape(-1), rest[2 * model + 2 * sizes.nc :], scale]


def unpack_vectors(flat, sizes, model, device, shift_len, gain_len):
    both = flat[: 4 * sizes.hc].reshape(2, 2, sizes.hc).transpose(1, 0, 2).reshape(-1)
    rest = flat[4 * sizes.hc :]
    up = rest[2 * model : 2 * model + 2 * sizes.nc].reshape(2, 8, sizes.nr).transpose(1, 0, 2)
    after = rest[2 * model + 2 * sizes.nc :]
    shifts = jnp.concatenate([both, rest[: 2 * model], up.reshape(-1), after[: 2 * model]])
    gains = after[2 * model :]
    return (
        lax.dynamic_slice_in_dim(shifts, device * shift_len, shift_len),
        lax.dynamic_slice_in_dim(gains, device * gain_len, gain_len),
    )


def make_dims(hidden_in, teacher, student):
    model = hidden_in.shape[2]
    layers = [
        layer_sizes(model, p[0].shape[1] // 3, p[2].shape[1] * DEPTH * SIDE) for p in (teacher, student)
    ]
    rows = layers[1].nr
    chunks = []
    for at, sizes in enumerate(layers):
        chunks += [("A", at, 0, part) for part in range(sizes.wide // model)]
        for which in (0, 1):
            chunks += [("F", at, which, part) for part in range(sizes.nr // rows)]
    counts, slot = {"A": 0, "F": 0}, []
    for chunk in chunks:
        slot.append(counts[chunk[0]])
        counts[chunk[0]] += 1
    rows_of, base, at = [], [], 0
    for sizes in layers:
        found, count = vec_rows(model, sizes)
        rows_of.append(found)
        base.append(at)
        at += count
    return types.SimpleNamespace(
        model=model,
        tok=4 * hidden_in.shape[1],
        seq=8 * hidden_in.shape[1],
        layers=layers,
        chunks=chunks,
        slot=slot,
        rows=rows,
        rows_of=rows_of,
        base=base,
        length_row=at,
        vec_rows=(at + 8) // 8 * 8,
        vmem=63 * 2**20,
    )


def fast_body(
    hidden_in,
    cotangent,
    lengths,
    *params,
):
    teacher, student = params[:6], params[6:]
    dims = make_dims(hidden_in, teacher, student)
    model = dims.model
    dp, mp = lax.axis_index("dp"), lax.axis_index("mp")
    core = lax.rem(dp, SIDE)
    device = dp * DEPTH * SIDE + mp
    pieces = []
    shards = []
    for sizes, p in zip(dims.layers, (teacher, student)):
        shards += list(pack_layer(*p[:4], core))
        pieces += pack_vectors(p[4], p[5], sizes, model, device)
    spans = jnp.zeros((dims.vec_rows * model - sum(p.shape[0] for p in pieces),), F32)
    own = jnp.where(mp == 0, lengths.astype(F32), jnp.zeros_like(lengths, F32))
    spans = lax.dynamic_update_slice_in_dim(spans, own, dp * lengths.shape[0], 0)
    vec = jnp.concatenate(pieces + [spans]).reshape(dims.vec_rows, model)
    out, grad_hidden, da0, df0, da1, df1, dvec = fused_call(hidden_in, cotangent, vec, shards, dims)
    results = [out, grad_hidden]
    flat = dvec.reshape(-1)
    for at, (sizes, p, attn, ffn) in enumerate(
        zip(dims.layers, (teacher, student), (da0, da1), (df0, df1))
    ):
        results += list(unpack_layer(attn, ffn, core))
        begin = dims.base[at] * model
        results += list(
            unpack_vectors(flat[begin:], sizes, model, device, p[4].shape[0], p[5].shape[0])
        )
    return tuple(results)


def body(axes, *args):
    rows, tokens, model = args[0].shape
    fits = axes["dp"] == SIDE * SIDE and axes["mp"] == DEPTH * SIDE
    if fits and rows == 2 and tokens % 16 == 0 and model % 256 == 0:
        return fast_body(*args)
    return general_body(*args)


def general_body(
    hidden_in,
    cotangent,
    lengths,
    teacher_attn_in,
    teacher_attn_out,
    teacher_ffn_in,
    teacher_ffn_out,
    teacher_shifts,
    teacher_gains,
    student_attn_in,
    student_attn_out,
    student_ffn_in,
    student_ffn_out,
    student_shifts,
    student_gains,
):
    span_len = hidden_in.shape[1] * lax.axis_size("mp")
    positions = jnp.arange(span_len)
    valid_keys = positions[None, :] < lengths[:, None]
    teacher = fetch(
        teacher_attn_in,
        teacher_attn_out,
        teacher_ffn_in,
        teacher_ffn_out,
        teacher_shifts,
        teacher_gains,
    )
    student = fetch(
        student_attn_in,
        student_attn_out,
        student_ffn_in,
        student_ffn_out,
        student_shifts,
        student_gains,
    )
    middle, teacher_kept = forward_layer(hidden_in.astype(jnp.float32), teacher, valid_keys)
    final, student_kept = forward_layer(middle, student, valid_keys)
    grad_middle, student_grads = backward_layer(
        cotangent.astype(jnp.float32), student_kept, student, valid_keys
    )
    grad_input, teacher_grads = backward_layer(grad_middle, teacher_kept, teacher, valid_keys)
    teacher_totals = reduce_grads(teacher_grads)
    student_totals = reduce_grads(student_grads)
    return (final.astype(jnp.bfloat16), grad_input) + teacher_totals + student_totals


def solution(mesh):
    in_specs = (
        P("dp", "mp", None),
        P("dp", "mp", None),
        P("dp"),
        P(("dp", "mp"), None),
        P(None, ("dp", "mp")),
        P("dp", "mp"),
        P("mp", "dp"),
        P(("dp", "mp")),
        P(("dp", "mp")),
        P(("dp", "mp"), None),
        P(None, ("dp", "mp")),
        P("dp", "mp"),
        P("mp", "dp"),
        P(("dp", "mp")),
        P(("dp", "mp")),
    )
    out_specs = (
        P("dp", "mp", None),
        P("dp", "mp", None),
        P(("dp", "mp"), None),
        P(None, ("dp", "mp")),
        P("dp", "mp"),
        P("mp", "dp"),
        P(("dp", "mp")),
        P(("dp", "mp")),
        P(("dp", "mp"), None),
        P(None, ("dp", "mp")),
        P("dp", "mp"),
        P("mp", "dp"),
        P(("dp", "mp")),
        P(("dp", "mp")),
    )
    return jax.shard_map(
        functools.partial(body, dict(mesh.shape)), mesh=mesh, in_specs=in_specs, out_specs=out_specs, check_vma=False)
```

```python
import functools
import types

import jax
import jax.numpy as jnp
from jax import lax
from jax.experimental import pallas as pl
from jax.experimental.pallas import tpu as pltpu
from jax.sharding import PartitionSpec as P

HEAD = 64


EPSILON = 1e-06
NEGATIVE = -1e30


def layer_norm(values, gain, shift):
    centered = values - jnp.mean(values, axis=-1, keepdims=True)
    variance = jnp.mean(centered * centered, axis=-1, keepdims=True)
    return centered * lax.rsqrt(variance + EPSILON) * gain + shift


def smooth_gate(pre_act):
    return jax.nn.gelu(pre_act, approximate=False)


def split_shifts(shifts, head_width, model_width, hidden_width):
    spans_list = [
        head_width,
        head_width,
        model_width,
        model_width,
        hidden_width,
        model_width,
        model_width,
    ]
    pieces = []
    offset = 0
    for length in spans_list:
        pieces.append(shifts[offset : offset + length])
        offset = offset + length
    return pieces


def to_heads(values):
    return values.reshape(values.shape[0], values.shape[1], values.shape[2] // HEAD, HEAD)


def score_block(queries, all_keys, valid_keys):
    raw = jnp.einsum(
        "rqhd,rkhd->rhqk", to_heads(queries), to_heads(all_keys), preferred_element_type=jnp.float32
    )
    return jnp.where(valid_keys[:, None, None, :], raw * 0.125, NEGATIVE)


def fetch(attn_in, attn_out, ffn_in, ffn_out, shifts, gains):
    whole_in, whole_out, whole_shifts, whole_gains = (
        lax.all_gather(attn_in, ("dp", "mp"), axis=0, tiled=True),
        lax.all_gather(attn_out, ("dp", "mp"), axis=1, tiled=True),
        lax.all_gather(shifts, ("dp", "mp"), axis=0, tiled=True),
        lax.all_gather(gains, ("dp", "mp"), axis=0, tiled=True),
    )
    ffn_first, ffn_second = (
        lax.all_gather(ffn_in, "dp", axis=0, tiled=True),
        lax.all_gather(ffn_out, "dp", axis=1, tiled=True),
    )
    return (
        whole_in,
        whole_out,
        ffn_first,
        ffn_second,
        whole_shifts.astype(jnp.float32),
        whole_gains.astype(jnp.float32),
    )


def forward_layer(hidden, params, valid_keys):
    attn_in, attn_out, ffn_first, ffn_second, shifts, gains = params
    model_width = hidden.shape[-1]
    head_width = attn_in.shape[1] // 3
    hidden_width = shifts.shape[0] - 2 * head_width - 4 * model_width
    pieces = split_shifts(shifts, head_width, model_width, hidden_width)
    bias_query, bias_value, bias_output, shift_one, bias_up, bias_down, shift_two = pieces
    hidden_low = hidden.astype(jnp.bfloat16)
    projected = jnp.einsum("rsd,de->rse", hidden_low, attn_in, preferred_element_type=jnp.float32)
    queries = (projected[..., :head_width] + bias_query).astype(jnp.bfloat16)
    local_keys = projected[..., head_width : 2 * head_width].astype(jnp.bfloat16)
    local_values = (projected[..., 2 * head_width :] + bias_value).astype(jnp.bfloat16)
    all_keys, all_values = (
        lax.all_gather(local_keys, "mp", axis=1, tiled=True),
        lax.all_gather(local_values, "mp", axis=1, tiled=True),
    )
    scores = score_block(queries, all_keys, valid_keys)
    row_max = jnp.max(scores, axis=-1, keepdims=True)
    exponent = jnp.exp(scores - row_max)
    row_total = jnp.sum(exponent, axis=-1, keepdims=True)
    log_total = row_max + jnp.log(row_total)
    weights_low = (exponent / row_total).astype(jnp.bfloat16)
    mixed = jnp.einsum(
        "rhqk,rkhd->rqhd", weights_low, to_heads(all_values), preferred_element_type=jnp.float32
    )
    context = mixed.reshape(queries.shape).astype(jnp.bfloat16)
    branch = (
        jnp.einsum("rsh,hd->rsd", context, attn_out, preferred_element_type=jnp.float32)
        + bias_output
    )
    summed_one = hidden + branch
    normed_one = layer_norm(summed_one, gains[:model_width], shift_one)
    normed_low = normed_one.astype(jnp.bfloat16)
    ffn_tokens = lax.all_gather(normed_low, "mp", axis=1, tiled=True)
    local_hidden = ffn_first.shape[1]
    bias_part = lax.dynamic_slice_in_dim(bias_up, lax.axis_index("mp") * local_hidden, local_hidden)
    pre_act = (
        jnp.einsum("rsd,df->rsf", ffn_tokens, ffn_first, preferred_element_type=jnp.float32)
        + bias_part
    )
    act_low = smooth_gate(pre_act).astype(jnp.bfloat16)
    down_terms = jnp.einsum("rsf,fd->rsd", act_low, ffn_second, preferred_element_type=jnp.float32)
    ffn_down = lax.psum_scatter(
        down_terms.astype(jnp.bfloat16), "mp", scatter_dimension=1, tiled=True
    ).astype(jnp.float32)
    summed_two = normed_one + ffn_down + bias_down
    result = layer_norm(summed_two, gains[model_width:], shift_two)
    key_store = (all_keys, all_values)
    kept = (
        hidden_low,
        queries,
        key_store,
        log_total,
        context,
        summed_one,
        ffn_tokens,
        pre_act,
        act_low,
        summed_two,
    )
    return (result, kept)


def backward_layer(grad_out, kept, params, valid_keys):
    attn_in, attn_out, ffn_first, ffn_second, shifts, gains = params
    (
        hidden_low,
        queries,
        key_store,
        log_total,
        context,
        summed_one,
        ffn_tokens,
        pre_act,
        act_low,
        summed_two,
    ) = kept
    model_width = summed_one.shape[-1]
    head_width = attn_in.shape[1] // 3
    hidden_width = shifts.shape[0] - 2 * head_width - 4 * model_width
    pieces = split_shifts(shifts, head_width, model_width, hidden_width)
    bias_query, bias_value, bias_output, shift_one, bias_up, bias_down, shift_two = pieces
    sum_axes = (0, 1)
    unused_two, norm_two_back = jax.vjp(layer_norm, summed_two, gains[model_width:], shift_two)
    grad_two, grad_gain_two, grad_shift_two = norm_two_back(grad_out)
    grad_down = grad_two.astype(jnp.bfloat16)
    grad_bias_down = jnp.sum(grad_down.astype(jnp.float32), axis=sum_axes)
    grad_tokens = lax.all_gather(grad_down, "mp", axis=1, tiled=True)
    grad_act = jnp.einsum(
        "rsd,fd->rsf", grad_tokens, ffn_second, preferred_element_type=jnp.float32
    )
    grad_second = jnp.einsum(
        "rsf,rsd->fd", act_low, grad_tokens, preferred_element_type=jnp.float32
    )
    unused_gate, gate_back = jax.vjp(smooth_gate, pre_act)
    grad_pre = gate_back(grad_act)[0].astype(jnp.bfloat16)
    grad_bias_part = jnp.sum(grad_pre.astype(jnp.float32), axis=sum_axes)
    grad_first = jnp.einsum("rsd,rsf->df", ffn_tokens, grad_pre, preferred_element_type=jnp.float32)
    back_terms = jnp.einsum("rsf,df->rsd", grad_pre, ffn_first, preferred_element_type=jnp.float32)
    grad_normed = lax.psum_scatter(
        back_terms.astype(jnp.bfloat16), "mp", scatter_dimension=1, tiled=True
    ).astype(jnp.float32)
    blank_bias = jnp.zeros((hidden_width,), jnp.float32)
    grad_bias_up = lax.dynamic_update_slice_in_dim(
        blank_bias, grad_bias_part, lax.axis_index("mp") * ffn_first.shape[1], 0
    )
    grad_normed = grad_normed + grad_two
    unused_one, norm_one_back = jax.vjp(layer_norm, summed_one, gains[:model_width], shift_one)
    grad_one, grad_gain_one, grad_shift_one = norm_one_back(grad_normed)
    grad_branch = grad_one.astype(jnp.bfloat16)
    grad_bias_output = jnp.sum(grad_branch.astype(jnp.float32), axis=sum_axes)
    grad_attn_out = jnp.einsum(
        "rsh,rsd->hd", context, grad_branch, preferred_element_type=jnp.float32
    )
    grad_context = jnp.einsum(
        "rsd,hd->rsh", grad_branch, attn_out, preferred_element_type=jnp.float32
    ).astype(jnp.bfloat16)
    stored_keys, stored_values = key_store
    all_keys, all_values = (stored_keys, stored_values)
    weights = jnp.exp(score_block(queries, all_keys, valid_keys) - log_total)
    context_heads = to_heads(grad_context)
    grad_weights = jnp.einsum(
        "rqhd,rkhd->rhqk", context_heads, to_heads(all_values), preferred_element_type=jnp.float32
    )
    inner_sum = jnp.sum(weights * grad_weights, axis=-1, keepdims=True)
    grad_raw = (0.125 * weights * (grad_weights - inner_sum)).astype(jnp.bfloat16)
    grad_queries = jnp.einsum(
        "rhqk,rkhd->rqhd", grad_raw, to_heads(all_keys), preferred_element_type=jnp.float32
    )
    grad_queries = grad_queries.reshape(queries.shape).astype(jnp.bfloat16)
    weights_low = weights.astype(jnp.bfloat16)
    value_terms = jnp.einsum(
        "rhqk,rqhd->rkhd", weights_low, context_heads, preferred_element_type=jnp.float32
    )
    key_terms = jnp.einsum(
        "rhqk,rqhd->rkhd", grad_raw, to_heads(queries), preferred_element_type=jnp.float32
    )
    key_terms = key_terms.reshape(all_keys.shape)
    value_terms = value_terms.reshape(all_values.shape)
    grad_keys, grad_values = (
        lax.psum_scatter(
            key_terms.astype(jnp.bfloat16), "mp", scatter_dimension=1, tiled=True
        ).astype(jnp.float32),
        lax.psum_scatter(
            value_terms.astype(jnp.bfloat16), "mp", scatter_dimension=1, tiled=True
        ).astype(jnp.float32),
    )
    grad_values_low = grad_values.astype(jnp.bfloat16)
    grad_projected = jnp.concatenate(
        [grad_queries, grad_keys.astype(jnp.bfloat16), grad_values_low], axis=-1
    )
    grad_attn_in = jnp.einsum(
        "rsd,rse->de", hidden_low, grad_projected, preferred_element_type=jnp.float32
    )
    grad_hidden = grad_one + jnp.einsum(
        "rse,de->rsd", grad_projected, attn_in, preferred_element_type=jnp.float32
    )
    grad_bias_query = jnp.sum(grad_queries.astype(jnp.float32), axis=sum_axes)
    grad_bias_value = jnp.sum(grad_values_low.astype(jnp.float32), axis=sum_axes)
    grad_shifts = jnp.concatenate(
        [
            grad_bias_query,
            grad_bias_value,
            grad_bias_output,
            grad_shift_one,
            grad_bias_up,
            grad_bias_down,
            grad_shift_two,
        ]
    )
    grad_gains = jnp.concatenate([grad_gain_one, grad_gain_two])
    return (
        grad_hidden,
        (grad_attn_in, grad_attn_out, grad_first, grad_second, grad_shifts, grad_gains),
    )


def reduce_grads(grads):
    grad_attn_in, grad_attn_out, grad_first, grad_second, grad_shifts, grad_gains = grads
    total_in, total_out, total_shifts, total_gains = (
        lax.psum_scatter(grad_attn_in, ("dp", "mp"), scatter_dimension=0, tiled=True),
        lax.psum_scatter(grad_attn_out, ("dp", "mp"), scatter_dimension=1, tiled=True),
        lax.psum_scatter(grad_shifts, ("dp", "mp"), scatter_dimension=0, tiled=True),
        lax.psum_scatter(grad_gains, ("dp", "mp"), scatter_dimension=0, tiled=True),
    )
    total_first, total_second = (
        lax.psum_scatter(
            grad_first.astype(jnp.bfloat16), "dp", scatter_dimension=0, tiled=True
        ).astype(jnp.float32),
        lax.psum_scatter(
            grad_second.astype(jnp.bfloat16), "dp", scatter_dimension=1, tiled=True
        ).astype(jnp.float32),
    )
    return (total_in, total_out, total_first, total_second, total_shifts, total_gains)


BF = jnp.bfloat16
F32 = jnp.float32
MESH = pl.DeviceIdType.MESH
SIDE = 2
DEPTH = 4
PARTNERS = 9


def mm(left, right, left_dim, right_dim):
    return lax.dot_general(
        left, right, (((left_dim,), (right_dim,)), ((), ())), preferred_element_type=F32
    )


def rowsum(values):
    return jnp.sum(values, axis=0, keepdims=True)


def normalize(values):
    centered = values - jnp.mean(values, axis=-1, keepdims=True)
    variance = jnp.mean(centered * centered, axis=-1, keepdims=True)
    scale = lax.rsqrt(variance + EPSILON)
    return centered * scale, scale


def normalize_back(grad, normed, scale):
    along = jnp.mean(grad * normed, axis=-1, keepdims=True)
    return scale * (grad - jnp.mean(grad, axis=-1, keepdims=True) - normed * along)


def layer_sizes(model, heads_width, hidden):
    half = heads_width // 2
    start = 3 * half // 128 * 128
    return types.SimpleNamespace(
        hc=half,
        heads=half // HEAD,
        wide=4 * half,
        start=start,
        pad=3 * half - start,
        nr=hidden // 16,
        nc=hidden // 2,
        zb=model * 8 // hidden,
    )


def vec_rows(model, sizes):
    lengths = dict(
        qv=4 * sizes.hc, bo=model, beta1=model, b1=2 * sizes.nc, b2=model, beta2=model, g1=model, g2=model
    )
    rows, at = {}, 0
    for name, length in lengths.items():
        rows[name] = at
        at += length // model
    return types.SimpleNamespace(**rows), at


def named(tree):
    if isinstance(tree, dict):
        return types.SimpleNamespace(**{key: named(value) for key, value in tree.items()})
    return [named(value) for value in tree] if isinstance(tree, list) else tree


def fused_kernel(dims, tree, *refs):
    given, outs, scratch, held, made = jax.tree.unflatten(tree, refs)
    lay = [named(a | b | d) for a, b, d in zip(held["lay"], made["lay"], scratch["lay"])]
    r = named(held | made | scratch)
    given, outs = named(given), named(outs)

    def fetch_copies():
        pairs = []
        for at in range(2):
            far, near = given.lay[at], lay[at]
            pairs += [(far.pai, near.pai), (far.pao, near.pao)]
            if at == 0:
                pairs += [(given.hid, r.hid)]
            pairs += [(far.pfi, near.pfi), (far.pfo, near.pfo), (far.psh, near.psh), (far.pga, near.pga)]
        pairs += [(given.len, r.len), (given.cot, r.cot)]
        return [pltpu.make_async_copy(src, dst, r.ins.at[i]) for i, (src, dst) in enumerate(pairs)]

    fetched = fetch_copies()
    for copy in fetched:
        copy.start()
    stored = []

    def store(src, dst):
        copy = pltpu.make_async_copy(src, dst, r.outs.at[len(stored)])
        copy.start()
        stored.append(copy)
    model, tok, seq, layers = dims.model, dims.tok, dims.seq, dims.layers
    half_lanes = model // 2
    dp, mp = lax.axis_index("dp"), lax.axis_index("mp")
    y, c = dp // SIDE, lax.rem(dp, SIDE)
    z, x = mp // SIDE, lax.rem(mp, SIDE)

    def device(c, x, y, z):
        return {"dp": y * SIDE + c, "mp": z * SIDE + x}

    sib = device(1 - c, x, y, z)
    xn, yn = device(c, 1 - x, y, z), device(c, x, 1 - y, z)
    zdev = [device(c, x, y, lax.rem(z + d, DEPTH)) for d in range(1, DEPTH)]
    zpair = z + 1 - 2 * lax.rem(z, 2)
    zn = device(c, x, y, zpair)
    zfar = device(c, x, y, lax.rem(z + 2, DEPTH))

    bar = pltpu.get_barrier_semaphore()
    for step in range(1, DEPTH * SIDE):
        other = lax.rem(mp + step, DEPTH * SIDE)
        pl.semaphore_signal(bar, inc=1, device_id={"dp": dp, "mp": other}, device_id_type=MESH)
    pl.semaphore_signal(bar, inc=1, device_id=sib, device_id_type=MESH)
    pl.semaphore_signal(bar, inc=1, device_id=yn, device_id_type=MESH)

    sent = []

    def remote(src, dst, send, recv, dev):
        return pltpu.make_async_remote_copy(
            src_ref=src, dst_ref=dst, send_sem=send, recv_sem=recv, device_id=dev, device_id_type=MESH
        )

    def push(src, dst, send, recv, dev):
        copy = remote(src, dst, send, recv, dev)
        copy.start()
        sent.append((None, copy))

    def arrived(dst, recv, send):
        remote(dst, dst, send, recv, sib).wait_recv()

    row_core = z // 2
    mine = c == row_core
    half = lax.rem(z, 2)

    def spread(src, land, sends, recvs):
        block = 2 * lax.rem(z, 2) + x
        target = 2 * c + z // 2
        for j in range(2):
            local = (x == j) & (z == target)
            copy = remote(src.at[j], land.at[block], sends.at[j], recvs.at[block], device(c, j, y, target))
            pl.when(local)(pltpu.make_async_copy(src.at[j], land.at[block], recvs.at[block]).start)
            pl.when(jnp.logical_not(local))(copy.start)

    def spread_done(src, land, sends, recvs, on_chip_send, on_chip_recv):
        target = 2 * c + z // 2
        for j in range(2):
            local = (x == j) & (z == target)
            copy = remote(src.at[j], land.at[0], sends.at[j], recvs.at[0], sib)
            pl.when(jnp.logical_not(local))(copy.wait_send)
        whole = remote(land, land, on_chip_send, on_chip_recv, sib)

        @pl.when(mine)
        def _():
            for block in range(4):
                arrived(land.at[block], recvs.at[block], sends.at[0])
            whole.start()
            whole.wait_send()

        @pl.when(jnp.logical_not(mine))
        def _():
            whole.wait_recv()

    def collect(src, land, sends, recvs):
        @pl.when(mine)
        def _():
            for block in range(4):
                z_to, x_to = 2 * half + block // 2, block % 2
                local = (x == x_to) & (z == z_to)
                slot = land.at[x]
                copy = remote(
                    src.at[block], slot, sends.at[block], recvs.at[x], device(c, x_to, y, z_to)
                )
                pl.when(local)(pltpu.make_async_copy(src.at[block], slot, recvs.at[x]).start)
                pl.when(jnp.logical_not(local))(copy.start)

    def collect_done(src, land, sends, recvs):
        for j in range(2):
            arrived(land.at[j], recvs.at[j], sends.at[0])

        @pl.when(mine)
        def _():
            for block in range(4):
                z_to, x_to = 2 * half + block // 2, block % 2
                local = (x == x_to) & (z == z_to)
                copy = remote(src.at[block], src.at[block], sends.at[block], recvs.at[0], sib)
                pl.when(jnp.logical_not(local))(copy.wait_send)

    chunks = dims.chunks
    every, first, second = pl.ds(0, DEPTH), pl.ds(0, 2), pl.ds(2, 2)
    both = pl.ds(0, 2)

    def view(i, grads, band, z_slice, x_at, y_at):
        kind, layer, which, part = chunks[i]
        full = dims.unit_rows[kind]
        begin, count = {"a": (0, full - 32), "b": (full - 32, 16), "c": (full - 16, 16)}[band]
        if kind == "A":
            ref = lay[layer].ga
            y_pick = both if y_at is None else y_at
            return ref.at[y_pick, z_slice, x_at, pl.ds(begin, count), pl.ds(part * model, model)]
        ref = lay[layer].dw if grads else lay[layer].w
        lanes = pl.ds(0, model)
        if y_at is not None:
            lanes = pl.ds(pl.multiple_of(y_at * half_lanes, 128), half_lanes)
        return ref.at[which, z_slice, x_at, pl.ds(part * full + begin, count), lanes]

    UP, DOWN, FAR, RELAY = range(4)
    z_far = lax.rem(z + 2, DEPTH)
    z_up, z_down = lax.rem(z + 1, DEPTH), lax.rem(z + DEPTH - 1, DEPTH)
    z_end = DEPTH - 1 - z
    has_up, has_down = z < DEPTH - 1, z > 0
    inner = (z == 1) | (z == 2)
    outer = (z == 0) | (z == 3)
    z_out = jnp.where(z == 1, 0, 3)
    z_in = jnp.where(z == 0, 1, 2)

    def push_if(cond, src, dst, send, recv, dev):
        copy = remote(src, dst, send, recv, dev)
        pl.when(cond)(copy.start)
        sent.append((cond, copy))

    def wait_sent():
        for cond, copy in sent:
            if cond is None:
                copy.wait_send()
            else:
                pl.when(cond)(copy.wait_send)
        sent.clear()

    def arrived_if(cond, dst, recv, send):
        pl.when(cond)(remote(dst, dst, send, recv, sib).wait_recv)

    def at_z(zz):
        return device(c, x, y, zz)

    def line_send(part, send, recv):
        own = part(z)
        push_if(has_up, own, own, send(UP), recv(UP), at_z(z_up))
        push_if(has_down, own, own, send(DOWN), recv(DOWN), at_z(z_down))
        push(own, own, send(FAR), recv(FAR), at_z(z_far))

    def line_relay(part, send, recv):
        far = part(z_far)
        arrived_if(inner, far, recv(FAR), send(FAR))
        push_if(inner, far, far, send(RELAY), recv(RELAY), at_z(z_out))

    def line_end(part, send, recv):
        arrived_if(has_down, part(z_down), recv(UP), send(UP))
        arrived_if(has_up, part(z_up), recv(DOWN), send(DOWN))
        arrived_if(outer, part(z_far), recv(FAR), send(FAR))
        arrived_if(outer, part(z_end), recv(RELAY), send(RELAY))

    def sems(ref_send, ref_recv, i, base):
        return (lambda k: ref_send.at[i, base + k]), (lambda k: ref_recv.at[i, base + k])

    def one(zz):
        return pl.ds(zz, 1)

    def parts_of(i, grads):
        return (
            lambda zz: view(i, grads, "a", one(zz), x, y),
            lambda zz: view(i, grads, "b", one(zz), both, y),
            lambda zz: view(i, grads, "c", one(zz), x, None),
        )

    def gather_sems(i, base):
        return sems(r.gs, r.gr, i, base)

    def gather_push(i, k, piece, dev):
        push(piece, piece, r.gs.at[i, k], r.gr.at[i, k], dev)

    def gather_wait(i, k, piece):
        arrived(piece, r.gr.at[i, k], r.gs.at[i, k])

    def gather_0(i):
        gather_push(i, 16, view(i, False, "b", one(z), x, y), xn)
        gather_push(i, 17, view(i, False, "c", one(z), x, y), yn)
        line_send(parts_of(i, False)[0], *gather_sems(i, 0))

    def gather_1(i):
        a, b, c_part = parts_of(i, False)
        gather_wait(i, 16, view(i, False, "b", one(z), 1 - x, y))
        line_send(b, *gather_sems(i, 4))
        gather_wait(i, 17, view(i, False, "c", one(z), x, 1 - y))
        line_send(c_part, *gather_sems(i, 8))
        line_relay(a, *gather_sems(i, 0))

    def gather_2(i):
        a, b, c_part = parts_of(i, False)
        line_end(a, *gather_sems(i, 0))
        own = view(i, False, "a", every, x, y)
        gather_push(i, 12, own, xn)
        gather_push(i, 13, own, yn)
        line_relay(b, *gather_sems(i, 4))
        line_relay(c_part, *gather_sems(i, 8))

    def gather_3(i):
        a, b, c_part = parts_of(i, False)
        line_end(b, *gather_sems(i, 4))
        gather_push(i, 18, view(i, False, "b", every, both, y), yn)
        line_end(c_part, *gather_sems(i, 8))
        gather_push(i, 19, view(i, False, "c", every, x, None), xn)
        gather_wait(i, 12, view(i, False, "a", every, 1 - x, y))
        gather_wait(i, 13, view(i, False, "a", every, x, 1 - y))
        gather_push(i, 14, view(i, False, "a", first, x, 1 - y), xn)
        gather_push(i, 15, view(i, False, "a", second, 1 - x, y), yn)

    def gather_4(i):
        gather_wait(i, 14, view(i, False, "a", first, 1 - x, 1 - y))
        gather_wait(i, 15, view(i, False, "a", second, 1 - x, 1 - y))
        gather_wait(i, 18, view(i, False, "b", every, both, 1 - y))
        gather_wait(i, 19, view(i, False, "c", every, 1 - x, None))

    def pump(step):
        for lag, stage in enumerate((gather_0, gather_1, gather_2, gather_3, gather_4)):
            if 0 <= step - lag < len(chunks):
                stage(step - lag)

    def add_into(ref, extra):
        total = ref[...].astype(F32)
        for more in extra:
            total = total + more[...].astype(F32)
        ref[...] = total.astype(BF)

    def slots(i, name):
        return getattr(r.red[chunks[i][0] == "F"], name).at[dims.slot[i]]

    def reduce_push(i, k, src, dst, dev):
        push(src, dst, r.ss.at[i, k], r.sr.at[i, k], dev)

    def reduce_wait(i, k, dst):
        arrived(dst, r.sr.at[i, k], r.ss.at[i, k])

    def line_reduce_send(part, land, send, recv):
        push_if(has_up, part(z_up), land.at[UP], send(UP), recv(UP), at_z(z_up))
        push_if(has_down, part(z_down), land.at[DOWN], send(DOWN), recv(DOWN), at_z(z_down))
        push_if(outer, part(z_end), land.at[RELAY], send(RELAY), recv(RELAY), at_z(z_in))
        push_if(outer, part(z_far), land.at[FAR], send(FAR), recv(FAR), at_z(z_far))

    def line_reduce_relay(part, land, send, recv):
        @pl.when(inner)
        def _():
            arrived(land.at[RELAY], recv(RELAY), send(RELAY))
            add_into(part(z_far), [land.at[RELAY]])

        push_if(inner, part(z_far), land.at[FAR], send(FAR), recv(FAR), at_z(z_far))

    def line_reduce_end(part, land, send, recv):
        arrived(land.at[FAR], recv(FAR), send(FAR))

        @pl.when(inner)
        def _():
            arrived(land.at[UP], recv(UP), send(UP))
            arrived(land.at[DOWN], recv(DOWN), send(DOWN))
            add_into(part(z), [land.at[FAR], land.at[UP], land.at[DOWN]])

        @pl.when(z == 0)
        def _():
            arrived(land.at[DOWN], recv(DOWN), send(DOWN))
            add_into(part(z), [land.at[FAR], land.at[DOWN]])

        @pl.when(z == DEPTH - 1)
        def _():
            arrived(land.at[UP], recv(UP), send(UP))
            add_into(part(z), [land.at[FAR], land.at[UP]])

    def reduce_sems(i, base):
        return sems(r.ss, r.sr, i, base)

    def reduce_0(i):
        over = slots(i, "ad")
        reduce_push(i, 14, view(i, True, "a", first, 1 - x, 1 - y), over.at[0], xn)
        reduce_push(i, 15, view(i, True, "a", second, 1 - x, 1 - y), over.at[1], yn)
        reduce_push(i, 18, view(i, True, "b", every, both, 1 - y), slots(i, "by"), yn)
        reduce_push(i, 19, view(i, True, "c", every, 1 - x, None), slots(i, "cx"), xn)

    def reduce_1(i):
        a, b, c_part = parts_of(i, True)
        over, beside = slots(i, "ad"), slots(i, "an")
        reduce_wait(i, 14, over.at[0])
        add_into(view(i, True, "a", first, x, 1 - y), [over.at[0]])
        reduce_push(i, 13, view(i, True, "a", every, x, 1 - y), beside.at[1], yn)
        reduce_wait(i, 15, over.at[1])
        add_into(view(i, True, "a", second, 1 - x, y), [over.at[1]])
        reduce_push(i, 12, view(i, True, "a", every, 1 - x, y), beside.at[0], xn)
        reduce_wait(i, 18, slots(i, "by"))
        add_into(view(i, True, "b", every, both, y), [slots(i, "by")])
        line_reduce_send(b, slots(i, "bz"), *reduce_sems(i, 4))
        reduce_wait(i, 19, slots(i, "cx"))
        add_into(view(i, True, "c", every, x, None), [slots(i, "cx")])
        line_reduce_send(c_part, slots(i, "cz"), *reduce_sems(i, 8))

    def reduce_2(i):
        a, b, c_part = parts_of(i, True)
        beside = slots(i, "an")
        reduce_wait(i, 12, beside.at[0])
        reduce_wait(i, 13, beside.at[1])
        add_into(view(i, True, "a", every, x, y), [beside.at[0], beside.at[1]])
        line_reduce_send(a, slots(i, "az"), *reduce_sems(i, 0))
        line_reduce_relay(b, slots(i, "bz"), *reduce_sems(i, 4))
        line_reduce_relay(c_part, slots(i, "cz"), *reduce_sems(i, 8))

    def reduce_3(i):
        a, b, c_part = parts_of(i, True)
        line_reduce_end(b, slots(i, "bz"), *reduce_sems(i, 4))
        reduce_push(i, 16, view(i, True, "b", one(z), 1 - x, y), slots(i, "bx"), xn)
        line_reduce_end(c_part, slots(i, "cz"), *reduce_sems(i, 8))
        reduce_push(i, 17, view(i, True, "c", one(z), x, 1 - y), slots(i, "cy"), yn)
        line_reduce_relay(a, slots(i, "az"), *reduce_sems(i, 0))

    def reduce_4(i):
        kind, layer, which, part = chunks[i]
        at = dims.slot[i]
        line_reduce_end(parts_of(i, True)[0], slots(i, "az"), *reduce_sems(i, 0))
        reduce_wait(i, 16, slots(i, "bx"))
        reduce_wait(i, 17, slots(i, "cy"))
        total = jnp.concatenate(
            [
                view(i, True, "a", one(z), x, y)[...].astype(F32)[0],
                (view(i, True, "b", one(z), x, y)[...].astype(F32) + slots(i, "bx")[...].astype(F32))[0],
                (view(i, True, "c", one(z), x, y)[...].astype(F32) + slots(i, "cy")[...].astype(F32))[0],
            ],
            axis=0,
        )
        if kind == "A":
            out = lay[layer].da
            rows = total.shape[0] // 2
            out[c, :, part * model : (part + 1) * model] = jnp.where(c == 0, total[:rows], total[rows:])
            r.fsa[at] = jnp.where(c == 0, total[rows:], total[:rows])
            push(r.fsa.at[at], r.fra.at[at], r.fs.at[i], r.fr.at[i], sib)
        else:
            out = lay[layer].df
            rows = pl.ds(part * dims.rows, dims.rows)
            lanes = total.shape[1] // 2
            out[c, which, rows, :] = jnp.where(c == 0, total[:, :lanes], total[:, lanes:])
            r.fsf[at] = jnp.where(c == 0, total[:, lanes:], total[:, :lanes])
            push(r.fsf.at[at], r.frf.at[at], r.fs.at[i], r.fr.at[i], sib)

    def reduce_out(i):
        kind, layer, which, part = chunks[i]
        at = dims.slot[i]
        if kind == "A":
            arrived(r.fra.at[at], r.fr.at[i], r.fs.at[i])
            lay[layer].da[1 - c, :, part * model : (part + 1) * model] = r.fra[at]
            if part == layers[layer].wide // model - 1:
                store(lay[layer].da, outs.lay[layer].da)
        else:
            arrived(r.frf.at[at], r.fr.at[i], r.fs.at[i])
            rows = pl.ds(part * dims.rows, dims.rows)
            lay[layer].df[1 - c, which, rows, :] = r.frf[at]
            if part == layers[layer].nr // dims.rows - 1:
                store(lay[layer].df.at[:, which], outs.lay[layer].df.at[:, which])

    def total_step(work, land, step, sends, recvs):
        dev = (sib, xn, yn, zn, zfar)[step]
        push(work.at[step], land.at[step], sends.at[step], recvs.at[step], dev)

    def total_add(work, land, step, sends, recvs):
        arrived(land.at[step], recvs.at[step], sends.at[step])
        work[step + 1] = work[step] + land[step]

    exchanges = []

    def exchange(part):
        slot = len(exchanges) % 2
        r.xs[slot] = part.astype(BF)
        copy = remote(r.xs.at[slot], r.xr.at[slot], r.es.at[slot], r.er.at[slot], sib)
        copy.start()
        exchanges.append(copy)

        def finish():
            copy.wait()
            return r.xs[slot].astype(F32) + r.xr[slot].astype(F32)

        return finish

    def vec_row(row):
        return r.vw[5, row : row + 1, :]

    def layer_vecs(at):
        sizes, rows, base = layers[at], dims.rows_of[at], dims.base[at]
        if sizes.hc * 2 == model:
            qv = r.vw[5, pl.ds(base + rows.qv + c, 1), :]
        else:
            both = vec_row(base + rows.qv)
            qv = jnp.where(c == 0, both[:, : 2 * sizes.hc], both[:, 2 * sizes.hc :])
        span = sizes.nc // model
        b1 = [r.vw[5, pl.ds(base + rows.b1 + c * span + s, 1), :] for s in range(span)]
        found = types.SimpleNamespace(bq=qv[:, : sizes.hc], bv=qv[:, sizes.hc :], b1=b1)
        for name, row in vars(rows).items():
            if not hasattr(found, name):
                setattr(found, name, vec_row(base + row))
        return found

    kept = lay
    wa = [one_layer.wa for one_layer in lay]
    weights = [one_layer.w for one_layer in lay]

    def order_rows(at, part):
        gathered, whole = lay[at].ga, wa[at]
        cols = slice(part * model, (part + 1) * model)
        rows = gathered.shape[3] // 2
        span = DEPTH * 2 * rows
        for y_at in range(SIDE):
            for z_at in range(DEPTH):
                left = gathered[y_at, z_at, 0, :, cols].astype(F32)
                right = gathered[y_at, z_at, 1, :, cols].astype(F32)
                for core in range(SIDE):
                    own = slice(core * rows, (core + 1) * rows)
                    both = jnp.concatenate([left[own], right[own]], axis=0).astype(BF)
                    begin = (y_at * SIDE + core) * span + z_at * 2 * rows
                    whole[begin : begin + 2 * rows, cols] = both

    def store_grad_rows(at, y_at, value, cols):
        blocks = lay[at].ga
        rows = blocks.shape[3] // 2
        span = DEPTH * 2 * rows
        for z_at in range(DEPTH):
            for x_at in range(SIDE):
                begin = (z_at * 2 + x_at) * rows
                both = [value[begin : begin + rows], value[span + begin : span + begin + rows]]
                blocks[y_at, z_at, x_at, :, cols] = jnp.concatenate(both, axis=0).astype(BF)

    def send_kv(at):
        kv = kept[at].kv
        push(kv.at[half], kv.at[half], r.ks.at[at], r.kr.at[at], zn)

    def wait_kv(at):
        kv = kept[at].kv
        arrived(kv.at[1 - half], r.kr.at[at], r.ks.at[at])

    def head_kv(at, h):
        sizes, kv = layers[at], kept[at].kv
        k = kv[:, :, h * HEAD : (h + 1) * HEAD].reshape(seq, HEAD)
        v = kv[:, :, sizes.hc + h * HEAD : sizes.hc + (h + 1) * HEAD].reshape(seq, HEAD)
        return k, v

    def attention(at):
        sizes, keep = layers[at], kept[at]
        lane = lax.broadcasted_iota(jnp.int32, (1, model), 1)
        first_lane = (y * SIDE + row_core) * group + x
        entry = vec_row(dims.length_row)
        entry = jnp.where(lane == first_lane, 256.0 * entry, jnp.where(lane == first_lane + 2, entry, 0.0))
        length = jnp.sum(entry, axis=1, keepdims=True)
        valid = lax.broadcasted_iota(jnp.int32, (1, seq), 1).astype(F32) < length
        for h in range(sizes.heads):
            q = keep.q[:, h * HEAD : (h + 1) * HEAD]
            k, v = head_kv(at, h)
            scores = jnp.where(valid, mm(q, k, 1, 1) * 0.125, NEGATIVE)
            exponent = jnp.exp(scores - jnp.max(scores, axis=1, keepdims=True))
            low = (exponent / jnp.sum(exponent, axis=1, keepdims=True)).astype(BF)
            keep.a[h] = low
            begin = sizes.pad + h * HEAD
            keep.ctx[:, begin : begin + HEAD] = mm(low, v, 1, 0).astype(BF)

    def attention_back(at, grad_ctx):
        sizes, keep = layers[at], kept[at]
        dkv, gp = lay[at].dkv, lay[at].dp
        for h in range(sizes.heads):
            q = keep.q[:, h * HEAD : (h + 1) * HEAD]
            k, v = head_kv(at, h)
            begin = sizes.pad + h * HEAD
            dc = grad_ctx[:, begin : begin + HEAD]
            low = keep.a[h]
            a = low.astype(F32)
            da = mm(dc, v, 1, 1)
            inner = jnp.sum(a * da, axis=1, keepdims=True)
            ds = (0.125 * a * (da - inner)).astype(BF)
            gp[:, h * HEAD : (h + 1) * HEAD] = mm(ds, k, 1, 0).astype(BF)
            dk = mm(ds, q, 0, 0).astype(BF).reshape(2, tok, HEAD)
            dv = mm(low, dc, 0, 0).astype(BF).reshape(2, tok, HEAD)
            dkv[:, :, h * HEAD : (h + 1) * HEAD] = dk
            dkv[:, :, sizes.hc + h * HEAD : sizes.hc + (h + 1) * HEAD] = dv

    def block(at, which, b):
        sizes = layers[at]
        w = weights[at][which, b * sizes.zb : (b + 1) * sizes.zb]
        return w.reshape(model, model)

    def up(at, vecs):
        sizes, keep = layers[at], kept[at]
        for b in range(sizes.nc // model):
            cols = slice(b * model, (b + 1) * model)
            u = mm(keep.hb[...], block(at, 0, b), 1, 1) + vecs.b1[b]
            phi = 0.5 * (1.0 + lax.erf(u * 0.7071067811865476))
            keep.g[:, cols] = (u * phi).astype(BF)
            density = jnp.exp(u * u * -0.5) * 0.3989422804014327
            keep.gp[:, cols] = (phi + u * density).astype(BF)

    def down(at):
        sizes, keep = layers[at], kept[at]
        total = None
        for b in range(sizes.nc // model):
            term = mm(keep.g[:, b * model : (b + 1) * model], block(at, 1, b), 1, 0)
            total = term if total is None else total + term
        return total

    def weight_grad(at, which, left, right):
        sizes = layers[at]
        dw = lay[at].dw
        span = model // 2
        zb = sizes.zb // 2
        for b in range(sizes.nc // span):
            value = mm(left[:, b * span : (b + 1) * span], right[...], 0, 0).astype(BF)
            dw[which, b * zb : (b + 1) * zb] = value.reshape(zb, 2, sizes.nr, model)


    def pack_a(at):
        sizes, width = layers[at], 2 * layers[at].hc
        rows_in = lay[at].pai[...].astype(F32)
        rows_out = lay[at].pao[...].astype(F32)
        halves = []
        for h in range(2):
            own = slice(h * sizes.hc, (h + 1) * sizes.hc)
            pieces = [rows_in[:, p * width : (p + 1) * width][:, own] for p in range(3)]
            halves.append(jnp.concatenate(pieces + [rows_out[:, own]], axis=1))
        send = lay[at].asend
        send[...] = jnp.where(c == 0, halves[1], halves[0])
        if at == 0:
            pl.semaphore_wait(bar, PARTNERS)
        push(send, lay[at].ar, r.is_.at[2 * at], r.ir.at[2 * at], sib)
        return jnp.where(c == 0, halves[0], halves[1])

    def pack_f(at):
        sizes = layers[at]
        first = lay[at].pfi[...].astype(F32).T
        second = lay[at].pfo[...].astype(F32)
        if dims.turned[at]:
            second = second.T
        send, own = lay[at].fsend, []
        for which, value in enumerate((first, second)):
            low_half, high_half = value[: sizes.nr], value[sizes.nr :]
            own.append(jnp.where(c == 0, low_half, high_half))
            send[which] = jnp.where(c == 0, high_half, low_half).astype(BF)
        push(send, lay[at].fr, r.is_.at[2 * at + 1], r.ir.at[2 * at + 1], sib)
        return own

    def prepare_a(at, own):
        land, blocks = lay[at].ar, lay[at].ga
        arrived(land, r.ir.at[2 * at], r.is_.at[2 * at])
        other = land[...]
        pair = [jnp.where(c == 0, own, other), jnp.where(c == 0, other, own)]
        blocks[y, z, x] = jnp.concatenate(pair, axis=0).astype(BF)

    def prepare_f(at, own):
        land = lay[at].fr
        arrived(land, r.ir.at[2 * at + 1], r.is_.at[2 * at + 1])
        lanes = pl.ds(pl.multiple_of(y * half_lanes, 128), half_lanes)
        for which in range(2):
            other = land[which].astype(F32)
            pair = [jnp.where(c == 0, own[which], other), jnp.where(c == 0, other, own[which])]
            weights[at][which, z, x, :, lanes] = jnp.concatenate(pair, axis=1).astype(BF)

    group = dims.group
    per_row = model // group
    index = dp * DEPTH * SIDE + mp

    def targets(at_group):
        result, begin = jnp.full_like(at_group, dims.length_row * per_row) + dp, 0
        for at, sizes in enumerate(layers):
            base = dims.base[at] * per_row
            head, count_b = sizes.hc // group, sizes.nr // group
            up_at = dims.rows_of[at].b1 * per_row
            count = dims.shift_groups[at]
            g = index * count + (at_group - begin)
            w = g % (2 * head)
            qv = (w // head) * (2 * head) + (g // (2 * head)) * head + w % head
            b = g - up_at
            up_to = up_at + ((b % (2 * count_b)) // count_b) * (8 * count_b)
            up_to = up_to + (b // (2 * count_b)) * count_b + b % count_b
            place = jnp.where(g < 4 * head, qv, jnp.where((b >= 0) & (b < 16 * count_b), up_to, g))
            inside = (at_group >= begin) & (at_group < begin + count)
            result = jnp.where(inside, base + place, result)
            begin += count
            count = dims.gain_groups[at]
            place = dims.rows_of[at].g1 * per_row + index * count + (at_group - begin)
            inside = (at_group >= begin) & (at_group < begin + count)
            result = jnp.where(inside, base + place, result)
            begin += count
        return result // per_row, result % per_row

    groups = dims.vec_rows
    lane_group = lax.broadcasted_iota(jnp.int32, (groups, dims.lanes), 1) // group
    lane_own = lane_group == lax.broadcasted_iota(jnp.int32, (groups, dims.lanes), 0)

    def place_masks():
        down = lax.broadcasted_iota(jnp.int32, (groups, 1), 0)
        across = lax.broadcasted_iota(jnp.int32, (1, groups), 1)
        row_down, place_down = targets(down)
        row_across, _ = targets(across)
        lane = lax.broadcasted_iota(jnp.int32, (groups, model), 1) // group
        to_row = jnp.where(row_across == down, 1.0, 0.0).astype(BF)
        from_row = jnp.where(row_down == across, 1.0, 0.0).astype(BF)
        return lane == place_down, to_row, from_row

    def pack_vectors():
        lengths = r.len[...].astype(F32).reshape(1, 2) * jnp.where(mp == 0, 1.0, 0.0)
        high = jnp.floor(lengths * (1.0 / 256.0))
        pieces = []
        for own in lay:
            pieces += [own.psh[...].astype(F32).reshape(1, -1), own.pga[...].astype(F32).reshape(1, -1)]
        pieces += [high, lengths - 256.0 * high]
        used = sum(p.shape[1] for p in pieces)
        values = jnp.concatenate(pieces + [jnp.zeros((1, dims.lanes - used), F32)], axis=1)
        spread_out = jnp.where(lane_own, values, 0.0).astype(BF)
        i = lax.broadcasted_iota(jnp.int32, (dims.lanes, model), 0) % group
        j = lax.broadcasted_iota(jnp.int32, (dims.lanes, model), 1) % group
        r.hot[...] = jnp.where(i == j, 1.0, 0.0).astype(BF)
        in_place, to_row, _ = place_masks()
        wide = jnp.where(in_place, mm(spread_out, r.hot[...], 1, 0), 0.0).astype(BF)
        return mm(to_row, wide, 1, 0)

    def unpack_vectors(values):
        in_place, _, from_row = place_masks()
        total, rest = None, values
        for _ in range(3):
            low_part = rest.astype(BF)
            rest = rest - low_part.astype(F32)
            wide = jnp.where(in_place, mm(from_row, low_part, 1, 0), 0.0).astype(BF)
            term = jnp.where(lane_own, mm(wide, r.hot[...], 1, 1), 0.0)
            total = term if total is None else total + term
        return rowsum(total)

    for copy in fetched[:2]:
        copy.wait()
    own_a = pack_a(0)
    fetched[2].wait()
    spread(r.hid, r.xin, r.hs, r.hr)
    for copy in fetched[3:5]:
        copy.wait()
    own_f = pack_f(0)
    prepare_a(0, own_a)
    pump(0)
    prepare_f(0, own_f)
    pump(1)
    for copy in fetched[5:]:
        copy.wait()
    r.vw[0] = pack_vectors()
    total_step(r.vw, r.vl, 0, r.vs, r.vr)
    own_a, own_f = pack_a(1), pack_f(1)
    total_add(r.vw, r.vl, 0, r.vs, r.vr)
    total_step(r.vw, r.vl, 1, r.vs, r.vr)
    prepare_a(1, own_a)
    prepare_f(1, own_f)
    total_add(r.vw, r.vl, 1, r.vs, r.vr)
    total_step(r.vw, r.vl, 2, r.vs, r.vr)
    pump(2)
    spread_done(r.hid, r.xin, r.hs, r.hr, r.os.at[0], r.os.at[1])
    total_add(r.vw, r.vl, 2, r.vs, r.vr)
    total_step(r.vw, r.vl, 3, r.vs, r.vr)
    pump(3)
    total_add(r.vw, r.vl, 3, r.vs, r.vr)
    total_step(r.vw, r.vl, 4, r.vs, r.vr)
    pump(4)
    total_add(r.vw, r.vl, 4, r.vs, r.vr)
    vecs = [layer_vecs(0), layer_vecs(1)]

    def project(at, hidden_low, parts):
        sizes, keep = layers[at], kept[at]
        for part in parts:
            order_rows(at, part)
        if sizes.wide == model:
            p = mm(hidden_low, wa[at][...], 1, 0)
            keep.q[...] = (p[:, : sizes.hc] + vecs[at].bq).astype(BF)
            keep.kv[half, :, : sizes.hc] = p[:, sizes.hc : 2 * sizes.hc].astype(BF)
            keep.kv[half, :, sizes.hc :] = (p[:, 2 * sizes.hc : 3 * sizes.hc] + vecs[at].bv).astype(BF)
        elif parts == (0,):
            p = mm(hidden_low, wa[at][:, : 2 * sizes.hc], 1, 0)
            keep.q[...] = (p[:, : sizes.hc] + vecs[at].bq).astype(BF)
            keep.kv[half, :, : sizes.hc] = p[:, sizes.hc :].astype(BF)
        else:
            p = mm(hidden_low, wa[at][:, 2 * sizes.hc : 3 * sizes.hc], 1, 0)
            keep.kv[half, :, sizes.hc :] = (p + vecs[at].bv).astype(BF)

    def attend_out(at):
        return mm(kept[at].ctx[...], wa[at][:, layers[at].start :], 1, 1)

    def norm_one(at, base, branch):
        keep, v = kept[at], vecs[at]
        normed, scale = normalize(base + branch + v.bo)
        keep.n1[...] = normed
        keep.s1[...] = scale
        result = normed * v.g1 + v.beta1
        keep.hb[...] = result.astype(BF)
        return result

    def norm_two(at, base, branch):
        keep, v = kept[at], vecs[at]
        normed, scale = normalize(base + branch + v.b2)
        keep.n2[...] = normed
        keep.s2[...] = scale
        return normed * v.g2 + v.beta2

    if layers[1].pad:
        kept[1].ctx[...] = jnp.zeros_like(kept[1].ctx)
        lay[1].dp[...] = jnp.zeros_like(lay[1].dp)
    kept[0].xb[...] = r.xin[...].reshape(tok, model)
    project(0, kept[0].xb[...], (0,))
    pump(5)
    project(0, kept[0].xb[...], (1,))
    send_kv(0)
    spread(r.cot, r.cin, r.cs, r.cr)
    pump(6)
    pump(7)
    wait_kv(0)
    attention(0)
    wait_branch = exchange(attend_out(0))
    pump(8)
    normed = norm_one(0, kept[0].xb[...].astype(F32), wait_branch())
    up(0, vecs[0])
    spread_done(r.cot, r.cin, r.cs, r.cr, r.os.at[2], r.os.at[3])
    pump(9)
    wait_branch = exchange(down(0))
    pump(10)
    middle = norm_two(0, normed, wait_branch())
    kept[1].xb[...] = middle.astype(BF)
    project(1, kept[1].xb[...], (0,))
    send_kv(1)
    pump(11)
    wait_kv(1)
    attention(1)
    wait_branch = exchange(attend_out(1))
    normed = norm_one(1, middle, wait_branch())
    up(1, vecs[1])
    pump(12)
    wait_branch = exchange(down(1))
    final = norm_two(1, normed, wait_branch())
    r.oblk[...] = final.astype(BF).reshape(r.oblk.shape)
    collect(r.oblk, r.oland, r.ys, r.yr)
    wait_sent()

    r.vw[0] = jnp.zeros_like(r.vw[0])
    once = jnp.where(c == 0, 1.0, 0.0)

    def put_vec(at, name, value):
        row = dims.base[at] + getattr(dims.rows_of[at], name)
        r.vw[0, row : row + 1, :] = value * once

    def back_two(at, grad):
        keep, v = kept[at], vecs[at]
        n2 = keep.n2[...]
        put_vec(at, "g2", rowsum(grad * n2))
        put_vec(at, "beta2", rowsum(grad))
        dz2 = normalize_back(grad * v.g2, n2, keep.s2[...])
        r.eo[...] = dz2.astype(BF)
        put_vec(at, "b2", rowsum(r.eo[...].astype(F32)))
        return dz2

    def back_up(at):
        sizes, keep = layers[at], kept[at]
        base = dims.base[at] + dims.rows_of[at].b1
        span = sizes.nc // model
        for b in range(span):
            cols = slice(b * model, (b + 1) * model)
            dg = mm(r.eo[...], block(at, 1, b), 1, 1)
            du = (dg * keep.gp[:, cols].astype(F32)).astype(BF)
            keep.g[:, cols] = du
            r.vw[0, pl.ds(base + c * span + b, 1), :] = rowsum(du.astype(F32))

    def back_in(at):
        sizes, keep = layers[at], kept[at]
        total = None
        for b in range(sizes.nc // model):
            term = mm(keep.g[:, b * model : (b + 1) * model], block(at, 0, b), 1, 0)
            total = term if total is None else total + term
        return total

    def back_one(at, grad):
        keep, v = kept[at], vecs[at]
        n1 = keep.n1[...]
        put_vec(at, "g1", rowsum(grad * n1))
        put_vec(at, "beta1", rowsum(grad))
        dz1 = normalize_back(grad * v.g1, n1, keep.s1[...])
        r.eo[...] = dz1.astype(BF)
        put_vec(at, "bo", rowsum(r.eo[...].astype(F32)))
        grad_ctx = mm(r.eo[...], wa[at][:, layers[at].start :], 1, 0).astype(BF)
        return dz1, grad_ctx

    def send_dkv(at):
        dkv, land = lay[at].dkv, lay[at].dkr
        push(dkv.at[1 - half], land, r.ks.at[2 + at], r.kr.at[2 + at], zn)

    def take_dkv(at):
        sizes = layers[at]
        dkv, land, gp = lay[at].dkv, lay[at].dkr, lay[at].dp
        arrived(land, r.kr.at[2 + at], r.ks.at[2 + at])
        total = (dkv[half].astype(F32) + land[...].astype(F32)).astype(BF)
        gp[:, sizes.hc : 3 * sizes.hc] = total
        qsum = rowsum(gp[:, : sizes.hc].astype(F32))
        vsum = rowsum(total[:, sizes.hc :].astype(F32))
        both = jnp.concatenate([qsum, vsum], axis=1)
        row = dims.base[at] + dims.rows_of[at].qv
        if 2 * sizes.hc == model:
            r.vw[0, pl.ds(row + c, 1), :] = both
        else:
            blank = jnp.zeros_like(both)
            left, right = jnp.where(c == 0, both, blank), jnp.where(c == 0, blank, both)
            r.vw[0, row : row + 1, :] = jnp.concatenate([left, right], axis=1)

    def projection_grad(at, part):
        sizes, keep, gp = layers[at], kept[at], lay[at].dp
        begin, end = part * model, (part + 1) * model
        for y_at in range(SIDE):
            rows = slice(y_at * half_lanes, (y_at + 1) * half_lanes)
            pieces = []
            xb = keep.xb[:, rows]
            split = min(end, sizes.start)
            if begin < split:
                pieces.append(mm(xb, gp[:, begin:split], 0, 0))
            if end > sizes.start:
                value = mm(r.eo[:, rows], keep.ctx[...], 0, 0)
                if sizes.pad:
                    value = value + mm(xb, gp[:, sizes.start : end], 0, 0)
                pieces.append(value)
            value = pieces[0] if len(pieces) == 1 else jnp.concatenate(pieces, axis=1)
            store_grad_rows(at, y_at, value, slice(begin, end))

    def back_hidden(at):
        gp = lay[at].dp
        width = gp.shape[1]
        return mm(gp[...], wa[at][:, :width], 1, 1)

    grad = r.cin[...].reshape(tok, model).astype(F32)
    dz2 = back_two(1, grad)
    weight_grad(1, 1, kept[1].g, r.eo)
    reduce_0(8)
    back_up(1)
    weight_grad(1, 0, kept[1].g, kept[1].hb)
    reduce_0(7)
    wait_branch = exchange(back_in(1))
    dz1, grad_ctx = back_one(1, dz2 + wait_branch())
    reduce_1(8)
    attention_back(1, grad_ctx)
    send_dkv(1)
    reduce_1(7)
    reduce_2(8)
    take_dkv(1)
    projection_grad(1, 0)
    reduce_0(6)
    wait_branch = exchange(back_hidden(1))
    reduce_2(7)
    reduce_3(8)
    grad = dz1 + wait_branch()
    dz2 = back_two(0, grad)
    weight_grad(0, 1, kept[0].g, r.eo)
    reduce_0(4)
    reduce_1(6)
    reduce_0(5)
    back_up(0)
    weight_grad(0, 0, kept[0].g, kept[0].hb)
    reduce_3(7)
    reduce_4(8)
    reduce_0(2)
    wait_branch = exchange(back_in(0))
    reduce_1(4)
    reduce_2(6)
    reduce_0(3)
    dz1, grad_ctx = back_one(0, dz2 + wait_branch())
    reduce_1(5)
    reduce_3(6)
    attention_back(0, grad_ctx)
    send_dkv(0)
    reduce_4(7)
    reduce_2(4)
    reduce_1(2)
    reduce_4(6)
    reduce_3(4)
    take_dkv(0)
    projection_grad(0, 0)
    reduce_0(0)
    projection_grad(0, 1)
    reduce_2(5)
    reduce_0(1)
    total_step(r.vw, r.vl, 0, r.ws, r.wr)
    wait_branch = exchange(back_hidden(0))
    reduce_1(3)
    reduce_4(4)
    reduce_3(5)
    reduce_2(2)
    grad = dz1 + wait_branch()
    r.gblk[...] = grad.astype(BF).reshape(r.gblk.shape)
    collect(r.gblk, r.gland, r.zs, r.zr)
    total_add(r.vw, r.vl, 0, r.ws, r.wr)
    total_step(r.vw, r.vl, 1, r.ws, r.wr)
    reduce_1(0)
    reduce_4(5)
    reduce_3(2)
    reduce_2(3)
    total_add(r.vw, r.vl, 1, r.ws, r.wr)
    total_step(r.vw, r.vl, 2, r.ws, r.wr)
    reduce_1(1)
    reduce_4(2)
    reduce_3(3)
    reduce_2(0)
    total_add(r.vw, r.vl, 2, r.ws, r.wr)
    total_step(r.vw, r.vl, 3, r.ws, r.wr)
    for i in (8, 7, 6, 4, 5):
        reduce_out(i)
    reduce_4(3)
    reduce_3(0)
    reduce_2(1)
    total_add(r.vw, r.vl, 3, r.ws, r.wr)
    total_step(r.vw, r.vl, 4, r.ws, r.wr)
    reduce_out(2)
    reduce_4(0)
    reduce_3(1)
    reduce_out(3)
    total_add(r.vw, r.vl, 4, r.ws, r.wr)
    r.dvec[...] = unpack_vectors(r.vw[5])
    store(r.dvec, outs.dvec)
    collect_done(r.oblk, r.oland, r.ys, r.yr)
    store(r.oland, outs.out)
    reduce_4(1)
    collect_done(r.gblk, r.gland, r.zs, r.zr)
    store(r.gland, outs.gh)
    reduce_out(0)
    reduce_out(1)
    wait_sent()
    for copy in stored:
        copy.wait()


def fused_call(hid, cot, lengths, params, dims):
    model, tok, seq = dims.model, dims.tok, dims.seq
    block = (4, tok // 4, model)
    vmem = pltpu.VMEM
    dma = pltpu.SemaphoreType.DMA
    rows_in = params[0][0].shape[0]
    shape = jax.ShapeDtypeStruct
    given = dict(hid=hid, cot=cot, len=lengths, lay=[])
    outs = dict(out=shape(hid.shape, BF), gh=shape(hid.shape, BF), lay=[], dvec=shape((1, dims.lanes), F32))
    for (ai, ao, fi, fo, sh, ga), sizes in zip(params, dims.layers):
        given["lay"].append(dict(pai=ai, pao=ao, pfi=fi, pfo=fo, psh=sh, pga=ga))
        outs["lay"].append(
            dict(
                da=shape((2, rows_in, sizes.wide), F32),
                df=shape((2, 2, sizes.nr, model // 4), F32),
            )
        )
    as_scratch = lambda tree: jax.tree.map(lambda v: vmem(v.shape, v.dtype), tree)
    held, made = as_scratch(given), as_scratch({key: outs[key] for key in ("lay", "dvec")})
    vec = (dims.vec_rows, model)
    rows_a = 2 * rows_in
    count_a = sum(chunk[0] == "A" for chunk in dims.chunks)
    count_f = len(dims.chunks) - count_a
    half = model // 2
    n = len(dims.chunks)
    scratch = dict(
        xin=vmem(block, BF),
        cin=vmem(block, BF),
        oblk=vmem(block, BF),
        gblk=vmem(block, BF),
        oland=vmem(hid.shape, BF),
        gland=vmem(hid.shape, BF),
        vw=vmem((6,) + vec, F32),
        vl=vmem((5,) + vec, F32),
        xs=vmem((2, tok, model), BF),
        xr=vmem((2, tok, model), BF),
        eo=vmem((tok, model), BF),
        fsa=vmem((count_a, rows_in, model), F32),
        fra=vmem((count_a, rows_in, model), F32),
        fsf=vmem((count_f, dims.rows, half // 2), F32),
        frf=vmem((count_f, dims.rows, half // 2), F32),
        hot=vmem((dims.lanes, model), BF),
        gs=dma((n, 20)),
        gr=dma((n, 20)),
        ss=dma((n, 20)),
        sr=dma((n, 20)),
        fs=dma((n,)),
        fr=dma((n,)),
        vs=dma((5,)),
        vr=dma((5,)),
        ws=dma((5,)),
        wr=dma((5,)),
        hs=dma((4,)),
        hr=dma((4,)),
        cs=dma((4,)),
        cr=dma((4,)),
        ys=dma((4,)),
        yr=dma((4,)),
        zs=dma((4,)),
        zr=dma((4,)),
        is_=dma((4,)),
        ir=dma((4,)),
        os=dma((4,)),
        ks=dma((4,)),
        kr=dma((4,)),
        es=dma((2,)),
        er=dma((2,)),
        ins=dma((16,)),
        outs=dma((10,)),
        red=[],
        lay=[],
    )
    for count, rows, wide, pair in (
        (count_a, rows_a - 32, model, (2, 4, 16, model)),
        (count_f, dims.rows - 32, half, (4, 16, model)),
    ):
        line = pair[:-3] + (1, 16, model)
        scratch["red"].append(
            dict(
                ad=vmem((count, 2, 2, rows, wide), BF),
                an=vmem((count, 2, 4, rows, wide), BF),
                az=vmem((count, 4, 1, rows, wide), BF),
                by=vmem((count, 4, 2, 16, wide), BF),
                bz=vmem((count, 4, 1, 2, 16, wide), BF),
                bx=vmem((count, 1, 16, wide), BF),
                cx=vmem((count,) + pair, BF),
                cz=vmem((count, 4) + line, BF),
                cy=vmem((count, 1, 16, wide), BF),
            )
        )
    for sizes in dims.layers:
        scratch["lay"].append(
            dict(
                ar=vmem((rows_in, sizes.wide), F32),
                asend=vmem((rows_in, sizes.wide), F32),
                fr=vmem((2, sizes.nr, model // 4), BF),
                fsend=vmem((2, sizes.nr, model // 4), BF),
                ga=vmem((SIDE, DEPTH, SIDE, rows_a, sizes.wide), BF),
                wa=vmem((model, sizes.wide), BF),
                w=vmem((2, DEPTH, SIDE, sizes.nr, model), BF),
                dw=vmem((2, DEPTH, SIDE, sizes.nr, model), BF),
                xb=vmem((tok, model), BF),
                q=vmem((tok, sizes.hc), BF),
                kv=vmem((2, tok, 2 * sizes.hc), BF),
                a=vmem((sizes.heads, tok, seq), BF),
                ctx=vmem((tok, sizes.wide - sizes.start), BF),
                n1=vmem((tok, model), F32),
                s1=vmem((tok, 1), F32),
                hb=vmem((tok, model), BF),
                g=vmem((tok, sizes.nc), BF),
                gp=vmem((tok, sizes.nc), BF),
                n2=vmem((tok, model), F32),
                s2=vmem((tok, 1), F32),
                dkv=vmem((2, tok, 2 * sizes.hc), BF),
                dkr=vmem((tok, 2 * sizes.hc), BF),
                dp=vmem((tok, sizes.wide if sizes.pad else sizes.start), BF),
            )
        )
    inputs, outputs = jax.tree.leaves(given), jax.tree.leaves(outs)
    whole = pl.BlockSpec(memory_space=pl.ANY)
    local = (scratch, held, made)
    values = pl.pallas_call(
        functools.partial(fused_kernel, dims, jax.tree.structure((given, outs) + local)),
        out_shape=outputs,
        in_specs=[whole] * len(inputs),
        out_specs=[whole] * len(outputs),
        scratch_shapes=jax.tree.leaves(local),
        compiler_params=pltpu.CompilerParams(
            collective_id=0, has_side_effects=True, vmem_limit_bytes=dims.vmem
        ),
        name="layers",
    )(*inputs)
    return jax.tree.unflatten(jax.tree.structure(outs), values)


def finish_kernel(dims, tree, *refs):
    given, (out, gh, *results) = jax.tree.unflatten(tree, refs)
    r = named(given)
    out[...] = r.out[...]
    gh[...] = r.gh[...].astype(F32)
    begin = 0
    for at, sizes in enumerate(dims.layers):
        attn, ffn = r.lay[at].da, r.lay[at].df
        to_ai, to_ao, to_fi, to_fo, to_sh, to_ga = results[6 * at : 6 * at + 6]
        for p in range(3):
            for h in range(2):
                to = (2 * p + h) * sizes.hc
                to_ai[:, to : to + sizes.hc] = attn[h, :, p * sizes.hc : (p + 1) * sizes.hc]
        for h in range(2):
            to_ao[:, h * sizes.hc : (h + 1) * sizes.hc] = attn[h, :, 3 * sizes.hc :]
        down = ffn[:, 1].reshape(2 * sizes.nr, ffn.shape[3])
        to_fo[...] = down.T if dims.turned[at] else down
        to_fi[...] = ffn[:, 0].reshape(2 * sizes.nr, ffn.shape[3]).T
        for ref in (to_sh, to_ga):
            ref[...] = r.dvec[0, begin : begin + ref.shape[0]]
            begin += ref.shape[0]


def finish_call(given, params, dims):
    leaves, tree = jax.tree.flatten(given)
    outs = [jax.ShapeDtypeStruct(given["out"].shape, d) for d in (BF, F32)]
    outs += [jax.ShapeDtypeStruct(p.shape, F32) for shards in params for p in shards]
    whole = pl.BlockSpec(memory_space=pltpu.VMEM)
    return pl.pallas_call(
        functools.partial(finish_kernel, dims, jax.tree.structure((given, outs))),
        out_shape=outs,
        in_specs=[whole] * len(leaves),
        out_specs=[whole] * len(outs),
        compiler_params=pltpu.CompilerParams(vmem_limit_bytes=dims.vmem),
        name="finish",
    )(*leaves)


def make_dims(hidden_in, teacher, student):
    model = hidden_in.shape[2]
    layers = [
        layer_sizes(model, p[0].shape[1] // 3, p[2].shape[1] * DEPTH * SIDE) for p in (teacher, student)
    ]
    rows = layers[1].nr
    chunks = []
    for at, sizes in enumerate(layers):
        chunks += [("A", at, 0, part) for part in range(sizes.wide // model)]
        for which in (0, 1):
            chunks += [("F", at, which, part) for part in range(sizes.nr // rows)]
    counts, slot = {"A": 0, "F": 0}, []
    for chunk in chunks:
        slot.append(counts[chunk[0]])
        counts[chunk[0]] += 1
    group = model // (SIDE * SIDE * DEPTH * SIDE)
    shift_groups = [p[4].shape[0] // group for p in (teacher, student)]
    gain_groups = [p[5].shape[0] // group for p in (teacher, student)]
    rows_of, base, at = [], [], 0
    for sizes in layers:
        found, count = vec_rows(model, sizes)
        rows_of.append(found)
        base.append(at)
        at += count
    return types.SimpleNamespace(
        model=model,
        tok=4 * hidden_in.shape[1],
        seq=8 * hidden_in.shape[1],
        layers=layers,
        chunks=chunks,
        slot=slot,
        rows=rows,
        unit_rows={"A": 2 * teacher[0].shape[0], "F": rows},
        rows_of=rows_of,
        base=base,
        length_row=at,
        vec_rows=(at + 8) // 8 * 8,
        turned=[p[3].shape[0] > p[3].shape[1] for p in (teacher, student)],
        group=group,
        lanes=(sum(shift_groups + gain_groups) * group + 4 + 127) // 128 * 128,
        shift_groups=shift_groups,
        gain_groups=gain_groups,
        vmem=63 * 2**20,
    )


def fast_body(hidden_in, cotangent, lengths, *shards):
    params = (shards[:6], shards[6:])
    dims = make_dims(hidden_in, *params)
    turn = lambda shards, turned: (shards[0], shards[1].T, shards[2], shards[3].T if turned else shards[3])
    params = [turn(p, turned) + p[4:] for p, turned in zip(params, dims.turned)]
    values = fused_call(hidden_in, cotangent, lengths, params, dims)
    out, grad_hidden, *grads = finish_call(values, params, dims)
    results = [out, grad_hidden]
    for at, turned in enumerate(dims.turned):
        own = tuple(grads[6 * at : 6 * at + 6])
        results += turn(own, turned) + own[4:]
    return tuple(results)


def body(axes, *args):
    rows, tokens, model = args[0].shape
    fits = axes["dp"] == SIDE * SIDE and axes["mp"] == DEPTH * SIDE
    if fits and rows == 2 and tokens % 16 == 0 and model % 256 == 0:
        return fast_body(*args)
    return general_body(*args)


def general_body(
    hidden_in,
    cotangent,
    lengths,
    teacher_attn_in,
    teacher_attn_out,
    teacher_ffn_in,
    teacher_ffn_out,
    teacher_shifts,
    teacher_gains,
    student_attn_in,
    student_attn_out,
    student_ffn_in,
    student_ffn_out,
    student_shifts,
    student_gains,
):
    span_len = hidden_in.shape[1] * lax.axis_size("mp")
    positions = jnp.arange(span_len)
    valid_keys = positions[None, :] < lengths[:, None]
    teacher = fetch(
        teacher_attn_in,
        teacher_attn_out,
        teacher_ffn_in,
        teacher_ffn_out,
        teacher_shifts,
        teacher_gains,
    )
    student = fetch(
        student_attn_in,
        student_attn_out,
        student_ffn_in,
        student_ffn_out,
        student_shifts,
        student_gains,
    )
    middle, teacher_kept = forward_layer(hidden_in.astype(jnp.float32), teacher, valid_keys)
    final, student_kept = forward_layer(middle, student, valid_keys)
    grad_middle, student_grads = backward_layer(
        cotangent.astype(jnp.float32), student_kept, student, valid_keys
    )
    grad_input, teacher_grads = backward_layer(grad_middle, teacher_kept, teacher, valid_keys)
    teacher_totals = reduce_grads(teacher_grads)
    student_totals = reduce_grads(student_grads)
    return (final.astype(jnp.bfloat16), grad_input) + teacher_totals + student_totals


def solution(mesh):
    in_specs = (
        P("dp", "mp", None),
        P("dp", "mp", None),
        P("dp"),
        P(("dp", "mp"), None),
        P(None, ("dp", "mp")),
        P("dp", "mp"),
        P("mp", "dp"),
        P(("dp", "mp")),
        P(("dp", "mp")),
        P(("dp", "mp"), None),
        P(None, ("dp", "mp")),
        P("dp", "mp"),
        P("mp", "dp"),
        P(("dp", "mp")),
        P(("dp", "mp")),
    )
    out_specs = (
        P("dp", "mp", None),
        P("dp", "mp", None),
        P(("dp", "mp"), None),
        P(None, ("dp", "mp")),
        P("dp", "mp"),
        P("mp", "dp"),
        P(("dp", "mp")),
        P(("dp", "mp")),
        P(("dp", "mp"), None),
        P(None, ("dp", "mp")),
        P("dp", "mp"),
        P("mp", "dp"),
        P(("dp", "mp")),
        P(("dp", "mp")),
    )
    return jax.shard_map(
        functools.partial(body, dict(mesh.shape)), mesh=mesh, in_specs=in_specs, out_specs=out_specs, check_vma=False)
```

```python
import functools
import types

import jax
import jax.numpy as jnp
from jax import lax
from jax.experimental import pallas as pl
from jax.experimental.pallas import tpu as pltpu
from jax.sharding import PartitionSpec as P

HEAD = 64


EPSILON = 1e-06
NEGATIVE = -1e30


def layer_norm(values, gain, shift):
    centered = values - jnp.mean(values, axis=-1, keepdims=True)
    variance = jnp.mean(centered * centered, axis=-1, keepdims=True)
    return centered * lax.rsqrt(variance + EPSILON) * gain + shift


def smooth_gate(pre_act):
    return jax.nn.gelu(pre_act, approximate=False)


def split_shifts(shifts, head_width, model_width, hidden_width):
    spans_list = [
        head_width,
        head_width,
        model_width,
        model_width,
        hidden_width,
        model_width,
        model_width,
    ]
    pieces = []
    offset = 0
    for length in spans_list:
        pieces.append(shifts[offset : offset + length])
        offset = offset + length
    return pieces


def to_heads(values):
    return values.reshape(values.shape[0], values.shape[1], values.shape[2] // HEAD, HEAD)


def score_block(queries, all_keys, valid_keys):
    raw = jnp.einsum(
        "rqhd,rkhd->rhqk", to_heads(queries), to_heads(all_keys), preferred_element_type=jnp.float32
    )
    return jnp.where(valid_keys[:, None, None, :], raw * 0.125, NEGATIVE)


def fetch(attn_in, attn_out, ffn_in, ffn_out, shifts, gains):
    whole_in, whole_out, whole_shifts, whole_gains = (
        lax.all_gather(attn_in, ("dp", "mp"), axis=0, tiled=True),
        lax.all_gather(attn_out, ("dp", "mp"), axis=1, tiled=True),
        lax.all_gather(shifts, ("dp", "mp"), axis=0, tiled=True),
        lax.all_gather(gains, ("dp", "mp"), axis=0, tiled=True),
    )
    ffn_first, ffn_second = (
        lax.all_gather(ffn_in, "dp", axis=0, tiled=True),
        lax.all_gather(ffn_out, "dp", axis=1, tiled=True),
    )
    return (
        whole_in,
        whole_out,
        ffn_first,
        ffn_second,
        whole_shifts.astype(jnp.float32),
        whole_gains.astype(jnp.float32),
    )


def forward_layer(hidden, params, valid_keys):
    attn_in, attn_out, ffn_first, ffn_second, shifts, gains = params
    model_width = hidden.shape[-1]
    head_width = attn_in.shape[1] // 3
    hidden_width = shifts.shape[0] - 2 * head_width - 4 * model_width
    pieces = split_shifts(shifts, head_width, model_width, hidden_width)
    bias_query, bias_value, bias_output, shift_one, bias_up, bias_down, shift_two = pieces
    hidden_low = hidden.astype(jnp.bfloat16)
    projected = jnp.einsum("rsd,de->rse", hidden_low, attn_in, preferred_element_type=jnp.float32)
    queries = (projected[..., :head_width] + bias_query).astype(jnp.bfloat16)
    local_keys = projected[..., head_width : 2 * head_width].astype(jnp.bfloat16)
    local_values = (projected[..., 2 * head_width :] + bias_value).astype(jnp.bfloat16)
    all_keys, all_values = (
        lax.all_gather(local_keys, "mp", axis=1, tiled=True),
        lax.all_gather(local_values, "mp", axis=1, tiled=True),
    )
    scores = score_block(queries, all_keys, valid_keys)
    row_max = jnp.max(scores, axis=-1, keepdims=True)
    exponent = jnp.exp(scores - row_max)
    row_total = jnp.sum(exponent, axis=-1, keepdims=True)
    log_total = row_max + jnp.log(row_total)
    weights_low = (exponent / row_total).astype(jnp.bfloat16)
    mixed = jnp.einsum(
        "rhqk,rkhd->rqhd", weights_low, to_heads(all_values), preferred_element_type=jnp.float32
    )
    context = mixed.reshape(queries.shape).astype(jnp.bfloat16)
    branch = (
        jnp.einsum("rsh,hd->rsd", context, attn_out, preferred_element_type=jnp.float32)
        + bias_output
    )
    summed_one = hidden + branch
    normed_one = layer_norm(summed_one, gains[:model_width], shift_one)
    normed_low = normed_one.astype(jnp.bfloat16)
    ffn_tokens = lax.all_gather(normed_low, "mp", axis=1, tiled=True)
    local_hidden = ffn_first.shape[1]
    bias_part = lax.dynamic_slice_in_dim(bias_up, lax.axis_index("mp") * local_hidden, local_hidden)
    pre_act = (
        jnp.einsum("rsd,df->rsf", ffn_tokens, ffn_first, preferred_element_type=jnp.float32)
        + bias_part
    )
    act_low = smooth_gate(pre_act).astype(jnp.bfloat16)
    down_terms = jnp.einsum("rsf,fd->rsd", act_low, ffn_second, preferred_element_type=jnp.float32)
    ffn_down = lax.psum_scatter(
        down_terms.astype(jnp.bfloat16), "mp", scatter_dimension=1, tiled=True
    ).astype(jnp.float32)
    summed_two = normed_one + ffn_down + bias_down
    result = layer_norm(summed_two, gains[model_width:], shift_two)
    key_store = (all_keys, all_values)
    kept = (
        hidden_low,
        queries,
        key_store,
        log_total,
        context,
        summed_one,
        ffn_tokens,
        pre_act,
        act_low,
        summed_two,
    )
    return (result, kept)


def backward_layer(grad_out, kept, params, valid_keys):
    attn_in, attn_out, ffn_first, ffn_second, shifts, gains = params
    (
        hidden_low,
        queries,
        key_store,
        log_total,
        context,
        summed_one,
        ffn_tokens,
        pre_act,
        act_low,
        summed_two,
    ) = kept
    model_width = summed_one.shape[-1]
    head_width = attn_in.shape[1] // 3
    hidden_width = shifts.shape[0] - 2 * head_width - 4 * model_width
    pieces = split_shifts(shifts, head_width, model_width, hidden_width)
    bias_query, bias_value, bias_output, shift_one, bias_up, bias_down, shift_two = pieces
    sum_axes = (0, 1)
    unused_two, norm_two_back = jax.vjp(layer_norm, summed_two, gains[model_width:], shift_two)
    grad_two, grad_gain_two, grad_shift_two = norm_two_back(grad_out)
    grad_down = grad_two.astype(jnp.bfloat16)
    grad_bias_down = jnp.sum(grad_down.astype(jnp.float32), axis=sum_axes)
    grad_tokens = lax.all_gather(grad_down, "mp", axis=1, tiled=True)
    grad_act = jnp.einsum(
        "rsd,fd->rsf", grad_tokens, ffn_second, preferred_element_type=jnp.float32
    )
    grad_second = jnp.einsum(
        "rsf,rsd->fd", act_low, grad_tokens, preferred_element_type=jnp.float32
    )
    unused_gate, gate_back = jax.vjp(smooth_gate, pre_act)
    grad_pre = gate_back(grad_act)[0].astype(jnp.bfloat16)
    grad_bias_part = jnp.sum(grad_pre.astype(jnp.float32), axis=sum_axes)
    grad_first = jnp.einsum("rsd,rsf->df", ffn_tokens, grad_pre, preferred_element_type=jnp.float32)
    back_terms = jnp.einsum("rsf,df->rsd", grad_pre, ffn_first, preferred_element_type=jnp.float32)
    grad_normed = lax.psum_scatter(
        back_terms.astype(jnp.bfloat16), "mp", scatter_dimension=1, tiled=True
    ).astype(jnp.float32)
    blank_bias = jnp.zeros((hidden_width,), jnp.float32)
    grad_bias_up = lax.dynamic_update_slice_in_dim(
        blank_bias, grad_bias_part, lax.axis_index("mp") * ffn_first.shape[1], 0
    )
    grad_normed = grad_normed + grad_two
    unused_one, norm_one_back = jax.vjp(layer_norm, summed_one, gains[:model_width], shift_one)
    grad_one, grad_gain_one, grad_shift_one = norm_one_back(grad_normed)
    grad_branch = grad_one.astype(jnp.bfloat16)
    grad_bias_output = jnp.sum(grad_branch.astype(jnp.float32), axis=sum_axes)
    grad_attn_out = jnp.einsum(
        "rsh,rsd->hd", context, grad_branch, preferred_element_type=jnp.float32
    )
    grad_context = jnp.einsum(
        "rsd,hd->rsh", grad_branch, attn_out, preferred_element_type=jnp.float32
    ).astype(jnp.bfloat16)
    stored_keys, stored_values = key_store
    all_keys, all_values = (stored_keys, stored_values)
    weights = jnp.exp(score_block(queries, all_keys, valid_keys) - log_total)
    context_heads = to_heads(grad_context)
    grad_weights = jnp.einsum(
        "rqhd,rkhd->rhqk", context_heads, to_heads(all_values), preferred_element_type=jnp.float32
    )
    inner_sum = jnp.sum(weights * grad_weights, axis=-1, keepdims=True)
    grad_raw = (0.125 * weights * (grad_weights - inner_sum)).astype(jnp.bfloat16)
    grad_queries = jnp.einsum(
        "rhqk,rkhd->rqhd", grad_raw, to_heads(all_keys), preferred_element_type=jnp.float32
    )
    grad_queries = grad_queries.reshape(queries.shape).astype(jnp.bfloat16)
    weights_low = weights.astype(jnp.bfloat16)
    value_terms = jnp.einsum(
        "rhqk,rqhd->rkhd", weights_low, context_heads, preferred_element_type=jnp.float32
    )
    key_terms = jnp.einsum(
        "rhqk,rqhd->rkhd", grad_raw, to_heads(queries), preferred_element_type=jnp.float32
    )
    key_terms = key_terms.reshape(all_keys.shape)
    value_terms = value_terms.reshape(all_values.shape)
    grad_keys, grad_values = (
        lax.psum_scatter(
            key_terms.astype(jnp.bfloat16), "mp", scatter_dimension=1, tiled=True
        ).astype(jnp.float32),
        lax.psum_scatter(
            value_terms.astype(jnp.bfloat16), "mp", scatter_dimension=1, tiled=True
        ).astype(jnp.float32),
    )
    grad_values_low = grad_values.astype(jnp.bfloat16)
    grad_projected = jnp.concatenate(
        [grad_queries, grad_keys.astype(jnp.bfloat16), grad_values_low], axis=-1
    )
    grad_attn_in = jnp.einsum(
        "rsd,rse->de", hidden_low, grad_projected, preferred_element_type=jnp.float32
    )
    grad_hidden = grad_one + jnp.einsum(
        "rse,de->rsd", grad_projected, attn_in, preferred_element_type=jnp.float32
    )
    grad_bias_query = jnp.sum(grad_queries.astype(jnp.float32), axis=sum_axes)
    grad_bias_value = jnp.sum(grad_values_low.astype(jnp.float32), axis=sum_axes)
    grad_shifts = jnp.concatenate(
        [
            grad_bias_query,
            grad_bias_value,
            grad_bias_output,
            grad_shift_one,
            grad_bias_up,
            grad_bias_down,
            grad_shift_two,
        ]
    )
    grad_gains = jnp.concatenate([grad_gain_one, grad_gain_two])
    return (
        grad_hidden,
        (grad_attn_in, grad_attn_out, grad_first, grad_second, grad_shifts, grad_gains),
    )


def reduce_grads(grads):
    grad_attn_in, grad_attn_out, grad_first, grad_second, grad_shifts, grad_gains = grads
    total_in, total_out, total_shifts, total_gains = (
        lax.psum_scatter(grad_attn_in, ("dp", "mp"), scatter_dimension=0, tiled=True),
        lax.psum_scatter(grad_attn_out, ("dp", "mp"), scatter_dimension=1, tiled=True),
        lax.psum_scatter(grad_shifts, ("dp", "mp"), scatter_dimension=0, tiled=True),
        lax.psum_scatter(grad_gains, ("dp", "mp"), scatter_dimension=0, tiled=True),
    )
    total_first, total_second = (
        lax.psum_scatter(
            grad_first.astype(jnp.bfloat16), "dp", scatter_dimension=0, tiled=True
        ).astype(jnp.float32),
        lax.psum_scatter(
            grad_second.astype(jnp.bfloat16), "dp", scatter_dimension=1, tiled=True
        ).astype(jnp.float32),
    )
    return (total_in, total_out, total_first, total_second, total_shifts, total_gains)


BF = jnp.bfloat16
F32 = jnp.float32
MESH = pl.DeviceIdType.MESH
SIDE = 2
DEPTH = 4
PARTNERS = 9


def mm(left, right, left_dim, right_dim):
    return lax.dot_general(
        left, right, (((left_dim,), (right_dim,)), ((), ())), preferred_element_type=F32
    )


def rowsum(values):
    return jnp.sum(values, axis=0, keepdims=True)


def normalize(values):
    centered = values - jnp.mean(values, axis=-1, keepdims=True)
    variance = jnp.mean(centered * centered, axis=-1, keepdims=True)
    scale = lax.rsqrt(variance + EPSILON)
    return centered * scale, scale


def normalize_back(grad, normed, scale):
    along = jnp.mean(grad * normed, axis=-1, keepdims=True)
    return scale * (grad - jnp.mean(grad, axis=-1, keepdims=True) - normed * along)


def layer_sizes(model, heads_width, hidden, pair):
    half = heads_width // 2
    start = 3 * half // 128 * 128
    return types.SimpleNamespace(
        hc=half,
        heads=half // HEAD,
        wide=4 * half,
        start=start,
        pad=3 * half - start,
        nr=hidden // 16,
        nc=hidden // 2,
        nl=hidden // 4 if pair else hidden // 2,
        pair=pair,
        sides=2 if pair else 1,
        zs=2 if pair else DEPTH,
        zb=model * 8 // hidden,
    )


def vec_rows(model, sizes):
    lengths = dict(
        qv=4 * sizes.hc, bo=model, beta1=model, b1=2 * sizes.nc, b2=model, beta2=model, g1=model, g2=model
    )
    rows, at = {}, 0
    for name, length in lengths.items():
        rows[name] = at
        at += length // model
    return types.SimpleNamespace(**rows), at


def named(tree):
    if isinstance(tree, dict):
        return types.SimpleNamespace(**{key: named(value) for key, value in tree.items()})
    return [named(value) for value in tree] if isinstance(tree, list) else tree


def fused_kernel(dims, tree, *refs):
    given, outs, scratch, held, made = jax.tree.unflatten(tree, refs)
    lay = [named(a | b | d) for a, b, d in zip(held["lay"], made["lay"], scratch["lay"])]
    r = named(held | made | scratch)
    given, outs = named(given), named(outs)

    def fetch_copies():
        pairs = []
        for at in range(2):
            far, near = given.lay[at], lay[at]
            pairs += [(far.pai, near.pai), (far.pao, near.pao)]
            if at == 0:
                pairs += [(given.hid, r.hid)]
            pairs += [(far.pfi, near.pfi), (far.pfo, near.pfo), (far.psh, near.psh), (far.pga, near.pga)]
        pairs += [(given.len, r.len), (given.cot, r.cot)]
        return [pltpu.make_async_copy(src, dst, r.ins.at[i]) for i, (src, dst) in enumerate(pairs)]

    fetched = fetch_copies()
    for copy in fetched:
        copy.start()
    stored = []

    def store(src, dst):
        copy = pltpu.make_async_copy(src, dst, r.outs.at[len(stored)])
        copy.start()
        stored.append(copy)
    model, tok, seq, layers = dims.model, dims.tok, dims.seq, dims.layers
    half_lanes = model // 2
    dp, mp = lax.axis_index("dp"), lax.axis_index("mp")
    y, c = dp // SIDE, lax.rem(dp, SIDE)
    z, x = mp // SIDE, lax.rem(mp, SIDE)

    def device(c, x, y, z):
        return {"dp": y * SIDE + c, "mp": z * SIDE + x}

    sib = device(1 - c, x, y, z)
    xn, yn = device(c, 1 - x, y, z), device(c, x, 1 - y, z)
    zdev = [device(c, x, y, lax.rem(z + d, DEPTH)) for d in range(1, DEPTH)]
    zpair = z + 1 - 2 * lax.rem(z, 2)
    zn = device(c, x, y, zpair)
    zfar = device(c, x, y, lax.rem(z + 2, DEPTH))

    bar = pltpu.get_barrier_semaphore()
    for step in range(1, DEPTH * SIDE):
        other = lax.rem(mp + step, DEPTH * SIDE)
        pl.semaphore_signal(bar, inc=1, device_id={"dp": dp, "mp": other}, device_id_type=MESH)
    pl.semaphore_signal(bar, inc=1, device_id=sib, device_id_type=MESH)
    pl.semaphore_signal(bar, inc=1, device_id=yn, device_id_type=MESH)

    sent = []

    def remote(src, dst, send, recv, dev):
        return pltpu.make_async_remote_copy(
            src_ref=src, dst_ref=dst, send_sem=send, recv_sem=recv, device_id=dev, device_id_type=MESH
        )

    def push(src, dst, send, recv, dev):
        copy = remote(src, dst, send, recv, dev)
        copy.start()
        sent.append((None, copy))

    def arrived(dst, recv, send):
        remote(dst, dst, send, recv, sib).wait_recv()

    row_core = z // 2
    mine = c == row_core
    half = lax.rem(z, 2)

    def spread(src, land, sends, recvs):
        block = 2 * lax.rem(z, 2) + x
        target = 2 * c + z // 2
        for j in range(2):
            local = (x == j) & (z == target)
            copy = remote(src.at[j], land.at[block], sends.at[j], recvs.at[block], device(c, j, y, target))
            pl.when(local)(pltpu.make_async_copy(src.at[j], land.at[block], recvs.at[block]).start)
            pl.when(jnp.logical_not(local))(copy.start)

    def spread_done(src, land, sends, recvs, on_chip_send, on_chip_recv):
        target = 2 * c + z // 2
        for j in range(2):
            local = (x == j) & (z == target)
            copy = remote(src.at[j], land.at[0], sends.at[j], recvs.at[0], sib)
            pl.when(jnp.logical_not(local))(copy.wait_send)
        whole = remote(land, land, on_chip_send, on_chip_recv, sib)

        @pl.when(mine)
        def _():
            for block in range(4):
                arrived(land.at[block], recvs.at[block], sends.at[0])
            whole.start()
            whole.wait_send()

        @pl.when(jnp.logical_not(mine))
        def _():
            whole.wait_recv()

    def collect(src, land, sends, recvs):
        @pl.when(mine)
        def _():
            for block in range(4):
                z_to, x_to = 2 * half + block // 2, block % 2
                local = (x == x_to) & (z == z_to)
                slot = land.at[x]
                copy = remote(
                    src.at[block], slot, sends.at[block], recvs.at[x], device(c, x_to, y, z_to)
                )
                pl.when(local)(pltpu.make_async_copy(src.at[block], slot, recvs.at[x]).start)
                pl.when(jnp.logical_not(local))(copy.start)

    def collect_done(src, land, sends, recvs):
        for j in range(2):
            arrived(land.at[j], recvs.at[j], sends.at[0])

        @pl.when(mine)
        def _():
            for block in range(4):
                z_to, x_to = 2 * half + block // 2, block % 2
                local = (x == x_to) & (z == z_to)
                copy = remote(src.at[block], src.at[block], sends.at[block], recvs.at[0], sib)
                pl.when(jnp.logical_not(local))(copy.wait_send)

    chunks = dims.chunks
    every, first, second = pl.ds(0, DEPTH), pl.ds(0, 2), pl.ds(2, 2)
    both = pl.ds(0, 2)

    def view(i, grads, band, z_slice, x_at, y_at):
        kind, layer, which, part = chunks[i]
        full = dims.unit_rows[kind]
        if kind == "P":
            ref = lay[layer].dw if grads else lay[layer].w
            lanes = pl.ds(pl.multiple_of(y_at * half_lanes, 128), half_lanes)
            return ref.at[which, z_slice, x_at, :, lanes]
        begin, count = {"a": (0, full - 32), "b": (full - 32, 16), "c": (full - 16, 16)}[band]
        if kind == "A":
            ref = lay[layer].ga
            y_pick = both if y_at is None else y_at
            return ref.at[y_pick, z_slice, x_at, pl.ds(begin, count), pl.ds(part * model, model)]
        ref = lay[layer].dw if grads else lay[layer].w
        lanes = pl.ds(0, model)
        if y_at is not None:
            lanes = pl.ds(pl.multiple_of(y_at * half_lanes, 128), half_lanes)
        return ref.at[which, z_slice, x_at, pl.ds(part * full + begin, count), lanes]

    UP, DOWN, FAR, RELAY = range(4)
    z_far = lax.rem(z + 2, DEPTH)
    z_up, z_down = lax.rem(z + 1, DEPTH), lax.rem(z + DEPTH - 1, DEPTH)
    z_end = DEPTH - 1 - z
    has_up, has_down = z < DEPTH - 1, z > 0
    inner = (z == 1) | (z == 2)
    outer = (z == 0) | (z == 3)
    z_out = jnp.where(z == 1, 0, 3)
    z_in = jnp.where(z == 0, 1, 2)

    def push_if(cond, src, dst, send, recv, dev):
        copy = remote(src, dst, send, recv, dev)
        pl.when(cond)(copy.start)
        sent.append((cond, copy))

    def wait_sent():
        for cond, copy in sent:
            if cond is None:
                copy.wait_send()
            else:
                pl.when(cond)(copy.wait_send)
        sent.clear()

    def arrived_if(cond, dst, recv, send):
        pl.when(cond)(remote(dst, dst, send, recv, sib).wait_recv)

    def at_z(zz):
        return device(c, x, y, zz)

    def line_send(part, send, recv):
        own = part(z)
        push_if(has_up, own, own, send(UP), recv(UP), at_z(z_up))
        push_if(has_down, own, own, send(DOWN), recv(DOWN), at_z(z_down))
        push(own, own, send(FAR), recv(FAR), at_z(z_far))

    def line_relay(part, send, recv):
        far = part(z_far)
        arrived_if(inner, far, recv(FAR), send(FAR))
        push_if(inner, far, far, send(RELAY), recv(RELAY), at_z(z_out))

    def line_end(part, send, recv):
        arrived_if(has_down, part(z_down), recv(UP), send(UP))
        arrived_if(has_up, part(z_up), recv(DOWN), send(DOWN))
        arrived_if(outer, part(z_far), recv(FAR), send(FAR))
        arrived_if(outer, part(z_end), recv(RELAY), send(RELAY))

    def sems(ref_send, ref_recv, i, base):
        return (lambda k: ref_send.at[i, base + k]), (lambda k: ref_recv.at[i, base + k])

    def one(zz):
        return pl.ds(zz, 1)

    def parts_of(i, grads):
        return (
            lambda zz: view(i, grads, "a", one(zz), x, y),
            lambda zz: view(i, grads, "b", one(zz), both, y),
            lambda zz: view(i, grads, "c", one(zz), x, None),
        )

    def gather_sems(i, base):
        return sems(r.gs, r.gr, i, base)

    def gather_push(i, k, piece, dev):
        push(piece, piece, r.gs.at[i, k], r.gr.at[i, k], dev)

    def gather_wait(i, k, piece):
        arrived(piece, r.gr.at[i, k], r.gs.at[i, k])

    z_own, z_other = z // 2, 1 - z // 2

    def pair_view(i, grads, z_slice, x_at, y_at):
        return view(i, grads, None, z_slice, x_at, y_at)

    def pair_0(i):
        gather_push(i, 0, pair_view(i, False, one(z_own), x, y), zfar)

    def pair_1(i):
        gather_wait(i, 0, pair_view(i, False, one(z_other), x, y))
        own = pair_view(i, False, both, x, y)
        gather_push(i, 1, own, xn)
        gather_push(i, 2, own, yn)

    def pair_2(i):
        gather_wait(i, 1, pair_view(i, False, both, 1 - x, y))
        gather_wait(i, 2, pair_view(i, False, both, x, 1 - y))
        gather_push(i, 3, pair_view(i, False, one(0), x, 1 - y), xn)
        gather_push(i, 4, pair_view(i, False, one(1), 1 - x, y), yn)

    def pair_3(i):
        gather_wait(i, 3, pair_view(i, False, one(0), 1 - x, 1 - y))
        gather_wait(i, 4, pair_view(i, False, one(1), 1 - x, 1 - y))

    def gather_0(i):
        gather_push(i, 16, view(i, False, "b", one(z), x, y), xn)
        gather_push(i, 17, view(i, False, "c", one(z), x, y), yn)
        line_send(parts_of(i, False)[0], *gather_sems(i, 0))

    def gather_1(i):
        a, b, c_part = parts_of(i, False)
        gather_wait(i, 16, view(i, False, "b", one(z), 1 - x, y))
        line_send(b, *gather_sems(i, 4))
        gather_wait(i, 17, view(i, False, "c", one(z), x, 1 - y))
        line_send(c_part, *gather_sems(i, 8))
        line_relay(a, *gather_sems(i, 0))

    def gather_2(i):
        a, b, c_part = parts_of(i, False)
        line_end(a, *gather_sems(i, 0))
        own = view(i, False, "a", every, x, y)
        gather_push(i, 12, own, xn)
        gather_push(i, 13, own, yn)
        line_relay(b, *gather_sems(i, 4))
        line_relay(c_part, *gather_sems(i, 8))

    def gather_3(i):
        a, b, c_part = parts_of(i, False)
        line_end(b, *gather_sems(i, 4))
        gather_push(i, 18, view(i, False, "b", every, both, y), yn)
        line_end(c_part, *gather_sems(i, 8))
        gather_push(i, 19, view(i, False, "c", every, x, None), xn)
        gather_wait(i, 12, view(i, False, "a", every, 1 - x, y))
        gather_wait(i, 13, view(i, False, "a", every, x, 1 - y))
        gather_push(i, 14, view(i, False, "a", first, x, 1 - y), xn)
        gather_push(i, 15, view(i, False, "a", second, 1 - x, y), yn)

    def gather_4(i):
        gather_wait(i, 14, view(i, False, "a", first, 1 - x, 1 - y))
        gather_wait(i, 15, view(i, False, "a", second, 1 - x, 1 - y))
        gather_wait(i, 18, view(i, False, "b", every, both, 1 - y))
        gather_wait(i, 19, view(i, False, "c", every, 1 - x, None))

    band_stages = (gather_0, gather_1, gather_2, gather_3, gather_4)
    pair_stages = (pair_0, pair_1, pair_2, pair_3)

    def pump(step):
        for lag in range(5):
            i = step - lag
            if 0 <= i < len(chunks):
                stages = pair_stages if chunks[i][0] == "P" else band_stages
                if lag < len(stages):
                    stages[lag](i)

    def add_into(ref, extra):
        total = ref[...].astype(F32)
        for more in extra:
            total = total + more[...].astype(F32)
        ref[...] = total.astype(BF)

    def slots(i, name):
        return getattr(r.red["AFP".index(chunks[i][0])], name).at[dims.slot[i]]

    def reduce_push(i, k, src, dst, dev):
        push(src, dst, r.ss.at[i, k], r.sr.at[i, k], dev)

    def reduce_wait(i, k, dst):
        arrived(dst, r.sr.at[i, k], r.ss.at[i, k])

    def line_reduce_send(part, land, send, recv):
        push_if(has_up, part(z_up), land.at[UP], send(UP), recv(UP), at_z(z_up))
        push_if(has_down, part(z_down), land.at[DOWN], send(DOWN), recv(DOWN), at_z(z_down))
        push_if(outer, part(z_end), land.at[RELAY], send(RELAY), recv(RELAY), at_z(z_in))
        push_if(outer, part(z_far), land.at[FAR], send(FAR), recv(FAR), at_z(z_far))

    def line_reduce_relay(part, land, send, recv):
        @pl.when(inner)
        def _():
            arrived(land.at[RELAY], recv(RELAY), send(RELAY))
            add_into(part(z_far), [land.at[RELAY]])

        push_if(inner, part(z_far), land.at[FAR], send(FAR), recv(FAR), at_z(z_far))

    def line_reduce_end(part, land, send, recv):
        arrived(land.at[FAR], recv(FAR), send(FAR))

        @pl.when(inner)
        def _():
            arrived(land.at[UP], recv(UP), send(UP))
            arrived(land.at[DOWN], recv(DOWN), send(DOWN))
            add_into(part(z), [land.at[FAR], land.at[UP], land.at[DOWN]])

        @pl.when(z == 0)
        def _():
            arrived(land.at[DOWN], recv(DOWN), send(DOWN))
            add_into(part(z), [land.at[FAR], land.at[DOWN]])

        @pl.when(z == DEPTH - 1)
        def _():
            arrived(land.at[UP], recv(UP), send(UP))
            add_into(part(z), [land.at[FAR], land.at[UP]])

    def reduce_sems(i, base):
        return sems(r.ss, r.sr, i, base)

    def band_reduce_0(i):
        over = slots(i, "ad")
        reduce_push(i, 14, view(i, True, "a", first, 1 - x, 1 - y), over.at[0], xn)
        reduce_push(i, 15, view(i, True, "a", second, 1 - x, 1 - y), over.at[1], yn)
        reduce_push(i, 18, view(i, True, "b", every, both, 1 - y), slots(i, "by"), yn)
        reduce_push(i, 19, view(i, True, "c", every, 1 - x, None), slots(i, "cx"), xn)

    def band_reduce_1(i):
        a, b, c_part = parts_of(i, True)
        over, beside = slots(i, "ad"), slots(i, "an")
        reduce_wait(i, 14, over.at[0])
        add_into(view(i, True, "a", first, x, 1 - y), [over.at[0]])
        reduce_push(i, 13, view(i, True, "a", every, x, 1 - y), beside.at[1], yn)
        reduce_wait(i, 15, over.at[1])
        add_into(view(i, True, "a", second, 1 - x, y), [over.at[1]])
        reduce_push(i, 12, view(i, True, "a", every, 1 - x, y), beside.at[0], xn)
        reduce_wait(i, 18, slots(i, "by"))
        add_into(view(i, True, "b", every, both, y), [slots(i, "by")])
        line_reduce_send(b, slots(i, "bz"), *reduce_sems(i, 4))
        reduce_wait(i, 19, slots(i, "cx"))
        add_into(view(i, True, "c", every, x, None), [slots(i, "cx")])
        line_reduce_send(c_part, slots(i, "cz"), *reduce_sems(i, 8))

    def band_reduce_2(i):
        a, b, c_part = parts_of(i, True)
        beside = slots(i, "an")
        reduce_wait(i, 12, beside.at[0])
        reduce_wait(i, 13, beside.at[1])
        add_into(view(i, True, "a", every, x, y), [beside.at[0], beside.at[1]])
        line_reduce_send(a, slots(i, "az"), *reduce_sems(i, 0))
        line_reduce_relay(b, slots(i, "bz"), *reduce_sems(i, 4))
        line_reduce_relay(c_part, slots(i, "cz"), *reduce_sems(i, 8))

    def band_reduce_3(i):
        a, b, c_part = parts_of(i, True)
        line_reduce_end(b, slots(i, "bz"), *reduce_sems(i, 4))
        reduce_push(i, 16, view(i, True, "b", one(z), 1 - x, y), slots(i, "bx"), xn)
        line_reduce_end(c_part, slots(i, "cz"), *reduce_sems(i, 8))
        reduce_push(i, 17, view(i, True, "c", one(z), x, 1 - y), slots(i, "cy"), yn)
        line_reduce_relay(a, slots(i, "az"), *reduce_sems(i, 0))

    def band_reduce_4(i):
        line_reduce_end(parts_of(i, True)[0], slots(i, "az"), *reduce_sems(i, 0))
        reduce_wait(i, 16, slots(i, "bx"))
        reduce_wait(i, 17, slots(i, "cy"))
        total = jnp.concatenate(
            [
                view(i, True, "a", one(z), x, y)[...].astype(F32)[0],
                (view(i, True, "b", one(z), x, y)[...].astype(F32) + slots(i, "bx")[...].astype(F32))[0],
                (view(i, True, "c", one(z), x, y)[...].astype(F32) + slots(i, "cy")[...].astype(F32))[0],
            ],
            axis=0,
        )
        reduce_store(i, total)

    def pair_reduce_0(i):
        over = slots(i, "ad")
        reduce_push(i, 3, pair_view(i, True, one(0), 1 - x, 1 - y), over.at[0], xn)
        reduce_push(i, 4, pair_view(i, True, one(1), 1 - x, 1 - y), over.at[1], yn)

    def pair_reduce_1(i):
        over, beside = slots(i, "ad"), slots(i, "an")
        reduce_wait(i, 3, over.at[0])
        add_into(pair_view(i, True, one(0), x, 1 - y), [over.at[0]])
        reduce_push(i, 2, pair_view(i, True, both, x, 1 - y), beside.at[1], yn)
        reduce_wait(i, 4, over.at[1])
        add_into(pair_view(i, True, one(1), 1 - x, y), [over.at[1]])
        reduce_push(i, 1, pair_view(i, True, both, 1 - x, y), beside.at[0], xn)

    def pair_reduce_2(i):
        beside = slots(i, "an")
        reduce_wait(i, 1, beside.at[0])
        reduce_wait(i, 2, beside.at[1])
        add_into(pair_view(i, True, both, x, y), [beside.at[0], beside.at[1]])
        reduce_push(i, 0, pair_view(i, True, one(z_other), x, y), slots(i, "az"), zfar)

    def pair_reduce_3(i):
        far = slots(i, "az")
        reduce_wait(i, 0, far)
        own = pair_view(i, True, one(z_own), x, y)
        reduce_store(i, (own[...].astype(F32) + far[...].astype(F32))[0])

    def reduce_store(i, total):
        kind, layer, which, part = chunks[i]
        send, land = slots(i, "fsend"), slots(i, "fland")
        if kind == "A":
            rows = total.shape[0] // 2
            cols = slice(part * model, (part + 1) * model)
            lay[layer].da[c, :, cols] = jnp.where(c == 0, total[:rows], total[rows:])
            send[...] = jnp.where(c == 0, total[rows:], total[:rows])
        else:
            full = dims.unit_rows[kind]
            rows, lanes = pl.ds(part * full, full), total.shape[1] // 2
            lay[layer].df[c, which, rows, :] = jnp.where(c == 0, total[:, :lanes], total[:, lanes:])
            send[...] = jnp.where(c == 0, total[:, lanes:], total[:, :lanes])
        push(send, land, r.fs.at[i], r.fr.at[i], sib)

    def reduce_out(i):
        kind, layer, which, part = chunks[i]
        land = slots(i, "fland")
        arrived(land, r.fr.at[i], r.fs.at[i])
        if kind == "A":
            lay[layer].da[1 - c, :, part * model : (part + 1) * model] = land[...]
            if part == 0:
                store(lay[layer].da, outs.lay[layer].da)
        else:
            full = dims.unit_rows[kind]
            lay[layer].df[1 - c, which, pl.ds(part * full, full), :] = land[...]
            if part == layers[layer].nr // full - 1:
                store(lay[layer].df.at[:, which], outs.lay[layer].df.at[:, which])

    band_reduces = (band_reduce_0, band_reduce_1, band_reduce_2, band_reduce_3, band_reduce_4)
    pair_reduces = (pair_reduce_0, pair_reduce_1, pair_reduce_2, pair_reduce_3)

    def reduce(i, stage):
        stages = pair_reduces if chunks[i][0] == "P" else band_reduces
        if stage < len(stages):
            stages[stage](i)

    def total_step(work, land, step, sends, recvs):
        dev = (sib, xn, yn, zn, zfar)[step]
        push(work.at[step], land.at[step], sends.at[step], recvs.at[step], dev)

    def total_add(work, land, step, sends, recvs):
        arrived(land.at[step], recvs.at[step], sends.at[step])
        work[step + 1] = work[step] + land[step]

    exchanges = []

    def exchange(part):
        slot = len(exchanges) % 2
        r.xs[slot] = part.astype(BF)
        copy = remote(r.xs.at[slot], r.xr.at[slot], r.es.at[slot], r.er.at[slot], sib)
        copy.start()
        exchanges.append(copy)

        def finish():
            copy.wait()
            return r.xs[slot].astype(F32) + r.xr[slot].astype(F32)

        return finish

    quarter = tok // 2
    own_rows = pl.ds(pl.multiple_of(c * quarter, 16), quarter)
    other_rows = pl.ds(pl.multiple_of((1 - c) * quarter, 16), quarter)

    def share(ref, k):
        piece = ref.at[half, own_rows]
        push(piece, piece, r.ps.at[k, 0], r.pr.at[k, 0], zn)

        def finish():
            got = ref.at[1 - half, own_rows]
            arrived(got, r.pr.at[k, 0], r.ps.at[k, 0])
            push(got, got, r.ps.at[k, 1], r.pr.at[k, 1], sib)
            arrived(ref.at[1 - half, other_rows], r.pr.at[k, 1], r.ps.at[k, 1])

        return finish

    def fold(make, k):
        r.px[...] = make(1 - half).astype(BF)
        push(r.px.at[other_rows], r.prx.at[k], r.ps.at[k, 2], r.pr.at[k, 2], sib)
        own = exchange(make(half))
        arrived(r.prx.at[k], r.pr.at[k, 2], r.ps.at[k, 2])
        r.pz[k] = (r.px[own_rows, :].astype(F32) + r.prx[k].astype(F32)).astype(BF)
        push(r.pz.at[k], r.pzr.at[k, c], r.ps.at[k, 3], r.pr.at[k, 3], zn)

        def finish():
            got = r.pzr.at[k, c]
            arrived(got, r.pr.at[k, 3], r.ps.at[k, 3])
            push(got, got, r.ps.at[k, 4], r.pr.at[k, 4], sib)
            arrived(r.pzr.at[k, 1 - c], r.pr.at[k, 4], r.ps.at[k, 4])
            return own() + r.pzr[k].reshape(tok, model).astype(F32)

        return finish

    def vec_row(row):
        return r.vw[5, row : row + 1, :]

    def layer_vecs(at):
        sizes, rows, base = layers[at], dims.rows_of[at], dims.base[at]
        if sizes.hc * 2 == model:
            qv = r.vw[5, pl.ds(base + rows.qv + c, 1), :]
        else:
            both = vec_row(base + rows.qv)
            qv = jnp.where(c == 0, both[:, : 2 * sizes.hc], both[:, 2 * sizes.hc :])
        span = sizes.nc // model
        b1 = [r.vw[5, pl.ds(base + rows.b1 + c * span + s, 1), :] for s in range(span)]
        if sizes.pair:
            cut = 2 * sizes.nr
            b1 = [jnp.concatenate([jnp.where(half == 0, v[:, :cut], v[:, cut:]) for v in b1], axis=1)]
        found = types.SimpleNamespace(bq=qv[:, : sizes.hc], bv=qv[:, sizes.hc :], b1=b1)
        for name, row in vars(rows).items():
            if not hasattr(found, name):
                setattr(found, name, vec_row(base + row))
        return found

    kept = lay
    wa = [one_layer.wa for one_layer in lay]
    weights = [one_layer.w for one_layer in lay]

    def order_rows(at, part):
        gathered, whole = lay[at].ga, wa[at]
        cols = slice(part * model, (part + 1) * model)
        rows = gathered.shape[3] // 2
        span = DEPTH * 2 * rows
        for y_at in range(SIDE):
            for z_at in range(DEPTH):
                left = gathered[y_at, z_at, 0, :, cols].astype(F32)
                right = gathered[y_at, z_at, 1, :, cols].astype(F32)
                for core in range(SIDE):
                    own = slice(core * rows, (core + 1) * rows)
                    both = jnp.concatenate([left[own], right[own]], axis=0).astype(BF)
                    begin = (y_at * SIDE + core) * span + z_at * 2 * rows
                    whole[begin : begin + 2 * rows, cols] = both

    def store_grad_rows(at, y_at, value, cols):
        blocks = lay[at].ga
        rows = blocks.shape[3] // 2
        span = DEPTH * 2 * rows
        for z_at in range(DEPTH):
            for x_at in range(SIDE):
                begin = (z_at * 2 + x_at) * rows
                both = [value[begin : begin + rows], value[span + begin : span + begin + rows]]
                blocks[y_at, z_at, x_at, :, cols] = jnp.concatenate(both, axis=0).astype(BF)

    def send_kv(at):
        kv = kept[at].kv
        push(kv.at[half], kv.at[half], r.ks.at[at], r.kr.at[at], zn)

    def wait_kv(at):
        kv = kept[at].kv
        arrived(kv.at[1 - half], r.kr.at[at], r.ks.at[at])

    def head_kv(at, h):
        sizes, kv = layers[at], kept[at].kv
        k = kv[:, :, h * HEAD : (h + 1) * HEAD].reshape(seq, HEAD)
        v = kv[:, :, sizes.hc + h * HEAD : sizes.hc + (h + 1) * HEAD].reshape(seq, HEAD)
        return k, v

    def attention(at):
        sizes, keep = layers[at], kept[at]
        lane = lax.broadcasted_iota(jnp.int32, (1, model), 1)
        first_lane = (y * SIDE + row_core) * group + x
        entry = vec_row(dims.length_row)
        entry = jnp.where(lane == first_lane, 256.0 * entry, jnp.where(lane == first_lane + 2, entry, 0.0))
        length = jnp.sum(entry, axis=1, keepdims=True)
        valid = lax.broadcasted_iota(jnp.int32, (1, seq), 1).astype(F32) < length
        for h in range(sizes.heads):
            q = keep.q[:, h * HEAD : (h + 1) * HEAD]
            k, v = head_kv(at, h)
            scores = jnp.where(valid, mm(q, k, 1, 1) * 0.125, NEGATIVE)
            exponent = jnp.exp(scores - jnp.max(scores, axis=1, keepdims=True))
            low = (exponent / jnp.sum(exponent, axis=1, keepdims=True)).astype(BF)
            keep.a[h] = low
            begin = sizes.pad + h * HEAD
            keep.ctx[:, begin : begin + HEAD] = mm(low, v, 1, 0).astype(BF)

    def attention_back(at, grad_ctx):
        sizes, keep = layers[at], kept[at]
        dkv, gp = lay[at].dkv, lay[at].dp
        for h in range(sizes.heads):
            q = keep.q[:, h * HEAD : (h + 1) * HEAD]
            k, v = head_kv(at, h)
            begin = sizes.pad + h * HEAD
            dc = grad_ctx[:, begin : begin + HEAD]
            low = keep.a[h]
            a = low.astype(F32)
            da = mm(dc, v, 1, 1)
            inner = jnp.sum(a * da, axis=1, keepdims=True)
            ds = (0.125 * a * (da - inner)).astype(BF)
            at_q = 2 * sizes.hc + h * HEAD
            gp[:, at_q : at_q + HEAD] = mm(ds, k, 1, 0).astype(BF)
            dk = mm(ds, q, 0, 0).astype(BF).reshape(2, tok, HEAD)
            dv = mm(low, dc, 0, 0).astype(BF).reshape(2, tok, HEAD)
            dkv[:, :, h * HEAD : (h + 1) * HEAD] = dk
            dkv[:, :, sizes.hc + h * HEAD : sizes.hc + (h + 1) * HEAD] = dv

    def block(at, which, b):
        sizes = layers[at]
        w = weights[at][which, b * sizes.zb : (b + 1) * sizes.zb]
        return w.reshape(model, model)

    def up(at, side):
        sizes, keep = layers[at], kept[at]
        for b in range(sizes.nl // model):
            cols = slice(b * model, (b + 1) * model)
            u = mm(keep.hb[side], block(at, 0, b), 1, 1) + vecs[at].b1[b]
            phi = 0.5 * (1.0 + lax.erf(u * 0.7071067811865476))
            keep.g[side, :, cols] = (u * phi).astype(BF)
            density = jnp.exp(u * u * -0.5) * 0.3989422804014327
            keep.gp[side, :, cols] = (phi + u * density).astype(BF)

    def times_block(at, which, side):
        sizes, keep = layers[at], kept[at]
        total = None
        for b in range(sizes.nl // model):
            term = mm(keep.g[side, :, b * model : (b + 1) * model], block(at, which, b), 1, 0)
            total = term if total is None else total + term
        return total

    def weight_grad(at, which, right):
        sizes, keep = layers[at], kept[at]
        span = model // 2
        zb = sizes.zb // 2
        rows = sizes.sides * tok
        wide = right[...].reshape(rows, model)
        for b in range(sizes.nl // span):
            left = keep.g[:, :, b * span : (b + 1) * span].reshape(rows, span)
            value = mm(left, wide, 0, 0).astype(BF)
            keep.dw[which, b * zb : (b + 1) * zb] = value.reshape(zb, 2, sizes.nr, model)


    def pack_a(at):
        sizes, width = layers[at], 2 * layers[at].hc
        rows_in = lay[at].pai[...].astype(F32)
        rows_out = lay[at].pao[...].astype(F32)
        halves = []
        for h in range(2):
            own = slice(h * sizes.hc, (h + 1) * sizes.hc)
            pieces = [rows_in[:, p * width : (p + 1) * width][:, own] for p in (1, 2, 0)]
            halves.append(jnp.concatenate(pieces + [rows_out[:, own]], axis=1))
        send = lay[at].asend
        send[...] = jnp.where(c == 0, halves[1], halves[0])
        if at == 0:
            pl.semaphore_wait(bar, PARTNERS)
        push(send, lay[at].ar, r.is_.at[2 * at], r.ir.at[2 * at], sib)
        return jnp.where(c == 0, halves[0], halves[1])

    def pack_f(at):
        sizes = layers[at]
        first = lay[at].pfi[...].astype(F32).T
        second = lay[at].pfo[...].astype(F32)
        if dims.turned[at]:
            second = second.T
        send, own = lay[at].fsend, []
        for which, value in enumerate((first, second)):
            low_half, high_half = value[: sizes.nr], value[sizes.nr :]
            own.append(jnp.where(c == 0, low_half, high_half))
            send[which] = jnp.where(c == 0, high_half, low_half).astype(BF)
        push(send, lay[at].fr, r.is_.at[2 * at + 1], r.ir.at[2 * at + 1], sib)
        return own

    def prepare_a(at, own):
        land, blocks = lay[at].ar, lay[at].ga
        arrived(land, r.ir.at[2 * at], r.is_.at[2 * at])
        other = land[...]
        pair = [jnp.where(c == 0, own, other), jnp.where(c == 0, other, own)]
        blocks[y, z, x] = jnp.concatenate(pair, axis=0).astype(BF)

    def prepare_f(at, own):
        land = lay[at].fr
        arrived(land, r.ir.at[2 * at + 1], r.is_.at[2 * at + 1])
        lanes = pl.ds(pl.multiple_of(y * half_lanes, 128), half_lanes)
        for which in range(2):
            other = land[which].astype(F32)
            pair = [jnp.where(c == 0, own[which], other), jnp.where(c == 0, other, own[which])]
            weights[at][which, z_own if layers[at].pair else z, x, :, lanes] = jnp.concatenate(pair, axis=1).astype(BF)

    group = dims.group
    per_row = model // group
    index = dp * DEPTH * SIDE + mp

    def targets(at_group):
        result, begin = jnp.full_like(at_group, dims.length_row * per_row) + dp, 0
        for at, sizes in enumerate(layers):
            base = dims.base[at] * per_row
            head, count_b = sizes.hc // group, sizes.nr // group
            up_at = dims.rows_of[at].b1 * per_row
            count = dims.shift_groups[at]
            g = index * count + (at_group - begin)
            w = g % (2 * head)
            qv = (w // head) * (2 * head) + (g // (2 * head)) * head + w % head
            b = g - up_at
            up_to = up_at + ((b % (2 * count_b)) // count_b) * (8 * count_b)
            up_to = up_to + (b // (2 * count_b)) * count_b + b % count_b
            place = jnp.where(g < 4 * head, qv, jnp.where((b >= 0) & (b < 16 * count_b), up_to, g))
            inside = (at_group >= begin) & (at_group < begin + count)
            result = jnp.where(inside, base + place, result)
            begin += count
            count = dims.gain_groups[at]
            place = dims.rows_of[at].g1 * per_row + index * count + (at_group - begin)
            inside = (at_group >= begin) & (at_group < begin + count)
            result = jnp.where(inside, base + place, result)
            begin += count
        return result // per_row, result % per_row

    groups = dims.vec_rows
    lane_group = lax.broadcasted_iota(jnp.int32, (groups, dims.lanes), 1) // group
    lane_own = lane_group == lax.broadcasted_iota(jnp.int32, (groups, dims.lanes), 0)

    def place_masks():
        down = lax.broadcasted_iota(jnp.int32, (groups, 1), 0)
        across = lax.broadcasted_iota(jnp.int32, (1, groups), 1)
        row_down, place_down = targets(down)
        row_across, _ = targets(across)
        lane = lax.broadcasted_iota(jnp.int32, (groups, model), 1) // group
        to_row = jnp.where(row_across == down, 1.0, 0.0).astype(BF)
        from_row = jnp.where(row_down == across, 1.0, 0.0).astype(BF)
        return lane == place_down, to_row, from_row

    def pack_vectors():
        lengths = r.len[...].astype(F32).reshape(1, 2) * jnp.where(mp == 0, 1.0, 0.0)
        high = jnp.floor(lengths * (1.0 / 256.0))
        pieces = []
        for own in lay:
            pieces += [own.psh[...].astype(F32).reshape(1, -1), own.pga[...].astype(F32).reshape(1, -1)]
        pieces += [high, lengths - 256.0 * high]
        used = sum(p.shape[1] for p in pieces)
        values = jnp.concatenate(pieces + [jnp.zeros((1, dims.lanes - used), F32)], axis=1)
        spread_out = jnp.where(lane_own, values, 0.0).astype(BF)
        i = lax.broadcasted_iota(jnp.int32, (dims.lanes, model), 0) % group
        j = lax.broadcasted_iota(jnp.int32, (dims.lanes, model), 1) % group
        r.hot[...] = jnp.where(i == j, 1.0, 0.0).astype(BF)
        in_place, to_row, _ = place_masks()
        wide = jnp.where(in_place, mm(spread_out, r.hot[...], 1, 0), 0.0).astype(BF)
        return mm(to_row, wide, 1, 0)

    def unpack_vectors(values):
        in_place, _, from_row = place_masks()
        total, rest = None, values
        for _ in range(3):
            low_part = rest.astype(BF)
            rest = rest - low_part.astype(F32)
            wide = jnp.where(in_place, mm(from_row, low_part, 1, 0), 0.0).astype(BF)
            term = jnp.where(lane_own, mm(wide, r.hot[...], 1, 1), 0.0)
            total = term if total is None else total + term
        return rowsum(total)

    for copy in fetched[:2]:
        copy.wait()
    own_a = pack_a(0)
    fetched[2].wait()
    spread(r.hid, r.xin, r.hs, r.hr)
    for copy in fetched[3:5]:
        copy.wait()
    own_f = pack_f(0)
    prepare_a(0, own_a)
    pump(0)
    prepare_f(0, own_f)
    pump(1)
    for copy in fetched[5:]:
        copy.wait()
    r.vw[0] = pack_vectors()
    total_step(r.vw, r.vl, 0, r.vs, r.vr)
    own_a, own_f = pack_a(1), pack_f(1)
    total_add(r.vw, r.vl, 0, r.vs, r.vr)
    total_step(r.vw, r.vl, 1, r.vs, r.vr)
    prepare_a(1, own_a)
    prepare_f(1, own_f)
    total_add(r.vw, r.vl, 1, r.vs, r.vr)
    total_step(r.vw, r.vl, 2, r.vs, r.vr)
    pump(2)
    spread_done(r.hid, r.xin, r.hs, r.hr, r.os.at[0], r.os.at[1])
    total_add(r.vw, r.vl, 2, r.vs, r.vr)
    total_step(r.vw, r.vl, 3, r.vs, r.vr)
    pump(3)
    total_add(r.vw, r.vl, 3, r.vs, r.vr)
    total_step(r.vw, r.vl, 4, r.vs, r.vr)
    pump(4)
    total_add(r.vw, r.vl, 4, r.vs, r.vr)
    vecs = [layer_vecs(0), layer_vecs(1)]

    def project(at, hidden_low, parts):
        sizes, keep = layers[at], kept[at]
        for part in parts:
            order_rows(at, part)
        if sizes.wide == model:
            p = mm(hidden_low, wa[at][...], 1, 0)
            kv, q = p[:, : 2 * sizes.hc], p[:, 2 * sizes.hc : 3 * sizes.hc]
        elif parts == (0,):
            kv, q = mm(hidden_low, wa[at][:, : 2 * sizes.hc], 1, 0), None
        else:
            kv, q = None, mm(hidden_low, wa[at][:, 2 * sizes.hc : 3 * sizes.hc], 1, 0)
        if q is not None:
            keep.q[...] = (q + vecs[at].bq).astype(BF)
        if kv is not None:
            keep.kv[half, :, : sizes.hc] = kv[:, : sizes.hc].astype(BF)
            keep.kv[half, :, sizes.hc :] = (kv[:, sizes.hc :] + vecs[at].bv).astype(BF)

    def attend_out(at):
        return mm(kept[at].ctx[...], wa[at][:, layers[at].start :], 1, 1)

    def norm_one(at, base, branch):
        keep, v = kept[at], vecs[at]
        normed, scale = normalize(base + branch + v.bo)
        keep.n1[...] = normed
        keep.s1[...] = scale
        result = normed * v.g1 + v.beta1
        keep.hb[half if layers[at].pair else 0] = result.astype(BF)
        return result

    def norm_two(at, base, branch):
        keep, v = kept[at], vecs[at]
        normed, scale = normalize(base + branch + v.b2)
        keep.n2[...] = normed
        keep.s2[...] = scale
        return normed * v.g2 + v.beta2

    if layers[1].pad:
        kept[1].ctx[...] = jnp.zeros_like(kept[1].ctx)
        lay[1].dp[...] = jnp.zeros_like(lay[1].dp)
    kept[0].xb[...] = r.xin[...].reshape(tok, model)
    project(0, kept[0].xb[...], (0,))
    send_kv(0)
    pump(5)
    project(0, kept[0].xb[...], (1,))
    spread(r.cot, r.cin, r.cs, r.cr)
    wait_kv(0)
    attention(0)
    wait_branch = exchange(attend_out(0))
    pump(6)
    normed = norm_one(0, kept[0].xb[...].astype(F32), wait_branch())
    wait_share = share(kept[0].hb, 0)
    up(0, half)
    pump(7)
    wait_share()
    up(0, 1 - half)
    wait_branch = fold(lambda side: times_block(0, 1, side), 0)
    spread_done(r.cot, r.cin, r.cs, r.cr, r.os.at[2], r.os.at[3])
    pump(8)
    middle = norm_two(0, normed, wait_branch())
    kept[1].xb[...] = middle.astype(BF)
    project(1, kept[1].xb[...], (0,))
    send_kv(1)
    pump(9)
    wait_kv(1)
    attention(1)
    wait_branch = exchange(attend_out(1))
    normed = norm_one(1, middle, wait_branch())
    up(1, 0)
    pump(10)
    wait_branch = exchange(times_block(1, 1, 0))
    final = norm_two(1, normed, wait_branch())
    r.oblk[...] = final.astype(BF).reshape(r.oblk.shape)
    collect(r.oblk, r.oland, r.ys, r.yr)
    wait_sent()

    r.vw[0] = jnp.zeros_like(r.vw[0])
    once = jnp.where(c == 0, 1.0, 0.0)

    def put_vec(at, name, value):
        row = dims.base[at] + getattr(dims.rows_of[at], name)
        r.vw[0, row : row + 1, :] = value * once

    def back_two(at, grad):
        keep, v = kept[at], vecs[at]
        n2 = keep.n2[...]
        put_vec(at, "g2", rowsum(grad * n2))
        put_vec(at, "beta2", rowsum(grad))
        dz2 = normalize_back(grad * v.g2, n2, keep.s2[...])
        low_dz2 = dz2.astype(BF)
        keep.eo[half if layers[at].pair else 0] = low_dz2
        put_vec(at, "b2", rowsum(low_dz2.astype(F32)))
        return dz2

    def back_up(at):
        sizes, keep = layers[at], kept[at]
        base = dims.base[at] + dims.rows_of[at].b1
        span, sums = sizes.nc // model, []
        for b in range(sizes.nl // model):
            cols = slice(b * model, (b + 1) * model)
            total = None
            for side in range(sizes.sides):
                dg = mm(keep.eo[side], block(at, 1, b), 1, 1)
                du = (dg * keep.gp[side, :, cols].astype(F32)).astype(BF)
                keep.g[side, :, cols] = du
                term = rowsum(du.astype(F32))
                total = term if total is None else total + term
            sums.append(total)
        if sizes.pair:
            cut = 2 * sizes.nr
            blank = jnp.zeros((1, cut), F32)
            pieces = [sums[0][:, b * cut : (b + 1) * cut] for b in range(span)]
            sums = [
                jnp.concatenate([jnp.where(half == 0, p, blank), jnp.where(half == 0, blank, p)], axis=1)
                for p in pieces
            ]
        for b, total in enumerate(sums):
            r.vw[0, pl.ds(base + c * span + b, 1), :] = total

    def back_one(at, grad):
        keep, v = kept[at], vecs[at]
        n1 = keep.n1[...]
        put_vec(at, "g1", rowsum(grad * n1))
        put_vec(at, "beta1", rowsum(grad))
        dz1 = normalize_back(grad * v.g1, n1, keep.s1[...])
        r.eo[...] = dz1.astype(BF)
        put_vec(at, "bo", rowsum(r.eo[...].astype(F32)))
        grad_ctx = mm(r.eo[...], wa[at][:, layers[at].start :], 1, 0).astype(BF)
        return dz1, grad_ctx

    def send_dkv(at):
        dkv, land = lay[at].dkv, lay[at].dkr
        push(dkv.at[1 - half], land, r.ks.at[2 + at], r.kr.at[2 + at], zn)

    def take_dkv(at):
        sizes = layers[at]
        dkv, land, gp = lay[at].dkv, lay[at].dkr, lay[at].dp
        arrived(land, r.kr.at[2 + at], r.ks.at[2 + at])
        total = (dkv[half].astype(F32) + land[...].astype(F32)).astype(BF)
        gp[:, : 2 * sizes.hc] = total
        qsum = rowsum(gp[:, 2 * sizes.hc : 3 * sizes.hc].astype(F32))
        vsum = rowsum(total[:, sizes.hc :].astype(F32))
        both = jnp.concatenate([qsum, vsum], axis=1)
        row = dims.base[at] + dims.rows_of[at].qv
        if 2 * sizes.hc == model:
            r.vw[0, pl.ds(row + c, 1), :] = both
        else:
            blank = jnp.zeros_like(both)
            left, right = jnp.where(c == 0, both, blank), jnp.where(c == 0, blank, both)
            r.vw[0, row : row + 1, :] = jnp.concatenate([left, right], axis=1)

    def projection_grad(at, part):
        sizes, keep, gp = layers[at], kept[at], lay[at].dp
        begin, end = part * model, (part + 1) * model
        for y_at in range(SIDE):
            rows = slice(y_at * half_lanes, (y_at + 1) * half_lanes)
            pieces = []
            xb = keep.xb[:, rows]
            split = min(end, sizes.start)
            if begin < split:
                pieces.append(mm(xb, gp[:, begin:split], 0, 0))
            if end > sizes.start:
                value = mm(r.eo[:, rows], keep.ctx[...], 0, 0)
                if sizes.pad:
                    value = value + mm(xb, gp[:, sizes.start : end], 0, 0)
                pieces.append(value)
            value = pieces[0] if len(pieces) == 1 else jnp.concatenate(pieces, axis=1)
            store_grad_rows(at, y_at, value, slice(begin, end))

    def back_hidden(at):
        gp = lay[at].dp
        width = gp.shape[1]
        return mm(gp[...], wa[at][:, :width], 1, 1)

    grad = r.cin[...].reshape(tok, model).astype(F32)
    dz2 = back_two(1, grad)
    weight_grad(1, 1, kept[1].eo)
    reduce(6, 0)
    back_up(1)
    weight_grad(1, 0, kept[1].hb)
    reduce(5, 0)
    wait_branch = exchange(times_block(1, 0, 0))
    dz1, grad_ctx = back_one(1, dz2 + wait_branch())
    reduce(6, 1)
    attention_back(1, grad_ctx)
    send_dkv(1)
    reduce(5, 1)
    reduce(6, 2)
    take_dkv(1)
    projection_grad(1, 0)
    reduce(4, 0)
    wait_branch = exchange(back_hidden(1))
    reduce(5, 2)
    reduce(6, 3)
    grad = dz1 + wait_branch()
    dz2 = back_two(0, grad)
    wait_share = share(kept[0].eo, 1)
    reduce(4, 1)
    reduce(5, 3)
    reduce(6, 4)
    wait_share()
    weight_grad(0, 1, kept[0].eo)
    reduce(3, 0)
    back_up(0)
    wait_branch = fold(lambda side: times_block(0, 0, side), 1)
    weight_grad(0, 0, kept[0].hb)
    reduce(2, 0)
    reduce(4, 2)
    dz1, grad_ctx = back_one(0, dz2 + wait_branch())
    reduce(3, 1)
    reduce(5, 4)
    attention_back(0, grad_ctx)
    send_dkv(0)
    projection_grad(0, 1)
    reduce(1, 0)
    reduce(2, 1)
    reduce(4, 3)
    reduce(3, 2)
    take_dkv(0)
    projection_grad(0, 0)
    reduce(0, 0)
    total_step(r.vw, r.vl, 0, r.ws, r.wr)
    wait_branch = exchange(back_hidden(0))
    reduce(1, 1)
    reduce(2, 2)
    reduce(4, 4)
    reduce(3, 3)
    grad = dz1 + wait_branch()
    r.gblk[...] = grad.astype(BF).reshape(r.gblk.shape)
    collect(r.gblk, r.gland, r.zs, r.zr)
    total_add(r.vw, r.vl, 0, r.ws, r.wr)
    total_step(r.vw, r.vl, 1, r.ws, r.wr)
    reduce(0, 1)
    reduce(1, 2)
    reduce(2, 3)
    total_add(r.vw, r.vl, 1, r.ws, r.wr)
    total_step(r.vw, r.vl, 2, r.ws, r.wr)
    for i in (6, 5, 4, 3):
        reduce_out(i)
    total_add(r.vw, r.vl, 2, r.ws, r.wr)
    total_step(r.vw, r.vl, 3, r.ws, r.wr)
    reduce(0, 2)
    reduce(1, 3)
    total_add(r.vw, r.vl, 3, r.ws, r.wr)
    total_step(r.vw, r.vl, 4, r.ws, r.wr)
    reduce_out(2)
    reduce(0, 3)
    reduce(1, 4)
    total_add(r.vw, r.vl, 4, r.ws, r.wr)
    r.dvec[...] = unpack_vectors(r.vw[5])
    store(r.dvec, outs.dvec)
    collect_done(r.oblk, r.oland, r.ys, r.yr)
    store(r.oland, outs.out)
    reduce_out(1)
    reduce(0, 4)
    collect_done(r.gblk, r.gland, r.zs, r.zr)
    store(r.gland, outs.gh)
    reduce_out(0)
    wait_sent()
    for copy in stored:
        copy.wait()


def fused_call(hid, cot, lengths, params, dims):
    model, tok, seq = dims.model, dims.tok, dims.seq
    block = (4, tok // 4, model)
    vmem = pltpu.VMEM
    dma = pltpu.SemaphoreType.DMA
    rows_in = params[0][0].shape[0]
    shape = jax.ShapeDtypeStruct
    given = dict(hid=hid, cot=cot, len=lengths, lay=[])
    outs = dict(out=shape(hid.shape, BF), gh=shape(hid.shape, BF), lay=[], dvec=shape((1, dims.lanes), F32))
    for (ai, ao, fi, fo, sh, ga), sizes in zip(params, dims.layers):
        given["lay"].append(dict(pai=ai, pao=ao, pfi=fi, pfo=fo, psh=sh, pga=ga))
        outs["lay"].append(
            dict(
                da=shape((2, rows_in, sizes.wide), F32),
                df=shape((2, 2, sizes.nr, model // 4), F32),
            )
        )
    as_scratch = lambda tree: jax.tree.map(lambda v: vmem(v.shape, v.dtype), tree)
    held, made = as_scratch(given), as_scratch({key: outs[key] for key in ("lay", "dvec")})
    vec = (dims.vec_rows, model)
    rows_a = 2 * rows_in
    counts = [sum(chunk[0] == kind for chunk in dims.chunks) for kind in "AFP"]
    half = model // 2
    n = len(dims.chunks)
    scratch = dict(
        xin=vmem(block, BF),
        cin=vmem(block, BF),
        oblk=vmem(block, BF),
        gblk=vmem(block, BF),
        oland=vmem(hid.shape, BF),
        gland=vmem(hid.shape, BF),
        vw=vmem((6,) + vec, F32),
        vl=vmem((5,) + vec, F32),
        xs=vmem((2, tok, model), BF),
        xr=vmem((2, tok, model), BF),
        eo=vmem((tok, model), BF),
        px=vmem((tok, model), BF),
        prx=vmem((2, tok // 2, model), BF),
        pz=vmem((2, tok // 2, model), BF),
        pzr=vmem((2, 2, tok // 2, model), BF),
        ps=dma((2, 5)),
        pr=dma((2, 5)),
        hot=vmem((dims.lanes, model), BF),
        gs=dma((n, 20)),
        gr=dma((n, 20)),
        ss=dma((n, 20)),
        sr=dma((n, 20)),
        fs=dma((n,)),
        fr=dma((n,)),
        vs=dma((5,)),
        vr=dma((5,)),
        ws=dma((5,)),
        wr=dma((5,)),
        hs=dma((4,)),
        hr=dma((4,)),
        cs=dma((4,)),
        cr=dma((4,)),
        ys=dma((4,)),
        yr=dma((4,)),
        zs=dma((4,)),
        zr=dma((4,)),
        is_=dma((4,)),
        ir=dma((4,)),
        os=dma((4,)),
        ks=dma((4,)),
        kr=dma((4,)),
        es=dma((2,)),
        er=dma((2,)),
        ins=dma((16,)),
        outs=dma((10,)),
        red=[],
        lay=[],
    )
    rows_f, rows_p = dims.unit_rows["F"], dims.unit_rows["P"]
    for count, rows, wide, pair, shard in (
        (counts[0], rows_a - 32, model, (2, 4, 16, model), (rows_in, model)),
        (counts[1], rows_f - 32, half, (4, 16, model), (rows_f, half // 2)),
    ):
        line = pair[:-3] + (1, 16, model)
        scratch["red"].append(
            dict(
                ad=vmem((count, 2, 2, rows, wide), BF),
                an=vmem((count, 2, 4, rows, wide), BF),
                az=vmem((count, 4, 1, rows, wide), BF),
                by=vmem((count, 4, 2, 16, wide), BF),
                bz=vmem((count, 4, 1, 2, 16, wide), BF),
                bx=vmem((count, 1, 16, wide), BF),
                cx=vmem((count,) + pair, BF),
                cz=vmem((count, 4) + line, BF),
                cy=vmem((count, 1, 16, wide), BF),
                fsend=vmem((count,) + shard, F32),
                fland=vmem((count,) + shard, F32),
            )
        )
    scratch["red"].append(
        dict(
            ad=vmem((counts[2], 2, 1, rows_p, half), BF),
            an=vmem((counts[2], 2, 2, rows_p, half), BF),
            az=vmem((counts[2], 1, rows_p, half), BF),
            fsend=vmem((counts[2], rows_p, half // 2), F32),
            fland=vmem((counts[2], rows_p, half // 2), F32),
        )
    )
    for sizes in dims.layers:
        scratch["lay"].append(
            dict(
                ar=vmem((rows_in, sizes.wide), F32),
                asend=vmem((rows_in, sizes.wide), F32),
                fr=vmem((2, sizes.nr, model // 4), BF),
                fsend=vmem((2, sizes.nr, model // 4), BF),
                ga=vmem((SIDE, DEPTH, SIDE, rows_a, sizes.wide), BF),
                wa=vmem((model, sizes.wide), BF),
                w=vmem((2, sizes.zs, SIDE, sizes.nr, model), BF),
                dw=vmem((2, sizes.zs, SIDE, sizes.nr, model), BF),
                xb=vmem((tok, model), BF),
                q=vmem((tok, sizes.hc), BF),
                kv=vmem((2, tok, 2 * sizes.hc), BF),
                a=vmem((sizes.heads, tok, seq), BF),
                ctx=vmem((tok, sizes.wide - sizes.start), BF),
                n1=vmem((tok, model), F32),
                s1=vmem((tok, 1), F32),
                hb=vmem((sizes.sides, tok, model), BF),
                eo=vmem((sizes.sides, tok, model), BF),
                g=vmem((sizes.sides, tok, sizes.nl), BF),
                gp=vmem((sizes.sides, tok, sizes.nl), BF),
                n2=vmem((tok, model), F32),
                s2=vmem((tok, 1), F32),
                dkv=vmem((2, tok, 2 * sizes.hc), BF),
                dkr=vmem((tok, 2 * sizes.hc), BF),
                dp=vmem((tok, sizes.wide if sizes.pad else sizes.start), BF),
            )
        )
    inputs, outputs = jax.tree.leaves(given), jax.tree.leaves(outs)
    whole = pl.BlockSpec(memory_space=pl.ANY)
    local = (scratch, held, made)
    values = pl.pallas_call(
        functools.partial(fused_kernel, dims, jax.tree.structure((given, outs) + local)),
        out_shape=outputs,
        in_specs=[whole] * len(inputs),
        out_specs=[whole] * len(outputs),
        scratch_shapes=jax.tree.leaves(local),
        compiler_params=pltpu.CompilerParams(
            collective_id=0, has_side_effects=True, vmem_limit_bytes=dims.vmem
        ),
        name="layers",
    )(*inputs)
    return jax.tree.unflatten(jax.tree.structure(outs), values)


def finish_kernel(dims, tree, *refs):
    given, (out, gh, *results) = jax.tree.unflatten(tree, refs)
    r = named(given)
    out[...] = r.out[...]
    gh[...] = r.gh[...].astype(F32)
    begin = 0
    for at, sizes in enumerate(dims.layers):
        attn, ffn = r.lay[at].da, r.lay[at].df
        to_ai, to_ao, to_fi, to_fo, to_sh, to_ga = results[6 * at : 6 * at + 6]
        for p in range(3):
            for h in range(2):
                to = (2 * ((p + 1) % 3) + h) * sizes.hc
                to_ai[:, to : to + sizes.hc] = attn[h, :, p * sizes.hc : (p + 1) * sizes.hc]
        for h in range(2):
            to_ao[:, h * sizes.hc : (h + 1) * sizes.hc] = attn[h, :, 3 * sizes.hc :]
        down = ffn[:, 1].reshape(2 * sizes.nr, ffn.shape[3])
        to_fo[...] = down.T if dims.turned[at] else down
        to_fi[...] = ffn[:, 0].reshape(2 * sizes.nr, ffn.shape[3]).T
        for ref in (to_sh, to_ga):
            ref[...] = r.dvec[0, begin : begin + ref.shape[0]]
            begin += ref.shape[0]


def finish_call(given, params, dims):
    leaves, tree = jax.tree.flatten(given)
    outs = [jax.ShapeDtypeStruct(given["out"].shape, d) for d in (BF, F32)]
    outs += [jax.ShapeDtypeStruct(p.shape, F32) for shards in params for p in shards]
    whole = pl.BlockSpec(memory_space=pltpu.VMEM)
    return pl.pallas_call(
        functools.partial(finish_kernel, dims, jax.tree.structure((given, outs))),
        out_shape=outs,
        in_specs=[whole] * len(leaves),
        out_specs=[whole] * len(outs),
        compiler_params=pltpu.CompilerParams(vmem_limit_bytes=dims.vmem),
        name="finish",
    )(*leaves)


def make_dims(hidden_in, teacher, student):
    model = hidden_in.shape[2]
    layers = [
        layer_sizes(model, p[0].shape[1] // 3, p[2].shape[1] * DEPTH * SIDE, pair)
        for p, pair in ((teacher, True), (student, False))
    ]
    rows = layers[1].nr
    chunks = []
    for at, sizes in enumerate(layers):
        chunks += [("A", at, 0, part) for part in range(sizes.wide // model)]
        for which in (0, 1):
            kind, count = ("P", 1) if sizes.pair else ("F", sizes.nr // rows)
            chunks += [(kind, at, which, part) for part in range(count)]
    counts, slot = {"A": 0, "F": 0, "P": 0}, []
    for chunk in chunks:
        slot.append(counts[chunk[0]])
        counts[chunk[0]] += 1
    group = model // (SIDE * SIDE * DEPTH * SIDE)
    shift_groups = [p[4].shape[0] // group for p in (teacher, student)]
    gain_groups = [p[5].shape[0] // group for p in (teacher, student)]
    rows_of, base, at = [], [], 0
    for sizes in layers:
        found, count = vec_rows(model, sizes)
        rows_of.append(found)
        base.append(at)
        at += count
    return types.SimpleNamespace(
        model=model,
        tok=4 * hidden_in.shape[1],
        seq=8 * hidden_in.shape[1],
        layers=layers,
        chunks=chunks,
        slot=slot,
        rows=rows,
        unit_rows={"A": 2 * teacher[0].shape[0], "F": rows, "P": layers[0].nr},
        rows_of=rows_of,
        base=base,
        length_row=at,
        vec_rows=(at + 8) // 8 * 8,
        turned=[p[3].shape[0] > p[3].shape[1] for p in (teacher, student)],
        group=group,
        lanes=(sum(shift_groups + gain_groups) * group + 4 + 127) // 128 * 128,
        shift_groups=shift_groups,
        gain_groups=gain_groups,
        vmem=63 * 2**20,
    )


def fast_body(hidden_in, cotangent, lengths, *shards):
    params = (shards[:6], shards[6:])
    dims = make_dims(hidden_in, *params)
    turn = lambda shards, turned: (shards[0], shards[1].T, shards[2], shards[3].T if turned else shards[3])
    params = [turn(p, turned) + p[4:] for p, turned in zip(params, dims.turned)]
    values = fused_call(hidden_in, cotangent, lengths, params, dims)
    out, grad_hidden, *grads = finish_call(values, params, dims)
    results = [out, grad_hidden]
    for at, turned in enumerate(dims.turned):
        own = tuple(grads[6 * at : 6 * at + 6])
        results += turn(own, turned) + own[4:]
    return tuple(results)


def body(axes, *args):
    rows, tokens, model = args[0].shape
    pair_fits = args[3 + 2].shape[1] * 2 == model
    fits = pair_fits and axes["dp"] == SIDE * SIDE and axes["mp"] == DEPTH * SIDE
    if fits and rows == 2 and tokens % 16 == 0 and model % 256 == 0:
        return fast_body(*args)
    return general_body(*args)


def general_body(
    hidden_in,
    cotangent,
    lengths,
    teacher_attn_in,
    teacher_attn_out,
    teacher_ffn_in,
    teacher_ffn_out,
    teacher_shifts,
    teacher_gains,
    student_attn_in,
    student_attn_out,
    student_ffn_in,
    student_ffn_out,
    student_shifts,
    student_gains,
):
    span_len = hidden_in.shape[1] * lax.axis_size("mp")
    positions = jnp.arange(span_len)
    valid_keys = positions[None, :] < lengths[:, None]
    teacher = fetch(
        teacher_attn_in,
        teacher_attn_out,
        teacher_ffn_in,
        teacher_ffn_out,
        teacher_shifts,
        teacher_gains,
    )
    student = fetch(
        student_attn_in,
        student_attn_out,
        student_ffn_in,
        student_ffn_out,
        student_shifts,
        student_gains,
    )
    middle, teacher_kept = forward_layer(hidden_in.astype(jnp.float32), teacher, valid_keys)
    final, student_kept = forward_layer(middle, student, valid_keys)
    grad_middle, student_grads = backward_layer(
        cotangent.astype(jnp.float32), student_kept, student, valid_keys
    )
    grad_input, teacher_grads = backward_layer(grad_middle, teacher_kept, teacher, valid_keys)
    teacher_totals = reduce_grads(teacher_grads)
    student_totals = reduce_grads(student_grads)
    return (final.astype(jnp.bfloat16), grad_input) + teacher_totals + student_totals


def solution(mesh):
    in_specs = (
        P("dp", "mp", None),
        P("dp", "mp", None),
        P("dp"),
        P(("dp", "mp"), None),
        P(None, ("dp", "mp")),
        P("dp", "mp"),
        P("mp", "dp"),
        P(("dp", "mp")),
        P(("dp", "mp")),
        P(("dp", "mp"), None),
        P(None, ("dp", "mp")),
        P("dp", "mp"),
        P("mp", "dp"),
        P(("dp", "mp")),
        P(("dp", "mp")),
    )
    out_specs = (
        P("dp", "mp", None),
        P("dp", "mp", None),
        P(("dp", "mp"), None),
        P(None, ("dp", "mp")),
        P("dp", "mp"),
        P("mp", "dp"),
        P(("dp", "mp")),
        P(("dp", "mp")),
        P(("dp", "mp"), None),
        P(None, ("dp", "mp")),
        P("dp", "mp"),
        P("mp", "dp"),
        P(("dp", "mp")),
        P(("dp", "mp")),
    )
    return jax.shard_map(
        functools.partial(body, dict(mesh.shape)), mesh=mesh, in_specs=in_specs, out_specs=out_specs, check_vma=False)
```

```python
import functools
import types

import jax
import jax.numpy as jnp
from jax import lax
from jax.experimental import pallas as pl
from jax.experimental.pallas import tpu as pltpu
from jax.sharding import PartitionSpec as P

HEAD = 64


EPSILON = 1e-06
NEGATIVE = -1e30


def layer_norm(values, gain, shift):
    centered = values - jnp.mean(values, axis=-1, keepdims=True)
    variance = jnp.mean(centered * centered, axis=-1, keepdims=True)
    return centered * lax.rsqrt(variance + EPSILON) * gain + shift


def smooth_gate(pre_act):
    return jax.nn.gelu(pre_act, approximate=False)


def split_shifts(shifts, head_width, model_width, hidden_width):
    spans_list = [
        head_width,
        head_width,
        model_width,
        model_width,
        hidden_width,
        model_width,
        model_width,
    ]
    pieces = []
    offset = 0
    for length in spans_list:
        pieces.append(shifts[offset : offset + length])
        offset = offset + length
    return pieces


def to_heads(values):
    return values.reshape(values.shape[0], values.shape[1], values.shape[2] // HEAD, HEAD)


def score_block(queries, all_keys, valid_keys):
    raw = jnp.einsum(
        "rqhd,rkhd->rhqk", to_heads(queries), to_heads(all_keys), preferred_element_type=jnp.float32
    )
    return jnp.where(valid_keys[:, None, None, :], raw * 0.125, NEGATIVE)


def fetch(attn_in, attn_out, ffn_in, ffn_out, shifts, gains):
    whole_in, whole_out, whole_shifts, whole_gains = (
        lax.all_gather(attn_in, ("dp", "mp"), axis=0, tiled=True),
        lax.all_gather(attn_out, ("dp", "mp"), axis=1, tiled=True),
        lax.all_gather(shifts, ("dp", "mp"), axis=0, tiled=True),
        lax.all_gather(gains, ("dp", "mp"), axis=0, tiled=True),
    )
    ffn_first, ffn_second = (
        lax.all_gather(ffn_in, "dp", axis=0, tiled=True),
        lax.all_gather(ffn_out, "dp", axis=1, tiled=True),
    )
    return (
        whole_in,
        whole_out,
        ffn_first,
        ffn_second,
        whole_shifts.astype(jnp.float32),
        whole_gains.astype(jnp.float32),
    )


def forward_layer(hidden, params, valid_keys):
    attn_in, attn_out, ffn_first, ffn_second, shifts, gains = params
    model_width = hidden.shape[-1]
    head_width = attn_in.shape[1] // 3
    hidden_width = shifts.shape[0] - 2 * head_width - 4 * model_width
    pieces = split_shifts(shifts, head_width, model_width, hidden_width)
    bias_query, bias_value, bias_output, shift_one, bias_up, bias_down, shift_two = pieces
    hidden_low = hidden.astype(jnp.bfloat16)
    projected = jnp.einsum("rsd,de->rse", hidden_low, attn_in, preferred_element_type=jnp.float32)
    queries = (projected[..., :head_width] + bias_query).astype(jnp.bfloat16)
    local_keys = projected[..., head_width : 2 * head_width].astype(jnp.bfloat16)
    local_values = (projected[..., 2 * head_width :] + bias_value).astype(jnp.bfloat16)
    all_keys, all_values = (
        lax.all_gather(local_keys, "mp", axis=1, tiled=True),
        lax.all_gather(local_values, "mp", axis=1, tiled=True),
    )
    scores = score_block(queries, all_keys, valid_keys)
    row_max = jnp.max(scores, axis=-1, keepdims=True)
    exponent = jnp.exp(scores - row_max)
    row_total = jnp.sum(exponent, axis=-1, keepdims=True)
    log_total = row_max + jnp.log(row_total)
    weights_low = (exponent / row_total).astype(jnp.bfloat16)
    mixed = jnp.einsum(
        "rhqk,rkhd->rqhd", weights_low, to_heads(all_values), preferred_element_type=jnp.float32
    )
    context = mixed.reshape(queries.shape).astype(jnp.bfloat16)
    branch = (
        jnp.einsum("rsh,hd->rsd", context, attn_out, preferred_element_type=jnp.float32)
        + bias_output
    )
    summed_one = hidden + branch
    normed_one = layer_norm(summed_one, gains[:model_width], shift_one)
    normed_low = normed_one.astype(jnp.bfloat16)
    ffn_tokens = lax.all_gather(normed_low, "mp", axis=1, tiled=True)
    local_hidden = ffn_first.shape[1]
    bias_part = lax.dynamic_slice_in_dim(bias_up, lax.axis_index("mp") * local_hidden, local_hidden)
    pre_act = (
        jnp.einsum("rsd,df->rsf", ffn_tokens, ffn_first, preferred_element_type=jnp.float32)
        + bias_part
    )
    act_low = smooth_gate(pre_act).astype(jnp.bfloat16)
    down_terms = jnp.einsum("rsf,fd->rsd", act_low, ffn_second, preferred_element_type=jnp.float32)
    ffn_down = lax.psum_scatter(
        down_terms.astype(jnp.bfloat16), "mp", scatter_dimension=1, tiled=True
    ).astype(jnp.float32)
    summed_two = normed_one + ffn_down + bias_down
    result = layer_norm(summed_two, gains[model_width:], shift_two)
    key_store = (all_keys, all_values)
    kept = (
        hidden_low,
        queries,
        key_store,
        log_total,
        context,
        summed_one,
        ffn_tokens,
        pre_act,
        act_low,
        summed_two,
    )
    return (result, kept)


def backward_layer(grad_out, kept, params, valid_keys):
    attn_in, attn_out, ffn_first, ffn_second, shifts, gains = params
    (
        hidden_low,
        queries,
        key_store,
        log_total,
        context,
        summed_one,
        ffn_tokens,
        pre_act,
        act_low,
        summed_two,
    ) = kept
    model_width = summed_one.shape[-1]
    head_width = attn_in.shape[1] // 3
    hidden_width = shifts.shape[0] - 2 * head_width - 4 * model_width
    pieces = split_shifts(shifts, head_width, model_width, hidden_width)
    bias_query, bias_value, bias_output, shift_one, bias_up, bias_down, shift_two = pieces
    sum_axes = (0, 1)
    unused_two, norm_two_back = jax.vjp(layer_norm, summed_two, gains[model_width:], shift_two)
    grad_two, grad_gain_two, grad_shift_two = norm_two_back(grad_out)
    grad_down = grad_two.astype(jnp.bfloat16)
    grad_bias_down = jnp.sum(grad_down.astype(jnp.float32), axis=sum_axes)
    grad_tokens = lax.all_gather(grad_down, "mp", axis=1, tiled=True)
    grad_act = jnp.einsum(
        "rsd,fd->rsf", grad_tokens, ffn_second, preferred_element_type=jnp.float32
    )
    grad_second = jnp.einsum(
        "rsf,rsd->fd", act_low, grad_tokens, preferred_element_type=jnp.float32
    )
    unused_gate, gate_back = jax.vjp(smooth_gate, pre_act)
    grad_pre = gate_back(grad_act)[0].astype(jnp.bfloat16)
    grad_bias_part = jnp.sum(grad_pre.astype(jnp.float32), axis=sum_axes)
    grad_first = jnp.einsum("rsd,rsf->df", ffn_tokens, grad_pre, preferred_element_type=jnp.float32)
    back_terms = jnp.einsum("rsf,df->rsd", grad_pre, ffn_first, preferred_element_type=jnp.float32)
    grad_normed = lax.psum_scatter(
        back_terms.astype(jnp.bfloat16), "mp", scatter_dimension=1, tiled=True
    ).astype(jnp.float32)
    blank_bias = jnp.zeros((hidden_width,), jnp.float32)
    grad_bias_up = lax.dynamic_update_slice_in_dim(
        blank_bias, grad_bias_part, lax.axis_index("mp") * ffn_first.shape[1], 0
    )
    grad_normed = grad_normed + grad_two
    unused_one, norm_one_back = jax.vjp(layer_norm, summed_one, gains[:model_width], shift_one)
    grad_one, grad_gain_one, grad_shift_one = norm_one_back(grad_normed)
    grad_branch = grad_one.astype(jnp.bfloat16)
    grad_bias_output = jnp.sum(grad_branch.astype(jnp.float32), axis=sum_axes)
    grad_attn_out = jnp.einsum(
        "rsh,rsd->hd", context, grad_branch, preferred_element_type=jnp.float32
    )
    grad_context = jnp.einsum(
        "rsd,hd->rsh", grad_branch, attn_out, preferred_element_type=jnp.float32
    ).astype(jnp.bfloat16)
    stored_keys, stored_values = key_store
    all_keys, all_values = (stored_keys, stored_values)
    weights = jnp.exp(score_block(queries, all_keys, valid_keys) - log_total)
    context_heads = to_heads(grad_context)
    grad_weights = jnp.einsum(
        "rqhd,rkhd->rhqk", context_heads, to_heads(all_values), preferred_element_type=jnp.float32
    )
    inner_sum = jnp.sum(weights * grad_weights, axis=-1, keepdims=True)
    grad_raw = (0.125 * weights * (grad_weights - inner_sum)).astype(jnp.bfloat16)
    grad_queries = jnp.einsum(
        "rhqk,rkhd->rqhd", grad_raw, to_heads(all_keys), preferred_element_type=jnp.float32
    )
    grad_queries = grad_queries.reshape(queries.shape).astype(jnp.bfloat16)
    weights_low = weights.astype(jnp.bfloat16)
    value_terms = jnp.einsum(
        "rhqk,rqhd->rkhd", weights_low, context_heads, preferred_element_type=jnp.float32
    )
    key_terms = jnp.einsum(
        "rhqk,rqhd->rkhd", grad_raw, to_heads(queries), preferred_element_type=jnp.float32
    )
    key_terms = key_terms.reshape(all_keys.shape)
    value_terms = value_terms.reshape(all_values.shape)
    grad_keys, grad_values = (
        lax.psum_scatter(
            key_terms.astype(jnp.bfloat16), "mp", scatter_dimension=1, tiled=True
        ).astype(jnp.float32),
        lax.psum_scatter(
            value_terms.astype(jnp.bfloat16), "mp", scatter_dimension=1, tiled=True
        ).astype(jnp.float32),
    )
    grad_values_low = grad_values.astype(jnp.bfloat16)
    grad_projected = jnp.concatenate(
        [grad_queries, grad_keys.astype(jnp.bfloat16), grad_values_low], axis=-1
    )
    grad_attn_in = jnp.einsum(
        "rsd,rse->de", hidden_low, grad_projected, preferred_element_type=jnp.float32
    )
    grad_hidden = grad_one + jnp.einsum(
        "rse,de->rsd", grad_projected, attn_in, preferred_element_type=jnp.float32
    )
    grad_bias_query = jnp.sum(grad_queries.astype(jnp.float32), axis=sum_axes)
    grad_bias_value = jnp.sum(grad_values_low.astype(jnp.float32), axis=sum_axes)
    grad_shifts = jnp.concatenate(
        [
            grad_bias_query,
            grad_bias_value,
            grad_bias_output,
            grad_shift_one,
            grad_bias_up,
            grad_bias_down,
            grad_shift_two,
        ]
    )
    grad_gains = jnp.concatenate([grad_gain_one, grad_gain_two])
    return (
        grad_hidden,
        (grad_attn_in, grad_attn_out, grad_first, grad_second, grad_shifts, grad_gains),
    )


def reduce_grads(grads):
    grad_attn_in, grad_attn_out, grad_first, grad_second, grad_shifts, grad_gains = grads
    total_in, total_out, total_shifts, total_gains = (
        lax.psum_scatter(grad_attn_in, ("dp", "mp"), scatter_dimension=0, tiled=True),
        lax.psum_scatter(grad_attn_out, ("dp", "mp"), scatter_dimension=1, tiled=True),
        lax.psum_scatter(grad_shifts, ("dp", "mp"), scatter_dimension=0, tiled=True),
        lax.psum_scatter(grad_gains, ("dp", "mp"), scatter_dimension=0, tiled=True),
    )
    total_first, total_second = (
        lax.psum_scatter(
            grad_first.astype(jnp.bfloat16), "dp", scatter_dimension=0, tiled=True
        ).astype(jnp.float32),
        lax.psum_scatter(
            grad_second.astype(jnp.bfloat16), "dp", scatter_dimension=1, tiled=True
        ).astype(jnp.float32),
    )
    return (total_in, total_out, total_first, total_second, total_shifts, total_gains)


BF = jnp.bfloat16
F32 = jnp.float32
MESH = pl.DeviceIdType.MESH
SIDE = 2
DEPTH = 4
PARTNERS = 9


def mm(left, right, left_dim, right_dim):
    return lax.dot_general(
        left, right, (((left_dim,), (right_dim,)), ((), ())), preferred_element_type=F32
    )


def rowsum(values):
    return jnp.sum(values, axis=0, keepdims=True)


def normalize(values):
    centered = values - jnp.mean(values, axis=-1, keepdims=True)
    variance = jnp.mean(centered * centered, axis=-1, keepdims=True)
    scale = lax.rsqrt(variance + EPSILON)
    return centered * scale, scale


def normalize_back(grad, normed, scale):
    along = jnp.mean(grad * normed, axis=-1, keepdims=True)
    return scale * (grad - jnp.mean(grad, axis=-1, keepdims=True) - normed * along)


def layer_sizes(model, heads_width, hidden, pair):
    half = heads_width // 2
    start = 3 * half // 128 * 128
    return types.SimpleNamespace(
        hc=half,
        heads=half // HEAD,
        wide=4 * half,
        start=start,
        qw=-(-half // 128) * 128,
        pad=3 * half - start,
        nr=hidden // 16,
        nc=hidden // 2,
        nl=hidden // 4 if pair else hidden // 2,
        pair=pair,
        sides=2 if pair else 1,
        zs=2 if pair else DEPTH,
        zb=model * 8 // hidden,
    )


def vec_rows(model, sizes):
    lengths = dict(
        qv=4 * sizes.hc, bo=model, beta1=model, b1=2 * sizes.nc, b2=model, beta2=model, g1=model, g2=model
    )
    rows, at = {}, 0
    for name, length in lengths.items():
        rows[name] = at
        at += length // model
    return types.SimpleNamespace(**rows), at


def named(tree):
    if isinstance(tree, dict):
        return types.SimpleNamespace(**{key: named(value) for key, value in tree.items()})
    return [named(value) for value in tree] if isinstance(tree, list) else tree


def fused_kernel(dims, tree, *refs):
    given, outs, scratch, held, made = jax.tree.unflatten(tree, refs)
    lay = [named(a | b | d) for a, b, d in zip(held["lay"], made["lay"], scratch["lay"])]
    r = named(held | made | scratch)
    given, outs = named(given), named(outs)

    def fetch_copies():
        pairs = []
        for at in range(2):
            far, near = given.lay[at], lay[at]
            pairs += [(far.pai, near.pai), (far.pao, near.pao)]
            if at == 0:
                pairs += [(given.hid, r.hid)]
            pairs += [(far.pfi, near.pfi), (far.pfo, near.pfo), (far.psh, near.psh), (far.pga, near.pga)]
        pairs += [(given.len, r.len), (given.cot, r.cot)]
        return [pltpu.make_async_copy(src, dst, r.ins.at[i]) for i, (src, dst) in enumerate(pairs)]

    fetched = fetch_copies()
    for copy in fetched:
        copy.start()
    stored = []

    def store(src, dst):
        copy = pltpu.make_async_copy(src, dst, r.outs.at[len(stored)])
        copy.start()
        stored.append(copy)
    model, tok, seq, layers = dims.model, dims.tok, dims.seq, dims.layers
    half_lanes = model // 2
    dp, mp = lax.axis_index("dp"), lax.axis_index("mp")
    y, c = dp // SIDE, lax.rem(dp, SIDE)
    z, x = mp // SIDE, lax.rem(mp, SIDE)

    def device(c, x, y, z):
        return {"dp": y * SIDE + c, "mp": z * SIDE + x}

    sib = device(1 - c, x, y, z)
    xn, yn = device(c, 1 - x, y, z), device(c, x, 1 - y, z)
    zdev = [device(c, x, y, lax.rem(z + d, DEPTH)) for d in range(1, DEPTH)]
    zpair = z + 1 - 2 * lax.rem(z, 2)
    zn = device(c, x, y, zpair)
    zfar = device(c, x, y, lax.rem(z + 2, DEPTH))

    bar = pltpu.get_barrier_semaphore()
    for step in range(1, DEPTH * SIDE):
        other = lax.rem(mp + step, DEPTH * SIDE)
        pl.semaphore_signal(bar, inc=1, device_id={"dp": dp, "mp": other}, device_id_type=MESH)
    pl.semaphore_signal(bar, inc=1, device_id=sib, device_id_type=MESH)
    pl.semaphore_signal(bar, inc=1, device_id=yn, device_id_type=MESH)

    sent = []

    def remote(src, dst, send, recv, dev):
        return pltpu.make_async_remote_copy(
            src_ref=src, dst_ref=dst, send_sem=send, recv_sem=recv, device_id=dev, device_id_type=MESH
        )

    def push(src, dst, send, recv, dev):
        copy = remote(src, dst, send, recv, dev)
        copy.start()
        sent.append((None, copy))

    def arrived(dst, recv, send):
        remote(dst, dst, send, recv, sib).wait_recv()

    row_core = z // 2
    mine = c == row_core
    half = lax.rem(z, 2)

    def spread(src, land, sends, recvs):
        block = 2 * lax.rem(z, 2) + x
        target = 2 * c + z // 2
        for j in range(2):
            local = (x == j) & (z == target)
            copy = remote(src.at[j], land.at[block], sends.at[j], recvs.at[block], device(c, j, y, target))
            pl.when(local)(pltpu.make_async_copy(src.at[j], land.at[block], recvs.at[block]).start)
            pl.when(jnp.logical_not(local))(copy.start)

    def spread_turn(src, land, sends, recvs, on_chip_send, on_chip_recv):
        target = 2 * c + z // 2
        for j in range(2):
            local = (x == j) & (z == target)
            copy = remote(src.at[j], land.at[0], sends.at[j], recvs.at[0], sib)
            pl.when(jnp.logical_not(local))(copy.wait_send)
        whole = remote(land, land, on_chip_send, on_chip_recv, sib)

        @pl.when(mine)
        def _():
            for block in range(4):
                arrived(land.at[block], recvs.at[block], sends.at[0])
            whole.start()

    def spread_end(land, on_chip_send, on_chip_recv):
        whole = remote(land, land, on_chip_send, on_chip_recv, sib)
        pl.when(mine)(whole.wait_send)
        pl.when(jnp.logical_not(mine))(whole.wait_recv)

    def collect(src, land, sends, recvs):
        @pl.when(mine)
        def _():
            for block in range(4):
                z_to, x_to = 2 * half + block // 2, block % 2
                local = (x == x_to) & (z == z_to)
                slot = land.at[x]
                copy = remote(
                    src.at[block], slot, sends.at[block], recvs.at[x], device(c, x_to, y, z_to)
                )
                pl.when(local)(pltpu.make_async_copy(src.at[block], slot, recvs.at[x]).start)
                pl.when(jnp.logical_not(local))(copy.start)

    def collect_done(src, land, sends, recvs):
        for j in range(2):
            arrived(land.at[j], recvs.at[j], sends.at[0])

        @pl.when(mine)
        def _():
            for block in range(4):
                z_to, x_to = 2 * half + block // 2, block % 2
                local = (x == x_to) & (z == z_to)
                copy = remote(src.at[block], src.at[block], sends.at[block], recvs.at[0], sib)
                pl.when(jnp.logical_not(local))(copy.wait_send)

    chunks = dims.chunks
    every, first, second = pl.ds(0, DEPTH), pl.ds(0, 2), pl.ds(2, 2)
    both = pl.ds(0, 2)

    def view(i, grads, band, z_slice, x_at, y_at):
        kind, layer, which, part = chunks[i]
        full = dims.unit_rows[kind]
        if kind == "P":
            ref = lay[layer].dw if grads else lay[layer].w
            lanes = pl.ds(pl.multiple_of(y_at * half_lanes, 128), half_lanes)
            return ref.at[which, z_slice, x_at, :, lanes]
        begin, count = {"a": (0, full - 32), "b": (full - 32, 16), "c": (full - 16, 16)}[band]
        if kind == "A":
            ref = lay[layer].ga
            y_pick = both if y_at is None else y_at
            return ref.at[y_pick, z_slice, x_at, pl.ds(begin, count), pl.ds(part * model, model)]
        ref = lay[layer].dw if grads else lay[layer].w
        lanes = pl.ds(0, model)
        if y_at is not None:
            lanes = pl.ds(pl.multiple_of(y_at * half_lanes, 128), half_lanes)
        return ref.at[which, z_slice, x_at, pl.ds(part * full + begin, count), lanes]

    UP, DOWN, FAR, RELAY = range(4)
    z_far = lax.rem(z + 2, DEPTH)
    z_up, z_down = lax.rem(z + 1, DEPTH), lax.rem(z + DEPTH - 1, DEPTH)
    z_end = DEPTH - 1 - z
    has_up, has_down = z < DEPTH - 1, z > 0
    inner = (z == 1) | (z == 2)
    outer = (z == 0) | (z == 3)
    z_out = jnp.where(z == 1, 0, 3)
    z_in = jnp.where(z == 0, 1, 2)

    def push_if(cond, src, dst, send, recv, dev):
        copy = remote(src, dst, send, recv, dev)
        pl.when(cond)(copy.start)
        sent.append((cond, copy))

    def wait_sent():
        for cond, copy in sent:
            if cond is None:
                copy.wait_send()
            else:
                pl.when(cond)(copy.wait_send)
        sent.clear()

    def arrived_if(cond, dst, recv, send):
        pl.when(cond)(remote(dst, dst, send, recv, sib).wait_recv)

    def at_z(zz):
        return device(c, x, y, zz)

    def line_send(part, send, recv):
        own = part(z)
        push_if(has_up, own, own, send(UP), recv(UP), at_z(z_up))
        push_if(has_down, own, own, send(DOWN), recv(DOWN), at_z(z_down))
        push(own, own, send(FAR), recv(FAR), at_z(z_far))

    def line_relay(part, send, recv):
        far = part(z_far)
        arrived_if(inner, far, recv(FAR), send(FAR))
        push_if(inner, far, far, send(RELAY), recv(RELAY), at_z(z_out))

    def line_end(part, send, recv):
        arrived_if(has_down, part(z_down), recv(UP), send(UP))
        arrived_if(has_up, part(z_up), recv(DOWN), send(DOWN))
        arrived_if(outer, part(z_far), recv(FAR), send(FAR))
        arrived_if(outer, part(z_end), recv(RELAY), send(RELAY))

    def sems(ref_send, ref_recv, i, base):
        return (lambda k: ref_send.at[i, base + k]), (lambda k: ref_recv.at[i, base + k])

    def one(zz):
        return pl.ds(zz, 1)

    def parts_of(i, grads):
        return (
            lambda zz: view(i, grads, "a", one(zz), x, y),
            lambda zz: view(i, grads, "b", one(zz), both, y),
            lambda zz: view(i, grads, "c", one(zz), x, None),
        )

    def gather_sems(i, base):
        return sems(r.gs, r.gr, i, base)

    def gather_push(i, k, piece, dev):
        push(piece, piece, r.gs.at[i, k], r.gr.at[i, k], dev)

    def gather_wait(i, k, piece):
        arrived(piece, r.gr.at[i, k], r.gs.at[i, k])

    z_own, z_other = z // 2, 1 - z // 2

    def pair_view(i, grads, z_slice, x_at, y_at):
        return view(i, grads, None, z_slice, x_at, y_at)

    def pair_0(i):
        gather_push(i, 0, pair_view(i, False, one(z_own), x, y), zfar)

    def pair_1(i):
        gather_wait(i, 0, pair_view(i, False, one(z_other), x, y))
        own = pair_view(i, False, both, x, y)
        gather_push(i, 1, own, xn)
        gather_push(i, 2, own, yn)

    def pair_2(i):
        gather_wait(i, 1, pair_view(i, False, both, 1 - x, y))
        gather_wait(i, 2, pair_view(i, False, both, x, 1 - y))
        gather_push(i, 3, pair_view(i, False, one(0), x, 1 - y), xn)
        gather_push(i, 4, pair_view(i, False, one(1), 1 - x, y), yn)

    def pair_3(i):
        gather_wait(i, 3, pair_view(i, False, one(0), 1 - x, 1 - y))
        gather_wait(i, 4, pair_view(i, False, one(1), 1 - x, 1 - y))

    def gather_0(i):
        gather_push(i, 16, view(i, False, "b", one(z), x, y), xn)
        gather_push(i, 17, view(i, False, "c", one(z), x, y), yn)
        line_send(parts_of(i, False)[0], *gather_sems(i, 0))

    def gather_1(i):
        a, b, c_part = parts_of(i, False)
        gather_wait(i, 16, view(i, False, "b", one(z), 1 - x, y))
        line_send(b, *gather_sems(i, 4))
        gather_wait(i, 17, view(i, False, "c", one(z), x, 1 - y))
        line_send(c_part, *gather_sems(i, 8))
        line_relay(a, *gather_sems(i, 0))

    def gather_2(i):
        a, b, c_part = parts_of(i, False)
        line_end(a, *gather_sems(i, 0))
        own = view(i, False, "a", every, x, y)
        gather_push(i, 12, own, xn)
        gather_push(i, 13, own, yn)
        line_relay(b, *gather_sems(i, 4))
        line_relay(c_part, *gather_sems(i, 8))

    def gather_3(i):
        a, b, c_part = parts_of(i, False)
        line_end(b, *gather_sems(i, 4))
        gather_push(i, 18, view(i, False, "b", every, both, y), yn)
        line_end(c_part, *gather_sems(i, 8))
        gather_push(i, 19, view(i, False, "c", every, x, None), xn)
        gather_wait(i, 12, view(i, False, "a", every, 1 - x, y))
        gather_wait(i, 13, view(i, False, "a", every, x, 1 - y))
        gather_push(i, 14, view(i, False, "a", first, x, 1 - y), xn)
        gather_push(i, 15, view(i, False, "a", second, 1 - x, y), yn)

    def gather_4(i):
        gather_wait(i, 14, view(i, False, "a", first, 1 - x, 1 - y))
        gather_wait(i, 15, view(i, False, "a", second, 1 - x, 1 - y))
        gather_wait(i, 18, view(i, False, "b", every, both, 1 - y))
        gather_wait(i, 19, view(i, False, "c", every, 1 - x, None))

    band_stages = (gather_0, gather_1, gather_2, gather_3, gather_4)
    pair_stages = (pair_0, pair_1, pair_2, pair_3)

    def gather(i, stage):
        stages = pair_stages if chunks[i][0] == "P" else band_stages
        stages[stage](i)

    def add_into(ref, extra):
        total = ref[...].astype(F32)
        for more in extra:
            total = total + more[...].astype(F32)
        ref[...] = total.astype(BF)

    def slots(i, name):
        return getattr(r.red["AFP".index(chunks[i][0])], name).at[dims.slot[i]]

    def reduce_push(i, k, src, dst, dev):
        push(src, dst, r.ss.at[i, k], r.sr.at[i, k], dev)

    def reduce_wait(i, k, dst):
        arrived(dst, r.sr.at[i, k], r.ss.at[i, k])

    def line_reduce_send(part, land, send, recv):
        push_if(has_up, part(z_up), land.at[UP], send(UP), recv(UP), at_z(z_up))
        push_if(has_down, part(z_down), land.at[DOWN], send(DOWN), recv(DOWN), at_z(z_down))
        push_if(outer, part(z_end), land.at[RELAY], send(RELAY), recv(RELAY), at_z(z_in))
        push_if(outer, part(z_far), land.at[FAR], send(FAR), recv(FAR), at_z(z_far))

    def line_reduce_relay(part, land, send, recv):
        @pl.when(inner)
        def _():
            arrived(land.at[RELAY], recv(RELAY), send(RELAY))
            add_into(part(z_far), [land.at[RELAY]])

        push_if(inner, part(z_far), land.at[FAR], send(FAR), recv(FAR), at_z(z_far))

    def line_reduce_end(part, land, send, recv):
        arrived(land.at[FAR], recv(FAR), send(FAR))

        @pl.when(inner)
        def _():
            arrived(land.at[UP], recv(UP), send(UP))
            arrived(land.at[DOWN], recv(DOWN), send(DOWN))
            add_into(part(z), [land.at[FAR], land.at[UP], land.at[DOWN]])

        @pl.when(z == 0)
        def _():
            arrived(land.at[DOWN], recv(DOWN), send(DOWN))
            add_into(part(z), [land.at[FAR], land.at[DOWN]])

        @pl.when(z == DEPTH - 1)
        def _():
            arrived(land.at[UP], recv(UP), send(UP))
            add_into(part(z), [land.at[FAR], land.at[UP]])

    def reduce_sems(i, base):
        return sems(r.ss, r.sr, i, base)

    def band_reduce_0(i):
        over = slots(i, "ad")
        reduce_push(i, 14, view(i, True, "a", first, 1 - x, 1 - y), over.at[0], xn)
        reduce_push(i, 15, view(i, True, "a", second, 1 - x, 1 - y), over.at[1], yn)
        reduce_push(i, 18, view(i, True, "b", every, both, 1 - y), slots(i, "by"), yn)
        reduce_push(i, 19, view(i, True, "c", every, 1 - x, None), slots(i, "cx"), xn)

    def band_reduce_1(i):
        a, b, c_part = parts_of(i, True)
        over, beside = slots(i, "ad"), slots(i, "an")
        reduce_wait(i, 14, over.at[0])
        add_into(view(i, True, "a", first, x, 1 - y), [over.at[0]])
        reduce_push(i, 13, view(i, True, "a", every, x, 1 - y), beside.at[1], yn)
        reduce_wait(i, 15, over.at[1])
        add_into(view(i, True, "a", second, 1 - x, y), [over.at[1]])
        reduce_push(i, 12, view(i, True, "a", every, 1 - x, y), beside.at[0], xn)
        reduce_wait(i, 18, slots(i, "by"))
        add_into(view(i, True, "b", every, both, y), [slots(i, "by")])
        line_reduce_send(b, slots(i, "bz"), *reduce_sems(i, 4))
        reduce_wait(i, 19, slots(i, "cx"))
        add_into(view(i, True, "c", every, x, None), [slots(i, "cx")])
        line_reduce_send(c_part, slots(i, "cz"), *reduce_sems(i, 8))

    def band_reduce_2(i):
        a, b, c_part = parts_of(i, True)
        beside = slots(i, "an")
        reduce_wait(i, 12, beside.at[0])
        reduce_wait(i, 13, beside.at[1])
        add_into(view(i, True, "a", every, x, y), [beside.at[0], beside.at[1]])
        line_reduce_send(a, slots(i, "az"), *reduce_sems(i, 0))
        line_reduce_relay(b, slots(i, "bz"), *reduce_sems(i, 4))
        line_reduce_relay(c_part, slots(i, "cz"), *reduce_sems(i, 8))

    def band_reduce_3(i):
        a, b, c_part = parts_of(i, True)
        line_reduce_end(b, slots(i, "bz"), *reduce_sems(i, 4))
        reduce_push(i, 16, view(i, True, "b", one(z), 1 - x, y), slots(i, "bx"), xn)
        line_reduce_end(c_part, slots(i, "cz"), *reduce_sems(i, 8))
        reduce_push(i, 17, view(i, True, "c", one(z), x, 1 - y), slots(i, "cy"), yn)
        line_reduce_relay(a, slots(i, "az"), *reduce_sems(i, 0))

    def band_reduce_4(i):
        line_reduce_end(parts_of(i, True)[0], slots(i, "az"), *reduce_sems(i, 0))
        reduce_wait(i, 16, slots(i, "bx"))
        reduce_wait(i, 17, slots(i, "cy"))
        total = jnp.concatenate(
            [
                view(i, True, "a", one(z), x, y)[...].astype(F32)[0],
                (view(i, True, "b", one(z), x, y)[...].astype(F32) + slots(i, "bx")[...].astype(F32))[0],
                (view(i, True, "c", one(z), x, y)[...].astype(F32) + slots(i, "cy")[...].astype(F32))[0],
            ],
            axis=0,
        )
        reduce_store(i, total)

    def pair_reduce_0(i):
        over = slots(i, "ad")
        reduce_push(i, 3, pair_view(i, True, one(0), 1 - x, 1 - y), over.at[0], xn)
        reduce_push(i, 4, pair_view(i, True, one(1), 1 - x, 1 - y), over.at[1], yn)

    def pair_reduce_1(i):
        over, beside = slots(i, "ad"), slots(i, "an")
        reduce_wait(i, 3, over.at[0])
        add_into(pair_view(i, True, one(0), x, 1 - y), [over.at[0]])
        reduce_push(i, 2, pair_view(i, True, both, x, 1 - y), beside.at[1], yn)
        reduce_wait(i, 4, over.at[1])
        add_into(pair_view(i, True, one(1), 1 - x, y), [over.at[1]])
        reduce_push(i, 1, pair_view(i, True, both, 1 - x, y), beside.at[0], xn)

    def pair_reduce_2(i):
        beside = slots(i, "an")
        reduce_wait(i, 1, beside.at[0])
        reduce_wait(i, 2, beside.at[1])
        add_into(pair_view(i, True, both, x, y), [beside.at[0], beside.at[1]])
        reduce_push(i, 0, pair_view(i, True, one(z_other), x, y), slots(i, "az"), zfar)

    def pair_reduce_3(i):
        far = slots(i, "az")
        reduce_wait(i, 0, far)
        own = pair_view(i, True, one(z_own), x, y)
        reduce_store(i, (own[...].astype(F32) + far[...].astype(F32))[0])

    def reduce_store(i, total):
        kind, layer, which, part = chunks[i]
        send, land = slots(i, "fsend"), slots(i, "fland")
        if kind == "A":
            rows = total.shape[0] // 2
            cols = slice(part * model, (part + 1) * model)
            lay[layer].da[c, :, cols] = jnp.where(c == 0, total[:rows], total[rows:])
            send[...] = jnp.where(c == 0, total[rows:], total[:rows])
        else:
            full = dims.unit_rows[kind]
            rows, lanes = pl.ds(part * full, full), total.shape[1] // 2
            lay[layer].df[c, which, rows, :] = jnp.where(c == 0, total[:, :lanes], total[:, lanes:])
            send[...] = jnp.where(c == 0, total[:, lanes:], total[:, :lanes])
        push(send, land, r.fs.at[i], r.fr.at[i], sib)

    def reduce_out(i):
        kind, layer, which, part = chunks[i]
        land = slots(i, "fland")
        arrived(land, r.fr.at[i], r.fs.at[i])
        if kind == "A":
            lay[layer].da[1 - c, :, part * model : (part + 1) * model] = land[...]
            if part == 0:
                store(lay[layer].da, outs.lay[layer].da)
        else:
            full = dims.unit_rows[kind]
            lay[layer].df[1 - c, which, pl.ds(part * full, full), :] = land[...]
            if part == layers[layer].nr // full - 1:
                store(lay[layer].df.at[:, which], outs.lay[layer].df.at[:, which])

    band_reduces = (band_reduce_0, band_reduce_1, band_reduce_2, band_reduce_3, band_reduce_4)
    pair_reduces = (pair_reduce_0, pair_reduce_1, pair_reduce_2, pair_reduce_3)

    def reduce(i, stage):
        stages = pair_reduces if chunks[i][0] == "P" else band_reduces
        if stage < len(stages):
            stages[stage](i)

    def total_step(work, land, step, sends, recvs):
        dev = (sib, xn, yn, zn, zfar)[step]
        push(work.at[step], land.at[step], sends.at[step], recvs.at[step], dev)

    def total_add(work, land, step, sends, recvs):
        arrived(land.at[step], recvs.at[step], sends.at[step])
        work[step + 1] = work[step] + land[step]

    exchanges = []

    def exchange(part):
        slot = len(exchanges) % 2
        r.xs[slot] = part.astype(BF)
        copy = remote(r.xs.at[slot], r.xr.at[slot], r.es.at[slot], r.er.at[slot], sib)
        copy.start()
        exchanges.append(copy)

        def finish():
            copy.wait()
            return r.xs[slot].astype(F32) + r.xr[slot].astype(F32)

        return finish

    quarter = tok // 2
    own_rows = pl.ds(pl.multiple_of(c * quarter, 16), quarter)
    other_rows = pl.ds(pl.multiple_of((1 - c) * quarter, 16), quarter)

    class Share:
        def __init__(self, ref, k):
            blocks = len(ref.shape) == 4
            self.own = pl.ds(2 * c, 2) if blocks else own_rows
            self.other = pl.ds(2 - 2 * c, 2) if blocks else other_rows
            self.ref, self.k = ref, k
            piece = ref.at[half, self.own]
            push(piece, piece, r.ps.at[k, 0], r.pr.at[k, 0], zn)

        def turn(self):
            got, k = self.ref.at[1 - half, self.own], self.k
            arrived(got, r.pr.at[k, 0], r.ps.at[k, 0])
            push(got, got, r.ps.at[k, 1], r.pr.at[k, 1], sib)

        def end(self):
            k = self.k
            arrived(self.ref.at[1 - half, self.other], r.pr.at[k, 1], r.ps.at[k, 1])

    class Fold:
        def __init__(self, make, k):
            self.make, self.k = make, k
            r.px[k] = make(1 - half, False).astype(BF)
            push(r.px.at[k, other_rows], r.prx.at[k], r.ps.at[k, 2], r.pr.at[k, 2], sib)

        def keep(self):
            self.own = exchange(self.make(half, True))

        def cross(self):
            k = self.k
            arrived(r.prx.at[k], r.pr.at[k, 2], r.ps.at[k, 2])
            r.pz[k] = (r.px[k, own_rows, :].astype(F32) + r.prx[k].astype(F32)).astype(BF)
            push(r.pz.at[k], r.pzr.at[k, c], r.ps.at[k, 3], r.pr.at[k, 3], zn)

        def turn(self):
            k = self.k
            got = r.pzr.at[k, c]
            arrived(got, r.pr.at[k, 3], r.ps.at[k, 3])
            push(got, got, r.ps.at[k, 4], r.pr.at[k, 4], sib)

        def end(self):
            k = self.k
            arrived(r.pzr.at[k, 1 - c], r.pr.at[k, 4], r.ps.at[k, 4])
            return self.own() + r.pzr[k].reshape(tok, model).astype(F32)

    def vec_row(row):
        return r.vw[5, row : row + 1, :]

    def layer_vecs(at):
        sizes, rows, base = layers[at], dims.rows_of[at], dims.base[at]
        if sizes.hc * 2 == model:
            qv = r.vw[5, pl.ds(base + rows.qv + c, 1), :]
        else:
            both = vec_row(base + rows.qv)
            qv = jnp.where(c == 0, both[:, : 2 * sizes.hc], both[:, 2 * sizes.hc :])
        span = sizes.nc // model
        b1 = [r.vw[5, pl.ds(base + rows.b1 + c * span + s, 1), :] for s in range(span)]
        if sizes.pair:
            cut = 2 * sizes.nr
            b1 = [jnp.concatenate([jnp.where(half == 0, v[:, :cut], v[:, cut:]) for v in b1], axis=1)]
        found = types.SimpleNamespace(bq=qv[:, : sizes.hc], bv=qv[:, sizes.hc :], b1=b1)
        for name, row in vars(rows).items():
            if not hasattr(found, name):
                setattr(found, name, vec_row(base + row))
        return found

    kept = lay
    wa = [one_layer.wa for one_layer in lay]
    weights = [one_layer.w for one_layer in lay]

    def order_rows(at, part):
        gathered, whole = lay[at].ga, wa[at]
        cols = slice(part * model, (part + 1) * model)
        rows = gathered.shape[3] // 2
        span = DEPTH * 2 * rows
        for y_at in range(SIDE):
            for z_at in range(DEPTH):
                left = gathered[y_at, z_at, 0, :, cols].astype(F32)
                right = gathered[y_at, z_at, 1, :, cols].astype(F32)
                for core in range(SIDE):
                    own = slice(core * rows, (core + 1) * rows)
                    both = jnp.concatenate([left[own], right[own]], axis=0).astype(BF)
                    begin = (y_at * SIDE + core) * span + z_at * 2 * rows
                    whole[begin : begin + 2 * rows, cols] = both

    def store_grad_rows(at, y_at, value, cols):
        blocks = lay[at].ga
        rows = blocks.shape[3] // 2
        span = DEPTH * 2 * rows
        for z_at in range(DEPTH):
            for x_at in range(SIDE):
                begin = (z_at * 2 + x_at) * rows
                both = [value[begin : begin + rows], value[span + begin : span + begin + rows]]
                blocks[y_at, z_at, x_at, :, cols] = jnp.concatenate(both, axis=0).astype(BF)

    def head_kv(at, h):
        sizes, kv = layers[at], kept[at].kv
        k = kv[:, :, h * HEAD : (h + 1) * HEAD].reshape(seq, HEAD)
        v = kv[:, :, sizes.hc + h * HEAD : sizes.hc + (h + 1) * HEAD].reshape(seq, HEAD)
        return k, v

    def attention(at):
        sizes, keep = layers[at], kept[at]
        lane = lax.broadcasted_iota(jnp.int32, (1, model), 1)
        first_lane = (y * SIDE + row_core) * group + x
        entry = vec_row(dims.length_row)
        entry = jnp.where(lane == first_lane, 256.0 * entry, jnp.where(lane == first_lane + 2, entry, 0.0))
        length = jnp.sum(entry, axis=1, keepdims=True)
        valid = lax.broadcasted_iota(jnp.int32, (1, seq), 1).astype(F32) < length
        for h in range(sizes.heads):
            q = keep.q[:, h * HEAD : (h + 1) * HEAD]
            k, v = head_kv(at, h)
            scores = jnp.where(valid, mm(q, k, 1, 1) * 0.125, NEGATIVE)
            exponent = jnp.exp(scores - jnp.max(scores, axis=1, keepdims=True))
            low = (exponent / jnp.sum(exponent, axis=1, keepdims=True)).astype(BF)
            keep.a[h] = low
            begin = sizes.pad + h * HEAD
            keep.ctx[:, begin : begin + HEAD] = mm(low, v, 1, 0).astype(BF)

    def attention_back(at, grad_ctx):
        sizes, keep = layers[at], kept[at]
        dkv, dq = lay[at].dkv, lay[at].dq
        for h in range(sizes.heads):
            q = keep.q[:, h * HEAD : (h + 1) * HEAD]
            k, v = head_kv(at, h)
            begin = sizes.pad + h * HEAD
            dc = grad_ctx[:, begin : begin + HEAD]
            low = keep.a[h]
            a = low.astype(F32)
            da = mm(dc, v, 1, 1)
            inner = jnp.sum(a * da, axis=1, keepdims=True)
            ds = (0.125 * a * (da - inner)).astype(BF)
            dq[:, h * HEAD : (h + 1) * HEAD] = mm(ds, k, 1, 0).astype(BF)
            dk = mm(ds, q, 0, 0).astype(BF).reshape(2, tok, HEAD)
            dv = mm(low, dc, 0, 0).astype(BF).reshape(2, tok, HEAD)
            dkv[:, :, h * HEAD : (h + 1) * HEAD] = dk
            dkv[:, :, sizes.hc + h * HEAD : sizes.hc + (h + 1) * HEAD] = dv

    def block(at, which, b):
        sizes = layers[at]
        w = weights[at][which, b * sizes.zb : (b + 1) * sizes.zb]
        return w.reshape(model, model)

    def up(at, side):
        sizes, keep = layers[at], kept[at]
        for b in range(sizes.nl // model):
            cols = slice(b * model, (b + 1) * model)
            u = mm(keep.hb[side], block(at, 0, b), 1, 1) + vecs[at].b1[b]
            phi = 0.5 * (1.0 + lax.erf(u * 0.7071067811865476))
            keep.g[side, :, cols] = (u * phi).astype(BF)
            density = jnp.exp(u * u * -0.5) * 0.3989422804014327
            keep.gp[side, :, cols] = (phi + u * density).astype(BF)

    def times_block(at, which, side):
        sizes, keep = layers[at], kept[at]
        total = None
        for b in range(sizes.nl // model):
            term = mm(keep.g[side, :, b * model : (b + 1) * model], block(at, which, b), 1, 0)
            total = term if total is None else total + term
        return total

    def weight_grad(at, which, right):
        sizes, keep = layers[at], kept[at]
        span = model // 2
        zb = sizes.zb // 2
        rows = sizes.sides * tok
        wide = right[...].reshape(rows, model)
        for b in range(sizes.nl // span):
            left = keep.g[:, :, b * span : (b + 1) * span].reshape(rows, span)
            value = mm(left, wide, 0, 0).astype(BF)
            keep.dw[which, b * zb : (b + 1) * zb] = value.reshape(zb, 2, sizes.nr, model)


    def pack_a(at):
        sizes, width = layers[at], 2 * layers[at].hc
        rows_in = lay[at].pai[...].astype(F32)
        rows_out = lay[at].pao[...].astype(F32)
        halves = []
        for h in range(2):
            own = slice(h * sizes.hc, (h + 1) * sizes.hc)
            pieces = [rows_in[:, p * width : (p + 1) * width][:, own] for p in (1, 2, 0)]
            halves.append(jnp.concatenate(pieces + [rows_out[:, own]], axis=1))
        send = lay[at].asend
        send[...] = jnp.where(c == 0, halves[1], halves[0])
        if at == 0:
            pl.semaphore_wait(bar, PARTNERS)
        push(send, lay[at].ar, r.is_.at[2 * at], r.ir.at[2 * at], sib)
        return jnp.where(c == 0, halves[0], halves[1])

    def pack_f(at):
        sizes = layers[at]
        first = lay[at].pfi[...].astype(F32).T
        second = lay[at].pfo[...].astype(F32)
        if dims.turned[at]:
            second = second.T
        send, own = lay[at].fsend, []
        for which, value in enumerate((first, second)):
            low_half, high_half = value[: sizes.nr], value[sizes.nr :]
            own.append(jnp.where(c == 0, low_half, high_half))
            send[which] = jnp.where(c == 0, high_half, low_half).astype(BF)
        push(send, lay[at].fr, r.is_.at[2 * at + 1], r.ir.at[2 * at + 1], sib)
        return own

    def prepare_a(at, own):
        land, blocks = lay[at].ar, lay[at].ga
        arrived(land, r.ir.at[2 * at], r.is_.at[2 * at])
        other = land[...]
        pair = [jnp.where(c == 0, own, other), jnp.where(c == 0, other, own)]
        blocks[y, z, x] = jnp.concatenate(pair, axis=0).astype(BF)

    def prepare_f(at, own):
        land = lay[at].fr
        arrived(land, r.ir.at[2 * at + 1], r.is_.at[2 * at + 1])
        lanes = pl.ds(pl.multiple_of(y * half_lanes, 128), half_lanes)
        for which in range(2):
            other = land[which].astype(F32)
            pair = [jnp.where(c == 0, own[which], other), jnp.where(c == 0, other, own[which])]
            weights[at][which, z_own if layers[at].pair else z, x, :, lanes] = jnp.concatenate(pair, axis=1).astype(BF)

    group = dims.group
    per_row = model // group
    index = dp * DEPTH * SIDE + mp

    def targets(at_group):
        result, begin = jnp.full_like(at_group, dims.length_row * per_row) + dp, 0
        for at, sizes in enumerate(layers):
            base = dims.base[at] * per_row
            head, count_b = sizes.hc // group, sizes.nr // group
            up_at = dims.rows_of[at].b1 * per_row
            count = dims.shift_groups[at]
            g = index * count + (at_group - begin)
            w = g % (2 * head)
            qv = (w // head) * (2 * head) + (g // (2 * head)) * head + w % head
            b = g - up_at
            up_to = up_at + ((b % (2 * count_b)) // count_b) * (8 * count_b)
            up_to = up_to + (b // (2 * count_b)) * count_b + b % count_b
            place = jnp.where(g < 4 * head, qv, jnp.where((b >= 0) & (b < 16 * count_b), up_to, g))
            inside = (at_group >= begin) & (at_group < begin + count)
            result = jnp.where(inside, base + place, result)
            begin += count
            count = dims.gain_groups[at]
            place = dims.rows_of[at].g1 * per_row + index * count + (at_group - begin)
            inside = (at_group >= begin) & (at_group < begin + count)
            result = jnp.where(inside, base + place, result)
            begin += count
        return result // per_row, result % per_row

    groups = dims.vec_rows
    lane_group = lax.broadcasted_iota(jnp.int32, (groups, dims.lanes), 1) // group
    lane_own = lane_group == lax.broadcasted_iota(jnp.int32, (groups, dims.lanes), 0)

    def place_masks():
        down = lax.broadcasted_iota(jnp.int32, (groups, 1), 0)
        across = lax.broadcasted_iota(jnp.int32, (1, groups), 1)
        row_down, place_down = targets(down)
        row_across, _ = targets(across)
        lane = lax.broadcasted_iota(jnp.int32, (groups, model), 1) // group
        to_row = jnp.where(row_across == down, 1.0, 0.0).astype(BF)
        from_row = jnp.where(row_down == across, 1.0, 0.0).astype(BF)
        return lane == place_down, to_row, from_row

    def pack_vectors():
        lengths = r.len[...].astype(F32).reshape(1, 2) * jnp.where(mp == 0, 1.0, 0.0)
        high = jnp.floor(lengths * (1.0 / 256.0))
        pieces = []
        for own in lay:
            pieces += [own.psh[...].astype(F32).reshape(1, -1), own.pga[...].astype(F32).reshape(1, -1)]
        pieces += [high, lengths - 256.0 * high]
        used = sum(p.shape[1] for p in pieces)
        values = jnp.concatenate(pieces + [jnp.zeros((1, dims.lanes - used), F32)], axis=1)
        spread_out = jnp.where(lane_own, values, 0.0).astype(BF)
        i = lax.broadcasted_iota(jnp.int32, (dims.lanes, model), 0) % group
        j = lax.broadcasted_iota(jnp.int32, (dims.lanes, model), 1) % group
        r.hot[...] = jnp.where(i == j, 1.0, 0.0).astype(BF)
        in_place, to_row, _ = place_masks()
        wide = jnp.where(in_place, mm(spread_out, r.hot[...], 1, 0), 0.0).astype(BF)
        return mm(to_row, wide, 1, 0)

    def unpack_vectors(values):
        in_place, _, from_row = place_masks()
        total, rest = None, values
        for _ in range(3):
            low_part = rest.astype(BF)
            rest = rest - low_part.astype(F32)
            wide = jnp.where(in_place, mm(from_row, low_part, 1, 0), 0.0).astype(BF)
            term = jnp.where(lane_own, mm(wide, r.hot[...], 1, 1), 0.0)
            total = term if total is None else total + term
        return rowsum(total)

    vecs = []
    block_shape = (4, tok // 4, model)

    def tokens(at, side):
        return kept[at].xb[side].reshape(tok, model)

    def project_kv(at, side):
        sizes, keep = layers[at], kept[at]
        kv = mm(tokens(at, side), wa[at][:, : 2 * sizes.hc], 1, 0)
        keep.kv[side, :, : sizes.hc] = kv[:, : sizes.hc].astype(BF)
        keep.kv[side, :, sizes.hc :] = (kv[:, sizes.hc :] + vecs[at].bv).astype(BF)

    def project_q(at):
        sizes, keep = layers[at], kept[at]
        q = mm(tokens(at, half), wa[at][:, 2 * sizes.hc : 2 * sizes.hc + sizes.qw], 1, 0)
        keep.q[...] = (q[:, : sizes.hc] + vecs[at].bq).astype(BF)

    def attend_out(at):
        return mm(kept[at].ctx[...], wa[at][:, layers[at].start :], 1, 1)

    def norm_one(at, base, branch):
        keep, v = kept[at], vecs[at]
        normed, scale = normalize(base + branch + v.bo)
        keep.n1[...] = normed
        keep.s1[...] = scale
        result = normed * v.g1 + v.beta1
        keep.hb[half if layers[at].pair else 0] = result.astype(BF)
        return result

    def norm_two(at, base, branch):
        keep, v = kept[at], vecs[at]
        normed, scale = normalize(base + branch + v.b2)
        keep.n2[...] = normed
        keep.s2[...] = scale
        return normed * v.g2 + v.beta2

    if layers[1].pad:
        kept[1].ctx[...] = jnp.zeros_like(kept[1].ctx)
        lay[1].dq[...] = jnp.zeros_like(lay[1].dq)
    for copy in fetched[:2]:
        copy.wait()
    own_a0 = pack_a(0)
    fetched[2].wait()
    spread(r.hid, kept[0].xb.at[lax.rem(z // 2, 2)], r.hs, r.hr)
    for copy in fetched[3:5]:
        copy.wait()
    own_f0 = pack_f(0)
    prepare_f(0, own_f0)
    gather(2, 0)
    spread_turn(r.hid, kept[0].xb.at[half], r.hs, r.hr, r.os.at[0], r.os.at[1])
    for copy in fetched[5:]:
        copy.wait()
    r.vw[0] = pack_vectors()
    own_a1 = pack_a(1)
    spread_end(kept[0].xb.at[half], r.os.at[0], r.os.at[1])
    gather(3, 0)
    prepare_a(0, own_a0)
    share_hid = Share(kept[0].xb, 2)
    total_step(r.vw, r.vl, 0, r.vs, r.vr)
    gather(2, 1)
    gather(0, 0)
    total_add(r.vw, r.vl, 0, r.vs, r.vr)
    gather(1, 0)
    gather(2, 2)
    total_step(r.vw, r.vl, 1, r.vs, r.vr)
    gather(0, 1)
    gather(3, 1)
    total_add(r.vw, r.vl, 1, r.vs, r.vr)
    own_f1 = pack_f(1)
    prepare_f(1, own_f1)
    gather(1, 1)
    total_step(r.vw, r.vl, 2, r.vs, r.vr)
    prepare_a(1, own_a1)
    share_hid.turn()
    gather(0, 2)
    total_add(r.vw, r.vl, 2, r.vs, r.vr)
    total_step(r.vw, r.vl, 3, r.vs, r.vr)
    share_hid.end()
    gather(4, 0)
    gather(1, 2)
    gather(6, 0)
    gather(2, 3)
    gather(0, 3)
    total_add(r.vw, r.vl, 3, r.vs, r.vr)
    total_step(r.vw, r.vl, 4, r.vs, r.vr)
    gather(1, 3)
    gather(6, 1)
    total_add(r.vw, r.vl, 4, r.vs, r.vr)
    vecs.extend([layer_vecs(0), layer_vecs(1)])
    gather(0, 4)
    gather(4, 1)
    order_rows(0, 0)
    project_kv(0, half)
    gather(3, 2)
    gather(6, 2)
    project_kv(0, 1 - half)
    gather(1, 4)
    gather(5, 0)
    order_rows(0, 1)
    project_q(0)
    attention(0)
    branch = exchange(attend_out(0))
    gather(4, 2)
    branch = branch()
    normed = norm_one(0, tokens(0, half).astype(F32), branch)
    share_normed = Share(kept[0].hb, 0)
    gather(3, 3)
    gather(4, 3)
    gather(6, 3)
    spread(r.cot, r.cin, r.cs, r.cr)
    gather(5, 1)
    share_normed.turn()
    up(0, half)
    share_normed.end()
    up(0, 1 - half)
    down = Fold(lambda side, own: times_block(0, 1, side), 0)
    down.keep()
    down.cross()
    gather(5, 2)
    gather(4, 4)
    down.turn()
    branch = down.end()
    middle = norm_two(0, normed, branch)
    kept[1].xb[half] = middle.astype(BF).reshape(block_shape)
    share_middle = Share(kept[1].xb, 3)
    order_rows(1, 0)
    project_kv(1, half)
    project_q(1)
    gather(5, 3)
    gather(6, 4)
    spread_turn(r.cot, r.cin, r.cs, r.cr, r.os.at[2], r.os.at[3])
    share_middle.turn()
    spread_end(r.cin, r.os.at[2], r.os.at[3])
    share_middle.end()
    project_kv(1, 1 - half)
    attention(1)
    branch = exchange(attend_out(1))
    gather(5, 4)
    branch = branch()
    normed = norm_one(1, middle, branch)
    up(1, 0)
    branch = exchange(times_block(1, 1, 0))
    branch = branch()
    final = norm_two(1, normed, branch)
    r.oblk[...] = final.astype(BF).reshape(r.oblk.shape)
    collect(r.oblk, r.oland, r.ys, r.yr)
    wait_sent()

    r.vw[0] = jnp.zeros_like(r.vw[0])
    once = jnp.where(c == 0, 1.0, 0.0)

    def put_vec(at, name, value):
        row = dims.base[at] + getattr(dims.rows_of[at], name)
        r.vw[0, row : row + 1, :] = value * once

    def back_two(at, grad):
        keep, v = kept[at], vecs[at]
        n2 = keep.n2[...]
        put_vec(at, "g2", rowsum(grad * n2))
        put_vec(at, "beta2", rowsum(grad))
        dz2 = normalize_back(grad * v.g2, n2, keep.s2[...])
        low_dz2 = dz2.astype(BF)
        keep.eo[half if layers[at].pair else 0] = low_dz2
        put_vec(at, "b2", rowsum(low_dz2.astype(F32)))
        return dz2

    def back_up(at):
        sizes, keep = layers[at], kept[at]
        base = dims.base[at] + dims.rows_of[at].b1
        span, sums = sizes.nc // model, []
        for b in range(sizes.nl // model):
            cols = slice(b * model, (b + 1) * model)
            total = None
            for side in range(sizes.sides):
                dg = mm(keep.eo[side], block(at, 1, b), 1, 1)
                du = (dg * keep.gp[side, :, cols].astype(F32)).astype(BF)
                keep.g[side, :, cols] = du
                term = rowsum(du.astype(F32))
                total = term if total is None else total + term
            sums.append(total)
        if sizes.pair:
            cut = 2 * sizes.nr
            blank = jnp.zeros((1, cut), F32)
            pieces = [sums[0][:, b * cut : (b + 1) * cut] for b in range(span)]
            sums = [
                jnp.concatenate([jnp.where(half == 0, p, blank), jnp.where(half == 0, blank, p)], axis=1)
                for p in pieces
            ]
        for b, total in enumerate(sums):
            r.vw[0, pl.ds(base + c * span + b, 1), :] = total

    def back_one(at, grad):
        keep, v = kept[at], vecs[at]
        n1 = keep.n1[...]
        put_vec(at, "g1", rowsum(grad * n1))
        put_vec(at, "beta1", rowsum(grad))
        dz1 = normalize_back(grad * v.g1, n1, keep.s1[...])
        r.eo[...] = dz1.astype(BF)
        put_vec(at, "bo", rowsum(r.eo[...].astype(F32)))
        grad_ctx = mm(r.eo[...], wa[at][:, layers[at].start :], 1, 0).astype(BF)
        return dz1, grad_ctx

    def bias_sums(at):
        sizes, dkv, dq = layers[at], lay[at].dkv, lay[at].dq
        qsum = rowsum(dq[:, : sizes.hc].astype(F32))
        vsum = rowsum(dkv[:, :, sizes.hc :].reshape(seq, sizes.hc).astype(F32))
        both = jnp.concatenate([qsum, vsum], axis=1)
        row = dims.base[at] + dims.rows_of[at].qv
        if 2 * sizes.hc == model:
            r.vw[0, pl.ds(row + c, 1), :] = both
        else:
            blank = jnp.zeros_like(both)
            left, right = jnp.where(c == 0, both, blank), jnp.where(c == 0, blank, both)
            r.vw[0, row : row + 1, :] = jnp.concatenate([left, right], axis=1)

    def projection_grad(at, part):
        sizes, keep = layers[at], kept[at]
        begin, end = part * model, (part + 1) * model
        for y_at in range(SIDE):
            rows = slice(y_at * half_lanes, (y_at + 1) * half_lanes)
            pieces = []
            if begin == 0:
                every_token = keep.xb[:, :, :, rows].reshape(seq, half_lanes)
                grads = keep.dkv[...].reshape(seq, 2 * sizes.hc)
                pieces.append(mm(every_token, grads, 0, 0))
            if end > 2 * sizes.hc:
                own = keep.xb[half, :, :, rows].reshape(tok, half_lanes)
                query = mm(own, keep.dq[...], 0, 0)
                output = mm(r.eo[:, rows], keep.ctx[...], 0, 0)
                if sizes.pad:
                    apart = sizes.start - 2 * sizes.hc
                    pieces += [query[:, :apart], query[:, apart:] + output]
                else:
                    pieces += [query, output]
            value = pieces[0] if len(pieces) == 1 else jnp.concatenate(pieces, axis=1)
            store_grad_rows(at, y_at, value, slice(begin, end))

    def back_hidden(at, side, own):
        sizes, keep = layers[at], kept[at]
        total = mm(keep.dkv[side], wa[at][:, : 2 * sizes.hc], 1, 1)
        if own:
            begin = 2 * sizes.hc
            total = total + mm(keep.dq[...], wa[at][:, begin : begin + keep.dq.shape[1]], 1, 1)
        return total

    grad = r.cin[...].reshape(tok, model).astype(F32)
    dz2 = back_two(1, grad)
    weight_grad(1, 1, kept[1].eo)
    reduce(6, 0)
    back_up(1)
    branch = exchange(times_block(1, 0, 0))
    branch = branch()
    dz1, grad_ctx = back_one(1, dz2 + branch)
    attention_back(1, grad_ctx)
    reduce(6, 1)
    down = Fold(lambda side, own: back_hidden(1, side, own), 2)
    down.keep()
    down.cross()
    projection_grad(1, 0)
    bias_sums(1)
    reduce(4, 0)
    weight_grad(1, 0, kept[1].hb)
    down.turn()
    reduce(5, 0)
    branch = down.end()
    dz2 = back_two(0, dz1 + branch)
    share_grad = Share(kept[0].eo, 1)
    reduce(4, 1)
    reduce(5, 1)
    share_grad.turn()
    share_grad.end()
    weight_grad(0, 1, kept[0].eo)
    reduce(3, 0)
    back_up(0)
    up_back = Fold(lambda side, own: times_block(0, 0, side), 1)
    weight_grad(0, 0, kept[0].hb)
    reduce(2, 0)
    up_back.keep()
    up_back.cross()
    reduce(6, 2)
    reduce(4, 2)
    reduce(5, 2)
    reduce(3, 1)
    up_back.turn()
    collect_done(r.oblk, r.oland, r.ys, r.yr)
    store(r.oland, outs.out)
    branch = up_back.end()
    reduce(2, 1)
    dz1, grad_ctx = back_one(0, dz2 + branch)
    attention_back(0, grad_ctx)
    reduce(3, 2)
    to_hidden = Fold(lambda side, own: back_hidden(0, side, own), 3)
    projection_grad(0, 1)
    reduce(1, 0)
    to_hidden.keep()
    to_hidden.cross()
    reduce(5, 3)
    reduce(2, 2)
    reduce(4, 3)
    projection_grad(0, 0)
    bias_sums(0)
    reduce(0, 0)
    total_step(r.vw, r.vl, 0, r.ws, r.wr)
    total_add(r.vw, r.vl, 0, r.ws, r.wr)
    reduce(1, 1)
    total_step(r.vw, r.vl, 1, r.ws, r.wr)
    reduce(6, 3)
    reduce(5, 4)
    reduce(1, 2)
    reduce(0, 1)
    total_add(r.vw, r.vl, 1, r.ws, r.wr)
    total_step(r.vw, r.vl, 2, r.ws, r.wr)
    to_hidden.turn()
    reduce(3, 3)
    total_add(r.vw, r.vl, 2, r.ws, r.wr)
    reduce(4, 4)
    reduce_out(3)
    total_step(r.vw, r.vl, 3, r.ws, r.wr)
    branch = to_hidden.end()
    reduce(6, 4)
    reduce(2, 3)
    reduce(1, 3)
    reduce(0, 2)
    reduce_out(5)
    total_add(r.vw, r.vl, 3, r.ws, r.wr)
    reduce(1, 4)
    reduce(0, 3)
    reduce_out(2)
    total_step(r.vw, r.vl, 4, r.ws, r.wr)
    reduce(0, 4)
    reduce_out(1)
    reduce_out(6)
    reduce_out(4)
    r.gblk[...] = (dz1 + branch).astype(BF).reshape(r.gblk.shape)
    collect(r.gblk, r.gland, r.zs, r.zr)
    reduce_out(0)
    total_add(r.vw, r.vl, 4, r.ws, r.wr)
    r.dvec[...] = unpack_vectors(r.vw[5])
    store(r.dvec, outs.dvec)
    collect_done(r.gblk, r.gland, r.zs, r.zr)
    store(r.gland, outs.gh)
    wait_sent()
    for copy in stored:
        copy.wait()


def fused_call(hid, cot, lengths, params, dims):
    model, tok, seq = dims.model, dims.tok, dims.seq
    block = (4, tok // 4, model)
    vmem = pltpu.VMEM
    dma = pltpu.SemaphoreType.DMA
    rows_in = params[0][0].shape[0]
    shape = jax.ShapeDtypeStruct
    given = dict(hid=hid, cot=cot, len=lengths, lay=[])
    outs = dict(out=shape(hid.shape, BF), gh=shape(hid.shape, BF), lay=[], dvec=shape((1, dims.lanes), F32))
    for (ai, ao, fi, fo, sh, ga), sizes in zip(params, dims.layers):
        given["lay"].append(dict(pai=ai, pao=ao, pfi=fi, pfo=fo, psh=sh, pga=ga))
        outs["lay"].append(
            dict(
                da=shape((2, rows_in, sizes.wide), F32),
                df=shape((2, 2, sizes.nr, model // 4), F32),
            )
        )
    as_scratch = lambda tree: jax.tree.map(lambda v: vmem(v.shape, v.dtype), tree)
    held, made = as_scratch(given), as_scratch({key: outs[key] for key in ("lay", "dvec")})
    vec = (dims.vec_rows, model)
    rows_a = 2 * rows_in
    counts = [sum(chunk[0] == kind for chunk in dims.chunks) for kind in "AFP"]
    half = model // 2
    n = len(dims.chunks)
    scratch = dict(
        cin=vmem(block, BF),
        oblk=vmem(block, BF),
        gblk=vmem(block, BF),
        oland=vmem(hid.shape, BF),
        gland=vmem(hid.shape, BF),
        vw=vmem((6,) + vec, F32),
        vl=vmem((5,) + vec, F32),
        xs=vmem((2, tok, model), BF),
        xr=vmem((2, tok, model), BF),
        eo=vmem((tok, model), BF),
        px=vmem((4, tok, model), BF),
        prx=vmem((4, tok // 2, model), BF),
        pz=vmem((4, tok // 2, model), BF),
        pzr=vmem((4, 2, tok // 2, model), BF),
        ps=dma((4, 5)),
        pr=dma((4, 5)),
        hot=vmem((dims.lanes, model), BF),
        gs=dma((n, 20)),
        gr=dma((n, 20)),
        ss=dma((n, 20)),
        sr=dma((n, 20)),
        fs=dma((n,)),
        fr=dma((n,)),
        vs=dma((5,)),
        vr=dma((5,)),
        ws=dma((5,)),
        wr=dma((5,)),
        hs=dma((4,)),
        hr=dma((4,)),
        cs=dma((4,)),
        cr=dma((4,)),
        ys=dma((4,)),
        yr=dma((4,)),
        zs=dma((4,)),
        zr=dma((4,)),
        is_=dma((4,)),
        ir=dma((4,)),
        os=dma((4,)),
        es=dma((2,)),
        er=dma((2,)),
        ins=dma((16,)),
        outs=dma((10,)),
        red=[],
        lay=[],
    )
    rows_f, rows_p = dims.unit_rows["F"], dims.unit_rows["P"]
    for count, rows, wide, pair, shard in (
        (counts[0], rows_a - 32, model, (2, 4, 16, model), (rows_in, model)),
        (counts[1], rows_f - 32, half, (4, 16, model), (rows_f, half // 2)),
    ):
        line = pair[:-3] + (1, 16, model)
        scratch["red"].append(
            dict(
                ad=vmem((count, 2, 2, rows, wide), BF),
                an=vmem((count, 2, 4, rows, wide), BF),
                az=vmem((count, 4, 1, rows, wide), BF),
                by=vmem((count, 4, 2, 16, wide), BF),
                bz=vmem((count, 4, 1, 2, 16, wide), BF),
                bx=vmem((count, 1, 16, wide), BF),
                cx=vmem((count,) + pair, BF),
                cz=vmem((count, 4) + line, BF),
                cy=vmem((count, 1, 16, wide), BF),
                fsend=vmem((count,) + shard, F32),
                fland=vmem((count,) + shard, F32),
            )
        )
    scratch["red"].append(
        dict(
            ad=vmem((counts[2], 2, 1, rows_p, half), BF),
            an=vmem((counts[2], 2, 2, rows_p, half), BF),
            az=vmem((counts[2], 1, rows_p, half), BF),
            fsend=vmem((counts[2], rows_p, half // 2), F32),
            fland=vmem((counts[2], rows_p, half // 2), F32),
        )
    )
    for sizes in dims.layers:
        scratch["lay"].append(
            dict(
                ar=vmem((rows_in, sizes.wide), F32),
                asend=vmem((rows_in, sizes.wide), F32),
                fr=vmem((2, sizes.nr, model // 4), BF),
                fsend=vmem((2, sizes.nr, model // 4), BF),
                ga=vmem((SIDE, DEPTH, SIDE, rows_a, sizes.wide), BF),
                wa=vmem((model, sizes.wide), BF),
                w=vmem((2, sizes.zs, SIDE, sizes.nr, model), BF),
                dw=vmem((2, sizes.zs, SIDE, sizes.nr, model), BF),
                xb=vmem((2,) + block, BF),
                q=vmem((tok, sizes.hc), BF),
                kv=vmem((2, tok, 2 * sizes.hc), BF),
                a=vmem((sizes.heads, tok, seq), BF),
                ctx=vmem((tok, sizes.wide - sizes.start), BF),
                n1=vmem((tok, model), F32),
                s1=vmem((tok, 1), F32),
                hb=vmem((sizes.sides, tok, model), BF),
                eo=vmem((sizes.sides, tok, model), BF),
                g=vmem((sizes.sides, tok, sizes.nl), BF),
                gp=vmem((sizes.sides, tok, sizes.nl), BF),
                n2=vmem((tok, model), F32),
                s2=vmem((tok, 1), F32),
                dkv=vmem((2, tok, 2 * sizes.hc), BF),
                dq=vmem((tok, 2 * sizes.hc if sizes.pad else sizes.hc), BF),
            )
        )
    inputs, outputs = jax.tree.leaves(given), jax.tree.leaves(outs)
    whole = pl.BlockSpec(memory_space=pl.ANY)
    local = (scratch, held, made)
    values = pl.pallas_call(
        functools.partial(fused_kernel, dims, jax.tree.structure((given, outs) + local)),
        out_shape=outputs,
        in_specs=[whole] * len(inputs),
        out_specs=[whole] * len(outputs),
        scratch_shapes=jax.tree.leaves(local),
        compiler_params=pltpu.CompilerParams(
            collective_id=0, has_side_effects=True, vmem_limit_bytes=dims.vmem
        ),
        name="layers",
    )(*inputs)
    return jax.tree.unflatten(jax.tree.structure(outs), values)


def finish_kernel(dims, tree, *refs):
    given, (out, gh, *results) = jax.tree.unflatten(tree, refs)
    r = named(given)
    out[...] = r.out[...]
    gh[...] = r.gh[...].astype(F32)
    begin = 0
    for at, sizes in enumerate(dims.layers):
        attn, ffn = r.lay[at].da, r.lay[at].df
        to_ai, to_ao, to_fi, to_fo, to_sh, to_ga = results[6 * at : 6 * at + 6]
        for p in range(3):
            for h in range(2):
                to = (2 * ((p + 1) % 3) + h) * sizes.hc
                to_ai[:, to : to + sizes.hc] = attn[h, :, p * sizes.hc : (p + 1) * sizes.hc]
        for h in range(2):
            to_ao[:, h * sizes.hc : (h + 1) * sizes.hc] = attn[h, :, 3 * sizes.hc :]
        down = ffn[:, 1].reshape(2 * sizes.nr, ffn.shape[3])
        to_fo[...] = down.T if dims.turned[at] else down
        to_fi[...] = ffn[:, 0].reshape(2 * sizes.nr, ffn.shape[3]).T
        for ref in (to_sh, to_ga):
            ref[...] = r.dvec[0, begin : begin + ref.shape[0]]
            begin += ref.shape[0]


def finish_call(given, params, dims):
    leaves, tree = jax.tree.flatten(given)
    outs = [jax.ShapeDtypeStruct(given["out"].shape, d) for d in (BF, F32)]
    outs += [jax.ShapeDtypeStruct(p.shape, F32) for shards in params for p in shards]
    whole = pl.BlockSpec(memory_space=pltpu.VMEM)
    return pl.pallas_call(
        functools.partial(finish_kernel, dims, jax.tree.structure((given, outs))),
        out_shape=outs,
        in_specs=[whole] * len(leaves),
        out_specs=[whole] * len(outs),
        compiler_params=pltpu.CompilerParams(vmem_limit_bytes=dims.vmem),
        name="finish",
    )(*leaves)


def make_dims(hidden_in, teacher, student):
    model = hidden_in.shape[2]
    layers = [
        layer_sizes(model, p[0].shape[1] // 3, p[2].shape[1] * DEPTH * SIDE, pair)
        for p, pair in ((teacher, True), (student, False))
    ]
    rows = layers[1].nr
    chunks = []
    for at, sizes in enumerate(layers):
        chunks += [("A", at, 0, part) for part in range(sizes.wide // model)]
        for which in (0, 1):
            kind, count = ("P", 1) if sizes.pair else ("F", sizes.nr // rows)
            chunks += [(kind, at, which, part) for part in range(count)]
    counts, slot = {"A": 0, "F": 0, "P": 0}, []
    for chunk in chunks:
        slot.append(counts[chunk[0]])
        counts[chunk[0]] += 1
    group = model // (SIDE * SIDE * DEPTH * SIDE)
    shift_groups = [p[4].shape[0] // group for p in (teacher, student)]
    gain_groups = [p[5].shape[0] // group for p in (teacher, student)]
    rows_of, base, at = [], [], 0
    for sizes in layers:
        found, count = vec_rows(model, sizes)
        rows_of.append(found)
        base.append(at)
        at += count
    return types.SimpleNamespace(
        model=model,
        tok=4 * hidden_in.shape[1],
        seq=8 * hidden_in.shape[1],
        layers=layers,
        chunks=chunks,
        slot=slot,
        rows=rows,
        unit_rows={"A": 2 * teacher[0].shape[0], "F": rows, "P": layers[0].nr},
        rows_of=rows_of,
        base=base,
        length_row=at,
        vec_rows=(at + 8) // 8 * 8,
        turned=[p[3].shape[0] > p[3].shape[1] for p in (teacher, student)],
        group=group,
        lanes=(sum(shift_groups + gain_groups) * group + 4 + 127) // 128 * 128,
        shift_groups=shift_groups,
        gain_groups=gain_groups,
        vmem=63 * 2**20,
    )


def fast_body(hidden_in, cotangent, lengths, *shards):
    params = (shards[:6], shards[6:])
    dims = make_dims(hidden_in, *params)
    turn = lambda shards, turned: (shards[0], shards[1].T, shards[2], shards[3].T if turned else shards[3])
    params = [turn(p, turned) + p[4:] for p, turned in zip(params, dims.turned)]
    values = fused_call(hidden_in, cotangent, lengths, params, dims)
    out, grad_hidden, *grads = finish_call(values, params, dims)
    results = [out, grad_hidden]
    for at, turned in enumerate(dims.turned):
        own = tuple(grads[6 * at : 6 * at + 6])
        results += turn(own, turned) + own[4:]
    return tuple(results)


def body(axes, *args):
    rows, tokens, model = args[0].shape
    pair_fits = args[3 + 2].shape[1] * 2 == model
    fits = pair_fits and axes["dp"] == SIDE * SIDE and axes["mp"] == DEPTH * SIDE
    if fits and rows == 2 and tokens % 16 == 0 and model % 256 == 0:
        return fast_body(*args)
    return general_body(*args)


def general_body(
    hidden_in,
    cotangent,
    lengths,
    teacher_attn_in,
    teacher_attn_out,
    teacher_ffn_in,
    teacher_ffn_out,
    teacher_shifts,
    teacher_gains,
    student_attn_in,
    student_attn_out,
    student_ffn_in,
    student_ffn_out,
    student_shifts,
    student_gains,
):
    span_len = hidden_in.shape[1] * lax.axis_size("mp")
    positions = jnp.arange(span_len)
    valid_keys = positions[None, :] < lengths[:, None]
    teacher = fetch(
        teacher_attn_in,
        teacher_attn_out,
        teacher_ffn_in,
        teacher_ffn_out,
        teacher_shifts,
        teacher_gains,
    )
    student = fetch(
        student_attn_in,
        student_attn_out,
        student_ffn_in,
        student_ffn_out,
        student_shifts,
        student_gains,
    )
    middle, teacher_kept = forward_layer(hidden_in.astype(jnp.float32), teacher, valid_keys)
    final, student_kept = forward_layer(middle, student, valid_keys)
    grad_middle, student_grads = backward_layer(
        cotangent.astype(jnp.float32), student_kept, student, valid_keys
    )
    grad_input, teacher_grads = backward_layer(grad_middle, teacher_kept, teacher, valid_keys)
    teacher_totals = reduce_grads(teacher_grads)
    student_totals = reduce_grads(student_grads)
    return (final.astype(jnp.bfloat16), grad_input) + teacher_totals + student_totals


def solution(mesh):
    in_specs = (
        P("dp", "mp", None),
        P("dp", "mp", None),
        P("dp"),
        P(("dp", "mp"), None),
        P(None, ("dp", "mp")),
        P("dp", "mp"),
        P("mp", "dp"),
        P(("dp", "mp")),
        P(("dp", "mp")),
        P(("dp", "mp"), None),
        P(None, ("dp", "mp")),
        P("dp", "mp"),
        P("mp", "dp"),
        P(("dp", "mp")),
        P(("dp", "mp")),
    )
    out_specs = (
        P("dp", "mp", None),
        P("dp", "mp", None),
        P(("dp", "mp"), None),
        P(None, ("dp", "mp")),
        P("dp", "mp"),
        P("mp", "dp"),
        P(("dp", "mp")),
        P(("dp", "mp")),
        P(("dp", "mp"), None),
        P(None, ("dp", "mp")),
        P("dp", "mp"),
        P("mp", "dp"),
        P(("dp", "mp")),
        P(("dp", "mp")),
    )
    return jax.shard_map(
        functools.partial(body, dict(mesh.shape)), mesh=mesh, in_specs=in_specs, out_specs=out_specs, check_vma=False)
```

```python
import functools
import types

import jax
import jax.numpy as jnp
from jax import lax
from jax.experimental import pallas as pl
from jax.experimental.pallas import tpu as pltpu
from jax.sharding import PartitionSpec as P

HEAD = 64


EPSILON = 1e-06
NEGATIVE = -1e30


def layer_norm(values, gain, shift):
    centered = values - jnp.mean(values, axis=-1, keepdims=True)
    variance = jnp.mean(centered * centered, axis=-1, keepdims=True)
    return centered * lax.rsqrt(variance + EPSILON) * gain + shift


def smooth_gate(pre_act):
    return jax.nn.gelu(pre_act, approximate=False)


def split_shifts(shifts, head_width, model_width, hidden_width):
    spans_list = [
        head_width,
        head_width,
        model_width,
        model_width,
        hidden_width,
        model_width,
        model_width,
    ]
    pieces = []
    offset = 0
    for length in spans_list:
        pieces.append(shifts[offset : offset + length])
        offset = offset + length
    return pieces


def to_heads(values):
    return values.reshape(values.shape[0], values.shape[1], values.shape[2] // HEAD, HEAD)


def score_block(queries, all_keys, valid_keys):
    raw = jnp.einsum(
        "rqhd,rkhd->rhqk", to_heads(queries), to_heads(all_keys), preferred_element_type=jnp.float32
    )
    return jnp.where(valid_keys[:, None, None, :], raw * 0.125, NEGATIVE)


def fetch(attn_in, attn_out, ffn_in, ffn_out, shifts, gains):
    whole_in, whole_out, whole_shifts, whole_gains = (
        lax.all_gather(attn_in, ("dp", "mp"), axis=0, tiled=True),
        lax.all_gather(attn_out, ("dp", "mp"), axis=1, tiled=True),
        lax.all_gather(shifts, ("dp", "mp"), axis=0, tiled=True),
        lax.all_gather(gains, ("dp", "mp"), axis=0, tiled=True),
    )
    ffn_first, ffn_second = (
        lax.all_gather(ffn_in, "dp", axis=0, tiled=True),
        lax.all_gather(ffn_out, "dp", axis=1, tiled=True),
    )
    return (
        whole_in,
        whole_out,
        ffn_first,
        ffn_second,
        whole_shifts.astype(jnp.float32),
        whole_gains.astype(jnp.float32),
    )


def forward_layer(hidden, params, valid_keys):
    attn_in, attn_out, ffn_first, ffn_second, shifts, gains = params
    model_width = hidden.shape[-1]
    head_width = attn_in.shape[1] // 3
    hidden_width = shifts.shape[0] - 2 * head_width - 4 * model_width
    pieces = split_shifts(shifts, head_width, model_width, hidden_width)
    bias_query, bias_value, bias_output, shift_one, bias_up, bias_down, shift_two = pieces
    hidden_low = hidden.astype(jnp.bfloat16)
    projected = jnp.einsum("rsd,de->rse", hidden_low, attn_in, preferred_element_type=jnp.float32)
    queries = (projected[..., :head_width] + bias_query).astype(jnp.bfloat16)
    local_keys = projected[..., head_width : 2 * head_width].astype(jnp.bfloat16)
    local_values = (projected[..., 2 * head_width :] + bias_value).astype(jnp.bfloat16)
    all_keys, all_values = (
        lax.all_gather(local_keys, "mp", axis=1, tiled=True),
        lax.all_gather(local_values, "mp", axis=1, tiled=True),
    )
    scores = score_block(queries, all_keys, valid_keys)
    row_max = jnp.max(scores, axis=-1, keepdims=True)
    exponent = jnp.exp(scores - row_max)
    row_total = jnp.sum(exponent, axis=-1, keepdims=True)
    log_total = row_max + jnp.log(row_total)
    weights_low = (exponent / row_total).astype(jnp.bfloat16)
    mixed = jnp.einsum(
        "rhqk,rkhd->rqhd", weights_low, to_heads(all_values), preferred_element_type=jnp.float32
    )
    context = mixed.reshape(queries.shape).astype(jnp.bfloat16)
    branch = (
        jnp.einsum("rsh,hd->rsd", context, attn_out, preferred_element_type=jnp.float32)
        + bias_output
    )
    summed_one = hidden + branch
    normed_one = layer_norm(summed_one, gains[:model_width], shift_one)
    normed_low = normed_one.astype(jnp.bfloat16)
    ffn_tokens = lax.all_gather(normed_low, "mp", axis=1, tiled=True)
    local_hidden = ffn_first.shape[1]
    bias_part = lax.dynamic_slice_in_dim(bias_up, lax.axis_index("mp") * local_hidden, local_hidden)
    pre_act = (
        jnp.einsum("rsd,df->rsf", ffn_tokens, ffn_first, preferred_element_type=jnp.float32)
        + bias_part
    )
    act_low = smooth_gate(pre_act).astype(jnp.bfloat16)
    down_terms = jnp.einsum("rsf,fd->rsd", act_low, ffn_second, preferred_element_type=jnp.float32)
    ffn_down = lax.psum_scatter(
        down_terms.astype(jnp.bfloat16), "mp", scatter_dimension=1, tiled=True
    ).astype(jnp.float32)
    summed_two = normed_one + ffn_down + bias_down
    result = layer_norm(summed_two, gains[model_width:], shift_two)
    key_store = (all_keys, all_values)
    kept = (
        hidden_low,
        queries,
        key_store,
        log_total,
        context,
        summed_one,
        ffn_tokens,
        pre_act,
        act_low,
        summed_two,
    )
    return (result, kept)


def backward_layer(grad_out, kept, params, valid_keys):
    attn_in, attn_out, ffn_first, ffn_second, shifts, gains = params
    (
        hidden_low,
        queries,
        key_store,
        log_total,
        context,
        summed_one,
        ffn_tokens,
        pre_act,
        act_low,
        summed_two,
    ) = kept
    model_width = summed_one.shape[-1]
    head_width = attn_in.shape[1] // 3
    hidden_width = shifts.shape[0] - 2 * head_width - 4 * model_width
    pieces = split_shifts(shifts, head_width, model_width, hidden_width)
    bias_query, bias_value, bias_output, shift_one, bias_up, bias_down, shift_two = pieces
    sum_axes = (0, 1)
    unused_two, norm_two_back = jax.vjp(layer_norm, summed_two, gains[model_width:], shift_two)
    grad_two, grad_gain_two, grad_shift_two = norm_two_back(grad_out)
    grad_down = grad_two.astype(jnp.bfloat16)
    grad_bias_down = jnp.sum(grad_down.astype(jnp.float32), axis=sum_axes)
    grad_tokens = lax.all_gather(grad_down, "mp", axis=1, tiled=True)
    grad_act = jnp.einsum(
        "rsd,fd->rsf", grad_tokens, ffn_second, preferred_element_type=jnp.float32
    )
    grad_second = jnp.einsum(
        "rsf,rsd->fd", act_low, grad_tokens, preferred_element_type=jnp.float32
    )
    unused_gate, gate_back = jax.vjp(smooth_gate, pre_act)
    grad_pre = gate_back(grad_act)[0].astype(jnp.bfloat16)
    grad_bias_part = jnp.sum(grad_pre.astype(jnp.float32), axis=sum_axes)
    grad_first = jnp.einsum("rsd,rsf->df", ffn_tokens, grad_pre, preferred_element_type=jnp.float32)
    back_terms = jnp.einsum("rsf,df->rsd", grad_pre, ffn_first, preferred_element_type=jnp.float32)
    grad_normed = lax.psum_scatter(
        back_terms.astype(jnp.bfloat16), "mp", scatter_dimension=1, tiled=True
    ).astype(jnp.float32)
    blank_bias = jnp.zeros((hidden_width,), jnp.float32)
    grad_bias_up = lax.dynamic_update_slice_in_dim(
        blank_bias, grad_bias_part, lax.axis_index("mp") * ffn_first.shape[1], 0
    )
    grad_normed = grad_normed + grad_two
    unused_one, norm_one_back = jax.vjp(layer_norm, summed_one, gains[:model_width], shift_one)
    grad_one, grad_gain_one, grad_shift_one = norm_one_back(grad_normed)
    grad_branch = grad_one.astype(jnp.bfloat16)
    grad_bias_output = jnp.sum(grad_branch.astype(jnp.float32), axis=sum_axes)
    grad_attn_out = jnp.einsum(
        "rsh,rsd->hd", context, grad_branch, preferred_element_type=jnp.float32
    )
    grad_context = jnp.einsum(
        "rsd,hd->rsh", grad_branch, attn_out, preferred_element_type=jnp.float32
    ).astype(jnp.bfloat16)
    stored_keys, stored_values = key_store
    all_keys, all_values = (stored_keys, stored_values)
    weights = jnp.exp(score_block(queries, all_keys, valid_keys) - log_total)
    context_heads = to_heads(grad_context)
    grad_weights = jnp.einsum(
        "rqhd,rkhd->rhqk", context_heads, to_heads(all_values), preferred_element_type=jnp.float32
    )
    inner_sum = jnp.sum(weights * grad_weights, axis=-1, keepdims=True)
    grad_raw = (0.125 * weights * (grad_weights - inner_sum)).astype(jnp.bfloat16)
    grad_queries = jnp.einsum(
        "rhqk,rkhd->rqhd", grad_raw, to_heads(all_keys), preferred_element_type=jnp.float32
    )
    grad_queries = grad_queries.reshape(queries.shape).astype(jnp.bfloat16)
    weights_low = weights.astype(jnp.bfloat16)
    value_terms = jnp.einsum(
        "rhqk,rqhd->rkhd", weights_low, context_heads, preferred_element_type=jnp.float32
    )
    key_terms = jnp.einsum(
        "rhqk,rqhd->rkhd", grad_raw, to_heads(queries), preferred_element_type=jnp.float32
    )
    key_terms = key_terms.reshape(all_keys.shape)
    value_terms = value_terms.reshape(all_values.shape)
    grad_keys, grad_values = (
        lax.psum_scatter(
            key_terms.astype(jnp.bfloat16), "mp", scatter_dimension=1, tiled=True
        ).astype(jnp.float32),
        lax.psum_scatter(
            value_terms.astype(jnp.bfloat16), "mp", scatter_dimension=1, tiled=True
        ).astype(jnp.float32),
    )
    grad_values_low = grad_values.astype(jnp.bfloat16)
    grad_projected = jnp.concatenate(
        [grad_queries, grad_keys.astype(jnp.bfloat16), grad_values_low], axis=-1
    )
    grad_attn_in = jnp.einsum(
        "rsd,rse->de", hidden_low, grad_projected, preferred_element_type=jnp.float32
    )
    grad_hidden = grad_one + jnp.einsum(
        "rse,de->rsd", grad_projected, attn_in, preferred_element_type=jnp.float32
    )
    grad_bias_query = jnp.sum(grad_queries.astype(jnp.float32), axis=sum_axes)
    grad_bias_value = jnp.sum(grad_values_low.astype(jnp.float32), axis=sum_axes)
    grad_shifts = jnp.concatenate(
        [
            grad_bias_query,
            grad_bias_value,
            grad_bias_output,
            grad_shift_one,
            grad_bias_up,
            grad_bias_down,
            grad_shift_two,
        ]
    )
    grad_gains = jnp.concatenate([grad_gain_one, grad_gain_two])
    return (
        grad_hidden,
        (grad_attn_in, grad_attn_out, grad_first, grad_second, grad_shifts, grad_gains),
    )


def reduce_grads(grads):
    grad_attn_in, grad_attn_out, grad_first, grad_second, grad_shifts, grad_gains = grads
    total_in, total_out, total_shifts, total_gains = (
        lax.psum_scatter(grad_attn_in, ("dp", "mp"), scatter_dimension=0, tiled=True),
        lax.psum_scatter(grad_attn_out, ("dp", "mp"), scatter_dimension=1, tiled=True),
        lax.psum_scatter(grad_shifts, ("dp", "mp"), scatter_dimension=0, tiled=True),
        lax.psum_scatter(grad_gains, ("dp", "mp"), scatter_dimension=0, tiled=True),
    )
    total_first, total_second = (
        lax.psum_scatter(
            grad_first.astype(jnp.bfloat16), "dp", scatter_dimension=0, tiled=True
        ).astype(jnp.float32),
        lax.psum_scatter(
            grad_second.astype(jnp.bfloat16), "dp", scatter_dimension=1, tiled=True
        ).astype(jnp.float32),
    )
    return (total_in, total_out, total_first, total_second, total_shifts, total_gains)


BF = jnp.bfloat16
F32 = jnp.float32
MESH = pl.DeviceIdType.MESH
SIDE = 2
DEPTH = 4
PARTNERS = 9


def mm(left, right, left_dim, right_dim):
    return lax.dot_general(
        left, right, (((left_dim,), (right_dim,)), ((), ())), preferred_element_type=F32
    )


def rowsum(values):
    return jnp.sum(values, axis=0, keepdims=True)


def normalize(values):
    centered = values - jnp.mean(values, axis=-1, keepdims=True)
    variance = jnp.mean(centered * centered, axis=-1, keepdims=True)
    scale = lax.rsqrt(variance + EPSILON)
    return centered * scale, scale


def normalize_back(grad, normed, scale):
    along = jnp.mean(grad * normed, axis=-1, keepdims=True)
    return scale * (grad - jnp.mean(grad, axis=-1, keepdims=True) - normed * along)


def layer_sizes(model, heads_width, hidden, pair):
    half = heads_width // 2
    start = 3 * half // 128 * 128
    return types.SimpleNamespace(
        hc=half,
        heads=half // HEAD,
        wide=4 * half,
        start=start,
        qw=-(-half // 128) * 128,
        pad=3 * half - start,
        nr=hidden // 16,
        nc=hidden // 2,
        nl=hidden // 4 if pair else hidden // 2,
        pair=pair,
        sides=2 if pair else 1,
        zs=2 if pair else DEPTH,
        zb=model * 8 // hidden,
    )


def vec_rows(model, sizes):
    lengths = dict(
        qv=4 * sizes.hc, bo=model, beta1=model, b1=2 * sizes.nc, b2=model, beta2=model, g1=model, g2=model
    )
    rows, at = {}, 0
    for name, length in lengths.items():
        rows[name] = at
        at += length // model
    return types.SimpleNamespace(**rows), at


def named(tree):
    if isinstance(tree, dict):
        return types.SimpleNamespace(**{key: named(value) for key, value in tree.items()})
    return [named(value) for value in tree] if isinstance(tree, list) else tree


def fused_kernel(dims, tree, *refs):
    given, outs, scratch, held, made = jax.tree.unflatten(tree, refs)
    lay = [named(a | b | d) for a, b, d in zip(held["lay"], made["lay"], scratch["lay"])]
    r = named(held | made | scratch)
    given, outs = named(given), named(outs)

    def fetch_copies():
        pairs = []
        for at in range(2):
            far, near = given.lay[at], lay[at]
            pairs += [(far.pai, near.pai), (far.pao, near.pao)]
            if at == 0:
                pairs += [(given.hid, r.hid)]
            pairs += [(far.pfi, near.pfi), (far.pfo, near.pfo), (far.psh, near.psh), (far.pga, near.pga)]
        pairs += [(given.len, r.len), (given.cot, r.cot)]
        return [pltpu.make_async_copy(src, dst, r.ins.at[i]) for i, (src, dst) in enumerate(pairs)]

    fetched = fetch_copies()
    for copy in fetched:
        copy.start()
    stored = []

    def store(src, dst):
        copy = pltpu.make_async_copy(src, dst, r.outs.at[len(stored)])
        copy.start()
        stored.append(copy)
    model, tok, seq, layers = dims.model, dims.tok, dims.seq, dims.layers
    half_lanes = model // 2
    dp, mp = lax.axis_index("dp"), lax.axis_index("mp")
    y, c = dp // SIDE, lax.rem(dp, SIDE)
    z, x = mp // SIDE, lax.rem(mp, SIDE)

    def device(c, x, y, z):
        return {"dp": y * SIDE + c, "mp": z * SIDE + x}

    sib = device(1 - c, x, y, z)
    xn, yn = device(c, 1 - x, y, z), device(c, x, 1 - y, z)
    zdev = [device(c, x, y, lax.rem(z + d, DEPTH)) for d in range(1, DEPTH)]
    zpair = z + 1 - 2 * lax.rem(z, 2)
    zn = device(c, x, y, zpair)
    zfar = device(c, x, y, lax.rem(z + 2, DEPTH))

    bar = pltpu.get_barrier_semaphore()
    for step in range(1, DEPTH * SIDE):
        other = lax.rem(mp + step, DEPTH * SIDE)
        pl.semaphore_signal(bar, inc=1, device_id={"dp": dp, "mp": other}, device_id_type=MESH)
    pl.semaphore_signal(bar, inc=1, device_id=sib, device_id_type=MESH)
    pl.semaphore_signal(bar, inc=1, device_id=yn, device_id_type=MESH)

    sent = []

    def remote(src, dst, send, recv, dev):
        return pltpu.make_async_remote_copy(
            src_ref=src, dst_ref=dst, send_sem=send, recv_sem=recv, device_id=dev, device_id_type=MESH
        )

    def push(src, dst, send, recv, dev):
        copy = remote(src, dst, send, recv, dev)
        copy.start()
        sent.append((None, copy))

    def arrived(dst, recv, send):
        remote(dst, dst, send, recv, sib).wait_recv()

    row_core = z // 2
    mine = c == row_core
    half = lax.rem(z, 2)

    def spread(src, land, sends, recvs):
        block = 2 * lax.rem(z, 2) + x
        target = 2 * c + z // 2
        for j in range(2):
            local = (x == j) & (z == target)
            copy = remote(src.at[j], land.at[block], sends.at[j], recvs.at[block], device(c, j, y, target))
            pl.when(local)(pltpu.make_async_copy(src.at[j], land.at[block], recvs.at[block]).start)
            pl.when(jnp.logical_not(local))(copy.start)

    def spread_turn(src, land, sends, recvs, on_chip_send, on_chip_recv):
        target = 2 * c + z // 2
        for j in range(2):
            local = (x == j) & (z == target)
            copy = remote(src.at[j], land.at[0], sends.at[j], recvs.at[0], sib)
            pl.when(jnp.logical_not(local))(copy.wait_send)
        whole = remote(land, land, on_chip_send, on_chip_recv, sib)

        @pl.when(mine)
        def _():
            for block in range(4):
                arrived(land.at[block], recvs.at[block], sends.at[0])
            whole.start()

    def spread_end(land, on_chip_send, on_chip_recv):
        whole = remote(land, land, on_chip_send, on_chip_recv, sib)
        pl.when(mine)(whole.wait_send)
        pl.when(jnp.logical_not(mine))(whole.wait_recv)

    def collect(src, land, sends, recvs):
        @pl.when(mine)
        def _():
            for block in range(4):
                z_to, x_to = 2 * half + block // 2, block % 2
                local = (x == x_to) & (z == z_to)
                slot = land.at[x]
                copy = remote(
                    src.at[block], slot, sends.at[block], recvs.at[x], device(c, x_to, y, z_to)
                )
                pl.when(local)(pltpu.make_async_copy(src.at[block], slot, recvs.at[x]).start)
                pl.when(jnp.logical_not(local))(copy.start)

    def collect_done(src, land, sends, recvs):
        for j in range(2):
            arrived(land.at[j], recvs.at[j], sends.at[0])

        @pl.when(mine)
        def _():
            for block in range(4):
                z_to, x_to = 2 * half + block // 2, block % 2
                local = (x == x_to) & (z == z_to)
                copy = remote(src.at[block], src.at[block], sends.at[block], recvs.at[0], sib)
                pl.when(jnp.logical_not(local))(copy.wait_send)

    chunks = dims.chunks
    every, first, second = pl.ds(0, DEPTH), pl.ds(0, 2), pl.ds(2, 2)
    both = pl.ds(0, 2)

    def view(i, grads, band, z_slice, x_at, y_at):
        kind, layer, which, part = chunks[i]
        full = dims.unit_rows[kind]
        if kind == "P":
            ref = lay[layer].dw if grads else lay[layer].w
            lanes = pl.ds(pl.multiple_of(y_at * half_lanes, 128), half_lanes)
            return ref.at[which, z_slice, x_at, :, lanes]
        if grads:
            begin, count = {"a": (0, full - 32), "b": (full - 32, 16), "c": (full - 16, 16)}[band]
        else:
            begin, count = 0, full
        if kind == "A":
            ref = lay[layer].ga
            y_pick = both if y_at is None else y_at
            return ref.at[y_pick, z_slice, x_at, pl.ds(begin, count), pl.ds(part * model, model)]
        ref = lay[layer].dw if grads else lay[layer].w
        lanes = pl.ds(0, model)
        if y_at is not None:
            lanes = pl.ds(pl.multiple_of(y_at * half_lanes, 128), half_lanes)
        return ref.at[which, z_slice, x_at, pl.ds(part * full + begin, count), lanes]

    UP, DOWN, FAR, RELAY = range(4)
    z_far = lax.rem(z + 2, DEPTH)
    z_up, z_down = lax.rem(z + 1, DEPTH), lax.rem(z + DEPTH - 1, DEPTH)
    z_end = DEPTH - 1 - z
    has_up, has_down = z < DEPTH - 1, z > 0
    inner = (z == 1) | (z == 2)
    outer = (z == 0) | (z == 3)
    z_out = jnp.where(z == 1, 0, 3)
    z_in = jnp.where(z == 0, 1, 2)

    def push_if(cond, src, dst, send, recv, dev):
        copy = remote(src, dst, send, recv, dev)
        pl.when(cond)(copy.start)
        sent.append((cond, copy))

    def wait_sent():
        for cond, copy in sent:
            if cond is None:
                copy.wait_send()
            else:
                pl.when(cond)(copy.wait_send)
        sent.clear()

    def arrived_if(cond, dst, recv, send):
        pl.when(cond)(remote(dst, dst, send, recv, sib).wait_recv)

    def at_z(zz):
        return device(c, x, y, zz)

    def line_send(part, send, recv):
        own = part(z)
        push_if(has_up, own, own, send(UP), recv(UP), at_z(z_up))
        push_if(has_down, own, own, send(DOWN), recv(DOWN), at_z(z_down))
        push(own, own, send(FAR), recv(FAR), at_z(z_far))

    def line_relay(part, send, recv):
        far = part(z_far)
        arrived_if(inner, far, recv(FAR), send(FAR))
        push_if(inner, far, far, send(RELAY), recv(RELAY), at_z(z_out))

    def line_end(part, send, recv):
        arrived_if(has_down, part(z_down), recv(UP), send(UP))
        arrived_if(has_up, part(z_up), recv(DOWN), send(DOWN))
        arrived_if(outer, part(z_far), recv(FAR), send(FAR))
        arrived_if(outer, part(z_end), recv(RELAY), send(RELAY))

    def sems(ref_send, ref_recv, i, base):
        return (lambda k: ref_send.at[i, base + k]), (lambda k: ref_recv.at[i, base + k])

    def one(zz):
        return pl.ds(zz, 1)

    def parts_of(i, grads):
        return (
            lambda zz: view(i, grads, "a", one(zz), x, y),
            lambda zz: view(i, grads, "b", one(zz), both, y),
            lambda zz: view(i, grads, "c", one(zz), x, None),
        )

    def gather_sems(i, base):
        return sems(r.gs, r.gr, i, base)

    def gather_push(i, k, piece, dev):
        push(piece, piece, r.gs.at[i, k], r.gr.at[i, k], dev)

    def gather_wait(i, k, piece):
        arrived(piece, r.gr.at[i, k], r.gs.at[i, k])

    z_own, z_other = z // 2, 1 - z // 2

    def pair_view(i, grads, z_slice, x_at, y_at):
        return view(i, grads, None, z_slice, x_at, y_at)

    def pair_0(i):
        gather_push(i, 0, pair_view(i, False, one(z_own), x, y), zfar)

    def pair_1(i):
        gather_wait(i, 0, pair_view(i, False, one(z_other), x, y))
        own = pair_view(i, False, both, x, y)
        gather_push(i, 1, own, xn)
        gather_push(i, 2, own, yn)

    def pair_2(i):
        gather_wait(i, 1, pair_view(i, False, both, 1 - x, y))
        gather_wait(i, 2, pair_view(i, False, both, x, 1 - y))
        gather_push(i, 3, pair_view(i, False, one(0), x, 1 - y), xn)
        gather_push(i, 4, pair_view(i, False, one(1), 1 - x, y), yn)

    def pair_3(i):
        gather_wait(i, 3, pair_view(i, False, one(0), 1 - x, 1 - y))
        gather_wait(i, 4, pair_view(i, False, one(1), 1 - x, 1 - y))

    def whole(i, z_slice, x_at, y_at):
        return view(i, False, None, z_slice, x_at, y_at)

    def line(i):
        return (lambda zz: whole(i, one(zz), x, y)), *gather_sems(i, 0)

    def gather_0(i):
        line_send(*line(i))

    def gather_1(i):
        line_relay(*line(i))

    def gather_2(i):
        line_end(*line(i))
        own = whole(i, every, x, y)
        gather_push(i, 4, own, xn)
        gather_push(i, 5, own, yn)

    def gather_3(i):
        gather_wait(i, 4, whole(i, every, 1 - x, y))
        gather_wait(i, 5, whole(i, every, x, 1 - y))
        gather_push(i, 6, whole(i, first, x, 1 - y), xn)
        gather_push(i, 7, whole(i, second, 1 - x, y), yn)

    def gather_4(i):
        gather_wait(i, 6, whole(i, first, 1 - x, 1 - y))
        gather_wait(i, 7, whole(i, second, 1 - x, 1 - y))

    band_stages = (gather_0, gather_1, gather_2, gather_3, gather_4)
    pair_stages = (pair_0, pair_1, pair_2, pair_3)

    def gather(i, stage):
        stages = pair_stages if chunks[i][0] == "P" else band_stages
        stages[stage](i)

    def add_into(ref, extra):
        total = ref[...].astype(F32)
        for more in extra:
            total = total + more[...].astype(F32)
        ref[...] = total.astype(BF)

    def slots(i, name):
        return getattr(r.red["AFP".index(chunks[i][0])], name).at[dims.slot[i]]

    def reduce_push(i, k, src, dst, dev):
        push(src, dst, r.ss.at[i, k], r.sr.at[i, k], dev)

    def reduce_wait(i, k, dst):
        arrived(dst, r.sr.at[i, k], r.ss.at[i, k])

    def line_reduce_send(part, land, send, recv):
        push_if(has_up, part(z_up), land.at[UP], send(UP), recv(UP), at_z(z_up))
        push_if(has_down, part(z_down), land.at[DOWN], send(DOWN), recv(DOWN), at_z(z_down))
        push_if(outer, part(z_end), land.at[RELAY], send(RELAY), recv(RELAY), at_z(z_in))
        push_if(outer, part(z_far), land.at[FAR], send(FAR), recv(FAR), at_z(z_far))

    def line_reduce_relay(part, land, send, recv):
        @pl.when(inner)
        def _():
            arrived(land.at[RELAY], recv(RELAY), send(RELAY))
            add_into(part(z_far), [land.at[RELAY]])

        push_if(inner, part(z_far), land.at[FAR], send(FAR), recv(FAR), at_z(z_far))

    def line_reduce_end(part, land, send, recv):
        arrived(land.at[FAR], recv(FAR), send(FAR))

        @pl.when(inner)
        def _():
            arrived(land.at[UP], recv(UP), send(UP))
            arrived(land.at[DOWN], recv(DOWN), send(DOWN))
            add_into(part(z), [land.at[FAR], land.at[UP], land.at[DOWN]])

        @pl.when(z == 0)
        def _():
            arrived(land.at[DOWN], recv(DOWN), send(DOWN))
            add_into(part(z), [land.at[FAR], land.at[DOWN]])

        @pl.when(z == DEPTH - 1)
        def _():
            arrived(land.at[UP], recv(UP), send(UP))
            add_into(part(z), [land.at[FAR], land.at[UP]])

    def reduce_sems(i, base):
        return sems(r.ss, r.sr, i, base)

    def band_reduce_0(i):
        over = slots(i, "ad")
        reduce_push(i, 14, view(i, True, "a", first, 1 - x, 1 - y), over.at[0], xn)
        reduce_push(i, 15, view(i, True, "a", second, 1 - x, 1 - y), over.at[1], yn)
        reduce_push(i, 18, view(i, True, "b", every, both, 1 - y), slots(i, "by"), yn)
        reduce_push(i, 19, view(i, True, "c", every, 1 - x, None), slots(i, "cx"), xn)

    def band_reduce_1(i):
        a, b, c_part = parts_of(i, True)
        over, beside = slots(i, "ad"), slots(i, "an")
        reduce_wait(i, 14, over.at[0])
        add_into(view(i, True, "a", first, x, 1 - y), [over.at[0]])
        reduce_push(i, 13, view(i, True, "a", every, x, 1 - y), beside.at[1], yn)
        reduce_wait(i, 15, over.at[1])
        add_into(view(i, True, "a", second, 1 - x, y), [over.at[1]])
        reduce_push(i, 12, view(i, True, "a", every, 1 - x, y), beside.at[0], xn)
        reduce_wait(i, 18, slots(i, "by"))
        add_into(view(i, True, "b", every, both, y), [slots(i, "by")])
        line_reduce_send(b, slots(i, "bz"), *reduce_sems(i, 4))
        reduce_wait(i, 19, slots(i, "cx"))
        add_into(view(i, True, "c", every, x, None), [slots(i, "cx")])
        line_reduce_send(c_part, slots(i, "cz"), *reduce_sems(i, 8))

    def band_reduce_2(i):
        a, b, c_part = parts_of(i, True)
        beside = slots(i, "an")
        reduce_wait(i, 12, beside.at[0])
        reduce_wait(i, 13, beside.at[1])
        add_into(view(i, True, "a", every, x, y), [beside.at[0], beside.at[1]])
        line_reduce_send(a, slots(i, "az"), *reduce_sems(i, 0))
        line_reduce_relay(b, slots(i, "bz"), *reduce_sems(i, 4))
        line_reduce_relay(c_part, slots(i, "cz"), *reduce_sems(i, 8))

    def band_reduce_3(i):
        a, b, c_part = parts_of(i, True)
        line_reduce_end(b, slots(i, "bz"), *reduce_sems(i, 4))
        reduce_push(i, 16, view(i, True, "b", one(z), 1 - x, y), slots(i, "bx"), xn)
        line_reduce_end(c_part, slots(i, "cz"), *reduce_sems(i, 8))
        reduce_push(i, 17, view(i, True, "c", one(z), x, 1 - y), slots(i, "cy"), yn)
        line_reduce_relay(a, slots(i, "az"), *reduce_sems(i, 0))

    def band_reduce_4(i):
        line_reduce_end(parts_of(i, True)[0], slots(i, "az"), *reduce_sems(i, 0))
        reduce_wait(i, 16, slots(i, "bx"))
        reduce_wait(i, 17, slots(i, "cy"))
        total = jnp.concatenate(
            [
                view(i, True, "a", one(z), x, y)[...].astype(F32)[0],
                (view(i, True, "b", one(z), x, y)[...].astype(F32) + slots(i, "bx")[...].astype(F32))[0],
                (view(i, True, "c", one(z), x, y)[...].astype(F32) + slots(i, "cy")[...].astype(F32))[0],
            ],
            axis=0,
        )
        reduce_store(i, total)

    def pair_reduce_0(i):
        over = slots(i, "ad")
        reduce_push(i, 3, pair_view(i, True, one(0), 1 - x, 1 - y), over.at[0], xn)
        reduce_push(i, 4, pair_view(i, True, one(1), 1 - x, 1 - y), over.at[1], yn)

    def pair_reduce_1(i):
        over, beside = slots(i, "ad"), slots(i, "an")
        reduce_wait(i, 3, over.at[0])
        add_into(pair_view(i, True, one(0), x, 1 - y), [over.at[0]])
        reduce_push(i, 2, pair_view(i, True, both, x, 1 - y), beside.at[1], yn)
        reduce_wait(i, 4, over.at[1])
        add_into(pair_view(i, True, one(1), 1 - x, y), [over.at[1]])
        reduce_push(i, 1, pair_view(i, True, both, 1 - x, y), beside.at[0], xn)

    def pair_reduce_2(i):
        beside = slots(i, "an")
        reduce_wait(i, 1, beside.at[0])
        reduce_wait(i, 2, beside.at[1])
        add_into(pair_view(i, True, both, x, y), [beside.at[0], beside.at[1]])
        reduce_push(i, 0, pair_view(i, True, one(z_other), x, y), slots(i, "az"), zfar)

    def pair_reduce_3(i):
        far = slots(i, "az")
        reduce_wait(i, 0, far)
        own = pair_view(i, True, one(z_own), x, y)
        reduce_store(i, (own[...].astype(F32) + far[...].astype(F32))[0])

    def reduce_store(i, total):
        kind, layer, which, part = chunks[i]
        send, land = slots(i, "fsend"), slots(i, "fland")
        if kind == "A":
            rows = total.shape[0] // 2
            cols = slice(part * model, (part + 1) * model)
            lay[layer].da[c, :, cols] = jnp.where(c == 0, total[:rows], total[rows:])
            send[...] = jnp.where(c == 0, total[rows:], total[:rows])
        else:
            full = dims.unit_rows[kind]
            rows, lanes = pl.ds(part * full, full), total.shape[1] // 2
            lay[layer].df[c, which, rows, :] = jnp.where(c == 0, total[:, :lanes], total[:, lanes:])
            send[...] = jnp.where(c == 0, total[:, lanes:], total[:, :lanes])
        push(send, land, r.fs.at[i], r.fr.at[i], sib)

    def reduce_out(i):
        kind, layer, which, part = chunks[i]
        land = slots(i, "fland")
        arrived(land, r.fr.at[i], r.fs.at[i])
        if kind == "A":
            lay[layer].da[1 - c, :, part * model : (part + 1) * model] = land[...]
            if part == 0:
                store(lay[layer].da, outs.lay[layer].da)
        else:
            full = dims.unit_rows[kind]
            lay[layer].df[1 - c, which, pl.ds(part * full, full), :] = land[...]
            if part == layers[layer].nr // full - 1:
                store(lay[layer].df.at[:, which], outs.lay[layer].df.at[:, which])

    band_reduces = (band_reduce_0, band_reduce_1, band_reduce_2, band_reduce_3, band_reduce_4)
    pair_reduces = (pair_reduce_0, pair_reduce_1, pair_reduce_2, pair_reduce_3)

    def reduce(i, stage):
        stages = pair_reduces if chunks[i][0] == "P" else band_reduces
        if stage < len(stages):
            stages[stage](i)

    def total_step(work, land, step, sends, recvs):
        dev = (sib, xn, yn, zn, zfar)[step]
        push(work.at[step], land.at[step], sends.at[step], recvs.at[step], dev)

    def total_add(work, land, step, sends, recvs):
        arrived(land.at[step], recvs.at[step], sends.at[step])
        work[step + 1] = work[step] + land[step]

    exchanges = []

    def exchange(part):
        slot = len(exchanges) % 2
        r.xs[slot] = part.astype(BF)
        copy = remote(r.xs.at[slot], r.xr.at[slot], r.es.at[slot], r.er.at[slot], sib)
        copy.start()
        exchanges.append(copy)

        def finish():
            copy.wait()
            return r.xs[slot].astype(F32) + r.xr[slot].astype(F32)

        return finish

    quarter = tok // 2
    own_rows = pl.ds(pl.multiple_of(c * quarter, 16), quarter)
    other_rows = pl.ds(pl.multiple_of((1 - c) * quarter, 16), quarter)

    class Share:
        def __init__(self, ref, k):
            blocks = len(ref.shape) == 4
            self.own = pl.ds(2 * c, 2) if blocks else own_rows
            self.other = pl.ds(2 - 2 * c, 2) if blocks else other_rows
            self.ref, self.k = ref, k
            piece = ref.at[half, self.own]
            push(piece, piece, r.ps.at[k, 0], r.pr.at[k, 0], zn)

        def turn(self):
            got, k = self.ref.at[1 - half, self.own], self.k
            arrived(got, r.pr.at[k, 0], r.ps.at[k, 0])
            push(got, got, r.ps.at[k, 1], r.pr.at[k, 1], sib)

        def end(self):
            k = self.k
            arrived(self.ref.at[1 - half, self.other], r.pr.at[k, 1], r.ps.at[k, 1])

    class Fold:
        def __init__(self, make, k):
            self.make, self.k = make, k
            r.px[k] = make(1 - half, False).astype(BF)
            push(r.px.at[k, other_rows], r.prx.at[k], r.ps.at[k, 2], r.pr.at[k, 2], sib)

        def keep(self):
            self.own = exchange(self.make(half, True))

        def cross(self):
            k = self.k
            arrived(r.prx.at[k], r.pr.at[k, 2], r.ps.at[k, 2])
            r.pz[k] = (r.px[k, own_rows, :].astype(F32) + r.prx[k].astype(F32)).astype(BF)
            push(r.pz.at[k], r.pzr.at[k, c], r.ps.at[k, 3], r.pr.at[k, 3], zn)

        def turn(self):
            k = self.k
            got = r.pzr.at[k, c]
            arrived(got, r.pr.at[k, 3], r.ps.at[k, 3])
            push(got, got, r.ps.at[k, 4], r.pr.at[k, 4], sib)

        def end(self):
            k = self.k
            arrived(r.pzr.at[k, 1 - c], r.pr.at[k, 4], r.ps.at[k, 4])
            return self.own() + r.pzr[k].reshape(tok, model).astype(F32)

    def vec_row(row):
        return r.vw[5, row : row + 1, :]

    def layer_vecs(at):
        sizes, rows, base = layers[at], dims.rows_of[at], dims.base[at]
        if sizes.hc * 2 == model:
            qv = r.vw[5, pl.ds(base + rows.qv + c, 1), :]
        else:
            both = vec_row(base + rows.qv)
            qv = jnp.where(c == 0, both[:, : 2 * sizes.hc], both[:, 2 * sizes.hc :])
        span = sizes.nc // model
        b1 = [r.vw[5, pl.ds(base + rows.b1 + c * span + s, 1), :] for s in range(span)]
        if sizes.pair:
            cut = 2 * sizes.nr
            b1 = [jnp.concatenate([jnp.where(half == 0, v[:, :cut], v[:, cut:]) for v in b1], axis=1)]
        found = types.SimpleNamespace(bq=qv[:, : sizes.hc], bv=qv[:, sizes.hc :], b1=b1)
        for name, row in vars(rows).items():
            if not hasattr(found, name):
                setattr(found, name, vec_row(base + row))
        return found

    kept = lay
    wa = [one_layer.wa for one_layer in lay]
    weights = [one_layer.w for one_layer in lay]

    def order_rows(at, part):
        gathered, whole = lay[at].ga, wa[at]
        cols = slice(part * model, (part + 1) * model)
        rows = gathered.shape[3] // 2
        span = DEPTH * 2 * rows
        for y_at in range(SIDE):
            for z_at in range(DEPTH):
                left = gathered[y_at, z_at, 0, :, cols].astype(F32)
                right = gathered[y_at, z_at, 1, :, cols].astype(F32)
                for core in range(SIDE):
                    own = slice(core * rows, (core + 1) * rows)
                    both = jnp.concatenate([left[own], right[own]], axis=0).astype(BF)
                    begin = (y_at * SIDE + core) * span + z_at * 2 * rows
                    whole[begin : begin + 2 * rows, cols] = both

    def store_grad_rows(at, y_at, value, cols):
        blocks = lay[at].ga
        rows = blocks.shape[3] // 2
        span = DEPTH * 2 * rows
        for z_at in range(DEPTH):
            for x_at in range(SIDE):
                begin = (z_at * 2 + x_at) * rows
                both = [value[begin : begin + rows], value[span + begin : span + begin + rows]]
                blocks[y_at, z_at, x_at, :, cols] = jnp.concatenate(both, axis=0).astype(BF)

    def head_kv(at, h):
        sizes, kv = layers[at], kept[at].kv
        k = kv[:, :, h * HEAD : (h + 1) * HEAD].reshape(seq, HEAD)
        v = kv[:, :, sizes.hc + h * HEAD : sizes.hc + (h + 1) * HEAD].reshape(seq, HEAD)
        return k, v

    def attention(at):
        sizes, keep = layers[at], kept[at]
        lane = lax.broadcasted_iota(jnp.int32, (1, model), 1)
        first_lane = (y * SIDE + row_core) * group + x
        entry = vec_row(dims.length_row)
        entry = jnp.where(lane == first_lane, 256.0 * entry, jnp.where(lane == first_lane + 2, entry, 0.0))
        length = jnp.sum(entry, axis=1, keepdims=True)
        valid = lax.broadcasted_iota(jnp.int32, (1, seq), 1).astype(F32) < length
        for h in range(sizes.heads):
            q = keep.q[:, h * HEAD : (h + 1) * HEAD]
            k, v = head_kv(at, h)
            scores = jnp.where(valid, mm(q, k, 1, 1) * 0.125, NEGATIVE)
            exponent = jnp.exp(scores - jnp.max(scores, axis=1, keepdims=True))
            low = (exponent / jnp.sum(exponent, axis=1, keepdims=True)).astype(BF)
            keep.a[h] = low
            begin = sizes.pad + h * HEAD
            keep.ctx[:, begin : begin + HEAD] = mm(low, v, 1, 0).astype(BF)

    def attention_back(at, grad_ctx):
        sizes, keep = layers[at], kept[at]
        dkv, dq = lay[at].dkv, lay[at].dq
        for h in range(sizes.heads):
            q = keep.q[:, h * HEAD : (h + 1) * HEAD]
            k, v = head_kv(at, h)
            begin = sizes.pad + h * HEAD
            dc = grad_ctx[:, begin : begin + HEAD]
            low = keep.a[h]
            a = low.astype(F32)
            da = mm(dc, v, 1, 1)
            inner = jnp.sum(a * da, axis=1, keepdims=True)
            ds = (0.125 * a * (da - inner)).astype(BF)
            dq[:, h * HEAD : (h + 1) * HEAD] = mm(ds, k, 1, 0).astype(BF)
            dk = mm(ds, q, 0, 0).astype(BF).reshape(2, tok, HEAD)
            dv = mm(low, dc, 0, 0).astype(BF).reshape(2, tok, HEAD)
            dkv[:, :, h * HEAD : (h + 1) * HEAD] = dk
            dkv[:, :, sizes.hc + h * HEAD : sizes.hc + (h + 1) * HEAD] = dv

    def block(at, which, b):
        sizes = layers[at]
        w = weights[at][which, b * sizes.zb : (b + 1) * sizes.zb]
        return w.reshape(model, model)

    def up(at, side):
        sizes, keep = layers[at], kept[at]
        for b in range(sizes.nl // model):
            cols = slice(b * model, (b + 1) * model)
            u = mm(keep.hb[side], block(at, 0, b), 1, 1) + vecs[at].b1[b]
            phi = 0.5 * (1.0 + lax.erf(u * 0.7071067811865476))
            keep.g[side, :, cols] = (u * phi).astype(BF)
            density = jnp.exp(u * u * -0.5) * 0.3989422804014327
            keep.gp[side, :, cols] = (phi + u * density).astype(BF)

    def times_block(at, which, side):
        sizes, keep = layers[at], kept[at]
        total = None
        for b in range(sizes.nl // model):
            term = mm(keep.g[side, :, b * model : (b + 1) * model], block(at, which, b), 1, 0)
            total = term if total is None else total + term
        return total

    def weight_grad(at, which, right):
        sizes, keep = layers[at], kept[at]
        span = model // 2
        zb = sizes.zb // 2
        rows = sizes.sides * tok
        wide = right[...].reshape(rows, model)
        for b in range(sizes.nl // span):
            left = keep.g[:, :, b * span : (b + 1) * span].reshape(rows, span)
            value = mm(left, wide, 0, 0).astype(BF)
            keep.dw[which, b * zb : (b + 1) * zb] = value.reshape(zb, 2, sizes.nr, model)


    def pack_a(at):
        sizes, width = layers[at], 2 * layers[at].hc
        rows_in = lay[at].pai[...].astype(F32)
        rows_out = lay[at].pao[...].astype(F32)
        halves = []
        for h in range(2):
            own = slice(h * sizes.hc, (h + 1) * sizes.hc)
            pieces = [rows_in[:, p * width : (p + 1) * width][:, own] for p in (1, 2, 0)]
            halves.append(jnp.concatenate(pieces + [rows_out[:, own]], axis=1))
        send = lay[at].asend
        send[...] = jnp.where(c == 0, halves[1], halves[0])
        if at == 0:
            pl.semaphore_wait(bar, PARTNERS)
        push(send, lay[at].ar, r.is_.at[2 * at], r.ir.at[2 * at], sib)
        return jnp.where(c == 0, halves[0], halves[1])

    def pack_f(at):
        sizes = layers[at]
        first = lay[at].pfi[...].astype(F32).T
        second = lay[at].pfo[...].astype(F32)
        if dims.turned[at]:
            second = second.T
        send, own = lay[at].fsend, []
        for which, value in enumerate((first, second)):
            low_half, high_half = value[: sizes.nr], value[sizes.nr :]
            own.append(jnp.where(c == 0, low_half, high_half))
            send[which] = jnp.where(c == 0, high_half, low_half).astype(BF)
        push(send, lay[at].fr, r.is_.at[2 * at + 1], r.ir.at[2 * at + 1], sib)
        return own

    def prepare_a(at, own):
        land, blocks = lay[at].ar, lay[at].ga
        arrived(land, r.ir.at[2 * at], r.is_.at[2 * at])
        other = land[...]
        pair = [jnp.where(c == 0, own, other), jnp.where(c == 0, other, own)]
        blocks[y, z, x] = jnp.concatenate(pair, axis=0).astype(BF)

    def prepare_f(at, own):
        land = lay[at].fr
        arrived(land, r.ir.at[2 * at + 1], r.is_.at[2 * at + 1])
        lanes = pl.ds(pl.multiple_of(y * half_lanes, 128), half_lanes)
        for which in range(2):
            other = land[which].astype(F32)
            pair = [jnp.where(c == 0, own[which], other), jnp.where(c == 0, other, own[which])]
            weights[at][which, z_own if layers[at].pair else z, x, :, lanes] = jnp.concatenate(pair, axis=1).astype(BF)

    group = dims.group
    per_row = model // group
    index = dp * DEPTH * SIDE + mp

    def targets(at_group):
        result, begin = jnp.full_like(at_group, dims.length_row * per_row) + dp, 0
        for at, sizes in enumerate(layers):
            base = dims.base[at] * per_row
            head, count_b = sizes.hc // group, sizes.nr // group
            up_at = dims.rows_of[at].b1 * per_row
            count = dims.shift_groups[at]
            g = index * count + (at_group - begin)
            w = g % (2 * head)
            qv = (w // head) * (2 * head) + (g // (2 * head)) * head + w % head
            b = g - up_at
            up_to = up_at + ((b % (2 * count_b)) // count_b) * (8 * count_b)
            up_to = up_to + (b // (2 * count_b)) * count_b + b % count_b
            place = jnp.where(g < 4 * head, qv, jnp.where((b >= 0) & (b < 16 * count_b), up_to, g))
            inside = (at_group >= begin) & (at_group < begin + count)
            result = jnp.where(inside, base + place, result)
            begin += count
            count = dims.gain_groups[at]
            place = dims.rows_of[at].g1 * per_row + index * count + (at_group - begin)
            inside = (at_group >= begin) & (at_group < begin + count)
            result = jnp.where(inside, base + place, result)
            begin += count
        return result // per_row, result % per_row

    groups = dims.vec_rows
    lane_group = lax.broadcasted_iota(jnp.int32, (groups, dims.lanes), 1) // group
    lane_own = lane_group == lax.broadcasted_iota(jnp.int32, (groups, dims.lanes), 0)

    def place_masks():
        down = lax.broadcasted_iota(jnp.int32, (groups, 1), 0)
        across = lax.broadcasted_iota(jnp.int32, (1, groups), 1)
        row_down, place_down = targets(down)
        row_across, _ = targets(across)
        lane = lax.broadcasted_iota(jnp.int32, (groups, model), 1) // group
        to_row = jnp.where(row_across == down, 1.0, 0.0).astype(BF)
        from_row = jnp.where(row_down == across, 1.0, 0.0).astype(BF)
        return lane == place_down, to_row, from_row

    def pack_vectors():
        lengths = r.len[...].astype(F32).reshape(1, 2) * jnp.where(mp == 0, 1.0, 0.0)
        high = jnp.floor(lengths * (1.0 / 256.0))
        pieces = []
        for own in lay:
            pieces += [own.psh[...].astype(F32).reshape(1, -1), own.pga[...].astype(F32).reshape(1, -1)]
        pieces += [high, lengths - 256.0 * high]
        used = sum(p.shape[1] for p in pieces)
        values = jnp.concatenate(pieces + [jnp.zeros((1, dims.lanes - used), F32)], axis=1)
        spread_out = jnp.where(lane_own, values, 0.0).astype(BF)
        i = lax.broadcasted_iota(jnp.int32, (dims.lanes, model), 0) % group
        j = lax.broadcasted_iota(jnp.int32, (dims.lanes, model), 1) % group
        r.hot[...] = jnp.where(i == j, 1.0, 0.0).astype(BF)
        in_place, to_row, _ = place_masks()
        wide = jnp.where(in_place, mm(spread_out, r.hot[...], 1, 0), 0.0).astype(BF)
        return mm(to_row, wide, 1, 0)

    def unpack_vectors(values):
        in_place, _, from_row = place_masks()
        total, rest = None, values
        for _ in range(3):
            low_part = rest.astype(BF)
            rest = rest - low_part.astype(F32)
            wide = jnp.where(in_place, mm(from_row, low_part, 1, 0), 0.0).astype(BF)
            term = jnp.where(lane_own, mm(wide, r.hot[...], 1, 1), 0.0)
            total = term if total is None else total + term
        return rowsum(total)

    vecs = []
    block_shape = (4, tok // 4, model)

    def tokens(at, side):
        return kept[at].xb[side].reshape(tok, model)

    def project_kv(at, side):
        sizes, keep = layers[at], kept[at]
        kv = mm(tokens(at, side), wa[at][:, : 2 * sizes.hc], 1, 0)
        keep.kv[side, :, : sizes.hc] = kv[:, : sizes.hc].astype(BF)
        keep.kv[side, :, sizes.hc :] = (kv[:, sizes.hc :] + vecs[at].bv).astype(BF)

    def project_q(at):
        sizes, keep = layers[at], kept[at]
        q = mm(tokens(at, half), wa[at][:, 2 * sizes.hc : 2 * sizes.hc + sizes.qw], 1, 0)
        keep.q[...] = (q[:, : sizes.hc] + vecs[at].bq).astype(BF)

    def attend_out(at):
        return mm(kept[at].ctx[...], wa[at][:, layers[at].start :], 1, 1)

    def norm_one(at, base, branch):
        keep, v = kept[at], vecs[at]
        normed, scale = normalize(base + branch + v.bo)
        keep.n1[...] = normed
        keep.s1[...] = scale
        result = normed * v.g1 + v.beta1
        keep.hb[half if layers[at].pair else 0] = result.astype(BF)
        return result

    def norm_two(at, base, branch):
        keep, v = kept[at], vecs[at]
        normed, scale = normalize(base + branch + v.b2)
        keep.n2[...] = normed
        keep.s2[...] = scale
        return normed * v.g2 + v.beta2

    if layers[1].pad:
        kept[1].ctx[...] = jnp.zeros_like(kept[1].ctx)
        lay[1].dq[...] = jnp.zeros_like(lay[1].dq)
    for copy in fetched[:2]:
        copy.wait()
    own_a0 = pack_a(0)
    prepare_a(0, own_a0)
    gather(0, 0)
    for copy in fetched[3:5]:
        copy.wait()
    own_f0 = pack_f(0)
    for copy in fetched[5:]:
        copy.wait()
    own_a1 = pack_a(1)
    r.vw[0] = pack_vectors()
    gather(0, 1)
    fetched[2].wait()
    spread(r.hid, kept[0].xb.at[lax.rem(z // 2, 2)], r.hs, r.hr)
    prepare_f(0, own_f0)
    prepare_a(1, own_a1)
    gather(1, 0)
    gather(0, 2)
    own_f1 = pack_f(1)
    total_step(r.vw, r.vl, 0, r.vs, r.vr)
    spread_turn(r.hid, kept[0].xb.at[half], r.hs, r.hr, r.os.at[0], r.os.at[1])
    gather(1, 1)
    spread_end(kept[0].xb.at[half], r.os.at[0], r.os.at[1])
    total_add(r.vw, r.vl, 0, r.vs, r.vr)
    total_step(r.vw, r.vl, 1, r.vs, r.vr)
    gather(2, 0)
    prepare_f(1, own_f1)
    gather(4, 0)
    share_hid = Share(kept[0].xb, 2)
    gather(1, 2)
    total_add(r.vw, r.vl, 1, r.vs, r.vr)
    total_step(r.vw, r.vl, 2, r.vs, r.vr)
    gather(0, 3)
    total_add(r.vw, r.vl, 2, r.vs, r.vr)
    total_step(r.vw, r.vl, 3, r.vs, r.vr)
    gather(2, 1)
    gather(3, 0)
    total_add(r.vw, r.vl, 3, r.vs, r.vr)
    gather(1, 3)
    share_hid.turn()
    total_step(r.vw, r.vl, 4, r.vs, r.vr)
    total_add(r.vw, r.vl, 4, r.vs, r.vr)
    vecs.extend([layer_vecs(0), layer_vecs(1)])
    gather(5, 0)
    gather(0, 4)
    share_hid.end()
    spread(r.cot, r.cin, r.cs, r.cr)
    gather(3, 1)
    order_rows(0, 0)
    project_kv(0, half)
    gather(1, 4)
    order_rows(0, 1)
    project_q(0)
    gather(4, 1)
    project_kv(0, 1 - half)
    attention(0)
    gather(2, 2)
    gather(6, 0)
    branch = exchange(attend_out(0))
    branch = branch()
    gather(3, 2)
    normed = norm_one(0, tokens(0, half).astype(F32), branch)
    share_normed = Share(kept[0].hb, 0)
    gather(5, 1)
    gather(4, 2)
    gather(3, 3)
    share_normed.turn()
    gather(2, 3)
    gather(6, 1)
    up(0, half)
    gather(5, 2)
    share_normed.end()
    up(0, 1 - half)
    down = Fold(lambda side, own: times_block(0, 1, side), 0)
    down.keep()
    down.cross()
    gather(4, 3)
    gather(6, 2)
    down.turn()
    branch = down.end()
    middle = norm_two(0, normed, branch)
    kept[1].xb[half] = middle.astype(BF).reshape(block_shape)
    share_middle = Share(kept[1].xb, 3)
    gather(4, 4)
    spread_turn(r.cot, r.cin, r.cs, r.cr, r.os.at[2], r.os.at[3])
    order_rows(1, 0)
    project_kv(1, half)
    project_q(1)
    gather(5, 3)
    share_middle.turn()
    share_middle.end()
    project_kv(1, 1 - half)
    gather(6, 3)
    attention(1)
    branch = exchange(attend_out(1))
    gather(5, 4)
    spread_end(r.cin, r.os.at[2], r.os.at[3])
    branch = branch()
    normed = norm_one(1, middle, branch)
    up(1, 0)
    gather(6, 4)
    branch = exchange(times_block(1, 1, 0))
    branch = branch()
    final = norm_two(1, normed, branch)
    r.oblk[...] = final.astype(BF).reshape(r.oblk.shape)
    collect(r.oblk, r.oland, r.ys, r.yr)
    wait_sent()

    r.vw[0] = jnp.zeros_like(r.vw[0])
    once = jnp.where(c == 0, 1.0, 0.0)

    def put_vec(at, name, value):
        row = dims.base[at] + getattr(dims.rows_of[at], name)
        r.vw[0, row : row + 1, :] = value * once

    def back_two(at, grad):
        keep, v = kept[at], vecs[at]
        n2 = keep.n2[...]
        put_vec(at, "g2", rowsum(grad * n2))
        put_vec(at, "beta2", rowsum(grad))
        dz2 = normalize_back(grad * v.g2, n2, keep.s2[...])
        low_dz2 = dz2.astype(BF)
        keep.eo[half if layers[at].pair else 0] = low_dz2
        put_vec(at, "b2", rowsum(low_dz2.astype(F32)))
        return dz2

    def back_up(at):
        sizes, keep = layers[at], kept[at]
        base = dims.base[at] + dims.rows_of[at].b1
        span, sums = sizes.nc // model, []
        for b in range(sizes.nl // model):
            cols = slice(b * model, (b + 1) * model)
            total = None
            for side in range(sizes.sides):
                dg = mm(keep.eo[side], block(at, 1, b), 1, 1)
                du = (dg * keep.gp[side, :, cols].astype(F32)).astype(BF)
                keep.g[side, :, cols] = du
                term = rowsum(du.astype(F32))
                total = term if total is None else total + term
            sums.append(total)
        if sizes.pair:
            cut = 2 * sizes.nr
            blank = jnp.zeros((1, cut), F32)
            pieces = [sums[0][:, b * cut : (b + 1) * cut] for b in range(span)]
            sums = [
                jnp.concatenate([jnp.where(half == 0, p, blank), jnp.where(half == 0, blank, p)], axis=1)
                for p in pieces
            ]
        for b, total in enumerate(sums):
            r.vw[0, pl.ds(base + c * span + b, 1), :] = total

    def back_one(at, grad):
        keep, v = kept[at], vecs[at]
        n1 = keep.n1[...]
        put_vec(at, "g1", rowsum(grad * n1))
        put_vec(at, "beta1", rowsum(grad))
        dz1 = normalize_back(grad * v.g1, n1, keep.s1[...])
        r.eo[...] = dz1.astype(BF)
        put_vec(at, "bo", rowsum(r.eo[...].astype(F32)))
        grad_ctx = mm(r.eo[...], wa[at][:, layers[at].start :], 1, 0).astype(BF)
        return dz1, grad_ctx

    def bias_sums(at):
        sizes, dkv, dq = layers[at], lay[at].dkv, lay[at].dq
        qsum = rowsum(dq[:, : sizes.hc].astype(F32))
        vsum = rowsum(dkv[:, :, sizes.hc :].reshape(seq, sizes.hc).astype(F32))
        both = jnp.concatenate([qsum, vsum], axis=1)
        row = dims.base[at] + dims.rows_of[at].qv
        if 2 * sizes.hc == model:
            r.vw[0, pl.ds(row + c, 1), :] = both
        else:
            blank = jnp.zeros_like(both)
            left, right = jnp.where(c == 0, both, blank), jnp.where(c == 0, blank, both)
            r.vw[0, row : row + 1, :] = jnp.concatenate([left, right], axis=1)

    def projection_grad(at, part):
        sizes, keep = layers[at], kept[at]
        begin, end = part * model, (part + 1) * model
        for y_at in range(SIDE):
            rows = slice(y_at * half_lanes, (y_at + 1) * half_lanes)
            pieces = []
            if begin == 0:
                every_token = keep.xb[:, :, :, rows].reshape(seq, half_lanes)
                grads = keep.dkv[...].reshape(seq, 2 * sizes.hc)
                pieces.append(mm(every_token, grads, 0, 0))
            if end > 2 * sizes.hc:
                own = keep.xb[half, :, :, rows].reshape(tok, half_lanes)
                query = mm(own, keep.dq[...], 0, 0)
                output = mm(r.eo[:, rows], keep.ctx[...], 0, 0)
                if sizes.pad:
                    apart = sizes.start - 2 * sizes.hc
                    pieces += [query[:, :apart], query[:, apart:] + output]
                else:
                    pieces += [query, output]
            value = pieces[0] if len(pieces) == 1 else jnp.concatenate(pieces, axis=1)
            store_grad_rows(at, y_at, value, slice(begin, end))

    def back_hidden(at, side, own):
        sizes, keep = layers[at], kept[at]
        total = mm(keep.dkv[side], wa[at][:, : 2 * sizes.hc], 1, 1)
        if own:
            begin = 2 * sizes.hc
            total = total + mm(keep.dq[...], wa[at][:, begin : begin + keep.dq.shape[1]], 1, 1)
        return total

    grad = r.cin[...].reshape(tok, model).astype(F32)
    dz2 = back_two(1, grad)
    weight_grad(1, 1, kept[1].eo)
    reduce(6, 0)
    back_up(1)
    branch = exchange(times_block(1, 0, 0))
    branch = branch()
    dz1, grad_ctx = back_one(1, dz2 + branch)
    attention_back(1, grad_ctx)
    reduce(6, 1)
    down = Fold(lambda side, own: back_hidden(1, side, own), 2)
    down.keep()
    down.cross()
    projection_grad(1, 0)
    bias_sums(1)
    reduce(4, 0)
    weight_grad(1, 0, kept[1].hb)
    down.turn()
    reduce(5, 0)
    branch = down.end()
    dz2 = back_two(0, dz1 + branch)
    share_grad = Share(kept[0].eo, 1)
    reduce(4, 1)
    reduce(5, 1)
    share_grad.turn()
    share_grad.end()
    weight_grad(0, 1, kept[0].eo)
    reduce(3, 0)
    back_up(0)
    up_back = Fold(lambda side, own: times_block(0, 0, side), 1)
    weight_grad(0, 0, kept[0].hb)
    reduce(2, 0)
    up_back.keep()
    up_back.cross()
    reduce(6, 2)
    reduce(4, 2)
    reduce(5, 2)
    reduce(3, 1)
    up_back.turn()
    collect_done(r.oblk, r.oland, r.ys, r.yr)
    store(r.oland, outs.out)
    branch = up_back.end()
    reduce(2, 1)
    dz1, grad_ctx = back_one(0, dz2 + branch)
    attention_back(0, grad_ctx)
    reduce(3, 2)
    to_hidden = Fold(lambda side, own: back_hidden(0, side, own), 3)
    projection_grad(0, 1)
    reduce(1, 0)
    to_hidden.keep()
    to_hidden.cross()
    reduce(5, 3)
    reduce(2, 2)
    reduce(4, 3)
    projection_grad(0, 0)
    bias_sums(0)
    reduce(0, 0)
    total_step(r.vw, r.vl, 0, r.ws, r.wr)
    total_add(r.vw, r.vl, 0, r.ws, r.wr)
    reduce(1, 1)
    total_step(r.vw, r.vl, 1, r.ws, r.wr)
    reduce(6, 3)
    reduce(5, 4)
    reduce(1, 2)
    reduce(0, 1)
    total_add(r.vw, r.vl, 1, r.ws, r.wr)
    total_step(r.vw, r.vl, 2, r.ws, r.wr)
    to_hidden.turn()
    reduce(3, 3)
    total_add(r.vw, r.vl, 2, r.ws, r.wr)
    reduce(4, 4)
    reduce_out(3)
    total_step(r.vw, r.vl, 3, r.ws, r.wr)
    branch = to_hidden.end()
    reduce(6, 4)
    reduce(2, 3)
    reduce(1, 3)
    reduce(0, 2)
    reduce_out(5)
    total_add(r.vw, r.vl, 3, r.ws, r.wr)
    reduce(1, 4)
    reduce(0, 3)
    reduce_out(2)
    total_step(r.vw, r.vl, 4, r.ws, r.wr)
    reduce(0, 4)
    reduce_out(1)
    reduce_out(6)
    reduce_out(4)
    r.gblk[...] = (dz1 + branch).astype(BF).reshape(r.gblk.shape)
    collect(r.gblk, r.gland, r.zs, r.zr)
    reduce_out(0)
    total_add(r.vw, r.vl, 4, r.ws, r.wr)
    r.dvec[...] = unpack_vectors(r.vw[5])
    store(r.dvec, outs.dvec)
    collect_done(r.gblk, r.gland, r.zs, r.zr)
    store(r.gland, outs.gh)
    wait_sent()
    for copy in stored:
        copy.wait()


def fused_call(hid, cot, lengths, params, dims):
    model, tok, seq = dims.model, dims.tok, dims.seq
    block = (4, tok // 4, model)
    vmem = pltpu.VMEM
    dma = pltpu.SemaphoreType.DMA
    rows_in = params[0][0].shape[0]
    shape = jax.ShapeDtypeStruct
    given = dict(hid=hid, cot=cot, len=lengths, lay=[])
    outs = dict(out=shape(hid.shape, BF), gh=shape(hid.shape, BF), lay=[], dvec=shape((1, dims.lanes), F32))
    for (ai, ao, fi, fo, sh, ga), sizes in zip(params, dims.layers):
        given["lay"].append(dict(pai=ai, pao=ao, pfi=fi, pfo=fo, psh=sh, pga=ga))
        outs["lay"].append(
            dict(
                da=shape((2, rows_in, sizes.wide), F32),
                df=shape((2, 2, sizes.nr, model // 4), F32),
            )
        )
    as_scratch = lambda tree: jax.tree.map(lambda v: vmem(v.shape, v.dtype), tree)
    held, made = as_scratch(given), as_scratch({key: outs[key] for key in ("lay", "dvec")})
    vec = (dims.vec_rows, model)
    rows_a = 2 * rows_in
    counts = [sum(chunk[0] == kind for chunk in dims.chunks) for kind in "AFP"]
    half = model // 2
    n = len(dims.chunks)
    scratch = dict(
        cin=vmem(block, BF),
        oblk=vmem(block, BF),
        gblk=vmem(block, BF),
        oland=vmem(hid.shape, BF),
        gland=vmem(hid.shape, BF),
        vw=vmem((6,) + vec, F32),
        vl=vmem((5,) + vec, F32),
        xs=vmem((2, tok, model), BF),
        xr=vmem((2, tok, model), BF),
        eo=vmem((tok, model), BF),
        px=vmem((4, tok, model), BF),
        prx=vmem((4, tok // 2, model), BF),
        pz=vmem((4, tok // 2, model), BF),
        pzr=vmem((4, 2, tok // 2, model), BF),
        ps=dma((4, 5)),
        pr=dma((4, 5)),
        hot=vmem((dims.lanes, model), BF),
        gs=dma((n, 20)),
        gr=dma((n, 20)),
        ss=dma((n, 20)),
        sr=dma((n, 20)),
        fs=dma((n,)),
        fr=dma((n,)),
        vs=dma((5,)),
        vr=dma((5,)),
        ws=dma((5,)),
        wr=dma((5,)),
        hs=dma((4,)),
        hr=dma((4,)),
        cs=dma((4,)),
        cr=dma((4,)),
        ys=dma((4,)),
        yr=dma((4,)),
        zs=dma((4,)),
        zr=dma((4,)),
        is_=dma((4,)),
        ir=dma((4,)),
        os=dma((4,)),
        es=dma((2,)),
        er=dma((2,)),
        ins=dma((16,)),
        outs=dma((10,)),
        red=[],
        lay=[],
    )
    rows_f, rows_p = dims.unit_rows["F"], dims.unit_rows["P"]
    for count, rows, wide, pair, shard in (
        (counts[0], rows_a - 32, model, (2, 4, 16, model), (rows_in, model)),
        (counts[1], rows_f - 32, half, (4, 16, model), (rows_f, half // 2)),
    ):
        line = pair[:-3] + (1, 16, model)
        scratch["red"].append(
            dict(
                ad=vmem((count, 2, 2, rows, wide), BF),
                an=vmem((count, 2, 4, rows, wide), BF),
                az=vmem((count, 4, 1, rows, wide), BF),
                by=vmem((count, 4, 2, 16, wide), BF),
                bz=vmem((count, 4, 1, 2, 16, wide), BF),
                bx=vmem((count, 1, 16, wide), BF),
                cx=vmem((count,) + pair, BF),
                cz=vmem((count, 4) + line, BF),
                cy=vmem((count, 1, 16, wide), BF),
                fsend=vmem((count,) + shard, F32),
                fland=vmem((count,) + shard, F32),
            )
        )
    scratch["red"].append(
        dict(
            ad=vmem((counts[2], 2, 1, rows_p, half), BF),
            an=vmem((counts[2], 2, 2, rows_p, half), BF),
            az=vmem((counts[2], 1, rows_p, half), BF),
            fsend=vmem((counts[2], rows_p, half // 2), F32),
            fland=vmem((counts[2], rows_p, half // 2), F32),
        )
    )
    for sizes in dims.layers:
        scratch["lay"].append(
            dict(
                ar=vmem((rows_in, sizes.wide), F32),
                asend=vmem((rows_in, sizes.wide), F32),
                fr=vmem((2, sizes.nr, model // 4), BF),
                fsend=vmem((2, sizes.nr, model // 4), BF),
                ga=vmem((SIDE, DEPTH, SIDE, rows_a, sizes.wide), BF),
                wa=vmem((model, sizes.wide), BF),
                w=vmem((2, sizes.zs, SIDE, sizes.nr, model), BF),
                dw=vmem((2, sizes.zs, SIDE, sizes.nr, model), BF),
                xb=vmem((2,) + block, BF),
                q=vmem((tok, sizes.hc), BF),
                kv=vmem((2, tok, 2 * sizes.hc), BF),
                a=vmem((sizes.heads, tok, seq), BF),
                ctx=vmem((tok, sizes.wide - sizes.start), BF),
                n1=vmem((tok, model), F32),
                s1=vmem((tok, 1), F32),
                hb=vmem((sizes.sides, tok, model), BF),
                eo=vmem((sizes.sides, tok, model), BF),
                g=vmem((sizes.sides, tok, sizes.nl), BF),
                gp=vmem((sizes.sides, tok, sizes.nl), BF),
                n2=vmem((tok, model), F32),
                s2=vmem((tok, 1), F32),
                dkv=vmem((2, tok, 2 * sizes.hc), BF),
                dq=vmem((tok, 2 * sizes.hc if sizes.pad else sizes.hc), BF),
            )
        )
    inputs, outputs = jax.tree.leaves(given), jax.tree.leaves(outs)
    whole = pl.BlockSpec(memory_space=pl.ANY)
    local = (scratch, held, made)
    values = pl.pallas_call(
        functools.partial(fused_kernel, dims, jax.tree.structure((given, outs) + local)),
        out_shape=outputs,
        in_specs=[whole] * len(inputs),
        out_specs=[whole] * len(outputs),
        scratch_shapes=jax.tree.leaves(local),
        compiler_params=pltpu.CompilerParams(
            collective_id=0, has_side_effects=True, vmem_limit_bytes=dims.vmem
        ),
        name="layers",
    )(*inputs)
    return jax.tree.unflatten(jax.tree.structure(outs), values)


def finish_kernel(dims, tree, *refs):
    given, (out, gh, *results) = jax.tree.unflatten(tree, refs)
    r = named(given)
    out[...] = r.out[...]
    gh[...] = r.gh[...].astype(F32)
    begin = 0
    for at, sizes in enumerate(dims.layers):
        attn, ffn = r.lay[at].da, r.lay[at].df
        to_ai, to_ao, to_fi, to_fo, to_sh, to_ga = results[6 * at : 6 * at + 6]
        for p in range(3):
            for h in range(2):
                to = (2 * ((p + 1) % 3) + h) * sizes.hc
                to_ai[:, to : to + sizes.hc] = attn[h, :, p * sizes.hc : (p + 1) * sizes.hc]
        for h in range(2):
            to_ao[:, h * sizes.hc : (h + 1) * sizes.hc] = attn[h, :, 3 * sizes.hc :]
        down = ffn[:, 1].reshape(2 * sizes.nr, ffn.shape[3])
        to_fo[...] = down.T if dims.turned[at] else down
        to_fi[...] = ffn[:, 0].reshape(2 * sizes.nr, ffn.shape[3]).T
        for ref in (to_sh, to_ga):
            ref[...] = r.dvec[0, begin : begin + ref.shape[0]]
            begin += ref.shape[0]


def finish_call(given, params, dims):
    leaves, tree = jax.tree.flatten(given)
    outs = [jax.ShapeDtypeStruct(given["out"].shape, d) for d in (BF, F32)]
    outs += [jax.ShapeDtypeStruct(p.shape, F32) for shards in params for p in shards]
    whole = pl.BlockSpec(memory_space=pltpu.VMEM)
    return pl.pallas_call(
        functools.partial(finish_kernel, dims, jax.tree.structure((given, outs))),
        out_shape=outs,
        in_specs=[whole] * len(leaves),
        out_specs=[whole] * len(outs),
        compiler_params=pltpu.CompilerParams(vmem_limit_bytes=dims.vmem),
        name="finish",
    )(*leaves)


def make_dims(hidden_in, teacher, student):
    model = hidden_in.shape[2]
    layers = [
        layer_sizes(model, p[0].shape[1] // 3, p[2].shape[1] * DEPTH * SIDE, pair)
        for p, pair in ((teacher, True), (student, False))
    ]
    rows = layers[1].nr
    chunks = []
    for at, sizes in enumerate(layers):
        chunks += [("A", at, 0, part) for part in range(sizes.wide // model)]
        for which in (0, 1):
            kind, count = ("P", 1) if sizes.pair else ("F", sizes.nr // rows)
            chunks += [(kind, at, which, part) for part in range(count)]
    counts, slot = {"A": 0, "F": 0, "P": 0}, []
    for chunk in chunks:
        slot.append(counts[chunk[0]])
        counts[chunk[0]] += 1
    group = model // (SIDE * SIDE * DEPTH * SIDE)
    shift_groups = [p[4].shape[0] // group for p in (teacher, student)]
    gain_groups = [p[5].shape[0] // group for p in (teacher, student)]
    rows_of, base, at = [], [], 0
    for sizes in layers:
        found, count = vec_rows(model, sizes)
        rows_of.append(found)
        base.append(at)
        at += count
    return types.SimpleNamespace(
        model=model,
        tok=4 * hidden_in.shape[1],
        seq=8 * hidden_in.shape[1],
        layers=layers,
        chunks=chunks,
        slot=slot,
        rows=rows,
        unit_rows={"A": 2 * teacher[0].shape[0], "F": rows, "P": layers[0].nr},
        rows_of=rows_of,
        base=base,
        length_row=at,
        vec_rows=(at + 8) // 8 * 8,
        turned=[p[3].shape[0] > p[3].shape[1] for p in (teacher, student)],
        group=group,
        lanes=(sum(shift_groups + gain_groups) * group + 4 + 127) // 128 * 128,
        shift_groups=shift_groups,
        gain_groups=gain_groups,
        vmem=63 * 2**20,
    )


def fast_body(hidden_in, cotangent, lengths, *shards):
    params = (shards[:6], shards[6:])
    dims = make_dims(hidden_in, *params)
    turn = lambda shards, turned: (shards[0], shards[1].T, shards[2], shards[3].T if turned else shards[3])
    params = [turn(p, turned) + p[4:] for p, turned in zip(params, dims.turned)]
    values = fused_call(hidden_in, cotangent, lengths, params, dims)
    out, grad_hidden, *grads = finish_call(values, params, dims)
    results = [out, grad_hidden]
    for at, turned in enumerate(dims.turned):
        own = tuple(grads[6 * at : 6 * at + 6])
        results += turn(own, turned) + own[4:]
    return tuple(results)


def body(axes, *args):
    rows, tokens, model = args[0].shape
    pair_fits = args[3 + 2].shape[1] * 2 == model
    fits = pair_fits and axes["dp"] == SIDE * SIDE and axes["mp"] == DEPTH * SIDE
    if fits and rows == 2 and tokens % 16 == 0 and model % 256 == 0:
        return fast_body(*args)
    return general_body(*args)


def general_body(
    hidden_in,
    cotangent,
    lengths,
    teacher_attn_in,
    teacher_attn_out,
    teacher_ffn_in,
    teacher_ffn_out,
    teacher_shifts,
    teacher_gains,
    student_attn_in,
    student_attn_out,
    student_ffn_in,
    student_ffn_out,
    student_shifts,
    student_gains,
):
    span_len = hidden_in.shape[1] * lax.axis_size("mp")
    positions = jnp.arange(span_len)
    valid_keys = positions[None, :] < lengths[:, None]
    teacher = fetch(
        teacher_attn_in,
        teacher_attn_out,
        teacher_ffn_in,
        teacher_ffn_out,
        teacher_shifts,
        teacher_gains,
    )
    student = fetch(
        student_attn_in,
        student_attn_out,
        student_ffn_in,
        student_ffn_out,
        student_shifts,
        student_gains,
    )
    middle, teacher_kept = forward_layer(hidden_in.astype(jnp.float32), teacher, valid_keys)
    final, student_kept = forward_layer(middle, student, valid_keys)
    grad_middle, student_grads = backward_layer(
        cotangent.astype(jnp.float32), student_kept, student, valid_keys
    )
    grad_input, teacher_grads = backward_layer(grad_middle, teacher_kept, teacher, valid_keys)
    teacher_totals = reduce_grads(teacher_grads)
    student_totals = reduce_grads(student_grads)
    return (final.astype(jnp.bfloat16), grad_input) + teacher_totals + student_totals


def solution(mesh):
    in_specs = (
        P("dp", "mp", None),
        P("dp", "mp", None),
        P("dp"),
        P(("dp", "mp"), None),
        P(None, ("dp", "mp")),
        P("dp", "mp"),
        P("mp", "dp"),
        P(("dp", "mp")),
        P(("dp", "mp")),
        P(("dp", "mp"), None),
        P(None, ("dp", "mp")),
        P("dp", "mp"),
        P("mp", "dp"),
        P(("dp", "mp")),
        P(("dp", "mp")),
    )
    out_specs = (
        P("dp", "mp", None),
        P("dp", "mp", None),
        P(("dp", "mp"), None),
        P(None, ("dp", "mp")),
        P("dp", "mp"),
        P("mp", "dp"),
        P(("dp", "mp")),
        P(("dp", "mp")),
        P(("dp", "mp"), None),
        P(None, ("dp", "mp")),
        P("dp", "mp"),
        P("mp", "dp"),
        P(("dp", "mp")),
        P(("dp", "mp")),
    )
    return jax.shard_map(
        functools.partial(body, dict(mesh.shape)), mesh=mesh, in_specs=in_specs, out_specs=out_specs, check_vma=False)
```

```python
import functools
import types

import jax
import jax.numpy as jnp
from jax import lax
from jax.experimental import pallas as pl
from jax.experimental.pallas import tpu as pltpu
from jax.sharding import PartitionSpec as P

HEAD = 64


EPSILON = 1e-06
NEGATIVE = -1e30


def layer_norm(values, gain, shift):
    centered = values - jnp.mean(values, axis=-1, keepdims=True)
    variance = jnp.mean(centered * centered, axis=-1, keepdims=True)
    return centered * lax.rsqrt(variance + EPSILON) * gain + shift


def smooth_gate(pre_act):
    return jax.nn.gelu(pre_act, approximate=False)


def split_shifts(shifts, head_width, model_width, hidden_width):
    spans_list = [
        head_width,
        head_width,
        model_width,
        model_width,
        hidden_width,
        model_width,
        model_width,
    ]
    pieces = []
    offset = 0
    for length in spans_list:
        pieces.append(shifts[offset : offset + length])
        offset = offset + length
    return pieces


def to_heads(values):
    return values.reshape(values.shape[0], values.shape[1], values.shape[2] // HEAD, HEAD)


def score_block(queries, all_keys, valid_keys):
    raw = jnp.einsum(
        "rqhd,rkhd->rhqk", to_heads(queries), to_heads(all_keys), preferred_element_type=jnp.float32
    )
    return jnp.where(valid_keys[:, None, None, :], raw * 0.125, NEGATIVE)


def fetch(attn_in, attn_out, ffn_in, ffn_out, shifts, gains):
    whole_in, whole_out, whole_shifts, whole_gains = (
        lax.all_gather(attn_in, ("dp", "mp"), axis=0, tiled=True),
        lax.all_gather(attn_out, ("dp", "mp"), axis=1, tiled=True),
        lax.all_gather(shifts, ("dp", "mp"), axis=0, tiled=True),
        lax.all_gather(gains, ("dp", "mp"), axis=0, tiled=True),
    )
    ffn_first, ffn_second = (
        lax.all_gather(ffn_in, "dp", axis=0, tiled=True),
        lax.all_gather(ffn_out, "dp", axis=1, tiled=True),
    )
    return (
        whole_in,
        whole_out,
        ffn_first,
        ffn_second,
        whole_shifts.astype(jnp.float32),
        whole_gains.astype(jnp.float32),
    )


def forward_layer(hidden, params, valid_keys):
    attn_in, attn_out, ffn_first, ffn_second, shifts, gains = params
    model_width = hidden.shape[-1]
    head_width = attn_in.shape[1] // 3
    hidden_width = shifts.shape[0] - 2 * head_width - 4 * model_width
    pieces = split_shifts(shifts, head_width, model_width, hidden_width)
    bias_query, bias_value, bias_output, shift_one, bias_up, bias_down, shift_two = pieces
    hidden_low = hidden.astype(jnp.bfloat16)
    projected = jnp.einsum("rsd,de->rse", hidden_low, attn_in, preferred_element_type=jnp.float32)
    queries = (projected[..., :head_width] + bias_query).astype(jnp.bfloat16)
    local_keys = projected[..., head_width : 2 * head_width].astype(jnp.bfloat16)
    local_values = (projected[..., 2 * head_width :] + bias_value).astype(jnp.bfloat16)
    all_keys, all_values = (
        lax.all_gather(local_keys, "mp", axis=1, tiled=True),
        lax.all_gather(local_values, "mp", axis=1, tiled=True),
    )
    scores = score_block(queries, all_keys, valid_keys)
    row_max = jnp.max(scores, axis=-1, keepdims=True)
    exponent = jnp.exp(scores - row_max)
    row_total = jnp.sum(exponent, axis=-1, keepdims=True)
    log_total = row_max + jnp.log(row_total)
    weights_low = (exponent / row_total).astype(jnp.bfloat16)
    mixed = jnp.einsum(
        "rhqk,rkhd->rqhd", weights_low, to_heads(all_values), preferred_element_type=jnp.float32
    )
    context = mixed.reshape(queries.shape).astype(jnp.bfloat16)
    branch = (
        jnp.einsum("rsh,hd->rsd", context, attn_out, preferred_element_type=jnp.float32)
        + bias_output
    )
    summed_one = hidden + branch
    normed_one = layer_norm(summed_one, gains[:model_width], shift_one)
    normed_low = normed_one.astype(jnp.bfloat16)
    ffn_tokens = lax.all_gather(normed_low, "mp", axis=1, tiled=True)
    local_hidden = ffn_first.shape[1]
    bias_part = lax.dynamic_slice_in_dim(bias_up, lax.axis_index("mp") * local_hidden, local_hidden)
    pre_act = (
        jnp.einsum("rsd,df->rsf", ffn_tokens, ffn_first, preferred_element_type=jnp.float32)
        + bias_part
    )
    act_low = smooth_gate(pre_act).astype(jnp.bfloat16)
    down_terms = jnp.einsum("rsf,fd->rsd", act_low, ffn_second, preferred_element_type=jnp.float32)
    ffn_down = lax.psum_scatter(
        down_terms.astype(jnp.bfloat16), "mp", scatter_dimension=1, tiled=True
    ).astype(jnp.float32)
    summed_two = normed_one + ffn_down + bias_down
    result = layer_norm(summed_two, gains[model_width:], shift_two)
    key_store = (all_keys, all_values)
    kept = (
        hidden_low,
        queries,
        key_store,
        log_total,
        context,
        summed_one,
        ffn_tokens,
        pre_act,
        act_low,
        summed_two,
    )
    return (result, kept)


def backward_layer(grad_out, kept, params, valid_keys):
    attn_in, attn_out, ffn_first, ffn_second, shifts, gains = params
    (
        hidden_low,
        queries,
        key_store,
        log_total,
        context,
        summed_one,
        ffn_tokens,
        pre_act,
        act_low,
        summed_two,
    ) = kept
    model_width = summed_one.shape[-1]
    head_width = attn_in.shape[1] // 3
    hidden_width = shifts.shape[0] - 2 * head_width - 4 * model_width
    pieces = split_shifts(shifts, head_width, model_width, hidden_width)
    bias_query, bias_value, bias_output, shift_one, bias_up, bias_down, shift_two = pieces
    sum_axes = (0, 1)
    unused_two, norm_two_back = jax.vjp(layer_norm, summed_two, gains[model_width:], shift_two)
    grad_two, grad_gain_two, grad_shift_two = norm_two_back(grad_out)
    grad_down = grad_two.astype(jnp.bfloat16)
    grad_bias_down = jnp.sum(grad_down.astype(jnp.float32), axis=sum_axes)
    grad_tokens = lax.all_gather(grad_down, "mp", axis=1, tiled=True)
    grad_act = jnp.einsum(
        "rsd,fd->rsf", grad_tokens, ffn_second, preferred_element_type=jnp.float32
    )
    grad_second = jnp.einsum(
        "rsf,rsd->fd", act_low, grad_tokens, preferred_element_type=jnp.float32
    )
    unused_gate, gate_back = jax.vjp(smooth_gate, pre_act)
    grad_pre = gate_back(grad_act)[0].astype(jnp.bfloat16)
    grad_bias_part = jnp.sum(grad_pre.astype(jnp.float32), axis=sum_axes)
    grad_first = jnp.einsum("rsd,rsf->df", ffn_tokens, grad_pre, preferred_element_type=jnp.float32)
    back_terms = jnp.einsum("rsf,df->rsd", grad_pre, ffn_first, preferred_element_type=jnp.float32)
    grad_normed = lax.psum_scatter(
        back_terms.astype(jnp.bfloat16), "mp", scatter_dimension=1, tiled=True
    ).astype(jnp.float32)
    blank_bias = jnp.zeros((hidden_width,), jnp.float32)
    grad_bias_up = lax.dynamic_update_slice_in_dim(
        blank_bias, grad_bias_part, lax.axis_index("mp") * ffn_first.shape[1], 0
    )
    grad_normed = grad_normed + grad_two
    unused_one, norm_one_back = jax.vjp(layer_norm, summed_one, gains[:model_width], shift_one)
    grad_one, grad_gain_one, grad_shift_one = norm_one_back(grad_normed)
    grad_branch = grad_one.astype(jnp.bfloat16)
    grad_bias_output = jnp.sum(grad_branch.astype(jnp.float32), axis=sum_axes)
    grad_attn_out = jnp.einsum(
        "rsh,rsd->hd", context, grad_branch, preferred_element_type=jnp.float32
    )
    grad_context = jnp.einsum(
        "rsd,hd->rsh", grad_branch, attn_out, preferred_element_type=jnp.float32
    ).astype(jnp.bfloat16)
    stored_keys, stored_values = key_store
    all_keys, all_values = (stored_keys, stored_values)
    weights = jnp.exp(score_block(queries, all_keys, valid_keys) - log_total)
    context_heads = to_heads(grad_context)
    grad_weights = jnp.einsum(
        "rqhd,rkhd->rhqk", context_heads, to_heads(all_values), preferred_element_type=jnp.float32
    )
    inner_sum = jnp.sum(weights * grad_weights, axis=-1, keepdims=True)
    grad_raw = (0.125 * weights * (grad_weights - inner_sum)).astype(jnp.bfloat16)
    grad_queries = jnp.einsum(
        "rhqk,rkhd->rqhd", grad_raw, to_heads(all_keys), preferred_element_type=jnp.float32
    )
    grad_queries = grad_queries.reshape(queries.shape).astype(jnp.bfloat16)
    weights_low = weights.astype(jnp.bfloat16)
    value_terms = jnp.einsum(
        "rhqk,rqhd->rkhd", weights_low, context_heads, preferred_element_type=jnp.float32
    )
    key_terms = jnp.einsum(
        "rhqk,rqhd->rkhd", grad_raw, to_heads(queries), preferred_element_type=jnp.float32
    )
    key_terms = key_terms.reshape(all_keys.shape)
    value_terms = value_terms.reshape(all_values.shape)
    grad_keys, grad_values = (
        lax.psum_scatter(
            key_terms.astype(jnp.bfloat16), "mp", scatter_dimension=1, tiled=True
        ).astype(jnp.float32),
        lax.psum_scatter(
            value_terms.astype(jnp.bfloat16), "mp", scatter_dimension=1, tiled=True
        ).astype(jnp.float32),
    )
    grad_values_low = grad_values.astype(jnp.bfloat16)
    grad_projected = jnp.concatenate(
        [grad_queries, grad_keys.astype(jnp.bfloat16), grad_values_low], axis=-1
    )
    grad_attn_in = jnp.einsum(
        "rsd,rse->de", hidden_low, grad_projected, preferred_element_type=jnp.float32
    )
    grad_hidden = grad_one + jnp.einsum(
        "rse,de->rsd", grad_projected, attn_in, preferred_element_type=jnp.float32
    )
    grad_bias_query = jnp.sum(grad_queries.astype(jnp.float32), axis=sum_axes)
    grad_bias_value = jnp.sum(grad_values_low.astype(jnp.float32), axis=sum_axes)
    grad_shifts = jnp.concatenate(
        [
            grad_bias_query,
            grad_bias_value,
            grad_bias_output,
            grad_shift_one,
            grad_bias_up,
            grad_bias_down,
            grad_shift_two,
        ]
    )
    grad_gains = jnp.concatenate([grad_gain_one, grad_gain_two])
    return (
        grad_hidden,
        (grad_attn_in, grad_attn_out, grad_first, grad_second, grad_shifts, grad_gains),
    )


def reduce_grads(grads):
    grad_attn_in, grad_attn_out, grad_first, grad_second, grad_shifts, grad_gains = grads
    total_in, total_out, total_shifts, total_gains = (
        lax.psum_scatter(grad_attn_in, ("dp", "mp"), scatter_dimension=0, tiled=True),
        lax.psum_scatter(grad_attn_out, ("dp", "mp"), scatter_dimension=1, tiled=True),
        lax.psum_scatter(grad_shifts, ("dp", "mp"), scatter_dimension=0, tiled=True),
        lax.psum_scatter(grad_gains, ("dp", "mp"), scatter_dimension=0, tiled=True),
    )
    total_first, total_second = (
        lax.psum_scatter(
            grad_first.astype(jnp.bfloat16), "dp", scatter_dimension=0, tiled=True
        ).astype(jnp.float32),
        lax.psum_scatter(
            grad_second.astype(jnp.bfloat16), "dp", scatter_dimension=1, tiled=True
        ).astype(jnp.float32),
    )
    return (total_in, total_out, total_first, total_second, total_shifts, total_gains)


BF = jnp.bfloat16
F32 = jnp.float32
MESH = pl.DeviceIdType.MESH
SIDE = 2
DEPTH = 4
PARTNERS = 9


def mm(left, right, left_dim, right_dim):
    return lax.dot_general(
        left, right, (((left_dim,), (right_dim,)), ((), ())), preferred_element_type=F32
    )


def rowsum(values):
    return jnp.sum(values, axis=0, keepdims=True)


def normalize(values):
    centered = values - jnp.mean(values, axis=-1, keepdims=True)
    variance = jnp.mean(centered * centered, axis=-1, keepdims=True)
    scale = lax.rsqrt(variance + EPSILON)
    return centered * scale, scale


def normalize_back(grad, normed, scale):
    along = jnp.mean(grad * normed, axis=-1, keepdims=True)
    return scale * (grad - jnp.mean(grad, axis=-1, keepdims=True) - normed * along)


def layer_sizes(model, heads_width, hidden, pair):
    half = heads_width // 2
    start = 3 * half // 128 * 128
    return types.SimpleNamespace(
        hc=half,
        heads=half // HEAD,
        wide=4 * half,
        start=start,
        qw=-(-half // 128) * 128,
        pad=3 * half - start,
        nr=hidden // 16,
        nc=hidden // 2,
        nl=hidden // 4 if pair else hidden // 2,
        pair=pair,
        sides=2 if pair else 1,
        zs=2 if pair else DEPTH,
        zb=model * 8 // hidden,
    )


def vec_rows(model, sizes):
    lengths = dict(
        qv=4 * sizes.hc, bo=model, beta1=model, b1=2 * sizes.nc, b2=model, beta2=model, g1=model, g2=model
    )
    rows, at = {}, 0
    for name, length in lengths.items():
        rows[name] = at
        at += length // model
    return types.SimpleNamespace(**rows), at


def named(tree):
    if isinstance(tree, dict):
        return types.SimpleNamespace(**{key: named(value) for key, value in tree.items()})
    return [named(value) for value in tree] if isinstance(tree, list) else tree


def fused_kernel(dims, tree, *refs):
    given, outs, scratch, held, made = jax.tree.unflatten(tree, refs)
    lay = [named(a | b | d) for a, b, d in zip(held["lay"], made["lay"], scratch["lay"])]
    r = named(held | made | scratch)
    given, outs = named(given), named(outs)

    def fetch_copies():
        pairs = []
        for at in range(2):
            far, near = given.lay[at], lay[at]
            pairs += [(far.pai, near.pai), (far.pao, near.pao)]
            if at == 0:
                pairs += [(given.hid, r.hid)]
            pairs += [(far.pfi, near.pfi), (far.pfo, near.pfo), (far.psh, near.psh), (far.pga, near.pga)]
        pairs += [(given.len, r.len), (given.cot, r.cot)]
        return [pltpu.make_async_copy(src, dst, r.ins.at[i]) for i, (src, dst) in enumerate(pairs)]

    fetched = fetch_copies()
    for copy in fetched:
        copy.start()
    stored = []

    def store(src, dst):
        copy = pltpu.make_async_copy(src, dst, r.outs.at[len(stored)])
        copy.start()
        stored.append(copy)
    model, tok, seq, layers = dims.model, dims.tok, dims.seq, dims.layers
    half_lanes = model // 2
    dp, mp = lax.axis_index("dp"), lax.axis_index("mp")
    y, c = dp // SIDE, lax.rem(dp, SIDE)
    z, x = mp // SIDE, lax.rem(mp, SIDE)

    def device(c, x, y, z):
        return {"dp": y * SIDE + c, "mp": z * SIDE + x}

    sib = device(1 - c, x, y, z)
    xn, yn = device(c, 1 - x, y, z), device(c, x, 1 - y, z)
    zdev = [device(c, x, y, lax.rem(z + d, DEPTH)) for d in range(1, DEPTH)]
    zpair = z + 1 - 2 * lax.rem(z, 2)
    zn = device(c, x, y, zpair)
    zfar = device(c, x, y, lax.rem(z + 2, DEPTH))

    bar = pltpu.get_barrier_semaphore()
    for step in range(1, DEPTH * SIDE):
        other = lax.rem(mp + step, DEPTH * SIDE)
        pl.semaphore_signal(bar, inc=1, device_id={"dp": dp, "mp": other}, device_id_type=MESH)
    pl.semaphore_signal(bar, inc=1, device_id=sib, device_id_type=MESH)
    pl.semaphore_signal(bar, inc=1, device_id=yn, device_id_type=MESH)

    sent = []

    def remote(src, dst, send, recv, dev):
        return pltpu.make_async_remote_copy(
            src_ref=src, dst_ref=dst, send_sem=send, recv_sem=recv, device_id=dev, device_id_type=MESH
        )

    def push(src, dst, send, recv, dev):
        copy = remote(src, dst, send, recv, dev)
        copy.start()
        sent.append((None, copy))

    def arrived(dst, recv, send):
        remote(dst, dst, send, recv, sib).wait_recv()

    row_core = z // 2
    mine = c == row_core
    half = lax.rem(z, 2)

    def spread(src, land, sends, recvs):
        block = 2 * lax.rem(z, 2) + x
        target = 2 * c + z // 2
        for j in range(2):
            local = (x == j) & (z == target)
            copy = remote(src.at[j], land.at[block], sends.at[j], recvs.at[block], device(c, j, y, target))
            pl.when(local)(pltpu.make_async_copy(src.at[j], land.at[block], recvs.at[block]).start)
            pl.when(jnp.logical_not(local))(copy.start)

    def spread_turn(src, land, sends, recvs, on_chip_send, on_chip_recv):
        target = 2 * c + z // 2
        for j in range(2):
            local = (x == j) & (z == target)
            copy = remote(src.at[j], land.at[0], sends.at[j], recvs.at[0], sib)
            pl.when(jnp.logical_not(local))(copy.wait_send)
        whole = remote(land, land, on_chip_send, on_chip_recv, sib)

        @pl.when(mine)
        def _():
            for block in range(4):
                arrived(land.at[block], recvs.at[block], sends.at[0])
            whole.start()

    def spread_end(land, on_chip_send, on_chip_recv):
        whole = remote(land, land, on_chip_send, on_chip_recv, sib)
        pl.when(mine)(whole.wait_send)
        pl.when(jnp.logical_not(mine))(whole.wait_recv)

    def collect(src, land, sends, recvs):
        @pl.when(mine)
        def _():
            for block in range(4):
                z_to, x_to = 2 * half + block // 2, block % 2
                local = (x == x_to) & (z == z_to)
                slot = land.at[x]
                copy = remote(
                    src.at[block], slot, sends.at[block], recvs.at[x], device(c, x_to, y, z_to)
                )
                pl.when(local)(pltpu.make_async_copy(src.at[block], slot, recvs.at[x]).start)
                pl.when(jnp.logical_not(local))(copy.start)

    def collect_done(src, land, sends, recvs):
        for j in range(2):
            arrived(land.at[j], recvs.at[j], sends.at[0])

        @pl.when(mine)
        def _():
            for block in range(4):
                z_to, x_to = 2 * half + block // 2, block % 2
                local = (x == x_to) & (z == z_to)
                copy = remote(src.at[block], src.at[block], sends.at[block], recvs.at[0], sib)
                pl.when(jnp.logical_not(local))(copy.wait_send)

    chunks = dims.chunks
    every, first, second = pl.ds(0, DEPTH), pl.ds(0, 2), pl.ds(2, 2)
    both = pl.ds(0, 2)

    def view(i, grads, band, z_slice, x_at, y_at):
        kind, layer, which, part = chunks[i]
        full = dims.unit_rows[kind]
        if kind == "P":
            ref = lay[layer].dw if grads else lay[layer].w
            lanes = pl.ds(pl.multiple_of(y_at * half_lanes, 128), half_lanes)
            return ref.at[which, z_slice, x_at, :, lanes]
        if band:
            begin, count = {"a": (0, full - 32), "b": (full - 32, 16), "c": (full - 16, 16)}[band]
        else:
            begin, count = 0, full
        if kind == "A":
            ref = lay[layer].ga
            y_pick = both if y_at is None else y_at
            return ref.at[y_pick, z_slice, x_at, pl.ds(begin, count), pl.ds(part * model, model)]
        ref = lay[layer].dw if grads else lay[layer].w
        lanes = pl.ds(0, model)
        if y_at is not None:
            lanes = pl.ds(pl.multiple_of(y_at * half_lanes, 128), half_lanes)
        return ref.at[which, z_slice, x_at, pl.ds(part * full + begin, count), lanes]

    UP, DOWN, FAR, RELAY = range(4)
    z_far = lax.rem(z + 2, DEPTH)
    z_up, z_down = lax.rem(z + 1, DEPTH), lax.rem(z + DEPTH - 1, DEPTH)
    z_end = DEPTH - 1 - z
    has_up, has_down = z < DEPTH - 1, z > 0
    inner = (z == 1) | (z == 2)
    outer = (z == 0) | (z == 3)
    z_out = jnp.where(z == 1, 0, 3)
    z_in = jnp.where(z == 0, 1, 2)

    def push_if(cond, src, dst, send, recv, dev):
        copy = remote(src, dst, send, recv, dev)
        pl.when(cond)(copy.start)
        sent.append((cond, copy))

    def wait_sent():
        for cond, copy in sent:
            if cond is None:
                copy.wait_send()
            else:
                pl.when(cond)(copy.wait_send)
        sent.clear()

    def arrived_if(cond, dst, recv, send):
        pl.when(cond)(remote(dst, dst, send, recv, sib).wait_recv)

    def at_z(zz):
        return device(c, x, y, zz)

    def line_send(part, send, recv):
        own = part(z)
        push_if(has_up, own, own, send(UP), recv(UP), at_z(z_up))
        push_if(has_down, own, own, send(DOWN), recv(DOWN), at_z(z_down))
        push(own, own, send(FAR), recv(FAR), at_z(z_far))

    def line_relay(part, send, recv):
        far = part(z_far)
        arrived_if(inner, far, recv(FAR), send(FAR))
        push_if(inner, far, far, send(RELAY), recv(RELAY), at_z(z_out))

    def line_end(part, send, recv):
        arrived_if(has_down, part(z_down), recv(UP), send(UP))
        arrived_if(has_up, part(z_up), recv(DOWN), send(DOWN))
        arrived_if(outer, part(z_far), recv(FAR), send(FAR))
        arrived_if(outer, part(z_end), recv(RELAY), send(RELAY))

    def sems(ref_send, ref_recv, i, base):
        return (lambda k: ref_send.at[i, base + k]), (lambda k: ref_recv.at[i, base + k])

    def one(zz):
        return pl.ds(zz, 1)

    def parts_of(i, grads):
        return (
            lambda zz: view(i, grads, "a", one(zz), x, y),
            lambda zz: view(i, grads, "b", one(zz), both, y),
            lambda zz: view(i, grads, "c", one(zz), x, None),
        )

    def gather_sems(i, base):
        return sems(r.gs, r.gr, i, base)

    def gather_push(i, k, piece, dev):
        push(piece, piece, r.gs.at[i, k], r.gr.at[i, k], dev)

    def gather_wait(i, k, piece):
        arrived(piece, r.gr.at[i, k], r.gs.at[i, k])

    z_own, z_other = z // 2, 1 - z // 2

    def pair_view(i, grads, z_slice, x_at, y_at):
        return view(i, grads, None, z_slice, x_at, y_at)

    def pair_0(i):
        gather_push(i, 0, pair_view(i, False, one(z_own), x, y), zfar)

    def pair_1(i):
        gather_wait(i, 0, pair_view(i, False, one(z_other), x, y))
        own = pair_view(i, False, both, x, y)
        gather_push(i, 1, own, xn)
        gather_push(i, 2, own, yn)

    def pair_2(i):
        gather_wait(i, 1, pair_view(i, False, both, 1 - x, y))
        gather_wait(i, 2, pair_view(i, False, both, x, 1 - y))
        gather_push(i, 3, pair_view(i, False, one(0), x, 1 - y), xn)
        gather_push(i, 4, pair_view(i, False, one(1), 1 - x, y), yn)

    def pair_3(i):
        gather_wait(i, 3, pair_view(i, False, one(0), 1 - x, 1 - y))
        gather_wait(i, 4, pair_view(i, False, one(1), 1 - x, 1 - y))

    def whole(i, z_slice, x_at, y_at):
        return view(i, False, None, z_slice, x_at, y_at)

    def line(i):
        return (lambda zz: whole(i, one(zz), x, y)), *gather_sems(i, 0)

    def gather_0(i):
        line_send(*line(i))

    def gather_1(i):
        line_relay(*line(i))

    def gather_2(i):
        line_end(*line(i))
        own = whole(i, every, x, y)
        gather_push(i, 4, own, xn)
        gather_push(i, 5, own, yn)

    def gather_3(i):
        gather_wait(i, 4, whole(i, every, 1 - x, y))
        gather_wait(i, 5, whole(i, every, x, 1 - y))
        gather_push(i, 6, whole(i, first, x, 1 - y), xn)
        gather_push(i, 7, whole(i, second, 1 - x, y), yn)

    def gather_4(i):
        gather_wait(i, 6, whole(i, first, 1 - x, 1 - y))
        gather_wait(i, 7, whole(i, second, 1 - x, 1 - y))

    band_stages = (gather_0, gather_1, gather_2, gather_3, gather_4)
    pair_stages = (pair_0, pair_1, pair_2, pair_3)

    def gather(i, stage):
        stages = pair_stages if chunks[i][0] == "P" else band_stages
        stages[stage](i)

    def add_into(ref, extra):
        total = ref[...].astype(F32)
        for more in extra:
            total = total + more[...].astype(F32)
        ref[...] = total.astype(BF)

    def slots(i, name):
        return getattr(r.red["AFP".index(chunks[i][0])], name).at[dims.slot[i]]

    def reduce_push(i, k, src, dst, dev):
        push(src, dst, r.ss.at[i, k], r.sr.at[i, k], dev)

    def reduce_wait(i, k, dst):
        arrived(dst, r.sr.at[i, k], r.ss.at[i, k])

    def line_reduce_send(part, land, send, recv):
        push_if(has_up, part(z_up), land.at[UP], send(UP), recv(UP), at_z(z_up))
        push_if(has_down, part(z_down), land.at[DOWN], send(DOWN), recv(DOWN), at_z(z_down))
        push_if(outer, part(z_end), land.at[RELAY], send(RELAY), recv(RELAY), at_z(z_in))
        push_if(outer, part(z_far), land.at[FAR], send(FAR), recv(FAR), at_z(z_far))

    def line_reduce_relay(part, land, send, recv):
        @pl.when(inner)
        def _():
            arrived(land.at[RELAY], recv(RELAY), send(RELAY))
            add_into(part(z_far), [land.at[RELAY]])

        push_if(inner, part(z_far), land.at[FAR], send(FAR), recv(FAR), at_z(z_far))

    def line_reduce_end(part, land, send, recv):
        arrived(land.at[FAR], recv(FAR), send(FAR))

        @pl.when(inner)
        def _():
            arrived(land.at[UP], recv(UP), send(UP))
            arrived(land.at[DOWN], recv(DOWN), send(DOWN))
            add_into(part(z), [land.at[FAR], land.at[UP], land.at[DOWN]])

        @pl.when(z == 0)
        def _():
            arrived(land.at[DOWN], recv(DOWN), send(DOWN))
            add_into(part(z), [land.at[FAR], land.at[DOWN]])

        @pl.when(z == DEPTH - 1)
        def _():
            arrived(land.at[UP], recv(UP), send(UP))
            add_into(part(z), [land.at[FAR], land.at[UP]])

    def reduce_sems(i, base):
        return sems(r.ss, r.sr, i, base)

    def band_reduce_0(i):
        over = slots(i, "ad")
        reduce_push(i, 14, view(i, True, "a", first, 1 - x, 1 - y), over.at[0], xn)
        reduce_push(i, 15, view(i, True, "a", second, 1 - x, 1 - y), over.at[1], yn)
        reduce_push(i, 18, view(i, True, "b", every, both, 1 - y), slots(i, "by"), yn)
        reduce_push(i, 19, view(i, True, "c", every, 1 - x, None), slots(i, "cx"), xn)

    def band_reduce_1(i):
        a, b, c_part = parts_of(i, True)
        over, beside = slots(i, "ad"), slots(i, "an")
        reduce_wait(i, 14, over.at[0])
        add_into(view(i, True, "a", first, x, 1 - y), [over.at[0]])
        reduce_push(i, 13, view(i, True, "a", every, x, 1 - y), beside.at[1], yn)
        reduce_wait(i, 15, over.at[1])
        add_into(view(i, True, "a", second, 1 - x, y), [over.at[1]])
        reduce_push(i, 12, view(i, True, "a", every, 1 - x, y), beside.at[0], xn)
        reduce_wait(i, 18, slots(i, "by"))
        add_into(view(i, True, "b", every, both, y), [slots(i, "by")])
        line_reduce_send(b, slots(i, "bz"), *reduce_sems(i, 4))
        reduce_wait(i, 19, slots(i, "cx"))
        add_into(view(i, True, "c", every, x, None), [slots(i, "cx")])
        line_reduce_send(c_part, slots(i, "cz"), *reduce_sems(i, 8))

    def band_reduce_2(i):
        a, b, c_part = parts_of(i, True)
        beside = slots(i, "an")
        reduce_wait(i, 12, beside.at[0])
        reduce_wait(i, 13, beside.at[1])
        add_into(view(i, True, "a", every, x, y), [beside.at[0], beside.at[1]])
        line_reduce_send(a, slots(i, "az"), *reduce_sems(i, 0))
        line_reduce_relay(b, slots(i, "bz"), *reduce_sems(i, 4))
        line_reduce_relay(c_part, slots(i, "cz"), *reduce_sems(i, 8))

    def band_reduce_3(i):
        a, b, c_part = parts_of(i, True)
        line_reduce_end(b, slots(i, "bz"), *reduce_sems(i, 4))
        reduce_push(i, 16, view(i, True, "b", one(z), 1 - x, y), slots(i, "bx"), xn)
        line_reduce_end(c_part, slots(i, "cz"), *reduce_sems(i, 8))
        reduce_push(i, 17, view(i, True, "c", one(z), x, 1 - y), slots(i, "cy"), yn)
        line_reduce_relay(a, slots(i, "az"), *reduce_sems(i, 0))

    def band_reduce_4(i):
        line_reduce_end(parts_of(i, True)[0], slots(i, "az"), *reduce_sems(i, 0))
        reduce_wait(i, 16, slots(i, "bx"))
        reduce_wait(i, 17, slots(i, "cy"))
        total = jnp.concatenate(
            [
                view(i, True, "a", one(z), x, y)[...].astype(F32)[0],
                (view(i, True, "b", one(z), x, y)[...].astype(F32) + slots(i, "bx")[...].astype(F32))[0],
                (view(i, True, "c", one(z), x, y)[...].astype(F32) + slots(i, "cy")[...].astype(F32))[0],
            ],
            axis=0,
        )
        reduce_store(i, total)

    def line_reduce(i):
        return (lambda zz: view(i, True, None, one(zz), x, y)), slots(i, "az"), *reduce_sems(i, 0)

    def whole_reduce_0(i):
        over = slots(i, "ad")
        reduce_push(i, 4, view(i, True, None, first, 1 - x, 1 - y), over.at[0], xn)
        reduce_push(i, 5, view(i, True, None, second, 1 - x, 1 - y), over.at[1], yn)

    def whole_reduce_1(i):
        over, beside = slots(i, "ad"), slots(i, "an")
        reduce_wait(i, 4, over.at[0])
        add_into(view(i, True, None, first, x, 1 - y), [over.at[0]])
        reduce_push(i, 6, view(i, True, None, every, x, 1 - y), beside.at[1], yn)
        reduce_wait(i, 5, over.at[1])
        add_into(view(i, True, None, second, 1 - x, y), [over.at[1]])
        reduce_push(i, 7, view(i, True, None, every, 1 - x, y), beside.at[0], xn)

    def whole_reduce_2(i):
        beside = slots(i, "an")
        reduce_wait(i, 6, beside.at[1])
        reduce_wait(i, 7, beside.at[0])
        add_into(view(i, True, None, every, x, y), [beside.at[0], beside.at[1]])
        line_reduce_send(*line_reduce(i))

    def whole_reduce_3(i):
        line_reduce_relay(*line_reduce(i))

    def whole_reduce_4(i):
        line_reduce_end(*line_reduce(i))
        reduce_store(i, view(i, True, None, one(z), x, y)[...].astype(F32)[0])

    whole_reduces = (whole_reduce_0, whole_reduce_1, whole_reduce_2, whole_reduce_3, whole_reduce_4)

    def pair_reduce_0(i):
        over = slots(i, "ad")
        reduce_push(i, 3, pair_view(i, True, one(0), 1 - x, 1 - y), over.at[0], xn)
        reduce_push(i, 4, pair_view(i, True, one(1), 1 - x, 1 - y), over.at[1], yn)

    def pair_reduce_1(i):
        over, beside = slots(i, "ad"), slots(i, "an")
        reduce_wait(i, 3, over.at[0])
        add_into(pair_view(i, True, one(0), x, 1 - y), [over.at[0]])
        reduce_push(i, 2, pair_view(i, True, both, x, 1 - y), beside.at[1], yn)
        reduce_wait(i, 4, over.at[1])
        add_into(pair_view(i, True, one(1), 1 - x, y), [over.at[1]])
        reduce_push(i, 1, pair_view(i, True, both, 1 - x, y), beside.at[0], xn)

    def pair_reduce_2(i):
        beside = slots(i, "an")
        reduce_wait(i, 1, beside.at[0])
        reduce_wait(i, 2, beside.at[1])
        add_into(pair_view(i, True, both, x, y), [beside.at[0], beside.at[1]])
        reduce_push(i, 0, pair_view(i, True, one(z_other), x, y), slots(i, "az"), zfar)

    def pair_reduce_3(i):
        far = slots(i, "az")
        reduce_wait(i, 0, far)
        own = pair_view(i, True, one(z_own), x, y)
        reduce_store(i, (own[...].astype(F32) + far[...].astype(F32))[0])

    def reduce_store(i, total):
        kind, layer, which, part = chunks[i]
        send, land = slots(i, "fsend"), slots(i, "fland")
        if kind == "A":
            rows = total.shape[0] // 2
            cols = slice(part * model, (part + 1) * model)
            lay[layer].da[c, :, cols] = jnp.where(c == 0, total[:rows], total[rows:])
            send[...] = jnp.where(c == 0, total[rows:], total[:rows])
        else:
            full = dims.unit_rows[kind]
            rows, lanes = pl.ds(part * full, full), total.shape[1] // 2
            lay[layer].df[c, which, rows, :] = jnp.where(c == 0, total[:, :lanes], total[:, lanes:])
            send[...] = jnp.where(c == 0, total[:, lanes:], total[:, :lanes])
        push(send, land, r.fs.at[i], r.fr.at[i], sib)

    def reduce_out(i):
        kind, layer, which, part = chunks[i]
        land = slots(i, "fland")
        arrived(land, r.fr.at[i], r.fs.at[i])
        if kind == "A":
            lay[layer].da[1 - c, :, part * model : (part + 1) * model] = land[...]
            if part == 0:
                store(lay[layer].da, outs.lay[layer].da)
        else:
            full = dims.unit_rows[kind]
            lay[layer].df[1 - c, which, pl.ds(part * full, full), :] = land[...]
            if part == layers[layer].nr // full - 1:
                store(lay[layer].df.at[:, which], outs.lay[layer].df.at[:, which])

    band_reduces = (band_reduce_0, band_reduce_1, band_reduce_2, band_reduce_3, band_reduce_4)
    pair_reduces = (pair_reduce_0, pair_reduce_1, pair_reduce_2, pair_reduce_3)

    def reduce(i, stage):
        stages = pair_reduces if chunks[i][0] == "P" else band_reduces
        if chunks[i][0] in dims.whole:
            stages = whole_reduces
        if stage < len(stages):
            stages[stage](i)

    def total_step(work, land, step, sends, recvs):
        dev = (sib, xn, yn, zn, zfar)[step]
        push(work.at[step], land.at[step], sends.at[step], recvs.at[step], dev)

    def total_add(work, land, step, sends, recvs):
        arrived(land.at[step], recvs.at[step], sends.at[step])
        work[step + 1] = work[step] + land[step]

    exchanges = []

    def exchange(part):
        slot = len(exchanges) % 2
        r.xs[slot] = part.astype(BF)
        copy = remote(r.xs.at[slot], r.xr.at[slot], r.es.at[slot], r.er.at[slot], sib)
        copy.start()
        exchanges.append(copy)

        def finish():
            copy.wait()
            return r.xs[slot].astype(F32) + r.xr[slot].astype(F32)

        return finish

    quarter = tok // 2
    own_rows = pl.ds(pl.multiple_of(c * quarter, 16), quarter)
    other_rows = pl.ds(pl.multiple_of((1 - c) * quarter, 16), quarter)

    class Share:
        def __init__(self, ref, k):
            blocks = len(ref.shape) == 4
            self.own = pl.ds(2 * c, 2) if blocks else own_rows
            self.other = pl.ds(2 - 2 * c, 2) if blocks else other_rows
            self.ref, self.k = ref, k
            piece = ref.at[half, self.own]
            push(piece, piece, r.ps.at[k, 0], r.pr.at[k, 0], zn)

        def turn(self):
            got, k = self.ref.at[1 - half, self.own], self.k
            arrived(got, r.pr.at[k, 0], r.ps.at[k, 0])
            push(got, got, r.ps.at[k, 1], r.pr.at[k, 1], sib)

        def end(self):
            k = self.k
            arrived(self.ref.at[1 - half, self.other], r.pr.at[k, 1], r.ps.at[k, 1])

    class Fold:
        def __init__(self, make, k):
            self.make, self.k = make, k
            r.px[k] = make(1 - half, False).astype(BF)
            push(r.px.at[k, other_rows], r.prx.at[k], r.ps.at[k, 2], r.pr.at[k, 2], sib)

        def keep(self):
            self.own = exchange(self.make(half, True))

        def cross(self):
            k = self.k
            arrived(r.prx.at[k], r.pr.at[k, 2], r.ps.at[k, 2])
            r.pz[k] = (r.px[k, own_rows, :].astype(F32) + r.prx[k].astype(F32)).astype(BF)
            push(r.pz.at[k], r.pzr.at[k, c], r.ps.at[k, 3], r.pr.at[k, 3], zn)

        def turn(self):
            k = self.k
            got = r.pzr.at[k, c]
            arrived(got, r.pr.at[k, 3], r.ps.at[k, 3])
            push(got, got, r.ps.at[k, 4], r.pr.at[k, 4], sib)

        def end(self):
            k = self.k
            arrived(r.pzr.at[k, 1 - c], r.pr.at[k, 4], r.ps.at[k, 4])
            return self.own() + r.pzr[k].reshape(tok, model).astype(F32)

    def vec_row(row):
        return r.vw[5, row : row + 1, :]

    def layer_vecs(at):
        sizes, rows, base = layers[at], dims.rows_of[at], dims.base[at]
        if sizes.hc * 2 == model:
            qv = r.vw[5, pl.ds(base + rows.qv + c, 1), :]
        else:
            both = vec_row(base + rows.qv)
            qv = jnp.where(c == 0, both[:, : 2 * sizes.hc], both[:, 2 * sizes.hc :])
        span = sizes.nc // model
        b1 = [r.vw[5, pl.ds(base + rows.b1 + c * span + s, 1), :] for s in range(span)]
        if sizes.pair:
            cut = 2 * sizes.nr
            b1 = [jnp.concatenate([jnp.where(half == 0, v[:, :cut], v[:, cut:]) for v in b1], axis=1)]
        found = types.SimpleNamespace(bq=qv[:, : sizes.hc], bv=qv[:, sizes.hc :], b1=b1)
        for name, row in vars(rows).items():
            if not hasattr(found, name):
                setattr(found, name, vec_row(base + row))
        return found

    kept = lay
    wa = [one_layer.wa for one_layer in lay]
    weights = [one_layer.w for one_layer in lay]

    def order_rows(at, part):
        gathered, whole = lay[at].ga, wa[at]
        cols = slice(part * model, (part + 1) * model)
        rows = gathered.shape[3] // 2
        span = DEPTH * 2 * rows
        for y_at in range(SIDE):
            for z_at in range(DEPTH):
                left = gathered[y_at, z_at, 0, :, cols].astype(F32)
                right = gathered[y_at, z_at, 1, :, cols].astype(F32)
                for core in range(SIDE):
                    own = slice(core * rows, (core + 1) * rows)
                    both = jnp.concatenate([left[own], right[own]], axis=0).astype(BF)
                    begin = (y_at * SIDE + core) * span + z_at * 2 * rows
                    whole[begin : begin + 2 * rows, cols] = both

    def store_grad_rows(at, y_at, value, cols):
        blocks = lay[at].ga
        rows = blocks.shape[3] // 2
        span = DEPTH * 2 * rows
        for z_at in range(DEPTH):
            for x_at in range(SIDE):
                begin = (z_at * 2 + x_at) * rows
                both = [value[begin : begin + rows], value[span + begin : span + begin + rows]]
                blocks[y_at, z_at, x_at, :, cols] = jnp.concatenate(both, axis=0).astype(BF)

    def head_kv(at, h):
        sizes, kv = layers[at], kept[at].kv
        k = kv[:, :, h * HEAD : (h + 1) * HEAD].reshape(seq, HEAD)
        v = kv[:, :, sizes.hc + h * HEAD : sizes.hc + (h + 1) * HEAD].reshape(seq, HEAD)
        return k, v

    def attention(at):
        sizes, keep = layers[at], kept[at]
        lane = lax.broadcasted_iota(jnp.int32, (1, model), 1)
        first_lane = (y * SIDE + row_core) * group + x
        entry = vec_row(dims.length_row)
        entry = jnp.where(lane == first_lane, 256.0 * entry, jnp.where(lane == first_lane + 2, entry, 0.0))
        length = jnp.sum(entry, axis=1, keepdims=True)
        valid = lax.broadcasted_iota(jnp.int32, (1, seq), 1).astype(F32) < length
        for h in range(sizes.heads):
            q = keep.q[:, h * HEAD : (h + 1) * HEAD]
            k, v = head_kv(at, h)
            scores = jnp.where(valid, mm(q, k, 1, 1) * 0.125, NEGATIVE)
            exponent = jnp.exp(scores - jnp.max(scores, axis=1, keepdims=True))
            low = (exponent / jnp.sum(exponent, axis=1, keepdims=True)).astype(BF)
            keep.a[h] = low
            begin = sizes.pad + h * HEAD
            keep.ctx[:, begin : begin + HEAD] = mm(low, v, 1, 0).astype(BF)

    def attention_back(at, grad_ctx):
        sizes, keep = layers[at], kept[at]
        dkv, dq = lay[at].dkv, lay[at].dq
        for h in range(sizes.heads):
            q = keep.q[:, h * HEAD : (h + 1) * HEAD]
            k, v = head_kv(at, h)
            begin = sizes.pad + h * HEAD
            dc = grad_ctx[:, begin : begin + HEAD]
            low = keep.a[h]
            a = low.astype(F32)
            da = mm(dc, v, 1, 1)
            inner = jnp.sum(a * da, axis=1, keepdims=True)
            ds = (0.125 * a * (da - inner)).astype(BF)
            dq[:, h * HEAD : (h + 1) * HEAD] = mm(ds, k, 1, 0).astype(BF)
            dk = mm(ds, q, 0, 0).astype(BF).reshape(2, tok, HEAD)
            dv = mm(low, dc, 0, 0).astype(BF).reshape(2, tok, HEAD)
            dkv[:, :, h * HEAD : (h + 1) * HEAD] = dk
            dkv[:, :, sizes.hc + h * HEAD : sizes.hc + (h + 1) * HEAD] = dv

    def block(at, which, b):
        sizes = layers[at]
        w = weights[at][which, b * sizes.zb : (b + 1) * sizes.zb]
        return w.reshape(model, model)

    def up(at, side):
        sizes, keep = layers[at], kept[at]
        for b in range(sizes.nl // model):
            cols = slice(b * model, (b + 1) * model)
            u = mm(keep.hb[side], block(at, 0, b), 1, 1) + vecs[at].b1[b]
            phi = 0.5 * (1.0 + lax.erf(u * 0.7071067811865476))
            keep.g[side, :, cols] = (u * phi).astype(BF)
            density = jnp.exp(u * u * -0.5) * 0.3989422804014327
            keep.gp[side, :, cols] = (phi + u * density).astype(BF)

    def times_block(at, which, side):
        sizes, keep = layers[at], kept[at]
        total = None
        for b in range(sizes.nl // model):
            term = mm(keep.g[side, :, b * model : (b + 1) * model], block(at, which, b), 1, 0)
            total = term if total is None else total + term
        return total

    def weight_grad(at, which, right):
        sizes, keep = layers[at], kept[at]
        span = model // 2
        zb = sizes.zb // 2
        rows = sizes.sides * tok
        wide = right[...].reshape(rows, model)
        for b in range(sizes.nl // span):
            left = keep.g[:, :, b * span : (b + 1) * span].reshape(rows, span)
            value = mm(left, wide, 0, 0).astype(BF)
            keep.dw[which, b * zb : (b + 1) * zb] = value.reshape(zb, 2, sizes.nr, model)


    def pack_a(at):
        sizes, width = layers[at], 2 * layers[at].hc
        rows_in = lay[at].pai[...].astype(F32)
        rows_out = lay[at].pao[...].astype(F32)
        halves = []
        for h in range(2):
            own = slice(h * sizes.hc, (h + 1) * sizes.hc)
            pieces = [rows_in[:, p * width : (p + 1) * width][:, own] for p in (1, 2, 0)]
            halves.append(jnp.concatenate(pieces + [rows_out[:, own]], axis=1))
        send = lay[at].asend
        send[...] = jnp.where(c == 0, halves[1], halves[0])
        if at == 0:
            pl.semaphore_wait(bar, PARTNERS)
        push(send, lay[at].ar, r.is_.at[2 * at], r.ir.at[2 * at], sib)
        return jnp.where(c == 0, halves[0], halves[1])

    def pack_f(at):
        sizes = layers[at]
        first = lay[at].pfi[...].astype(F32).T
        second = lay[at].pfo[...].astype(F32)
        if dims.turned[at]:
            second = second.T
        send, own = lay[at].fsend, []
        for which, value in enumerate((first, second)):
            low_half, high_half = value[: sizes.nr], value[sizes.nr :]
            own.append(jnp.where(c == 0, low_half, high_half))
            send[which] = jnp.where(c == 0, high_half, low_half).astype(BF)
        push(send, lay[at].fr, r.is_.at[2 * at + 1], r.ir.at[2 * at + 1], sib)
        return own

    def prepare_a(at, own):
        land, blocks = lay[at].ar, lay[at].ga
        arrived(land, r.ir.at[2 * at], r.is_.at[2 * at])
        other = land[...]
        pair = [jnp.where(c == 0, own, other), jnp.where(c == 0, other, own)]
        blocks[y, z, x] = jnp.concatenate(pair, axis=0).astype(BF)

    def prepare_f(at, own):
        land = lay[at].fr
        arrived(land, r.ir.at[2 * at + 1], r.is_.at[2 * at + 1])
        lanes = pl.ds(pl.multiple_of(y * half_lanes, 128), half_lanes)
        for which in range(2):
            other = land[which].astype(F32)
            pair = [jnp.where(c == 0, own[which], other), jnp.where(c == 0, other, own[which])]
            weights[at][which, z_own if layers[at].pair else z, x, :, lanes] = jnp.concatenate(pair, axis=1).astype(BF)

    group = dims.group
    per_row = model // group
    index = dp * DEPTH * SIDE + mp

    def targets(at_group):
        result, begin = jnp.full_like(at_group, dims.length_row * per_row) + dp, 0
        for at, sizes in enumerate(layers):
            base = dims.base[at] * per_row
            head, count_b = sizes.hc // group, sizes.nr // group
            up_at = dims.rows_of[at].b1 * per_row
            count = dims.shift_groups[at]
            g = index * count + (at_group - begin)
            w = g % (2 * head)
            qv = (w // head) * (2 * head) + (g // (2 * head)) * head + w % head
            b = g - up_at
            up_to = up_at + ((b % (2 * count_b)) // count_b) * (8 * count_b)
            up_to = up_to + (b // (2 * count_b)) * count_b + b % count_b
            place = jnp.where(g < 4 * head, qv, jnp.where((b >= 0) & (b < 16 * count_b), up_to, g))
            inside = (at_group >= begin) & (at_group < begin + count)
            result = jnp.where(inside, base + place, result)
            begin += count
            count = dims.gain_groups[at]
            place = dims.rows_of[at].g1 * per_row + index * count + (at_group - begin)
            inside = (at_group >= begin) & (at_group < begin + count)
            result = jnp.where(inside, base + place, result)
            begin += count
        return result // per_row, result % per_row

    groups = dims.vec_rows
    lane_group = lax.broadcasted_iota(jnp.int32, (groups, dims.lanes), 1) // group
    lane_own = lane_group == lax.broadcasted_iota(jnp.int32, (groups, dims.lanes), 0)

    def place_masks():
        down = lax.broadcasted_iota(jnp.int32, (groups, 1), 0)
        across = lax.broadcasted_iota(jnp.int32, (1, groups), 1)
        row_down, place_down = targets(down)
        row_across, _ = targets(across)
        lane = lax.broadcasted_iota(jnp.int32, (groups, model), 1) // group
        to_row = jnp.where(row_across == down, 1.0, 0.0).astype(BF)
        from_row = jnp.where(row_down == across, 1.0, 0.0).astype(BF)
        return lane == place_down, to_row, from_row

    def pack_vectors():
        lengths = r.len[...].astype(F32).reshape(1, 2) * jnp.where(mp == 0, 1.0, 0.0)
        high = jnp.floor(lengths * (1.0 / 256.0))
        pieces = []
        for own in lay:
            pieces += [own.psh[...].astype(F32).reshape(1, -1), own.pga[...].astype(F32).reshape(1, -1)]
        pieces += [high, lengths - 256.0 * high]
        used = sum(p.shape[1] for p in pieces)
        values = jnp.concatenate(pieces + [jnp.zeros((1, dims.lanes - used), F32)], axis=1)
        spread_out = jnp.where(lane_own, values, 0.0).astype(BF)
        i = lax.broadcasted_iota(jnp.int32, (dims.lanes, model), 0) % group
        j = lax.broadcasted_iota(jnp.int32, (dims.lanes, model), 1) % group
        r.hot[...] = jnp.where(i == j, 1.0, 0.0).astype(BF)
        in_place, to_row, _ = place_masks()
        wide = jnp.where(in_place, mm(spread_out, r.hot[...], 1, 0), 0.0).astype(BF)
        return mm(to_row, wide, 1, 0)

    def unpack_vectors(values):
        in_place, _, from_row = place_masks()
        total, rest = None, values
        for _ in range(3):
            low_part = rest.astype(BF)
            rest = rest - low_part.astype(F32)
            wide = jnp.where(in_place, mm(from_row, low_part, 1, 0), 0.0).astype(BF)
            term = jnp.where(lane_own, mm(wide, r.hot[...], 1, 1), 0.0)
            total = term if total is None else total + term
        return rowsum(total)

    vecs = []
    block_shape = (4, tok // 4, model)

    def tokens(at, side):
        return kept[at].xb[side].reshape(tok, model)

    def project_kv(at, side):
        sizes, keep = layers[at], kept[at]
        kv = mm(tokens(at, side), wa[at][:, : 2 * sizes.hc], 1, 0)
        keep.kv[side, :, : sizes.hc] = kv[:, : sizes.hc].astype(BF)
        keep.kv[side, :, sizes.hc :] = (kv[:, sizes.hc :] + vecs[at].bv).astype(BF)

    def project_q(at):
        sizes, keep = layers[at], kept[at]
        q = mm(tokens(at, half), wa[at][:, 2 * sizes.hc : 2 * sizes.hc + sizes.qw], 1, 0)
        keep.q[...] = (q[:, : sizes.hc] + vecs[at].bq).astype(BF)

    def attend_out(at):
        return mm(kept[at].ctx[...], wa[at][:, layers[at].start :], 1, 1)

    def norm_one(at, base, branch):
        keep, v = kept[at], vecs[at]
        normed, scale = normalize(base + branch + v.bo)
        keep.n1[...] = normed
        keep.s1[...] = scale
        result = normed * v.g1 + v.beta1
        keep.hb[half if layers[at].pair else 0] = result.astype(BF)
        return result

    def norm_two(at, base, branch):
        keep, v = kept[at], vecs[at]
        normed, scale = normalize(base + branch + v.b2)
        keep.n2[...] = normed
        keep.s2[...] = scale
        return normed * v.g2 + v.beta2

    if layers[1].pad:
        kept[1].ctx[...] = jnp.zeros_like(kept[1].ctx)
        lay[1].dq[...] = jnp.zeros_like(lay[1].dq)
    for copy in fetched[:2]:
        copy.wait()
    own_a0 = pack_a(0)
    prepare_a(0, own_a0)
    gather(0, 0)
    for copy in fetched[3:5]:
        copy.wait()
    own_f0 = pack_f(0)
    for copy in fetched[5:]:
        copy.wait()
    own_a1 = pack_a(1)
    r.vw[0] = pack_vectors()
    gather(0, 1)
    fetched[2].wait()
    spread(r.hid, kept[0].xb.at[lax.rem(z // 2, 2)], r.hs, r.hr)
    total_step(r.vw, r.vl, 0, r.vs, r.vr)
    total_add(r.vw, r.vl, 0, r.vs, r.vr)
    total_step(r.vw, r.vl, 1, r.vs, r.vr)
    prepare_a(1, own_a1)
    gather(1, 0)
    gather(0, 2)
    gather(1, 1)
    total_add(r.vw, r.vl, 1, r.vs, r.vr)
    prepare_f(0, own_f0)
    own_f1 = pack_f(1)
    spread_turn(r.hid, kept[0].xb.at[half], r.hs, r.hr, r.os.at[0], r.os.at[1])
    spread_end(kept[0].xb.at[half], r.os.at[0], r.os.at[1])
    total_step(r.vw, r.vl, 2, r.vs, r.vr)
    gather(2, 0)
    gather(1, 2)
    share_hid = Share(kept[0].xb, 2)
    total_add(r.vw, r.vl, 2, r.vs, r.vr)
    gather(0, 3)
    prepare_f(1, own_f1)
    gather(3, 0)
    total_step(r.vw, r.vl, 3, r.vs, r.vr)
    gather(1, 3)
    total_add(r.vw, r.vl, 3, r.vs, r.vr)
    gather(2, 1)
    total_step(r.vw, r.vl, 4, r.vs, r.vr)
    share_hid.turn()
    gather(3, 1)
    gather(4, 0)
    share_hid.end()
    gather(0, 4)
    total_add(r.vw, r.vl, 4, r.vs, r.vr)
    vecs.extend([layer_vecs(0), layer_vecs(1)])
    order_rows(0, 0)
    project_kv(0, half)
    gather(1, 4)
    order_rows(0, 1)
    project_q(0)
    project_kv(0, 1 - half)
    gather(5, 0)
    attention(0)
    gather(4, 1)
    spread(r.cot, r.cin, r.cs, r.cr)
    gather(2, 2)
    branch = exchange(attend_out(0))
    branch = branch()
    gather(5, 1)
    normed = norm_one(0, tokens(0, half).astype(F32), branch)
    share_normed = Share(kept[0].hb, 0)
    gather(3, 2)
    gather(2, 3)
    gather(6, 0)
    gather(4, 2)
    up(0, half)
    share_normed.turn()
    gather(3, 3)
    share_normed.end()
    up(0, 1 - half)
    gather(6, 1)
    gather(5, 2)
    down = Fold(lambda side, own: times_block(0, 1, side), 0)
    down.keep()
    down.cross()
    gather(4, 3)
    down.turn()
    spread_turn(r.cot, r.cin, r.cs, r.cr, r.os.at[2], r.os.at[3])
    gather(6, 2)
    branch = down.end()
    middle = norm_two(0, normed, branch)
    kept[1].xb[half] = middle.astype(BF).reshape(block_shape)
    share_middle = Share(kept[1].xb, 3)
    gather(4, 4)
    order_rows(1, 0)
    project_kv(1, half)
    project_q(1)
    gather(5, 3)
    share_middle.turn()
    share_middle.end()
    project_kv(1, 1 - half)
    spread_end(r.cin, r.os.at[2], r.os.at[3])
    attention(1)
    gather(6, 3)
    branch = exchange(attend_out(1))
    branch = branch()
    gather(5, 4)
    normed = norm_one(1, middle, branch)
    up(1, 0)
    gather(6, 4)
    branch = exchange(times_block(1, 1, 0))
    branch = branch()
    final = norm_two(1, normed, branch)
    r.oblk[...] = final.astype(BF).reshape(r.oblk.shape)
    collect(r.oblk, r.oland, r.ys, r.yr)
    wait_sent()

    r.vw[0] = jnp.zeros_like(r.vw[0])
    once = jnp.where(c == 0, 1.0, 0.0)

    def put_vec(at, name, value):
        row = dims.base[at] + getattr(dims.rows_of[at], name)
        r.vw[0, row : row + 1, :] = value * once

    def back_two(at, grad):
        keep, v = kept[at], vecs[at]
        n2 = keep.n2[...]
        put_vec(at, "g2", rowsum(grad * n2))
        put_vec(at, "beta2", rowsum(grad))
        dz2 = normalize_back(grad * v.g2, n2, keep.s2[...])
        low_dz2 = dz2.astype(BF)
        keep.eo[half if layers[at].pair else 0] = low_dz2
        put_vec(at, "b2", rowsum(low_dz2.astype(F32)))
        return dz2

    def back_up(at):
        sizes, keep = layers[at], kept[at]
        base = dims.base[at] + dims.rows_of[at].b1
        span, sums = sizes.nc // model, []
        for b in range(sizes.nl // model):
            cols = slice(b * model, (b + 1) * model)
            total = None
            for side in range(sizes.sides):
                dg = mm(keep.eo[side], block(at, 1, b), 1, 1)
                du = (dg * keep.gp[side, :, cols].astype(F32)).astype(BF)
                keep.g[side, :, cols] = du
                term = rowsum(du.astype(F32))
                total = term if total is None else total + term
            sums.append(total)
        if sizes.pair:
            cut = 2 * sizes.nr
            blank = jnp.zeros((1, cut), F32)
            pieces = [sums[0][:, b * cut : (b + 1) * cut] for b in range(span)]
            sums = [
                jnp.concatenate([jnp.where(half == 0, p, blank), jnp.where(half == 0, blank, p)], axis=1)
                for p in pieces
            ]
        for b, total in enumerate(sums):
            r.vw[0, pl.ds(base + c * span + b, 1), :] = total

    def back_one(at, grad):
        keep, v = kept[at], vecs[at]
        n1 = keep.n1[...]
        put_vec(at, "g1", rowsum(grad * n1))
        put_vec(at, "beta1", rowsum(grad))
        dz1 = normalize_back(grad * v.g1, n1, keep.s1[...])
        r.eo[...] = dz1.astype(BF)
        put_vec(at, "bo", rowsum(r.eo[...].astype(F32)))
        grad_ctx = mm(r.eo[...], wa[at][:, layers[at].start :], 1, 0).astype(BF)
        return dz1, grad_ctx

    def bias_sums(at):
        sizes, dkv, dq = layers[at], lay[at].dkv, lay[at].dq
        qsum = rowsum(dq[:, : sizes.hc].astype(F32))
        vsum = rowsum(dkv[:, :, sizes.hc :].reshape(seq, sizes.hc).astype(F32))
        both = jnp.concatenate([qsum, vsum], axis=1)
        row = dims.base[at] + dims.rows_of[at].qv
        if 2 * sizes.hc == model:
            r.vw[0, pl.ds(row + c, 1), :] = both
        else:
            blank = jnp.zeros_like(both)
            left, right = jnp.where(c == 0, both, blank), jnp.where(c == 0, blank, both)
            r.vw[0, row : row + 1, :] = jnp.concatenate([left, right], axis=1)

    def projection_grad(at, part):
        sizes, keep = layers[at], kept[at]
        begin, end = part * model, (part + 1) * model
        for y_at in range(SIDE):
            rows = slice(y_at * half_lanes, (y_at + 1) * half_lanes)
            pieces = []
            if begin == 0:
                every_token = keep.xb[:, :, :, rows].reshape(seq, half_lanes)
                grads = keep.dkv[...].reshape(seq, 2 * sizes.hc)
                pieces.append(mm(every_token, grads, 0, 0))
            if end > 2 * sizes.hc:
                own = keep.xb[half, :, :, rows].reshape(tok, half_lanes)
                query = mm(own, keep.dq[...], 0, 0)
                output = mm(r.eo[:, rows], keep.ctx[...], 0, 0)
                if sizes.pad:
                    apart = sizes.start - 2 * sizes.hc
                    pieces += [query[:, :apart], query[:, apart:] + output]
                else:
                    pieces += [query, output]
            value = pieces[0] if len(pieces) == 1 else jnp.concatenate(pieces, axis=1)
            store_grad_rows(at, y_at, value, slice(begin, end))

    def back_hidden(at, side, own):
        sizes, keep = layers[at], kept[at]
        total = mm(keep.dkv[side], wa[at][:, : 2 * sizes.hc], 1, 1)
        if own:
            begin = 2 * sizes.hc
            total = total + mm(keep.dq[...], wa[at][:, begin : begin + keep.dq.shape[1]], 1, 1)
        return total

    grad = r.cin[...].reshape(tok, model).astype(F32)
    dz2 = back_two(1, grad)
    weight_grad(1, 1, kept[1].eo)
    reduce(6, 0)
    back_up(1)
    branch = exchange(times_block(1, 0, 0))
    weight_grad(1, 0, kept[1].hb)
    reduce(5, 0)
    branch = branch()
    dz1, grad_ctx = back_one(1, dz2 + branch)
    attention_back(1, grad_ctx)
    down = Fold(lambda side, own: back_hidden(1, side, own), 2)
    down.keep()
    down.cross()
    reduce(6, 1)
    projection_grad(1, 0)
    bias_sums(1)
    reduce(4, 0)
    down.turn()
    branch = down.end()
    dz2 = back_two(0, dz1 + branch)
    share_grad = Share(kept[0].eo, 1)
    reduce(5, 1)
    reduce(4, 1)
    share_grad.turn()
    share_grad.end()
    weight_grad(0, 1, kept[0].eo)
    reduce(3, 0)
    back_up(0)
    weight_grad(0, 0, kept[0].hb)
    reduce(2, 0)
    up_back = Fold(lambda side, own: times_block(0, 0, side), 1)
    up_back.keep()
    reduce(3, 1)
    up_back.cross()
    reduce(2, 1)
    reduce(6, 2)
    reduce(5, 2)
    up_back.turn()
    collect_done(r.oblk, r.oland, r.ys, r.yr)
    store(r.oland, outs.out)
    branch = up_back.end()
    dz1, grad_ctx = back_one(0, dz2 + branch)
    attention_back(0, grad_ctx)
    reduce(6, 3)
    projection_grad(0, 1)
    reduce(1, 0)
    projection_grad(0, 0)
    bias_sums(0)
    total_step(r.vw, r.vl, 0, r.ws, r.wr)
    reduce(4, 2)
    reduce(0, 0)
    total_add(r.vw, r.vl, 0, r.ws, r.wr)
    reduce(3, 2)
    to_hidden = Fold(lambda side, own: back_hidden(0, side, own), 3)
    reduce(6, 4)
    total_step(r.vw, r.vl, 1, r.ws, r.wr)
    to_hidden.keep()
    to_hidden.cross()
    reduce(1, 1)
    total_add(r.vw, r.vl, 1, r.ws, r.wr)
    total_step(r.vw, r.vl, 2, r.ws, r.wr)
    reduce(2, 2)
    to_hidden.turn()
    reduce(0, 1)
    reduce(5, 3)
    reduce(1, 2)
    total_add(r.vw, r.vl, 2, r.ws, r.wr)
    reduce(4, 3)
    reduce(2, 3)
    reduce(1, 3)
    reduce(3, 3)
    total_step(r.vw, r.vl, 3, r.ws, r.wr)
    reduce(0, 2)
    reduce(0, 3)
    branch = to_hidden.end()
    reduce(1, 4)
    total_add(r.vw, r.vl, 3, r.ws, r.wr)
    reduce_out(6)
    reduce(5, 4)
    reduce_out(1)
    reduce(4, 4)
    reduce_out(2)
    total_step(r.vw, r.vl, 4, r.ws, r.wr)
    reduce_out(5)
    reduce_out(3)
    reduce_out(4)
    r.gblk[...] = (dz1 + branch).astype(BF).reshape(r.gblk.shape)
    collect(r.gblk, r.gland, r.zs, r.zr)
    reduce(0, 4)
    reduce_out(0)
    total_add(r.vw, r.vl, 4, r.ws, r.wr)
    r.dvec[...] = unpack_vectors(r.vw[5])
    store(r.dvec, outs.dvec)
    collect_done(r.gblk, r.gland, r.zs, r.zr)
    store(r.gland, outs.gh)
    wait_sent()
    for copy in stored:
        copy.wait()


def fused_call(hid, cot, lengths, params, dims):
    model, tok, seq = dims.model, dims.tok, dims.seq
    block = (4, tok // 4, model)
    vmem = pltpu.VMEM
    dma = pltpu.SemaphoreType.DMA
    rows_in = params[0][0].shape[0]
    shape = jax.ShapeDtypeStruct
    given = dict(hid=hid, cot=cot, len=lengths, lay=[])
    outs = dict(out=shape(hid.shape, BF), gh=shape(hid.shape, BF), lay=[], dvec=shape((1, dims.lanes), F32))
    for (ai, ao, fi, fo, sh, ga), sizes in zip(params, dims.layers):
        given["lay"].append(dict(pai=ai, pao=ao, pfi=fi, pfo=fo, psh=sh, pga=ga))
        outs["lay"].append(
            dict(
                da=shape((2, rows_in, sizes.wide), F32),
                df=shape((2, 2, sizes.nr, model // 4), F32),
            )
        )
    as_scratch = lambda tree: jax.tree.map(lambda v: vmem(v.shape, v.dtype), tree)
    held, made = as_scratch(given), as_scratch({key: outs[key] for key in ("lay", "dvec")})
    vec = (dims.vec_rows, model)
    rows_a = 2 * rows_in
    counts = [sum(chunk[0] == kind for chunk in dims.chunks) for kind in "AFP"]
    half = model // 2
    n = len(dims.chunks)
    scratch = dict(
        cin=vmem(block, BF),
        oblk=vmem(block, BF),
        gblk=vmem(block, BF),
        oland=vmem(hid.shape, BF),
        gland=vmem(hid.shape, BF),
        vw=vmem((6,) + vec, F32),
        vl=vmem((5,) + vec, F32),
        xs=vmem((2, tok, model), BF),
        xr=vmem((2, tok, model), BF),
        eo=vmem((tok, model), BF),
        px=vmem((4, tok, model), BF),
        prx=vmem((4, tok // 2, model), BF),
        pz=vmem((4, tok // 2, model), BF),
        pzr=vmem((4, 2, tok // 2, model), BF),
        ps=dma((4, 5)),
        pr=dma((4, 5)),
        hot=vmem((dims.lanes, model), BF),
        gs=dma((n, 20)),
        gr=dma((n, 20)),
        ss=dma((n, 20)),
        sr=dma((n, 20)),
        fs=dma((n,)),
        fr=dma((n,)),
        vs=dma((5,)),
        vr=dma((5,)),
        ws=dma((5,)),
        wr=dma((5,)),
        hs=dma((4,)),
        hr=dma((4,)),
        cs=dma((4,)),
        cr=dma((4,)),
        ys=dma((4,)),
        yr=dma((4,)),
        zs=dma((4,)),
        zr=dma((4,)),
        is_=dma((4,)),
        ir=dma((4,)),
        os=dma((4,)),
        es=dma((2,)),
        er=dma((2,)),
        ins=dma((16,)),
        outs=dma((10,)),
        red=[],
        lay=[],
    )
    rows_f, rows_p = dims.unit_rows["F"], dims.unit_rows["P"]
    for count, rows, wide, pair, shard, kind in (
        (counts[0], rows_a, model, (2, 4, 16, model), (rows_in, model), "A"),
        (counts[1], rows_f, half, (4, 16, model), (rows_f, half // 2), "F"),
    ):
        line = pair[:-3] + (1, 16, model)
        rows -= 0 if kind in dims.whole else 32
        scratch["red"].append(
            dict(
                ad=vmem((count, 2, 2, rows, wide), BF),
                an=vmem((count, 2, 4, rows, wide), BF),
                az=vmem((count, 4, 1, rows, wide), BF),
                by=vmem((count, 4, 2, 16, wide), BF),
                bz=vmem((count, 4, 1, 2, 16, wide), BF),
                bx=vmem((count, 1, 16, wide), BF),
                cx=vmem((count,) + pair, BF),
                cz=vmem((count, 4) + line, BF),
                cy=vmem((count, 1, 16, wide), BF),
                fsend=vmem((count,) + shard, F32),
                fland=vmem((count,) + shard, F32),
            )
        )
    scratch["red"].append(
        dict(
            ad=vmem((counts[2], 2, 1, rows_p, half), BF),
            an=vmem((counts[2], 2, 2, rows_p, half), BF),
            az=vmem((counts[2], 1, rows_p, half), BF),
            fsend=vmem((counts[2], rows_p, half // 2), F32),
            fland=vmem((counts[2], rows_p, half // 2), F32),
        )
    )
    for sizes in dims.layers:
        scratch["lay"].append(
            dict(
                ar=vmem((rows_in, sizes.wide), F32),
                asend=vmem((rows_in, sizes.wide), F32),
                fr=vmem((2, sizes.nr, model // 4), BF),
                fsend=vmem((2, sizes.nr, model // 4), BF),
                ga=vmem((SIDE, DEPTH, SIDE, rows_a, sizes.wide), BF),
                wa=vmem((model, sizes.wide), BF),
                w=vmem((2, sizes.zs, SIDE, sizes.nr, model), BF),
                dw=vmem((2, sizes.zs, SIDE, sizes.nr, model), BF),
                xb=vmem((2,) + block, BF),
                q=vmem((tok, sizes.hc), BF),
                kv=vmem((2, tok, 2 * sizes.hc), BF),
                a=vmem((sizes.heads, tok, seq), BF),
                ctx=vmem((tok, sizes.wide - sizes.start), BF),
                n1=vmem((tok, model), F32),
                s1=vmem((tok, 1), F32),
                hb=vmem((sizes.sides, tok, model), BF),
                eo=vmem((sizes.sides, tok, model), BF),
                g=vmem((sizes.sides, tok, sizes.nl), BF),
                gp=vmem((sizes.sides, tok, sizes.nl), BF),
                n2=vmem((tok, model), F32),
                s2=vmem((tok, 1), F32),
                dkv=vmem((2, tok, 2 * sizes.hc), BF),
                dq=vmem((tok, 2 * sizes.hc if sizes.pad else sizes.hc), BF),
            )
        )
    inputs, outputs = jax.tree.leaves(given), jax.tree.leaves(outs)
    whole = pl.BlockSpec(memory_space=pl.ANY)
    local = (scratch, held, made)
    values = pl.pallas_call(
        functools.partial(fused_kernel, dims, jax.tree.structure((given, outs) + local)),
        out_shape=outputs,
        in_specs=[whole] * len(inputs),
        out_specs=[whole] * len(outputs),
        scratch_shapes=jax.tree.leaves(local),
        compiler_params=pltpu.CompilerParams(
            collective_id=0, has_side_effects=True, vmem_limit_bytes=dims.vmem
        ),
        name="layers",
    )(*inputs)
    return jax.tree.unflatten(jax.tree.structure(outs), values)


def finish_kernel(dims, tree, *refs):
    given, (out, gh, *results) = jax.tree.unflatten(tree, refs)
    r = named(given)
    out[...] = r.out[...]
    gh[...] = r.gh[...].astype(F32)
    begin = 0
    for at, sizes in enumerate(dims.layers):
        attn, ffn = r.lay[at].da, r.lay[at].df
        to_ai, to_ao, to_fi, to_fo, to_sh, to_ga = results[6 * at : 6 * at + 6]
        for p in range(3):
            for h in range(2):
                to = (2 * ((p + 1) % 3) + h) * sizes.hc
                to_ai[:, to : to + sizes.hc] = attn[h, :, p * sizes.hc : (p + 1) * sizes.hc]
        for h in range(2):
            to_ao[:, h * sizes.hc : (h + 1) * sizes.hc] = attn[h, :, 3 * sizes.hc :]
        down = ffn[:, 1].reshape(2 * sizes.nr, ffn.shape[3])
        to_fo[...] = down.T if dims.turned[at] else down
        to_fi[...] = ffn[:, 0].reshape(2 * sizes.nr, ffn.shape[3]).T
        for ref in (to_sh, to_ga):
            ref[...] = r.dvec[0, begin : begin + ref.shape[0]]
            begin += ref.shape[0]


def finish_call(given, params, dims):
    leaves, tree = jax.tree.flatten(given)
    outs = [jax.ShapeDtypeStruct(given["out"].shape, d) for d in (BF, F32)]
    outs += [jax.ShapeDtypeStruct(p.shape, F32) for shards in params for p in shards]
    whole = pl.BlockSpec(memory_space=pltpu.VMEM)
    return pl.pallas_call(
        functools.partial(finish_kernel, dims, jax.tree.structure((given, outs))),
        out_shape=outs,
        in_specs=[whole] * len(leaves),
        out_specs=[whole] * len(outs),
        compiler_params=pltpu.CompilerParams(vmem_limit_bytes=dims.vmem),
        name="finish",
    )(*leaves)


def make_dims(hidden_in, teacher, student):
    model = hidden_in.shape[2]
    layers = [
        layer_sizes(model, p[0].shape[1] // 3, p[2].shape[1] * DEPTH * SIDE, pair)
        for p, pair in ((teacher, True), (student, False))
    ]
    rows = layers[1].nr
    chunks = []
    for at, sizes in enumerate(layers):
        chunks += [("A", at, 0, part) for part in range(sizes.wide // model)]
        for which in (0, 1):
            kind, count = ("P", 1) if sizes.pair else ("F", sizes.nr // rows)
            chunks += [(kind, at, which, part) for part in range(count)]
    counts, slot = {"A": 0, "F": 0, "P": 0}, []
    for chunk in chunks:
        slot.append(counts[chunk[0]])
        counts[chunk[0]] += 1
    group = model // (SIDE * SIDE * DEPTH * SIDE)
    shift_groups = [p[4].shape[0] // group for p in (teacher, student)]
    gain_groups = [p[5].shape[0] // group for p in (teacher, student)]
    rows_of, base, at = [], [], 0
    for sizes in layers:
        found, count = vec_rows(model, sizes)
        rows_of.append(found)
        base.append(at)
        at += count
    return types.SimpleNamespace(
        model=model,
        tok=4 * hidden_in.shape[1],
        seq=8 * hidden_in.shape[1],
        layers=layers,
        chunks=chunks,
        slot=slot,
        rows=rows,
        whole='A',
        unit_rows={"A": 2 * teacher[0].shape[0], "F": rows, "P": layers[0].nr},
        rows_of=rows_of,
        base=base,
        length_row=at,
        vec_rows=(at + 8) // 8 * 8,
        turned=[p[3].shape[0] > p[3].shape[1] for p in (teacher, student)],
        group=group,
        lanes=(sum(shift_groups + gain_groups) * group + 4 + 127) // 128 * 128,
        shift_groups=shift_groups,
        gain_groups=gain_groups,
        vmem=63 * 2**20,
    )


def fast_body(hidden_in, cotangent, lengths, *shards):
    params = (shards[:6], shards[6:])
    dims = make_dims(hidden_in, *params)
    turn = lambda shards, turned: (shards[0], shards[1].T, shards[2], shards[3].T if turned else shards[3])
    params = [turn(p, turned) + p[4:] for p, turned in zip(params, dims.turned)]
    values = fused_call(hidden_in, cotangent, lengths, params, dims)
    out, grad_hidden, *grads = finish_call(values, params, dims)
    results = [out, grad_hidden]
    for at, turned in enumerate(dims.turned):
        own = tuple(grads[6 * at : 6 * at + 6])
        results += turn(own, turned) + own[4:]
    return tuple(results)


def body(axes, *args):
    rows, tokens, model = args[0].shape
    pair_fits = args[3 + 2].shape[1] * 2 == model
    fits = pair_fits and axes["dp"] == SIDE * SIDE and axes["mp"] == DEPTH * SIDE
    if fits and rows == 2 and tokens % 16 == 0 and model % 256 == 0:
        return fast_body(*args)
    return general_body(*args)


def general_body(
    hidden_in,
    cotangent,
    lengths,
    teacher_attn_in,
    teacher_attn_out,
    teacher_ffn_in,
    teacher_ffn_out,
    teacher_shifts,
    teacher_gains,
    student_attn_in,
    student_attn_out,
    student_ffn_in,
    student_ffn_out,
    student_shifts,
    student_gains,
):
    span_len = hidden_in.shape[1] * lax.axis_size("mp")
    positions = jnp.arange(span_len)
    valid_keys = positions[None, :] < lengths[:, None]
    teacher = fetch(
        teacher_attn_in,
        teacher_attn_out,
        teacher_ffn_in,
        teacher_ffn_out,
        teacher_shifts,
        teacher_gains,
    )
    student = fetch(
        student_attn_in,
        student_attn_out,
        student_ffn_in,
        student_ffn_out,
        student_shifts,
        student_gains,
    )
    middle, teacher_kept = forward_layer(hidden_in.astype(jnp.float32), teacher, valid_keys)
    final, student_kept = forward_layer(middle, student, valid_keys)
    grad_middle, student_grads = backward_layer(
        cotangent.astype(jnp.float32), student_kept, student, valid_keys
    )
    grad_input, teacher_grads = backward_layer(grad_middle, teacher_kept, teacher, valid_keys)
    teacher_totals = reduce_grads(teacher_grads)
    student_totals = reduce_grads(student_grads)
    return (final.astype(jnp.bfloat16), grad_input) + teacher_totals + student_totals


def solution(mesh):
    in_specs = (
        P("dp", "mp", None),
        P("dp", "mp", None),
        P("dp"),
        P(("dp", "mp"), None),
        P(None, ("dp", "mp")),
        P("dp", "mp"),
        P("mp", "dp"),
        P(("dp", "mp")),
        P(("dp", "mp")),
        P(("dp", "mp"), None),
        P(None, ("dp", "mp")),
        P("dp", "mp"),
        P("mp", "dp"),
        P(("dp", "mp")),
        P(("dp", "mp")),
    )
    out_specs = (
        P("dp", "mp", None),
        P("dp", "mp", None),
        P(("dp", "mp"), None),
        P(None, ("dp", "mp")),
        P("dp", "mp"),
        P("mp", "dp"),
        P(("dp", "mp")),
        P(("dp", "mp")),
        P(("dp", "mp"), None),
        P(None, ("dp", "mp")),
        P("dp", "mp"),
        P("mp", "dp"),
        P(("dp", "mp")),
        P(("dp", "mp")),
    )
    return jax.shard_map(
        functools.partial(body, dict(mesh.shape)), mesh=mesh, in_specs=in_specs, out_specs=out_specs, check_vma=False)
```

```python
import functools
import types

import jax
import jax.numpy as jnp
from jax import lax
from jax.experimental import pallas as pl
from jax.experimental.pallas import tpu as pltpu
from jax.sharding import PartitionSpec as P

HEAD = 64


EPSILON = 1e-06
NEGATIVE = -1e30


def layer_norm(values, gain, shift):
    centered = values - jnp.mean(values, axis=-1, keepdims=True)
    variance = jnp.mean(centered * centered, axis=-1, keepdims=True)
    return centered * lax.rsqrt(variance + EPSILON) * gain + shift


def smooth_gate(pre_act):
    return jax.nn.gelu(pre_act, approximate=False)


def split_shifts(shifts, head_width, model_width, hidden_width):
    spans_list = [
        head_width,
        head_width,
        model_width,
        model_width,
        hidden_width,
        model_width,
        model_width,
    ]
    pieces = []
    offset = 0
    for length in spans_list:
        pieces.append(shifts[offset : offset + length])
        offset = offset + length
    return pieces


def to_heads(values):
    return values.reshape(values.shape[0], values.shape[1], values.shape[2] // HEAD, HEAD)


def score_block(queries, all_keys, valid_keys):
    raw = jnp.einsum(
        "rqhd,rkhd->rhqk", to_heads(queries), to_heads(all_keys), preferred_element_type=jnp.float32
    )
    return jnp.where(valid_keys[:, None, None, :], raw * 0.125, NEGATIVE)


def fetch(attn_in, attn_out, ffn_in, ffn_out, shifts, gains):
    whole_in, whole_out, whole_shifts, whole_gains = (
        lax.all_gather(attn_in, ("dp", "mp"), axis=0, tiled=True),
        lax.all_gather(attn_out, ("dp", "mp"), axis=1, tiled=True),
        lax.all_gather(shifts, ("dp", "mp"), axis=0, tiled=True),
        lax.all_gather(gains, ("dp", "mp"), axis=0, tiled=True),
    )
    ffn_first, ffn_second = (
        lax.all_gather(ffn_in, "dp", axis=0, tiled=True),
        lax.all_gather(ffn_out, "dp", axis=1, tiled=True),
    )
    return (
        whole_in,
        whole_out,
        ffn_first,
        ffn_second,
        whole_shifts.astype(jnp.float32),
        whole_gains.astype(jnp.float32),
    )


def forward_layer(hidden, params, valid_keys):
    attn_in, attn_out, ffn_first, ffn_second, shifts, gains = params
    model_width = hidden.shape[-1]
    head_width = attn_in.shape[1] // 3
    hidden_width = shifts.shape[0] - 2 * head_width - 4 * model_width
    pieces = split_shifts(shifts, head_width, model_width, hidden_width)
    bias_query, bias_value, bias_output, shift_one, bias_up, bias_down, shift_two = pieces
    hidden_low = hidden.astype(jnp.bfloat16)
    projected = jnp.einsum("rsd,de->rse", hidden_low, attn_in, preferred_element_type=jnp.float32)
    queries = (projected[..., :head_width] + bias_query).astype(jnp.bfloat16)
    local_keys = projected[..., head_width : 2 * head_width].astype(jnp.bfloat16)
    local_values = (projected[..., 2 * head_width :] + bias_value).astype(jnp.bfloat16)
    all_keys, all_values = (
        lax.all_gather(local_keys, "mp", axis=1, tiled=True),
        lax.all_gather(local_values, "mp", axis=1, tiled=True),
    )
    scores = score_block(queries, all_keys, valid_keys)
    row_max = jnp.max(scores, axis=-1, keepdims=True)
    exponent = jnp.exp(scores - row_max)
    row_total = jnp.sum(exponent, axis=-1, keepdims=True)
    log_total = row_max + jnp.log(row_total)
    weights_low = (exponent / row_total).astype(jnp.bfloat16)
    mixed = jnp.einsum(
        "rhqk,rkhd->rqhd", weights_low, to_heads(all_values), preferred_element_type=jnp.float32
    )
    context = mixed.reshape(queries.shape).astype(jnp.bfloat16)
    branch = (
        jnp.einsum("rsh,hd->rsd", context, attn_out, preferred_element_type=jnp.float32)
        + bias_output
    )
    summed_one = hidden + branch
    normed_one = layer_norm(summed_one, gains[:model_width], shift_one)
    normed_low = normed_one.astype(jnp.bfloat16)
    ffn_tokens = lax.all_gather(normed_low, "mp", axis=1, tiled=True)
    local_hidden = ffn_first.shape[1]
    bias_part = lax.dynamic_slice_in_dim(bias_up, lax.axis_index("mp") * local_hidden, local_hidden)
    pre_act = (
        jnp.einsum("rsd,df->rsf", ffn_tokens, ffn_first, preferred_element_type=jnp.float32)
        + bias_part
    )
    act_low = smooth_gate(pre_act).astype(jnp.bfloat16)
    down_terms = jnp.einsum("rsf,fd->rsd", act_low, ffn_second, preferred_element_type=jnp.float32)
    ffn_down = lax.psum_scatter(
        down_terms.astype(jnp.bfloat16), "mp", scatter_dimension=1, tiled=True
    ).astype(jnp.float32)
    summed_two = normed_one + ffn_down + bias_down
    result = layer_norm(summed_two, gains[model_width:], shift_two)
    key_store = (all_keys, all_values)
    kept = (
        hidden_low,
        queries,
        key_store,
        log_total,
        context,
        summed_one,
        ffn_tokens,
        pre_act,
        act_low,
        summed_two,
    )
    return (result, kept)


def backward_layer(grad_out, kept, params, valid_keys):
    attn_in, attn_out, ffn_first, ffn_second, shifts, gains = params
    (
        hidden_low,
        queries,
        key_store,
        log_total,
        context,
        summed_one,
        ffn_tokens,
        pre_act,
        act_low,
        summed_two,
    ) = kept
    model_width = summed_one.shape[-1]
    head_width = attn_in.shape[1] // 3
    hidden_width = shifts.shape[0] - 2 * head_width - 4 * model_width
    pieces = split_shifts(shifts, head_width, model_width, hidden_width)
    bias_query, bias_value, bias_output, shift_one, bias_up, bias_down, shift_two = pieces
    sum_axes = (0, 1)
    unused_two, norm_two_back = jax.vjp(layer_norm, summed_two, gains[model_width:], shift_two)
    grad_two, grad_gain_two, grad_shift_two = norm_two_back(grad_out)
    grad_down = grad_two.astype(jnp.bfloat16)
    grad_bias_down = jnp.sum(grad_down.astype(jnp.float32), axis=sum_axes)
    grad_tokens = lax.all_gather(grad_down, "mp", axis=1, tiled=True)
    grad_act = jnp.einsum(
        "rsd,fd->rsf", grad_tokens, ffn_second, preferred_element_type=jnp.float32
    )
    grad_second = jnp.einsum(
        "rsf,rsd->fd", act_low, grad_tokens, preferred_element_type=jnp.float32
    )
    unused_gate, gate_back = jax.vjp(smooth_gate, pre_act)
    grad_pre = gate_back(grad_act)[0].astype(jnp.bfloat16)
    grad_bias_part = jnp.sum(grad_pre.astype(jnp.float32), axis=sum_axes)
    grad_first = jnp.einsum("rsd,rsf->df", ffn_tokens, grad_pre, preferred_element_type=jnp.float32)
    back_terms = jnp.einsum("rsf,df->rsd", grad_pre, ffn_first, preferred_element_type=jnp.float32)
    grad_normed = lax.psum_scatter(
        back_terms.astype(jnp.bfloat16), "mp", scatter_dimension=1, tiled=True
    ).astype(jnp.float32)
    blank_bias = jnp.zeros((hidden_width,), jnp.float32)
    grad_bias_up = lax.dynamic_update_slice_in_dim(
        blank_bias, grad_bias_part, lax.axis_index("mp") * ffn_first.shape[1], 0
    )
    grad_normed = grad_normed + grad_two
    unused_one, norm_one_back = jax.vjp(layer_norm, summed_one, gains[:model_width], shift_one)
    grad_one, grad_gain_one, grad_shift_one = norm_one_back(grad_normed)
    grad_branch = grad_one.astype(jnp.bfloat16)
    grad_bias_output = jnp.sum(grad_branch.astype(jnp.float32), axis=sum_axes)
    grad_attn_out = jnp.einsum(
        "rsh,rsd->hd", context, grad_branch, preferred_element_type=jnp.float32
    )
    grad_context = jnp.einsum(
        "rsd,hd->rsh", grad_branch, attn_out, preferred_element_type=jnp.float32
    ).astype(jnp.bfloat16)
    stored_keys, stored_values = key_store
    all_keys, all_values = (stored_keys, stored_values)
    weights = jnp.exp(score_block(queries, all_keys, valid_keys) - log_total)
    context_heads = to_heads(grad_context)
    grad_weights = jnp.einsum(
        "rqhd,rkhd->rhqk", context_heads, to_heads(all_values), preferred_element_type=jnp.float32
    )
    inner_sum = jnp.sum(weights * grad_weights, axis=-1, keepdims=True)
    grad_raw = (0.125 * weights * (grad_weights - inner_sum)).astype(jnp.bfloat16)
    grad_queries = jnp.einsum(
        "rhqk,rkhd->rqhd", grad_raw, to_heads(all_keys), preferred_element_type=jnp.float32
    )
    grad_queries = grad_queries.reshape(queries.shape).astype(jnp.bfloat16)
    weights_low = weights.astype(jnp.bfloat16)
    value_terms = jnp.einsum(
        "rhqk,rqhd->rkhd", weights_low, context_heads, preferred_element_type=jnp.float32
    )
    key_terms = jnp.einsum(
        "rhqk,rqhd->rkhd", grad_raw, to_heads(queries), preferred_element_type=jnp.float32
    )
    key_terms = key_terms.reshape(all_keys.shape)
    value_terms = value_terms.reshape(all_values.shape)
    grad_keys, grad_values = (
        lax.psum_scatter(
            key_terms.astype(jnp.bfloat16), "mp", scatter_dimension=1, tiled=True
        ).astype(jnp.float32),
        lax.psum_scatter(
            value_terms.astype(jnp.bfloat16), "mp", scatter_dimension=1, tiled=True
        ).astype(jnp.float32),
    )
    grad_values_low = grad_values.astype(jnp.bfloat16)
    grad_projected = jnp.concatenate(
        [grad_queries, grad_keys.astype(jnp.bfloat16), grad_values_low], axis=-1
    )
    grad_attn_in = jnp.einsum(
        "rsd,rse->de", hidden_low, grad_projected, preferred_element_type=jnp.float32
    )
    grad_hidden = grad_one + jnp.einsum(
        "rse,de->rsd", grad_projected, attn_in, preferred_element_type=jnp.float32
    )
    grad_bias_query = jnp.sum(grad_queries.astype(jnp.float32), axis=sum_axes)
    grad_bias_value = jnp.sum(grad_values_low.astype(jnp.float32), axis=sum_axes)
    grad_shifts = jnp.concatenate(
        [
            grad_bias_query,
            grad_bias_value,
            grad_bias_output,
            grad_shift_one,
            grad_bias_up,
            grad_bias_down,
            grad_shift_two,
        ]
    )
    grad_gains = jnp.concatenate([grad_gain_one, grad_gain_two])
    return (
        grad_hidden,
        (grad_attn_in, grad_attn_out, grad_first, grad_second, grad_shifts, grad_gains),
    )


def reduce_grads(grads):
    grad_attn_in, grad_attn_out, grad_first, grad_second, grad_shifts, grad_gains = grads
    total_in, total_out, total_shifts, total_gains = (
        lax.psum_scatter(grad_attn_in, ("dp", "mp"), scatter_dimension=0, tiled=True),
        lax.psum_scatter(grad_attn_out, ("dp", "mp"), scatter_dimension=1, tiled=True),
        lax.psum_scatter(grad_shifts, ("dp", "mp"), scatter_dimension=0, tiled=True),
        lax.psum_scatter(grad_gains, ("dp", "mp"), scatter_dimension=0, tiled=True),
    )
    total_first, total_second = (
        lax.psum_scatter(
            grad_first.astype(jnp.bfloat16), "dp", scatter_dimension=0, tiled=True
        ).astype(jnp.float32),
        lax.psum_scatter(
            grad_second.astype(jnp.bfloat16), "dp", scatter_dimension=1, tiled=True
        ).astype(jnp.float32),
    )
    return (total_in, total_out, total_first, total_second, total_shifts, total_gains)


BF = jnp.bfloat16
F32 = jnp.float32
MESH = pl.DeviceIdType.MESH
SIDE = 2
DEPTH = 4
PARTNERS = 9


def mm(left, right, left_dim, right_dim):
    return lax.dot_general(
        left, right, (((left_dim,), (right_dim,)), ((), ())), preferred_element_type=F32
    )


def rowsum(values):
    return jnp.sum(values, axis=0, keepdims=True)


def normalize(values):
    centered = values - jnp.mean(values, axis=-1, keepdims=True)
    variance = jnp.mean(centered * centered, axis=-1, keepdims=True)
    scale = lax.rsqrt(variance + EPSILON)
    return centered * scale, scale


def normalize_back(grad, normed, scale):
    along = jnp.mean(grad * normed, axis=-1, keepdims=True)
    return scale * (grad - jnp.mean(grad, axis=-1, keepdims=True) - normed * along)


def layer_sizes(model, heads_width, hidden, pair):
    half = heads_width // 2
    start = 3 * half // 128 * 128
    return types.SimpleNamespace(
        hc=half,
        heads=half // HEAD,
        wide=4 * half,
        start=start,
        qw=-(-half // 128) * 128,
        pad=3 * half - start,
        nr=hidden // 16,
        nc=hidden // 2,
        nl=hidden // 4 if pair else hidden // 2,
        pair=pair,
        sides=2 if pair else 1,
        zs=2 if pair else DEPTH,
        zb=model * 8 // hidden,
    )


def vec_rows(model, sizes):
    lengths = dict(
        qv=4 * sizes.hc, bo=model, beta1=model, b1=2 * sizes.nc, b2=model, beta2=model, g1=model, g2=model
    )
    rows, at = {}, 0
    for name, length in lengths.items():
        rows[name] = at
        at += length // model
    return types.SimpleNamespace(**rows), at


def named(tree):
    if isinstance(tree, dict):
        return types.SimpleNamespace(**{key: named(value) for key, value in tree.items()})
    return [named(value) for value in tree] if isinstance(tree, list) else tree


def fused_kernel(dims, tree, *refs):
    given, outs, scratch, held, made = jax.tree.unflatten(tree, refs)
    lay = [named(a | b | d) for a, b, d in zip(held["lay"], made["lay"], scratch["lay"])]
    r = named(held | made | scratch)
    given, outs = named(given), named(outs)

    def fetch_copies():
        pairs = []
        for at in range(2):
            far, near = given.lay[at], lay[at]
            pairs += [(far.pai, near.pai), (far.pao, near.pao)]
            if at == 0:
                pairs += [(given.hid, r.hid)]
            pairs += [(far.pfi, near.pfi), (far.pfo, near.pfo), (far.psh, near.psh), (far.pga, near.pga)]
        pairs += [(given.len, r.len), (given.cot, r.cot)]
        return [pltpu.make_async_copy(src, dst, r.ins.at[i]) for i, (src, dst) in enumerate(pairs)]

    fetched = fetch_copies()
    for copy in fetched:
        copy.start()
    stored = []

    def store(src, dst):
        copy = pltpu.make_async_copy(src, dst, r.outs.at[len(stored)])
        copy.start()
        stored.append(copy)
    model, tok, seq, layers = dims.model, dims.tok, dims.seq, dims.layers
    half_lanes = model // 2
    dp, mp = lax.axis_index("dp"), lax.axis_index("mp")
    y, c = dp // SIDE, lax.rem(dp, SIDE)
    z, x = mp // SIDE, lax.rem(mp, SIDE)

    def device(c, x, y, z):
        return {"dp": y * SIDE + c, "mp": z * SIDE + x}

    sib = device(1 - c, x, y, z)
    xn, yn = device(c, 1 - x, y, z), device(c, x, 1 - y, z)
    zdev = [device(c, x, y, lax.rem(z + d, DEPTH)) for d in range(1, DEPTH)]
    zpair = z + 1 - 2 * lax.rem(z, 2)
    zn = device(c, x, y, zpair)
    zfar = device(c, x, y, lax.rem(z + 2, DEPTH))

    bar = pltpu.get_barrier_semaphore()
    for step in range(1, DEPTH * SIDE):
        other = lax.rem(mp + step, DEPTH * SIDE)
        pl.semaphore_signal(bar, inc=1, device_id={"dp": dp, "mp": other}, device_id_type=MESH)
    pl.semaphore_signal(bar, inc=1, device_id=sib, device_id_type=MESH)
    pl.semaphore_signal(bar, inc=1, device_id=yn, device_id_type=MESH)

    sent = []

    def remote(src, dst, send, recv, dev):
        return pltpu.make_async_remote_copy(
            src_ref=src, dst_ref=dst, send_sem=send, recv_sem=recv, device_id=dev, device_id_type=MESH
        )

    def push(src, dst, send, recv, dev):
        copy = remote(src, dst, send, recv, dev)
        copy.start()
        sent.append((None, copy))

    def arrived(dst, recv, send):
        remote(dst, dst, send, recv, sib).wait_recv()

    row_core = z // 2
    mine = c == row_core
    half = lax.rem(z, 2)

    def spread(src, land, sends, recvs):
        block = 2 * lax.rem(z, 2) + x
        target = 2 * c + z // 2
        for j in range(2):
            local = (x == j) & (z == target)
            copy = remote(src.at[j], land.at[block], sends.at[j], recvs.at[block], device(c, j, y, target))
            pl.when(local)(pltpu.make_async_copy(src.at[j], land.at[block], recvs.at[block]).start)
            pl.when(jnp.logical_not(local))(copy.start)

    def spread_turn(src, land, sends, recvs, on_chip_send, on_chip_recv):
        target = 2 * c + z // 2
        for j in range(2):
            local = (x == j) & (z == target)
            copy = remote(src.at[j], land.at[0], sends.at[j], recvs.at[0], sib)
            pl.when(jnp.logical_not(local))(copy.wait_send)
        whole = remote(land, land, on_chip_send, on_chip_recv, sib)

        @pl.when(mine)
        def _():
            for block in range(4):
                arrived(land.at[block], recvs.at[block], sends.at[0])
            whole.start()

    def spread_end(land, on_chip_send, on_chip_recv):
        whole = remote(land, land, on_chip_send, on_chip_recv, sib)
        pl.when(mine)(whole.wait_send)
        pl.when(jnp.logical_not(mine))(whole.wait_recv)

    def collect(src, land, sends, recvs):
        @pl.when(mine)
        def _():
            for block in range(4):
                z_to, x_to = 2 * half + block // 2, block % 2
                local = (x == x_to) & (z == z_to)
                slot = land.at[x]
                copy = remote(
                    src.at[block], slot, sends.at[block], recvs.at[x], device(c, x_to, y, z_to)
                )
                pl.when(local)(pltpu.make_async_copy(src.at[block], slot, recvs.at[x]).start)
                pl.when(jnp.logical_not(local))(copy.start)

    def collect_done(src, land, sends, recvs):
        for j in range(2):
            arrived(land.at[j], recvs.at[j], sends.at[0])

        @pl.when(mine)
        def _():
            for block in range(4):
                z_to, x_to = 2 * half + block // 2, block % 2
                local = (x == x_to) & (z == z_to)
                copy = remote(src.at[block], src.at[block], sends.at[block], recvs.at[0], sib)
                pl.when(jnp.logical_not(local))(copy.wait_send)

    chunks = dims.chunks
    every, first, second = pl.ds(0, DEPTH), pl.ds(0, 2), pl.ds(2, 2)
    both = pl.ds(0, 2)

    def view(i, grads, band, z_slice, x_at, y_at):
        kind, layer, which, part = chunks[i]
        full = dims.unit_rows[kind]
        if kind == "P":
            ref = lay[layer].dw if grads else lay[layer].w
            lanes = pl.ds(pl.multiple_of(y_at * half_lanes, 128), half_lanes)
            return ref.at[which, z_slice, x_at, :, lanes]
        if band:
            begin, count = {"a": (0, full - 32), "b": (full - 32, 16), "c": (full - 16, 16)}[band]
        else:
            begin, count = 0, full
        if kind == "A":
            ref = lay[layer].ga
            y_pick = both if y_at is None else y_at
            return ref.at[y_pick, z_slice, x_at, pl.ds(begin, count), pl.ds(part * model, model)]
        ref = lay[layer].dw if grads else lay[layer].w
        lanes = pl.ds(0, model)
        if y_at is not None:
            lanes = pl.ds(pl.multiple_of(y_at * half_lanes, 128), half_lanes)
        return ref.at[which, z_slice, x_at, pl.ds(part * full + begin, count), lanes]

    UP, DOWN, FAR, RELAY = range(4)
    z_far = lax.rem(z + 2, DEPTH)
    z_up, z_down = lax.rem(z + 1, DEPTH), lax.rem(z + DEPTH - 1, DEPTH)
    z_end = DEPTH - 1 - z
    has_up, has_down = z < DEPTH - 1, z > 0
    inner = (z == 1) | (z == 2)
    outer = (z == 0) | (z == 3)
    z_out = jnp.where(z == 1, 0, 3)
    z_in = jnp.where(z == 0, 1, 2)

    def push_if(cond, src, dst, send, recv, dev):
        copy = remote(src, dst, send, recv, dev)
        pl.when(cond)(copy.start)
        sent.append((cond, copy))

    def wait_sent():
        for cond, copy in sent:
            if cond is None:
                copy.wait_send()
            else:
                pl.when(cond)(copy.wait_send)
        sent.clear()

    def arrived_if(cond, dst, recv, send):
        pl.when(cond)(remote(dst, dst, send, recv, sib).wait_recv)

    def at_z(zz):
        return device(c, x, y, zz)

    def line_send(part, send, recv):
        own = part(z)
        push_if(has_up, own, own, send(UP), recv(UP), at_z(z_up))
        push_if(has_down, own, own, send(DOWN), recv(DOWN), at_z(z_down))
        push(own, own, send(FAR), recv(FAR), at_z(z_far))

    def line_relay(part, send, recv):
        far = part(z_far)
        arrived_if(inner, far, recv(FAR), send(FAR))
        push_if(inner, far, far, send(RELAY), recv(RELAY), at_z(z_out))

    def line_end(part, send, recv):
        arrived_if(has_down, part(z_down), recv(UP), send(UP))
        arrived_if(has_up, part(z_up), recv(DOWN), send(DOWN))
        arrived_if(outer, part(z_far), recv(FAR), send(FAR))
        arrived_if(outer, part(z_end), recv(RELAY), send(RELAY))

    def sems(ref_send, ref_recv, i, base):
        return (lambda k: ref_send.at[i, base + k]), (lambda k: ref_recv.at[i, base + k])

    def one(zz):
        return pl.ds(zz, 1)

    def parts_of(i, grads):
        return (
            lambda zz: view(i, grads, "a", one(zz), x, y),
            lambda zz: view(i, grads, "b", one(zz), both, y),
            lambda zz: view(i, grads, "c", one(zz), x, None),
        )

    def gather_sems(i, base):
        return sems(r.gs, r.gr, i, base)

    def gather_push(i, k, piece, dev):
        push(piece, piece, r.gs.at[i, k], r.gr.at[i, k], dev)

    def gather_wait(i, k, piece):
        arrived(piece, r.gr.at[i, k], r.gs.at[i, k])

    z_own, z_other = z // 2, 1 - z // 2

    def pair_view(i, grads, z_slice, x_at, y_at):
        return view(i, grads, None, z_slice, x_at, y_at)

    def pair_0(i):
        gather_push(i, 0, pair_view(i, False, one(z_own), x, y), zfar)

    def pair_1(i):
        gather_wait(i, 0, pair_view(i, False, one(z_other), x, y))
        own = pair_view(i, False, both, x, y)
        gather_push(i, 1, own, xn)
        gather_push(i, 2, own, yn)

    def pair_2(i):
        gather_wait(i, 1, pair_view(i, False, both, 1 - x, y))
        gather_wait(i, 2, pair_view(i, False, both, x, 1 - y))
        gather_push(i, 3, pair_view(i, False, one(0), x, 1 - y), xn)
        gather_push(i, 4, pair_view(i, False, one(1), 1 - x, y), yn)

    def pair_3(i):
        gather_wait(i, 3, pair_view(i, False, one(0), 1 - x, 1 - y))
        gather_wait(i, 4, pair_view(i, False, one(1), 1 - x, 1 - y))

    def whole(i, z_slice, x_at, y_at):
        return view(i, False, None, z_slice, x_at, y_at)

    def line(i):
        return (lambda zz: whole(i, one(zz), x, y)), *gather_sems(i, 0)

    def gather_0(i):
        line_send(*line(i))

    def gather_1(i):
        line_relay(*line(i))

    def gather_2(i):
        line_end(*line(i))
        own = whole(i, every, x, y)
        gather_push(i, 4, own, xn)
        gather_push(i, 5, own, yn)

    def gather_3(i):
        gather_wait(i, 4, whole(i, every, 1 - x, y))
        gather_wait(i, 5, whole(i, every, x, 1 - y))
        gather_push(i, 6, whole(i, first, x, 1 - y), xn)
        gather_push(i, 7, whole(i, second, 1 - x, y), yn)

    def gather_4(i):
        gather_wait(i, 6, whole(i, first, 1 - x, 1 - y))
        gather_wait(i, 7, whole(i, second, 1 - x, 1 - y))

    band_stages = (gather_0, gather_1, gather_2, gather_3, gather_4)
    pair_stages = (pair_0, pair_1, pair_2, pair_3)

    def gather(i, stage):
        stages = pair_stages if chunks[i][0] == "P" else band_stages
        stages[stage](i)

    def add_into(ref, extra):
        total = ref[...].astype(F32)
        for more in extra:
            total = total + more[...].astype(F32)
        ref[...] = total.astype(BF)

    def slots(i, name):
        return getattr(r.red["AFP".index(chunks[i][0])], name).at[dims.slot[i]]

    def reduce_push(i, k, src, dst, dev):
        push(src, dst, r.ss.at[i, k], r.sr.at[i, k], dev)

    def reduce_wait(i, k, dst):
        arrived(dst, r.sr.at[i, k], r.ss.at[i, k])

    def line_reduce_send(part, land, send, recv):
        push_if(has_up, part(z_up), land.at[UP], send(UP), recv(UP), at_z(z_up))
        push_if(has_down, part(z_down), land.at[DOWN], send(DOWN), recv(DOWN), at_z(z_down))
        push_if(outer, part(z_end), land.at[RELAY], send(RELAY), recv(RELAY), at_z(z_in))
        push_if(outer, part(z_far), land.at[FAR], send(FAR), recv(FAR), at_z(z_far))

    def line_reduce_relay(part, land, send, recv):
        @pl.when(inner)
        def _():
            arrived(land.at[RELAY], recv(RELAY), send(RELAY))
            add_into(part(z_far), [land.at[RELAY]])

        push_if(inner, part(z_far), land.at[FAR], send(FAR), recv(FAR), at_z(z_far))

    def line_reduce_end(part, land, send, recv):
        arrived(land.at[FAR], recv(FAR), send(FAR))

        @pl.when(inner)
        def _():
            arrived(land.at[UP], recv(UP), send(UP))
            arrived(land.at[DOWN], recv(DOWN), send(DOWN))
            add_into(part(z), [land.at[FAR], land.at[UP], land.at[DOWN]])

        @pl.when(z == 0)
        def _():
            arrived(land.at[DOWN], recv(DOWN), send(DOWN))
            add_into(part(z), [land.at[FAR], land.at[DOWN]])

        @pl.when(z == DEPTH - 1)
        def _():
            arrived(land.at[UP], recv(UP), send(UP))
            add_into(part(z), [land.at[FAR], land.at[UP]])

    def reduce_sems(i, base):
        return sems(r.ss, r.sr, i, base)

    def band_reduce_0(i):
        over = slots(i, "ad")
        reduce_push(i, 14, view(i, True, "a", first, 1 - x, 1 - y), over.at[0], xn)
        reduce_push(i, 15, view(i, True, "a", second, 1 - x, 1 - y), over.at[1], yn)
        reduce_push(i, 18, view(i, True, "b", every, both, 1 - y), slots(i, "by"), yn)
        reduce_push(i, 19, view(i, True, "c", every, 1 - x, None), slots(i, "cx"), xn)

    def band_reduce_1(i):
        a, b, c_part = parts_of(i, True)
        over, beside = slots(i, "ad"), slots(i, "an")
        reduce_wait(i, 14, over.at[0])
        add_into(view(i, True, "a", first, x, 1 - y), [over.at[0]])
        reduce_push(i, 13, view(i, True, "a", every, x, 1 - y), beside.at[1], yn)
        reduce_wait(i, 15, over.at[1])
        add_into(view(i, True, "a", second, 1 - x, y), [over.at[1]])
        reduce_push(i, 12, view(i, True, "a", every, 1 - x, y), beside.at[0], xn)
        reduce_wait(i, 18, slots(i, "by"))
        add_into(view(i, True, "b", every, both, y), [slots(i, "by")])
        line_reduce_send(b, slots(i, "bz"), *reduce_sems(i, 4))
        reduce_wait(i, 19, slots(i, "cx"))
        add_into(view(i, True, "c", every, x, None), [slots(i, "cx")])
        line_reduce_send(c_part, slots(i, "cz"), *reduce_sems(i, 8))

    def band_reduce_2(i):
        a, b, c_part = parts_of(i, True)
        beside = slots(i, "an")
        reduce_wait(i, 12, beside.at[0])
        reduce_wait(i, 13, beside.at[1])
        add_into(view(i, True, "a", every, x, y), [beside.at[0], beside.at[1]])
        line_reduce_send(a, slots(i, "az"), *reduce_sems(i, 0))
        line_reduce_relay(b, slots(i, "bz"), *reduce_sems(i, 4))
        line_reduce_relay(c_part, slots(i, "cz"), *reduce_sems(i, 8))

    def band_reduce_3(i):
        a, b, c_part = parts_of(i, True)
        line_reduce_end(b, slots(i, "bz"), *reduce_sems(i, 4))
        reduce_push(i, 16, view(i, True, "b", one(z), 1 - x, y), slots(i, "bx"), xn)
        line_reduce_end(c_part, slots(i, "cz"), *reduce_sems(i, 8))
        reduce_push(i, 17, view(i, True, "c", one(z), x, 1 - y), slots(i, "cy"), yn)
        line_reduce_relay(a, slots(i, "az"), *reduce_sems(i, 0))

    def band_reduce_4(i):
        line_reduce_end(parts_of(i, True)[0], slots(i, "az"), *reduce_sems(i, 0))
        reduce_wait(i, 16, slots(i, "bx"))
        reduce_wait(i, 17, slots(i, "cy"))
        total = jnp.concatenate(
            [
                view(i, True, "a", one(z), x, y)[...].astype(F32)[0],
                (view(i, True, "b", one(z), x, y)[...].astype(F32) + slots(i, "bx")[...].astype(F32))[0],
                (view(i, True, "c", one(z), x, y)[...].astype(F32) + slots(i, "cy")[...].astype(F32))[0],
            ],
            axis=0,
        )
        reduce_store(i, total)

    def line_reduce(i):
        return (lambda zz: view(i, True, None, one(zz), x, y)), slots(i, "az"), *reduce_sems(i, 0)

    def whole_reduce_0(i):
        over = slots(i, "ad")
        reduce_push(i, 4, view(i, True, None, first, 1 - x, 1 - y), over.at[0], xn)
        reduce_push(i, 5, view(i, True, None, second, 1 - x, 1 - y), over.at[1], yn)

    def whole_reduce_1(i):
        over, beside = slots(i, "ad"), slots(i, "an")
        reduce_wait(i, 4, over.at[0])
        add_into(view(i, True, None, first, x, 1 - y), [over.at[0]])
        reduce_push(i, 6, view(i, True, None, every, x, 1 - y), beside.at[1], yn)
        reduce_wait(i, 5, over.at[1])
        add_into(view(i, True, None, second, 1 - x, y), [over.at[1]])
        reduce_push(i, 7, view(i, True, None, every, 1 - x, y), beside.at[0], xn)

    def whole_reduce_2(i):
        beside = slots(i, "an")
        reduce_wait(i, 6, beside.at[1])
        reduce_wait(i, 7, beside.at[0])
        add_into(view(i, True, None, every, x, y), [beside.at[0], beside.at[1]])
        line_reduce_send(*line_reduce(i))

    def whole_reduce_3(i):
        line_reduce_relay(*line_reduce(i))

    def whole_reduce_4(i):
        line_reduce_end(*line_reduce(i))
        reduce_store(i, view(i, True, None, one(z), x, y)[...].astype(F32)[0])

    whole_reduces = (whole_reduce_0, whole_reduce_1, whole_reduce_2, whole_reduce_3, whole_reduce_4)

    def pair_reduce_0(i):
        over = slots(i, "ad")
        reduce_push(i, 3, pair_view(i, True, one(0), 1 - x, 1 - y), over.at[0], xn)
        reduce_push(i, 4, pair_view(i, True, one(1), 1 - x, 1 - y), over.at[1], yn)

    def pair_reduce_1(i):
        over, beside = slots(i, "ad"), slots(i, "an")
        reduce_wait(i, 3, over.at[0])
        add_into(pair_view(i, True, one(0), x, 1 - y), [over.at[0]])
        reduce_push(i, 2, pair_view(i, True, both, x, 1 - y), beside.at[1], yn)
        reduce_wait(i, 4, over.at[1])
        add_into(pair_view(i, True, one(1), 1 - x, y), [over.at[1]])
        reduce_push(i, 1, pair_view(i, True, both, 1 - x, y), beside.at[0], xn)

    def pair_reduce_2(i):
        beside = slots(i, "an")
        reduce_wait(i, 1, beside.at[0])
        reduce_wait(i, 2, beside.at[1])
        add_into(pair_view(i, True, both, x, y), [beside.at[0], beside.at[1]])
        reduce_push(i, 0, pair_view(i, True, one(z_other), x, y), slots(i, "az"), zfar)

    def pair_reduce_3(i):
        far = slots(i, "az")
        reduce_wait(i, 0, far)
        own = pair_view(i, True, one(z_own), x, y)
        reduce_store(i, (own[...].astype(F32) + far[...].astype(F32))[0])

    def reduce_store(i, total):
        kind, layer, which, part = chunks[i]
        send, land = slots(i, "fsend"), slots(i, "fland")
        if kind == "A":
            rows = total.shape[0] // 2
            cols = slice(part * model, (part + 1) * model)
            lay[layer].da[c, :, cols] = jnp.where(c == 0, total[:rows], total[rows:])
            send[...] = jnp.where(c == 0, total[rows:], total[:rows])
        else:
            full = dims.unit_rows[kind]
            rows, lanes = pl.ds(part * full, full), total.shape[1] // 2
            lay[layer].df[c, which, rows, :] = jnp.where(c == 0, total[:, :lanes], total[:, lanes:])
            send[...] = jnp.where(c == 0, total[:, lanes:], total[:, :lanes])
        push(send, land, r.fs.at[i], r.fr.at[i], sib)

    def reduce_out(i):
        kind, layer, which, part = chunks[i]
        land = slots(i, "fland")
        arrived(land, r.fr.at[i], r.fs.at[i])
        if kind == "A":
            lay[layer].da[1 - c, :, part * model : (part + 1) * model] = land[...]
            if part == 0:
                store(lay[layer].da, outs.lay[layer].da)
        else:
            full = dims.unit_rows[kind]
            lay[layer].df[1 - c, which, pl.ds(part * full, full), :] = land[...]
            if part == layers[layer].nr // full - 1:
                store(lay[layer].df.at[:, which], outs.lay[layer].df.at[:, which])

    band_reduces = (band_reduce_0, band_reduce_1, band_reduce_2, band_reduce_3, band_reduce_4)
    pair_reduces = (pair_reduce_0, pair_reduce_1, pair_reduce_2, pair_reduce_3)

    def reduce(i, stage):
        stages = pair_reduces if chunks[i][0] == "P" else band_reduces
        if chunks[i][0] in dims.whole:
            stages = whole_reduces
        if stage < len(stages):
            stages[stage](i)

    def total_step(work, land, step, sends, recvs):
        dev = (sib, xn, yn, zn, zfar)[step]
        push(work.at[step], land.at[step], sends.at[step], recvs.at[step], dev)

    def total_add(work, land, step, sends, recvs):
        arrived(land.at[step], recvs.at[step], sends.at[step])
        work[step + 1] = work[step] + land[step]

    exchanges = []

    def exchange(part):
        slot = len(exchanges) % 2
        r.xs[slot] = part.astype(BF)
        copy = remote(r.xs.at[slot], r.xr.at[slot], r.es.at[slot], r.er.at[slot], sib)
        copy.start()
        exchanges.append(copy)

        def finish():
            copy.wait()
            return r.xs[slot].astype(F32) + r.xr[slot].astype(F32)

        return finish

    quarter = tok // 2
    own_rows = pl.ds(pl.multiple_of(c * quarter, 16), quarter)
    other_rows = pl.ds(pl.multiple_of((1 - c) * quarter, 16), quarter)

    class Share:
        def __init__(self, ref, k):
            blocks = len(ref.shape) == 4
            self.own = pl.ds(2 * c, 2) if blocks else own_rows
            self.other = pl.ds(2 - 2 * c, 2) if blocks else other_rows
            self.ref, self.k = ref, k
            piece = ref.at[half, self.own]
            push(piece, piece, r.ps.at[k, 0], r.pr.at[k, 0], zn)

        def turn(self):
            got, k = self.ref.at[1 - half, self.own], self.k
            arrived(got, r.pr.at[k, 0], r.ps.at[k, 0])
            push(got, got, r.ps.at[k, 1], r.pr.at[k, 1], sib)

        def end(self):
            k = self.k
            arrived(self.ref.at[1 - half, self.other], r.pr.at[k, 1], r.ps.at[k, 1])

    class Fold:
        def __init__(self, make, k):
            self.make, self.k = make, k
            r.px[k] = make(1 - half, False).astype(BF)
            push(r.px.at[k, other_rows], r.prx.at[k], r.ps.at[k, 2], r.pr.at[k, 2], sib)

        def keep(self):
            self.own = exchange(self.make(half, True))

        def cross(self):
            k = self.k
            arrived(r.prx.at[k], r.pr.at[k, 2], r.ps.at[k, 2])
            r.pz[k] = (r.px[k, own_rows, :].astype(F32) + r.prx[k].astype(F32)).astype(BF)
            push(r.pz.at[k], r.pzr.at[k, c], r.ps.at[k, 3], r.pr.at[k, 3], zn)

        def turn(self):
            k = self.k
            got = r.pzr.at[k, c]
            arrived(got, r.pr.at[k, 3], r.ps.at[k, 3])
            push(got, got, r.ps.at[k, 4], r.pr.at[k, 4], sib)

        def end(self):
            k = self.k
            arrived(r.pzr.at[k, 1 - c], r.pr.at[k, 4], r.ps.at[k, 4])
            return self.own() + r.pzr[k].reshape(tok, model).astype(F32)

    def vec_row(row):
        return r.vw[5, row : row + 1, :]

    def layer_vecs(at):
        sizes, rows, base = layers[at], dims.rows_of[at], dims.base[at]
        if sizes.hc * 2 == model:
            qv = r.vw[5, pl.ds(base + rows.qv + c, 1), :]
        else:
            both = vec_row(base + rows.qv)
            qv = jnp.where(c == 0, both[:, : 2 * sizes.hc], both[:, 2 * sizes.hc :])
        span = sizes.nc // model
        b1 = [r.vw[5, pl.ds(base + rows.b1 + c * span + s, 1), :] for s in range(span)]
        if sizes.pair:
            cut = 2 * sizes.nr
            b1 = [jnp.concatenate([jnp.where(half == 0, v[:, :cut], v[:, cut:]) for v in b1], axis=1)]
        found = types.SimpleNamespace(bq=qv[:, : sizes.hc], bv=qv[:, sizes.hc :], b1=b1)
        for name, row in vars(rows).items():
            if not hasattr(found, name):
                setattr(found, name, vec_row(base + row))
        return found

    kept = lay
    wa = [one_layer.wa for one_layer in lay]
    weights = [one_layer.w for one_layer in lay]

    def order_rows(at, part):
        gathered, whole = lay[at].ga, wa[at]
        cols = slice(part * model, (part + 1) * model)
        rows = gathered.shape[3] // 2
        span = DEPTH * 2 * rows
        for y_at in range(SIDE):
            for z_at in range(DEPTH):
                left = gathered[y_at, z_at, 0, :, cols].astype(F32)
                right = gathered[y_at, z_at, 1, :, cols].astype(F32)
                for core in range(SIDE):
                    own = slice(core * rows, (core + 1) * rows)
                    both = jnp.concatenate([left[own], right[own]], axis=0).astype(BF)
                    begin = (y_at * SIDE + core) * span + z_at * 2 * rows
                    whole[begin : begin + 2 * rows, cols] = both

    def store_grad_rows(at, y_at, value, cols):
        blocks = lay[at].ga
        rows = blocks.shape[3] // 2
        span = DEPTH * 2 * rows
        for z_at in range(DEPTH):
            for x_at in range(SIDE):
                begin = (z_at * 2 + x_at) * rows
                both = [value[begin : begin + rows], value[span + begin : span + begin + rows]]
                blocks[y_at, z_at, x_at, :, cols] = jnp.concatenate(both, axis=0).astype(BF)

    def head_kv(at, h):
        sizes, kv = layers[at], kept[at].kv
        k = kv[:, :, h * HEAD : (h + 1) * HEAD].reshape(seq, HEAD)
        v = kv[:, :, sizes.hc + h * HEAD : sizes.hc + (h + 1) * HEAD].reshape(seq, HEAD)
        return k, v

    def attention(at):
        sizes, keep = layers[at], kept[at]
        lane = lax.broadcasted_iota(jnp.int32, (1, model), 1)
        first_lane = (y * SIDE + row_core) * group + x
        entry = vec_row(dims.length_row)
        entry = jnp.where(lane == first_lane, 256.0 * entry, jnp.where(lane == first_lane + 2, entry, 0.0))
        length = jnp.sum(entry, axis=1, keepdims=True)
        valid = lax.broadcasted_iota(jnp.int32, (1, seq), 1).astype(F32) < length
        for h in range(sizes.heads):
            q = keep.q[:, h * HEAD : (h + 1) * HEAD]
            k, v = head_kv(at, h)
            scores = jnp.where(valid, mm(q, k, 1, 1) * 0.125, NEGATIVE)
            exponent = jnp.exp(scores - jnp.max(scores, axis=1, keepdims=True))
            low = (exponent * (1.0 / jnp.sum(exponent, axis=1, keepdims=True))).astype(BF)
            keep.a[h] = low
            begin = sizes.pad + h * HEAD
            keep.ctx[:, begin : begin + HEAD] = mm(low, v, 1, 0).astype(BF)

    def attention_back(at, grad_ctx):
        sizes, keep = layers[at], kept[at]
        dkv, dq = lay[at].dkv, lay[at].dq
        for h in range(sizes.heads):
            q = keep.q[:, h * HEAD : (h + 1) * HEAD]
            k, v = head_kv(at, h)
            begin = sizes.pad + h * HEAD
            dc = grad_ctx[:, begin : begin + HEAD]
            low = keep.a[h]
            a = low.astype(F32)
            da = mm(dc, v, 1, 1)
            inner = jnp.sum(a * da, axis=1, keepdims=True)
            ds = (0.125 * a * (da - inner)).astype(BF)
            dq[:, h * HEAD : (h + 1) * HEAD] = mm(ds, k, 1, 0).astype(BF)
            dk = mm(ds, q, 0, 0).astype(BF).reshape(2, tok, HEAD)
            dv = mm(low, dc, 0, 0).astype(BF).reshape(2, tok, HEAD)
            dkv[:, :, h * HEAD : (h + 1) * HEAD] = dk
            dkv[:, :, sizes.hc + h * HEAD : sizes.hc + (h + 1) * HEAD] = dv

    def block(at, which, b):
        sizes = layers[at]
        w = weights[at][which, b * sizes.zb : (b + 1) * sizes.zb]
        return w.reshape(model, model)

    def up(at, side):
        sizes, keep = layers[at], kept[at]
        for b in range(sizes.nl // model):
            cols = slice(b * model, (b + 1) * model)
            u = mm(keep.hb[side], block(at, 0, b), 1, 1) + vecs[at].b1[b]
            phi = 0.5 * (1.0 + lax.erf(u * 0.7071067811865476))
            keep.g[side, :, cols] = (u * phi).astype(BF)
            density = jnp.exp(u * u * -0.5) * 0.3989422804014327
            keep.gp[side, :, cols] = (phi + u * density).astype(BF)

    def times_block(at, which, side):
        sizes, keep = layers[at], kept[at]
        total = None
        for b in range(sizes.nl // model):
            term = mm(keep.g[side, :, b * model : (b + 1) * model], block(at, which, b), 1, 0)
            total = term if total is None else total + term
        return total

    def weight_grad(at, which, right):
        sizes, keep = layers[at], kept[at]
        span = model // 2
        zb = sizes.zb // 2
        rows = sizes.sides * tok
        wide = right[...].reshape(rows, model)
        for b in range(sizes.nl // span):
            left = keep.g[:, :, b * span : (b + 1) * span].reshape(rows, span)
            value = mm(left, wide, 0, 0).astype(BF)
            keep.dw[which, b * zb : (b + 1) * zb] = value.reshape(zb, 2, sizes.nr, model)


    def pack_a(at):
        sizes, width = layers[at], 2 * layers[at].hc
        rows_in = lay[at].pai[...].astype(F32)
        rows_out = lay[at].pao[...].astype(F32)
        halves = []
        for h in range(2):
            own = slice(h * sizes.hc, (h + 1) * sizes.hc)
            pieces = [rows_in[:, p * width : (p + 1) * width][:, own] for p in (1, 2, 0)]
            halves.append(jnp.concatenate(pieces + [rows_out[:, own]], axis=1))
        send = lay[at].asend
        send[...] = jnp.where(c == 0, halves[1], halves[0])
        if at == 0:
            pl.semaphore_wait(bar, PARTNERS)
        push(send, lay[at].ar, r.is_.at[2 * at], r.ir.at[2 * at], sib)
        return jnp.where(c == 0, halves[0], halves[1])

    def pack_f(at):
        sizes = layers[at]
        first = lay[at].pfi[...].astype(F32).T
        second = lay[at].pfo[...].astype(F32)
        if dims.turned[at]:
            second = second.T
        send, own = lay[at].fsend, []
        for which, value in enumerate((first, second)):
            low_half, high_half = value[: sizes.nr], value[sizes.nr :]
            own.append(jnp.where(c == 0, low_half, high_half))
            send[which] = jnp.where(c == 0, high_half, low_half).astype(BF)
        push(send, lay[at].fr, r.is_.at[2 * at + 1], r.ir.at[2 * at + 1], sib)
        return own

    def prepare_a(at, own):
        land, blocks = lay[at].ar, lay[at].ga
        arrived(land, r.ir.at[2 * at], r.is_.at[2 * at])
        other = land[...]
        pair = [jnp.where(c == 0, own, other), jnp.where(c == 0, other, own)]
        blocks[y, z, x] = jnp.concatenate(pair, axis=0).astype(BF)

    def prepare_f(at, own):
        land = lay[at].fr
        arrived(land, r.ir.at[2 * at + 1], r.is_.at[2 * at + 1])
        lanes = pl.ds(pl.multiple_of(y * half_lanes, 128), half_lanes)
        for which in range(2):
            other = land[which].astype(F32)
            pair = [jnp.where(c == 0, own[which], other), jnp.where(c == 0, other, own[which])]
            weights[at][which, z_own if layers[at].pair else z, x, :, lanes] = jnp.concatenate(pair, axis=1).astype(BF)

    group = dims.group
    per_row = model // group
    index = dp * DEPTH * SIDE + mp

    def targets(at_group):
        result, begin = jnp.full_like(at_group, dims.length_row * per_row) + dp, 0
        for at, sizes in enumerate(layers):
            base = dims.base[at] * per_row
            head, count_b = sizes.hc // group, sizes.nr // group
            up_at = dims.rows_of[at].b1 * per_row
            count = dims.shift_groups[at]
            g = index * count + (at_group - begin)
            w = g % (2 * head)
            qv = (w // head) * (2 * head) + (g // (2 * head)) * head + w % head
            b = g - up_at
            up_to = up_at + ((b % (2 * count_b)) // count_b) * (8 * count_b)
            up_to = up_to + (b // (2 * count_b)) * count_b + b % count_b
            place = jnp.where(g < 4 * head, qv, jnp.where((b >= 0) & (b < 16 * count_b), up_to, g))
            inside = (at_group >= begin) & (at_group < begin + count)
            result = jnp.where(inside, base + place, result)
            begin += count
            count = dims.gain_groups[at]
            place = dims.rows_of[at].g1 * per_row + index * count + (at_group - begin)
            inside = (at_group >= begin) & (at_group < begin + count)
            result = jnp.where(inside, base + place, result)
            begin += count
        return result // per_row, result % per_row

    groups = dims.vec_rows
    lane_group = lax.broadcasted_iota(jnp.int32, (groups, dims.lanes), 1) // group
    lane_own = lane_group == lax.broadcasted_iota(jnp.int32, (groups, dims.lanes), 0)

    def place_masks():
        down = lax.broadcasted_iota(jnp.int32, (groups, 1), 0)
        across = lax.broadcasted_iota(jnp.int32, (1, groups), 1)
        row_down, place_down = targets(down)
        row_across, _ = targets(across)
        lane = lax.broadcasted_iota(jnp.int32, (groups, model), 1) // group
        to_row = jnp.where(row_across == down, 1.0, 0.0).astype(BF)
        from_row = jnp.where(row_down == across, 1.0, 0.0).astype(BF)
        return lane == place_down, to_row, from_row

    def pack_vectors():
        lengths = r.len[...].astype(F32).reshape(1, 2) * jnp.where(mp == 0, 1.0, 0.0)
        high = jnp.floor(lengths * (1.0 / 256.0))
        pieces = []
        for own in lay:
            pieces += [own.psh[...].astype(F32).reshape(1, -1), own.pga[...].astype(F32).reshape(1, -1)]
        pieces += [high, lengths - 256.0 * high]
        used = sum(p.shape[1] for p in pieces)
        values = jnp.concatenate(pieces + [jnp.zeros((1, dims.lanes - used), F32)], axis=1)
        spread_out = jnp.where(lane_own, values, 0.0).astype(BF)
        i = lax.broadcasted_iota(jnp.int32, (dims.lanes, model), 0) % group
        j = lax.broadcasted_iota(jnp.int32, (dims.lanes, model), 1) % group
        r.hot[...] = jnp.where(i == j, 1.0, 0.0).astype(BF)
        in_place, to_row, _ = place_masks()
        wide = jnp.where(in_place, mm(spread_out, r.hot[...], 1, 0), 0.0).astype(BF)
        return mm(to_row, wide, 1, 0)

    def unpack_vectors(values):
        in_place, _, from_row = place_masks()
        total, rest = None, values
        for _ in range(3):
            low_part = rest.astype(BF)
            rest = rest - low_part.astype(F32)
            wide = jnp.where(in_place, mm(from_row, low_part, 1, 0), 0.0).astype(BF)
            term = jnp.where(lane_own, mm(wide, r.hot[...], 1, 1), 0.0)
            total = term if total is None else total + term
        return rowsum(total)

    vecs = []
    block_shape = (4, tok // 4, model)

    def tokens(at, side):
        return kept[at].xb[side].reshape(tok, model)

    def project_kv(at, side):
        sizes, keep = layers[at], kept[at]
        kv = mm(tokens(at, side), wa[at][:, : 2 * sizes.hc], 1, 0)
        keep.kv[side, :, : sizes.hc] = kv[:, : sizes.hc].astype(BF)
        keep.kv[side, :, sizes.hc :] = (kv[:, sizes.hc :] + vecs[at].bv).astype(BF)

    def project_q(at):
        sizes, keep = layers[at], kept[at]
        q = mm(tokens(at, half), wa[at][:, 2 * sizes.hc : 2 * sizes.hc + sizes.qw], 1, 0)
        keep.q[...] = (q[:, : sizes.hc] + vecs[at].bq).astype(BF)

    def attend_out(at):
        return mm(kept[at].ctx[...], wa[at][:, layers[at].start :], 1, 1)

    def norm_one(at, base, branch):
        keep, v = kept[at], vecs[at]
        normed, scale = normalize(base + branch + v.bo)
        keep.n1[...] = normed
        keep.s1[...] = scale
        result = normed * v.g1 + v.beta1
        keep.hb[half if layers[at].pair else 0] = result.astype(BF)
        return result

    def norm_two(at, base, branch):
        keep, v = kept[at], vecs[at]
        normed, scale = normalize(base + branch + v.b2)
        keep.n2[...] = normed
        keep.s2[...] = scale
        return normed * v.g2 + v.beta2

    if layers[1].pad:
        kept[1].ctx[...] = jnp.zeros_like(kept[1].ctx)
        lay[1].dq[...] = jnp.zeros_like(lay[1].dq)
    for copy in fetched[:2]:
        copy.wait()
    own_a0 = pack_a(0)
    prepare_a(0, own_a0)
    gather(0, 0)
    for copy in fetched[3:5]:
        copy.wait()
    own_f0 = pack_f(0)
    for copy in fetched[5:]:
        copy.wait()
    own_a1 = pack_a(1)
    r.vw[0] = pack_vectors()
    gather(0, 1)
    fetched[2].wait()
    spread(r.hid, kept[0].xb.at[lax.rem(z // 2, 2)], r.hs, r.hr)
    total_step(r.vw, r.vl, 0, r.vs, r.vr)
    total_add(r.vw, r.vl, 0, r.vs, r.vr)
    total_step(r.vw, r.vl, 1, r.vs, r.vr)
    prepare_a(1, own_a1)
    gather(1, 0)
    gather(0, 2)
    gather(1, 1)
    total_add(r.vw, r.vl, 1, r.vs, r.vr)
    prepare_f(0, own_f0)
    own_f1 = pack_f(1)
    spread_turn(r.hid, kept[0].xb.at[half], r.hs, r.hr, r.os.at[0], r.os.at[1])
    spread_end(kept[0].xb.at[half], r.os.at[0], r.os.at[1])
    total_step(r.vw, r.vl, 2, r.vs, r.vr)
    gather(2, 0)
    gather(1, 2)
    share_hid = Share(kept[0].xb, 2)
    total_add(r.vw, r.vl, 2, r.vs, r.vr)
    gather(0, 3)
    prepare_f(1, own_f1)
    gather(3, 0)
    total_step(r.vw, r.vl, 3, r.vs, r.vr)
    gather(1, 3)
    total_add(r.vw, r.vl, 3, r.vs, r.vr)
    gather(2, 1)
    total_step(r.vw, r.vl, 4, r.vs, r.vr)
    share_hid.turn()
    gather(3, 1)
    gather(4, 0)
    share_hid.end()
    gather(0, 4)
    total_add(r.vw, r.vl, 4, r.vs, r.vr)
    vecs.extend([layer_vecs(0), layer_vecs(1)])
    order_rows(0, 0)
    project_kv(0, half)
    gather(1, 4)
    order_rows(0, 1)
    project_q(0)
    project_kv(0, 1 - half)
    gather(5, 0)
    attention(0)
    gather(4, 1)
    spread(r.cot, r.cin, r.cs, r.cr)
    gather(2, 2)
    branch = exchange(attend_out(0))
    branch = branch()
    gather(5, 1)
    normed = norm_one(0, tokens(0, half).astype(F32), branch)
    share_normed = Share(kept[0].hb, 0)
    gather(3, 2)
    gather(2, 3)
    gather(6, 0)
    gather(4, 2)
    up(0, half)
    share_normed.turn()
    gather(3, 3)
    share_normed.end()
    up(0, 1 - half)
    gather(6, 1)
    gather(5, 2)
    down = Fold(lambda side, own: times_block(0, 1, side), 0)
    down.keep()
    down.cross()
    gather(4, 3)
    down.turn()
    spread_turn(r.cot, r.cin, r.cs, r.cr, r.os.at[2], r.os.at[3])
    gather(6, 2)
    branch = down.end()
    middle = norm_two(0, normed, branch)
    kept[1].xb[half] = middle.astype(BF).reshape(block_shape)
    share_middle = Share(kept[1].xb, 3)
    gather(4, 4)
    order_rows(1, 0)
    project_kv(1, half)
    project_q(1)
    gather(5, 3)
    share_middle.turn()
    share_middle.end()
    project_kv(1, 1 - half)
    spread_end(r.cin, r.os.at[2], r.os.at[3])
    attention(1)
    gather(6, 3)
    branch = exchange(attend_out(1))
    branch = branch()
    gather(5, 4)
    normed = norm_one(1, middle, branch)
    up(1, 0)
    gather(6, 4)
    branch = exchange(times_block(1, 1, 0))
    branch = branch()
    final = norm_two(1, normed, branch)
    r.oblk[...] = final.astype(BF).reshape(r.oblk.shape)
    collect(r.oblk, r.oland, r.ys, r.yr)
    wait_sent()

    r.vw[0] = jnp.zeros_like(r.vw[0])
    once = jnp.where(c == 0, 1.0, 0.0)

    def put_vec(at, name, value):
        row = dims.base[at] + getattr(dims.rows_of[at], name)
        r.vw[0, row : row + 1, :] = value * once

    def back_two(at, grad):
        keep, v = kept[at], vecs[at]
        n2 = keep.n2[...]
        put_vec(at, "g2", rowsum(grad * n2))
        put_vec(at, "beta2", rowsum(grad))
        dz2 = normalize_back(grad * v.g2, n2, keep.s2[...])
        low_dz2 = dz2.astype(BF)
        keep.eo[half if layers[at].pair else 0] = low_dz2
        put_vec(at, "b2", rowsum(low_dz2.astype(F32)))
        return dz2

    def back_up(at):
        sizes, keep = layers[at], kept[at]
        base = dims.base[at] + dims.rows_of[at].b1
        span, sums = sizes.nc // model, []
        for b in range(sizes.nl // model):
            cols = slice(b * model, (b + 1) * model)
            total = None
            for side in range(sizes.sides):
                dg = mm(keep.eo[side], block(at, 1, b), 1, 1)
                du = (dg * keep.gp[side, :, cols].astype(F32)).astype(BF)
                keep.g[side, :, cols] = du
                term = rowsum(du.astype(F32))
                total = term if total is None else total + term
            sums.append(total)
        if sizes.pair:
            cut = 2 * sizes.nr
            blank = jnp.zeros((1, cut), F32)
            pieces = [sums[0][:, b * cut : (b + 1) * cut] for b in range(span)]
            sums = [
                jnp.concatenate([jnp.where(half == 0, p, blank), jnp.where(half == 0, blank, p)], axis=1)
                for p in pieces
            ]
        for b, total in enumerate(sums):
            r.vw[0, pl.ds(base + c * span + b, 1), :] = total

    def back_one(at, grad):
        keep, v = kept[at], vecs[at]
        n1 = keep.n1[...]
        put_vec(at, "g1", rowsum(grad * n1))
        put_vec(at, "beta1", rowsum(grad))
        dz1 = normalize_back(grad * v.g1, n1, keep.s1[...])
        r.eo[...] = dz1.astype(BF)
        put_vec(at, "bo", rowsum(r.eo[...].astype(F32)))
        grad_ctx = mm(r.eo[...], wa[at][:, layers[at].start :], 1, 0).astype(BF)
        return dz1, grad_ctx

    def bias_sums(at):
        sizes, dkv, dq = layers[at], lay[at].dkv, lay[at].dq
        qsum = rowsum(dq[:, : sizes.hc].astype(F32))
        vsum = rowsum(dkv[:, :, sizes.hc :].reshape(seq, sizes.hc).astype(F32))
        both = jnp.concatenate([qsum, vsum], axis=1)
        row = dims.base[at] + dims.rows_of[at].qv
        if 2 * sizes.hc == model:
            r.vw[0, pl.ds(row + c, 1), :] = both
        else:
            blank = jnp.zeros_like(both)
            left, right = jnp.where(c == 0, both, blank), jnp.where(c == 0, blank, both)
            r.vw[0, row : row + 1, :] = jnp.concatenate([left, right], axis=1)

    def projection_grad(at, part):
        sizes, keep = layers[at], kept[at]
        begin, end = part * model, (part + 1) * model
        for y_at in range(SIDE):
            rows = slice(y_at * half_lanes, (y_at + 1) * half_lanes)
            pieces = []
            if begin == 0:
                every_token = keep.xb[:, :, :, rows].reshape(seq, half_lanes)
                grads = keep.dkv[...].reshape(seq, 2 * sizes.hc)
                pieces.append(mm(every_token, grads, 0, 0))
            if end > 2 * sizes.hc:
                own = keep.xb[half, :, :, rows].reshape(tok, half_lanes)
                query = mm(own, keep.dq[...], 0, 0)
                output = mm(r.eo[:, rows], keep.ctx[...], 0, 0)
                if sizes.pad:
                    apart = sizes.start - 2 * sizes.hc
                    pieces += [query[:, :apart], query[:, apart:] + output]
                else:
                    pieces += [query, output]
            value = pieces[0] if len(pieces) == 1 else jnp.concatenate(pieces, axis=1)
            store_grad_rows(at, y_at, value, slice(begin, end))

    def back_hidden(at, side, own):
        sizes, keep = layers[at], kept[at]
        total = mm(keep.dkv[side], wa[at][:, : 2 * sizes.hc], 1, 1)
        if own:
            begin = 2 * sizes.hc
            total = total + mm(keep.dq[...], wa[at][:, begin : begin + keep.dq.shape[1]], 1, 1)
        return total

    grad = r.cin[...].reshape(tok, model).astype(F32)
    dz2 = back_two(1, grad)
    weight_grad(1, 1, kept[1].eo)
    reduce(6, 0)
    back_up(1)
    branch = exchange(times_block(1, 0, 0))
    weight_grad(1, 0, kept[1].hb)
    reduce(5, 0)
    branch = branch()
    dz1, grad_ctx = back_one(1, dz2 + branch)
    attention_back(1, grad_ctx)
    down = Fold(lambda side, own: back_hidden(1, side, own), 2)
    down.keep()
    down.cross()
    reduce(6, 1)
    projection_grad(1, 0)
    bias_sums(1)
    reduce(4, 0)
    down.turn()
    branch = down.end()
    dz2 = back_two(0, dz1 + branch)
    share_grad = Share(kept[0].eo, 1)
    reduce(5, 1)
    reduce(4, 1)
    share_grad.turn()
    share_grad.end()
    weight_grad(0, 1, kept[0].eo)
    reduce(3, 0)
    back_up(0)
    weight_grad(0, 0, kept[0].hb)
    reduce(2, 0)
    up_back = Fold(lambda side, own: times_block(0, 0, side), 1)
    up_back.keep()
    reduce(3, 1)
    up_back.cross()
    reduce(2, 1)
    reduce(6, 2)
    reduce(5, 2)
    up_back.turn()
    collect_done(r.oblk, r.oland, r.ys, r.yr)
    store(r.oland, outs.out)
    branch = up_back.end()
    dz1, grad_ctx = back_one(0, dz2 + branch)
    attention_back(0, grad_ctx)
    reduce(6, 3)
    projection_grad(0, 1)
    reduce(1, 0)
    projection_grad(0, 0)
    bias_sums(0)
    total_step(r.vw, r.vl, 0, r.ws, r.wr)
    reduce(4, 2)
    reduce(0, 0)
    total_add(r.vw, r.vl, 0, r.ws, r.wr)
    reduce(3, 2)
    to_hidden = Fold(lambda side, own: back_hidden(0, side, own), 3)
    reduce(6, 4)
    total_step(r.vw, r.vl, 1, r.ws, r.wr)
    to_hidden.keep()
    to_hidden.cross()
    reduce(1, 1)
    total_add(r.vw, r.vl, 1, r.ws, r.wr)
    total_step(r.vw, r.vl, 2, r.ws, r.wr)
    reduce(2, 2)
    to_hidden.turn()
    reduce(0, 1)
    reduce(5, 3)
    reduce(1, 2)
    total_add(r.vw, r.vl, 2, r.ws, r.wr)
    reduce(4, 3)
    reduce(2, 3)
    reduce(1, 3)
    reduce(3, 3)
    total_step(r.vw, r.vl, 3, r.ws, r.wr)
    reduce(0, 2)
    reduce(0, 3)
    branch = to_hidden.end()
    reduce(1, 4)
    total_add(r.vw, r.vl, 3, r.ws, r.wr)
    reduce_out(6)
    reduce(5, 4)
    reduce_out(1)
    reduce(4, 4)
    reduce_out(2)
    total_step(r.vw, r.vl, 4, r.ws, r.wr)
    reduce_out(5)
    reduce_out(3)
    reduce_out(4)
    r.gblk[...] = (dz1 + branch).astype(BF).reshape(r.gblk.shape)
    collect(r.gblk, r.gland, r.zs, r.zr)
    reduce(0, 4)
    reduce_out(0)
    total_add(r.vw, r.vl, 4, r.ws, r.wr)
    r.dvec[...] = unpack_vectors(r.vw[5])
    store(r.dvec, outs.dvec)
    collect_done(r.gblk, r.gland, r.zs, r.zr)
    store(r.gland, outs.gh)
    wait_sent()
    for copy in stored:
        copy.wait()


def fused_call(hid, cot, lengths, params, dims):
    model, tok, seq = dims.model, dims.tok, dims.seq
    block = (4, tok // 4, model)
    vmem = pltpu.VMEM
    dma = pltpu.SemaphoreType.DMA
    rows_in = params[0][0].shape[0]
    shape = jax.ShapeDtypeStruct
    given = dict(hid=hid, cot=cot, len=lengths, lay=[])
    outs = dict(out=shape(hid.shape, BF), gh=shape(hid.shape, BF), lay=[], dvec=shape((1, dims.lanes), F32))
    for (ai, ao, fi, fo, sh, ga), sizes in zip(params, dims.layers):
        given["lay"].append(dict(pai=ai, pao=ao, pfi=fi, pfo=fo, psh=sh, pga=ga))
        outs["lay"].append(
            dict(
                da=shape((2, rows_in, sizes.wide), F32),
                df=shape((2, 2, sizes.nr, model // 4), F32),
            )
        )
    as_scratch = lambda tree: jax.tree.map(lambda v: vmem(v.shape, v.dtype), tree)
    held, made = as_scratch(given), as_scratch({key: outs[key] for key in ("lay", "dvec")})
    vec = (dims.vec_rows, model)
    rows_a = 2 * rows_in
    counts = [sum(chunk[0] == kind for chunk in dims.chunks) for kind in "AFP"]
    half = model // 2
    n = len(dims.chunks)
    scratch = dict(
        cin=vmem(block, BF),
        oblk=vmem(block, BF),
        gblk=vmem(block, BF),
        oland=vmem(hid.shape, BF),
        gland=vmem(hid.shape, BF),
        vw=vmem((6,) + vec, F32),
        vl=vmem((5,) + vec, F32),
        xs=vmem((2, tok, model), BF),
        xr=vmem((2, tok, model), BF),
        eo=vmem((tok, model), BF),
        px=vmem((4, tok, model), BF),
        prx=vmem((4, tok // 2, model), BF),
        pz=vmem((4, tok // 2, model), BF),
        pzr=vmem((4, 2, tok // 2, model), BF),
        ps=dma((4, 5)),
        pr=dma((4, 5)),
        hot=vmem((dims.lanes, model), BF),
        gs=dma((n, 20)),
        gr=dma((n, 20)),
        ss=dma((n, 20)),
        sr=dma((n, 20)),
        fs=dma((n,)),
        fr=dma((n,)),
        vs=dma((5,)),
        vr=dma((5,)),
        ws=dma((5,)),
        wr=dma((5,)),
        hs=dma((4,)),
        hr=dma((4,)),
        cs=dma((4,)),
        cr=dma((4,)),
        ys=dma((4,)),
        yr=dma((4,)),
        zs=dma((4,)),
        zr=dma((4,)),
        is_=dma((4,)),
        ir=dma((4,)),
        os=dma((4,)),
        es=dma((2,)),
        er=dma((2,)),
        ins=dma((16,)),
        outs=dma((10,)),
        red=[],
        lay=[],
    )
    rows_f, rows_p = dims.unit_rows["F"], dims.unit_rows["P"]
    for count, rows, wide, pair, shard, kind in (
        (counts[0], rows_a, model, (2, 4, 16, model), (rows_in, model), "A"),
        (counts[1], rows_f, half, (4, 16, model), (rows_f, half // 2), "F"),
    ):
        line = pair[:-3] + (1, 16, model)
        rows -= 0 if kind in dims.whole else 32
        scratch["red"].append(
            dict(
                ad=vmem((count, 2, 2, rows, wide), BF),
                an=vmem((count, 2, 4, rows, wide), BF),
                az=vmem((count, 4, 1, rows, wide), BF),
                by=vmem((count, 4, 2, 16, wide), BF),
                bz=vmem((count, 4, 1, 2, 16, wide), BF),
                bx=vmem((count, 1, 16, wide), BF),
                cx=vmem((count,) + pair, BF),
                cz=vmem((count, 4) + line, BF),
                cy=vmem((count, 1, 16, wide), BF),
                fsend=vmem((count,) + shard, F32),
                fland=vmem((count,) + shard, F32),
            )
        )
    scratch["red"].append(
        dict(
            ad=vmem((counts[2], 2, 1, rows_p, half), BF),
            an=vmem((counts[2], 2, 2, rows_p, half), BF),
            az=vmem((counts[2], 1, rows_p, half), BF),
            fsend=vmem((counts[2], rows_p, half // 2), F32),
            fland=vmem((counts[2], rows_p, half // 2), F32),
        )
    )
    for sizes in dims.layers:
        scratch["lay"].append(
            dict(
                ar=vmem((rows_in, sizes.wide), F32),
                asend=vmem((rows_in, sizes.wide), F32),
                fr=vmem((2, sizes.nr, model // 4), BF),
                fsend=vmem((2, sizes.nr, model // 4), BF),
                ga=vmem((SIDE, DEPTH, SIDE, rows_a, sizes.wide), BF),
                wa=vmem((model, sizes.wide), BF),
                w=vmem((2, sizes.zs, SIDE, sizes.nr, model), BF),
                dw=vmem((2, sizes.zs, SIDE, sizes.nr, model), BF),
                xb=vmem((2,) + block, BF),
                q=vmem((tok, sizes.hc), BF),
                kv=vmem((2, tok, 2 * sizes.hc), BF),
                a=vmem((sizes.heads, tok, seq), BF),
                ctx=vmem((tok, sizes.wide - sizes.start), BF),
                n1=vmem((tok, model), F32),
                s1=vmem((tok, 1), F32),
                hb=vmem((sizes.sides, tok, model), BF),
                eo=vmem((sizes.sides, tok, model), BF),
                g=vmem((sizes.sides, tok, sizes.nl), BF),
                gp=vmem((sizes.sides, tok, sizes.nl), BF),
                n2=vmem((tok, model), F32),
                s2=vmem((tok, 1), F32),
                dkv=vmem((2, tok, 2 * sizes.hc), BF),
                dq=vmem((tok, 2 * sizes.hc if sizes.pad else sizes.hc), BF),
            )
        )
    inputs, outputs = jax.tree.leaves(given), jax.tree.leaves(outs)
    whole = pl.BlockSpec(memory_space=pl.ANY)
    local = (scratch, held, made)
    values = pl.pallas_call(
        functools.partial(fused_kernel, dims, jax.tree.structure((given, outs) + local)),
        out_shape=outputs,
        in_specs=[whole] * len(inputs),
        out_specs=[whole] * len(outputs),
        scratch_shapes=jax.tree.leaves(local),
        compiler_params=pltpu.CompilerParams(
            collective_id=0, has_side_effects=True, vmem_limit_bytes=dims.vmem
        ),
        name="layers",
    )(*inputs)
    return jax.tree.unflatten(jax.tree.structure(outs), values)


def finish_kernel(dims, tree, *refs):
    given, (out, gh, *results) = jax.tree.unflatten(tree, refs)
    r = named(given)
    out[...] = r.out[...]
    gh[...] = r.gh[...].astype(F32)
    begin = 0
    for at, sizes in enumerate(dims.layers):
        attn, ffn = r.lay[at].da, r.lay[at].df
        to_ai, to_ao, to_fi, to_fo, to_sh, to_ga = results[6 * at : 6 * at + 6]
        for p in range(3):
            for h in range(2):
                to = (2 * ((p + 1) % 3) + h) * sizes.hc
                to_ai[:, to : to + sizes.hc] = attn[h, :, p * sizes.hc : (p + 1) * sizes.hc]
        for h in range(2):
            to_ao[:, h * sizes.hc : (h + 1) * sizes.hc] = attn[h, :, 3 * sizes.hc :]
        down = ffn[:, 1].reshape(2 * sizes.nr, ffn.shape[3])
        to_fo[...] = down.T if dims.turned[at] else down
        to_fi[...] = ffn[:, 0].reshape(2 * sizes.nr, ffn.shape[3]).T
        for ref in (to_sh, to_ga):
            ref[...] = r.dvec[0, begin : begin + ref.shape[0]]
            begin += ref.shape[0]


def finish_call(given, params, dims):
    leaves, tree = jax.tree.flatten(given)
    outs = [jax.ShapeDtypeStruct(given["out"].shape, d) for d in (BF, F32)]
    outs += [jax.ShapeDtypeStruct(p.shape, F32) for shards in params for p in shards]
    whole = pl.BlockSpec(memory_space=pltpu.VMEM)
    return pl.pallas_call(
        functools.partial(finish_kernel, dims, jax.tree.structure((given, outs))),
        out_shape=outs,
        in_specs=[whole] * len(leaves),
        out_specs=[whole] * len(outs),
        compiler_params=pltpu.CompilerParams(vmem_limit_bytes=dims.vmem),
        name="finish",
    )(*leaves)


def make_dims(hidden_in, teacher, student):
    model = hidden_in.shape[2]
    layers = [
        layer_sizes(model, p[0].shape[1] // 3, p[2].shape[1] * DEPTH * SIDE, pair)
        for p, pair in ((teacher, True), (student, False))
    ]
    rows = layers[1].nr
    chunks = []
    for at, sizes in enumerate(layers):
        chunks += [("A", at, 0, part) for part in range(sizes.wide // model)]
        for which in (0, 1):
            kind, count = ("P", 1) if sizes.pair else ("F", sizes.nr // rows)
            chunks += [(kind, at, which, part) for part in range(count)]
    counts, slot = {"A": 0, "F": 0, "P": 0}, []
    for chunk in chunks:
        slot.append(counts[chunk[0]])
        counts[chunk[0]] += 1
    group = model // (SIDE * SIDE * DEPTH * SIDE)
    shift_groups = [p[4].shape[0] // group for p in (teacher, student)]
    gain_groups = [p[5].shape[0] // group for p in (teacher, student)]
    rows_of, base, at = [], [], 0
    for sizes in layers:
        found, count = vec_rows(model, sizes)
        rows_of.append(found)
        base.append(at)
        at += count
    return types.SimpleNamespace(
        model=model,
        tok=4 * hidden_in.shape[1],
        seq=8 * hidden_in.shape[1],
        layers=layers,
        chunks=chunks,
        slot=slot,
        rows=rows,
        whole='A',
        unit_rows={"A": 2 * teacher[0].shape[0], "F": rows, "P": layers[0].nr},
        rows_of=rows_of,
        base=base,
        length_row=at,
        vec_rows=(at + 8) // 8 * 8,
        turned=[p[3].shape[0] > p[3].shape[1] for p in (teacher, student)],
        group=group,
        lanes=(sum(shift_groups + gain_groups) * group + 4 + 127) // 128 * 128,
        shift_groups=shift_groups,
        gain_groups=gain_groups,
        vmem=63 * 2**20,
    )


def fast_body(hidden_in, cotangent, lengths, *shards):
    params = (shards[:6], shards[6:])
    dims = make_dims(hidden_in, *params)
    turn = lambda shards, turned: (shards[0], shards[1].T, shards[2], shards[3].T if turned else shards[3])
    params = [turn(p, turned) + p[4:] for p, turned in zip(params, dims.turned)]
    values = fused_call(hidden_in, cotangent, lengths, params, dims)
    out, grad_hidden, *grads = finish_call(values, params, dims)
    results = [out, grad_hidden]
    for at, turned in enumerate(dims.turned):
        own = tuple(grads[6 * at : 6 * at + 6])
        results += turn(own, turned) + own[4:]
    return tuple(results)


def body(axes, *args):
    rows, tokens, model = args[0].shape
    pair_fits = args[3 + 2].shape[1] * 2 == model
    fits = pair_fits and axes["dp"] == SIDE * SIDE and axes["mp"] == DEPTH * SIDE
    if fits and rows == 2 and tokens % 16 == 0 and model % 256 == 0:
        return fast_body(*args)
    return general_body(*args)


def general_body(
    hidden_in,
    cotangent,
    lengths,
    teacher_attn_in,
    teacher_attn_out,
    teacher_ffn_in,
    teacher_ffn_out,
    teacher_shifts,
    teacher_gains,
    student_attn_in,
    student_attn_out,
    student_ffn_in,
    student_ffn_out,
    student_shifts,
    student_gains,
):
    span_len = hidden_in.shape[1] * lax.axis_size("mp")
    positions = jnp.arange(span_len)
    valid_keys = positions[None, :] < lengths[:, None]
    teacher = fetch(
        teacher_attn_in,
        teacher_attn_out,
        teacher_ffn_in,
        teacher_ffn_out,
        teacher_shifts,
        teacher_gains,
    )
    student = fetch(
        student_attn_in,
        student_attn_out,
        student_ffn_in,
        student_ffn_out,
        student_shifts,
        student_gains,
    )
    middle, teacher_kept = forward_layer(hidden_in.astype(jnp.float32), teacher, valid_keys)
    final, student_kept = forward_layer(middle, student, valid_keys)
    grad_middle, student_grads = backward_layer(
        cotangent.astype(jnp.float32), student_kept, student, valid_keys
    )
    grad_input, teacher_grads = backward_layer(grad_middle, teacher_kept, teacher, valid_keys)
    teacher_totals = reduce_grads(teacher_grads)
    student_totals = reduce_grads(student_grads)
    return (final.astype(jnp.bfloat16), grad_input) + teacher_totals + student_totals


def solution(mesh):
    in_specs = (
        P("dp", "mp", None),
        P("dp", "mp", None),
        P("dp"),
        P(("dp", "mp"), None),
        P(None, ("dp", "mp")),
        P("dp", "mp"),
        P("mp", "dp"),
        P(("dp", "mp")),
        P(("dp", "mp")),
        P(("dp", "mp"), None),
        P(None, ("dp", "mp")),
        P("dp", "mp"),
        P("mp", "dp"),
        P(("dp", "mp")),
        P(("dp", "mp")),
    )
    out_specs = (
        P("dp", "mp", None),
        P("dp", "mp", None),
        P(("dp", "mp"), None),
        P(None, ("dp", "mp")),
        P("dp", "mp"),
        P("mp", "dp"),
        P(("dp", "mp")),
        P(("dp", "mp")),
        P(("dp", "mp"), None),
        P(None, ("dp", "mp")),
        P("dp", "mp"),
        P("mp", "dp"),
        P(("dp", "mp")),
        P(("dp", "mp")),
    )
    return jax.shard_map(
        functools.partial(body, dict(mesh.shape)), mesh=mesh, in_specs=in_specs, out_specs=out_specs, check_vma=False)
```
